32 devices in a mesh: seq: 4 (over y, x), fsdp: 8 (over z, core).
Axes of the slice: x: 2, y: 2, z: 4, core: 2. Of those that a mesh axis runs over, the one named last changes fastest.
Arguments:
- images: bfloat16 [16, 1024, 1024], P('fsdp', 'seq'), may hold values from -20 to 20
- out_grad: bfloat16 [16, 1024, 1024], P('fsdp', 'seq'), may hold values from -6 to 6
- lengths: int32 [16], P('fsdp'), may hold values from 512 to 1024, as said below
- images_held: int32 [8], replicated, may hold values from 1 to 2, as said below
- first_gain: bfloat16 [1024], P('fsdp'), may hold values from 0.5 to 1.5
- first_shift: bfloat16 [1024], P('fsdp'), may hold values from -4 to 4
- entry_weight: bfloat16 [1024, 3072], P('fsdp'), may hold values from -1 to 1
- entry_bias: bfloat16 [2048], P('fsdp'), may hold values from -6 to 6
- exit_weight: bfloat16 [1024, 1024], P('fsdp'), may hold values from -1.5 to 1.5
- exit_bias: bfloat16 [1024], P('fsdp'), may hold values from -4 to 4
- first_scale: bfloat16 [1024], P('fsdp'), may hold values from 0.5 to 2
- second_gain: bfloat16 [1024], P('fsdp'), may hold values from 0.5 to 1.5
- second_shift: bfloat16 [1024], P('fsdp'), may hold values from -4 to 4
- up_weight: bfloat16 [1024, 4096], P('fsdp'), may hold values from -0.1875 to 0.1875
- up_bias: bfloat16 [4096], P('fsdp'), may hold values from -6 to 6
- down_weight: bfloat16 [4096, 1024], P('fsdp'), may hold values from -0.09375 to 0.09375
- down_bias: bfloat16 [1024], P('fsdp'), may hold values from -4 to 4
- second_scale: bfloat16 [1024], P('fsdp'), may hold values from 0.5 to 2
Outputs:
- layer_out: bfloat16 [16, 1024, 1024], P('fsdp', 'seq')
- input_grad: float32 [16, 1024, 1024], P('fsdp', 'seq')
- first_gain_grad: float32 [1024], P('fsdp')
- first_shift_grad: float32 [1024], P('fsdp')
- entry_weight_grad: float32 [1024, 3072], P('fsdp')
- entry_bias_grad: float32 [2048], P('fsdp')
- exit_weight_grad: float32 [1024, 1024], P('fsdp')
- exit_bias_grad: float32 [1024], P('fsdp')
- first_scale_grad: float32 [1024], P('fsdp')
- second_gain_grad: float32 [1024], P('fsdp')
- second_shift_grad: float32 [1024], P('fsdp')
- up_weight_grad: float32 [1024, 4096], P('fsdp')
- up_bias_grad: float32 [4096], P('fsdp')
- down_weight_grad: float32 [4096, 1024], P('fsdp')
- down_bias_grad: float32 [1024], P('fsdp')
- second_scale_grad: float32 [1024], P('fsdp')
The draws below stay inside these ranges and needn't reach their ends.
Inputs may be any that keep to these rules, and one draw needn't show every extreme that they name: `images_held`: entry g is how many images fsdp group g holds; they fill its first slots. `lengths`: positions from the length on are padding.
All inputs are finite; a program needn't handle non-finite values.
Results may differ from the reference program's by a relative error of at most 0.017.
The reference program's roundings to bfloat16 on the way count: a program that leaves them out, or rounds other values in their place, can miss the bound.
Values may be sent and summed in bfloat16 or wider, within the bound.
A program may use at most 320 MiB of HBM per device.

```python
import math
import jax
import jax.numpy as jnp
from jax import lax

D = 1024
HEADS = 16
HEAD_DIM = 64
FF = 4096
MAX_LEN = 1024
SLOTS = 2
GROUPS = 8
IMAGES = 16
PAD_LEN = 1024


def two_picks(key, count):
    first_pick = jax.random.randint(jax.random.fold_in(key, 1), (), 0, count)
    offset = jax.random.randint(jax.random.fold_in(key, 2), (), 0, count - 1)
    second_pick = (first_pick + 1 + offset) % count
    return (first_pick, second_pick)


def draw_images(key, part):
    shape = (IMAGES, PAD_LEN, D)
    base_part = jax.random.normal(jax.random.fold_in(key, 11), shape, jnp.float32)
    return jnp.clip(base_part, -6.0, 6.0).astype(jnp.bfloat16)


def draw_entry_weight(key, part):
    drawn_part = jax.random.normal(jax.random.fold_in(key, 21), (D, 3 * D), jnp.float32)
    drawn_part = jnp.clip(drawn_part, -6.0, 6.0) * D ** (-0.5)
    return drawn_part.astype(jnp.bfloat16)


def draw_lengths(key, part):
    values = jax.random.randint(jax.random.fold_in(key, 31), (IMAGES,), MAX_LEN // 2, MAX_LEN + 1)
    first_pick, second_pick = two_picks(jax.random.fold_in(key, 32), IMAGES)
    return values.at[first_pick].set(MAX_LEN).at[second_pick].set(MAX_LEN // 2)


def draw_images_held(key, part):
    values = jax.random.randint(jax.random.fold_in(key, 41), (GROUPS,), 1, SLOTS + 1)
    first_pick, second_pick = two_picks(jax.random.fold_in(key, 42), GROUPS)
    return values.at[first_pick].set(SLOTS).at[second_pick].set(1)


def steps_of(key, shape, cuts, least, top_value):
    level, own = 1.0, jax.random.fold_in(key, 6)
    for axis_at, shards_of in cuts:
        steps = jnp.exp(jax.random.uniform(jax.random.fold_in(own, axis_at), (shards_of,), jnp.float32, least / len(cuts), top_value / len(cuts)))
        level = level * jnp.repeat(steps, shape[axis_at] // shards_of).reshape([-1 if axis == axis_at else 1 for axis in range(len(shape))])
    return level


def scatter_about(stream_key, shape, width, bound, pieces=(), held_as=jnp.bfloat16):
    drawn = width * jax.random.normal(stream_key, shape, jnp.float32)
    if pieces:
        drawn = drawn * steps_of(stream_key, shape, pieces, -0.22, 0.18)
    return jnp.clip(drawn, -bound, bound).astype(held_as)


def setup_inputs(seed: int = 0) -> dict:
    key_of = jax.random.split(jax.random.key(seed), 19)
    return {
        "images": draw_images(jax.random.fold_in(key_of[18], 71), 0),
        "out_grad": scatter_about(key_of[1], (IMAGES, PAD_LEN, D), 1.0, 6.0, ((0, 8), (1, 4))),
        "lengths": draw_lengths(jax.random.fold_in(key_of[18], 71), 0),
        "images_held": draw_images_held(jax.random.fold_in(key_of[18], 71), 0),
        "first_gain": jnp.clip(1.0 + 0.1 * jax.random.normal(key_of[4], (D,), jnp.float32), 0.5, 1.5).astype(jnp.bfloat16),
        "first_shift": scatter_about(key_of[5], (D,), 0.3, 4.0, ((0, 8),)),
        "entry_weight": draw_entry_weight(jax.random.fold_in(key_of[18], 71), 0),
        "entry_bias": scatter_about(key_of[7], (2 * D,), 0.5, 6.0, ((0, 8),)),
        "exit_weight": scatter_about(key_of[8], (D, D), (max(1, 16 * D // MAX_LEN)) ** -0.5, 1.5, ((0, 8),)),
        "exit_bias": scatter_about(key_of[9], (D,), 0.3, 4.0, ((0, 8),)),
        "first_scale": jnp.clip(jnp.exp(math.log(2.0) - 1.3862944 * jax.random.uniform(key_of[10], (D,), jnp.float32) ** steps_of(key_of[10], (D,), ((0, 8),), -0.2, 0.2)), 0.5, 2.0).astype(jnp.bfloat16),
        "second_gain": jnp.clip(1.0 + 0.1 * jax.random.normal(key_of[11], (D,), jnp.float32), 0.5, 1.5).astype(jnp.bfloat16),
        "second_shift": scatter_about(key_of[12], (D,), 0.3, 4.0, ((0, 8),)),
        "up_weight": scatter_about(key_of[13], (D, FF), D ** -0.5, 0.1875, ((0, 8),)),
        "up_bias": scatter_about(key_of[14], (FF,), 0.5, 6.0, ((0, 8),)),
        "down_weight": scatter_about(key_of[15], (FF, D), FF ** -0.5, 0.09375, ((0, 8),)),
        "down_bias": scatter_about(key_of[16], (D,), 0.3, 4.0, ((0, 8),)),
        "second_scale": jnp.clip(jnp.exp(math.log(2.0) - 1.3862944 * jax.random.uniform(key_of[17], (D,), jnp.float32) ** steps_of(key_of[17], (D,), ((0, 8),), -0.2, 0.2)), 0.5, 2.0).astype(jnp.bfloat16),
    }


EPSILON = 1e-06
NEG_LARGE = -1e+30

def rounded(values):
    return lax.optimization_barrier(values.astype(jnp.bfloat16))

def layer_norm(values):
    centre = lax.optimization_barrier(jnp.mean(values, axis=-1, keepdims=True))
    shifted = values - centre
    spread = lax.optimization_barrier(jnp.mean(shifted * shifted, axis=-1, keepdims=True))
    inverse = lax.rsqrt(spread + EPSILON)
    return (shifted * inverse, inverse)

def norm_back(normed_cot, normed, inverse):
    return inverse * (normed_cot - lax.optimization_barrier(jnp.mean(normed_cot, axis=-1, keepdims=True)) - normed * lax.optimization_barrier(jnp.mean(normed_cot * normed, axis=-1, keepdims=True)))

def gelu_parts(pre_act):
    cumul = 0.5 * (1.0 + lax.erf(pre_act * (1.0 / math.sqrt(2.0))))
    density = jnp.exp(-0.5 * pre_act * pre_act) * (1.0 / math.sqrt(2.0 * math.pi))
    return (pre_act * cumul, cumul + pre_act * density)

def score_rows(queries, key_rows, key_valid, score_scale):
    scores = jnp.einsum('qhd,khd->hqk', queries.astype(jnp.float32), key_rows.astype(jnp.float32)) * score_scale
    return jnp.where(key_valid[None, None, :], scores, NEG_LARGE)

def attend(queries, key_rows, value_rows, key_valid, score_scale):
    scores = score_rows(queries, key_rows, key_valid, score_scale)
    highest = lax.optimization_barrier(jnp.max(scores, axis=2, keepdims=True))
    logsum = highest + jnp.log(lax.optimization_barrier(jnp.sum(jnp.exp(scores - highest), axis=2, keepdims=True)))
    weights = rounded(jnp.exp(scores - logsum))
    attended = jnp.einsum('hqk,khd->qhd', weights.astype(jnp.float32), value_rows.astype(jnp.float32))
    return (rounded(attended), logsum)

def attend_back(queries, key_rows, value_rows, attended, attended_cot, logsum, key_valid, score_scale):
    scores = score_rows(queries, key_rows, key_valid, score_scale)
    probability = jnp.exp(scores - logsum)
    weights = rounded(probability)
    cot_wide = attended_cot.astype(jnp.float32)
    row_delta = lax.optimization_barrier(jnp.sum(attended.astype(jnp.float32) * cot_wide, axis=2))
    score_grad = jnp.einsum('qhd,khd->hqk', cot_wide, value_rows.astype(jnp.float32))
    score_cot = probability * (score_grad - jnp.transpose(row_delta)[:, :, None])
    scaled = rounded(score_cot * score_scale).astype(jnp.float32)
    query_cot = rounded(jnp.einsum('hqk,khd->qhd', scaled, key_rows.astype(jnp.float32)))
    key_cot = rounded(jnp.einsum('hqk,qhd->khd', scaled, queries.astype(jnp.float32)))
    value_cot = rounded(jnp.einsum('hqk,qhd->khd', weights.astype(jnp.float32), cot_wide))
    return (query_cot, key_cot, value_cot)

def reference(images, out_grad, lengths, images_held, first_gain, first_shift, entry_weight, entry_bias, exit_weight, exit_bias, first_scale, second_gain, second_shift, up_weight, up_bias, down_weight, down_bias, second_scale):
    score_scale = HEAD_DIM ** (-0.5)
    slot_ids = jnp.arange(IMAGES, dtype=jnp.int32)
    owners = (slot_ids // SLOTS).astype(jnp.int32)
    alive_slots = slot_ids % SLOTS < images_held[owners]
    gain_one = first_gain.astype(jnp.float32)
    shift_one = first_shift.astype(jnp.float32)
    query_bias = entry_bias[:D].astype(jnp.float32)
    value_bias = entry_bias[D:].astype(jnp.float32)
    exit_vec = exit_bias.astype(jnp.float32)
    scale_one = first_scale.astype(jnp.float32)
    gain_two = second_gain.astype(jnp.float32)
    shift_two = second_shift.astype(jnp.float32)
    up_vec = up_bias.astype(jnp.float32)
    down_vec = down_bias.astype(jnp.float32)
    scale_two = second_scale.astype(jnp.float32)
    positions = jnp.arange(PAD_LEN, dtype=jnp.int32)
    head_shape = (PAD_LEN, HEADS, HEAD_DIM)
    params = (first_gain, first_shift, entry_weight, entry_bias, exit_weight, exit_bias, first_scale, second_gain, second_shift, up_weight, up_bias, down_weight, down_bias, second_scale)
    zero_grads = tuple((jnp.zeros(portion.shape, jnp.float32) for portion in params))

    def one_image(weight_cotangent_bundle, inputs):
        picture, cotangent, length, alive = inputs
        key_valid = positions < length
        token_mask = jnp.where(key_valid & alive, 1.0, 0.0).astype(jnp.float32)[:, None]
        pixels = picture.astype(jnp.float32)
        leading_standardize_result, first_inverse = layer_norm(pixels)
        leading_standardize_source = rounded(leading_standardize_result * gain_one + shift_one)
        projected = jnp.dot(leading_standardize_source, entry_weight, preferred_element_type=jnp.float32)
        queries = rounded(projected[:, :D] + query_bias)
        key_rows = rounded(projected[:, D:2 * D])
        value_rows = rounded(projected[:, 2 * D:] + value_bias)
        head_queries = queries.reshape(head_shape)
        head_keys = key_rows.reshape(head_shape)
        head_values = value_rows.reshape(head_shape)
        attended, logsum = attend(head_queries, head_keys, head_values, key_valid, score_scale)
        softmax_blend_tokens_out = attended.reshape(PAD_LEN, D)
        softmax_blend_result = jnp.dot(softmax_blend_tokens_out, exit_weight, preferred_element_type=jnp.float32) + exit_vec
        residual = pixels + scale_one * softmax_blend_result
        later_standardize_result, second_inverse = layer_norm(residual)
        later_standardize_source = rounded(later_standardize_result * gain_two + shift_two)
        hidden_pre = jnp.dot(later_standardize_source, up_weight, preferred_element_type=jnp.float32) + up_vec
        activated_full, slope = gelu_parts(hidden_pre)
        gelu_applied_inner = rounded(activated_full)
        contract_map_result = jnp.dot(gelu_applied_inner, down_weight, preferred_element_type=jnp.float32) + down_vec
        layer_rows = (token_mask * (residual + scale_two * contract_map_result)).astype(jnp.bfloat16)
        incoming_cotangent = token_mask * cotangent.astype(jnp.float32)
        contract_map_piece = incoming_cotangent * scale_two
        contract_map_cotangent = rounded(contract_map_piece)
        act_cot = jnp.dot(contract_map_cotangent, down_weight.T, preferred_element_type=jnp.float32)
        before_gelu_cotangent = act_cot * slope
        before_gelu_narrowed = rounded(before_gelu_cotangent)
        later_standardize_cotangent = jnp.dot(before_gelu_narrowed, up_weight.T, preferred_element_type=jnp.float32)
        skip_path_cotangent = incoming_cotangent + norm_back(later_standardize_cotangent * gain_two, later_standardize_result, second_inverse)
        softmax_blend_cotangent_sum = skip_path_cotangent * scale_one
        softmax_blend_narrowed = rounded(softmax_blend_cotangent_sum)
        attended_cot = rounded(jnp.dot(softmax_blend_narrowed, exit_weight.T, preferred_element_type=jnp.float32))
        query_cot, key_cot, value_cot = attend_back(head_queries, head_keys, head_values, attended, attended_cot.reshape(head_shape), logsum, key_valid, score_scale)
        asking_vectors_merged = query_cot.reshape(PAD_LEN, D)
        content_vectors_merged = value_cot.reshape(PAD_LEN, D)
        expand_map_cotangent = jnp.concatenate([asking_vectors_merged, key_cot.reshape(PAD_LEN, D), content_vectors_merged], axis=1)
        leading_standardize_cotangent = jnp.dot(expand_map_cotangent, entry_weight.T, preferred_element_type=jnp.float32)
        input_rows = skip_path_cotangent + norm_back(leading_standardize_cotangent * gain_one, leading_standardize_result, first_inverse)
        cotangent_pieces_list = (lax.optimization_barrier(jnp.sum(leading_standardize_cotangent * leading_standardize_result, axis=0)), lax.optimization_barrier(jnp.sum(leading_standardize_cotangent, axis=0)), jnp.dot(leading_standardize_source.T, expand_map_cotangent, preferred_element_type=jnp.float32), jnp.concatenate([lax.optimization_barrier(jnp.sum(asking_vectors_merged.astype(jnp.float32), axis=0)), lax.optimization_barrier(jnp.sum(content_vectors_merged.astype(jnp.float32), axis=0))]), jnp.dot(softmax_blend_tokens_out.T, softmax_blend_narrowed, preferred_element_type=jnp.float32), lax.optimization_barrier(jnp.sum(softmax_blend_cotangent_sum, axis=0)), lax.optimization_barrier(jnp.sum(skip_path_cotangent * softmax_blend_result, axis=0)), lax.optimization_barrier(jnp.sum(later_standardize_cotangent * later_standardize_result, axis=0)), lax.optimization_barrier(jnp.sum(later_standardize_cotangent, axis=0)), jnp.dot(later_standardize_source.T, before_gelu_narrowed, preferred_element_type=jnp.float32), lax.optimization_barrier(jnp.sum(before_gelu_cotangent, axis=0)), jnp.dot(gelu_applied_inner.T, contract_map_cotangent, preferred_element_type=jnp.float32), lax.optimization_barrier(jnp.sum(contract_map_piece, axis=0)), lax.optimization_barrier(jnp.sum(incoming_cotangent * contract_map_result, axis=0)))
        refreshed_block_carry = tuple((accumulated_sum + cotangent_piece for accumulated_sum, cotangent_piece in zip(weight_cotangent_bundle, cotangent_pieces_list)))
        return (refreshed_block_carry, (layer_rows, input_rows))
    weight_cotangent_bundle, outputs = lax.scan(one_image, zero_grads, (images, out_grad, lengths, alive_slots))
    layer_out, input_grad = outputs
    return (layer_out, input_grad, weight_cotangent_bundle[0], weight_cotangent_bundle[1], weight_cotangent_bundle[2], weight_cotangent_bundle[3], weight_cotangent_bundle[4], weight_cotangent_bundle[5], weight_cotangent_bundle[6], weight_cotangent_bundle[7], weight_cotangent_bundle[8], weight_cotangent_bundle[9], weight_cotangent_bundle[10], weight_cotangent_bundle[11], weight_cotangent_bundle[12], weight_cotangent_bundle[13])
```

```python
import functools
import math

import jax
import jax.numpy as jnp
from jax import lax
from jax.experimental import pallas as pl
from jax.experimental.pallas import tpu as pltpu
from jax.sharding import PartitionSpec as P

HEAD_DIM = 64
EPSILON = 1e-06
NEG_LARGE = -1e30

MESH = pl.DeviceIdType.MESH
DMA = pltpu.SemaphoreType.DMA
ANY = pl.BlockSpec(memory_space=pl.ANY)
VM = pl.BlockSpec(memory_space=pltpu.VMEM)


def remote(src, dst, ssem, rsem, dev):
    return pltpu.make_async_remote_copy(
        src_ref=src, dst_ref=dst, send_sem=ssem, recv_sem=rsem, device_id=dev, device_id_type=MESH
    )


class Place:
    def __init__(self, S, F):
        self.S, self.F, self.Z = S, F, F // 2
        self.bits = [1 << b for b in range(S.bit_length() - 1)]
        self.nbits = len(self.bits)
        self.order = [self.bits, self.bits[1:] + self.bits[:1]]
        self.s = lax.axis_index("seq")
        self.f = lax.axis_index("fsdp")
        self.z, self.c = self.f // 2, lax.rem(self.f, 2)
        self.mate = (self.s, self.f ^ 1)

    def at(self, zz):
        return (self.s, zz * 2 + self.c)

    def meet(self, fsdp=True, seq=True):
        bar = pltpu.get_barrier_semaphore()
        count = 0
        if fsdp:
            for k in range(1, self.F):
                pl.semaphore_signal(bar, inc=1, device_id=(self.s, lax.rem(self.f + k, self.F)), device_id_type=MESH)
            count += self.F - 1
        if seq:
            for k in range(1, self.S):
                pl.semaphore_signal(bar, inc=1, device_id=(self.s ^ k, self.f), device_id_type=MESH)
            count += self.S - 1
        pl.semaphore_wait(bar, count)


def span(bits):
    out = [0]
    for b in bits:
        out = out + [m | b for m in out]
    return out


def ds(start, size):
    return pl.ds(pl.multiple_of(start, size), size)


class Gather:
    LAG = 8

    def __init__(self, g, NB, own, full, bounce, sems):
        self.g, self.NB, self.own, self.full, self.bounce = g, NB, own, full, bounce
        self.zs, self.zr, self.xs, self.xr, self.cs, self.cr, self.ls = sems
        self.R, self.D = full.shape[2:]
        self.C = self.D // g.S
        self.nitems = (g.Z - 1) * NB * 2
        self.steps = self.nitems + self.LAG * g.nbits

    @staticmethod
    def scratch(S, F, NB, R, D, dtype=jnp.bfloat16):
        Z, nb = F // 2, S.bit_length() - 1
        return [pltpu.VMEM((NB, R, D), dtype), DMA((2, NB, Z)), DMA((NB, Z)), DMA((NB, Z, 2, nb)), DMA((NB, Z, 2, nb)),
                DMA((NB, Z)), DMA((NB, Z)), DMA((NB,))]

    def cols(self, q):
        return ds(q * self.C, self.C)

    def half(self, p):
        return pl.ds(p * (self.R // 2), self.R // 2)

    def zcopy(self, src, b, zz, way, to):
        g = self.g
        return remote(src, self.full.at[zz * 2 + g.c, b, :, self.cols(g.s)], self.zs.at[way, b, zz], self.zr.at[b, zz], g.at(to))

    def zfull(self, b, zz):
        return self.full.at[zz * 2 + self.g.c, b, :, self.cols(self.g.s)]

    def mate_copy(self, src, b, zz, core):
        return remote(src, self.full.at[zz * 2 + core, b], self.cs.at[b, zz], self.cr.at[b, zz], self.g.mate)

    def start(self):
        g = self.g
        for b in range(self.NB):
            piece = self.own(b, self.cols(g.s))
            @pl.when(g.z < g.Z - 1)
            def _():
                self.zcopy(piece, b, g.z, 0, g.z + 1).start()
            @pl.when(g.z > 0)
            def _():
                self.zcopy(piece, b, g.z, 1, g.z - 1).start()
        for b in range(self.NB):
            pltpu.make_async_copy(self.own(b, slice(None)), self.bounce.at[b], self.ls.at[b]).start()
        for b in range(self.NB):
            self.mate_copy(self.own(b, slice(None)), b, g.z, g.c).start()
        for b in range(self.NB):
            pltpu.make_async_copy(self.own(b, slice(None)), self.bounce.at[b], self.ls.at[b]).wait()
            pltpu.make_async_copy(self.bounce.at[b], self.full.at[g.f, b], self.ls.at[b]).start()

    def xcopies(self, b, zz, p, j):
        g = self.g
        f = zz * 2 + g.c
        to = (g.s ^ g.order[p][j], g.f)
        out = []
        for m in span(g.order[p][:j]):
            ref = self.full.at[f, b, self.half(p), self.cols(g.s ^ m)]
            out.append(remote(ref, ref, self.xs.at[b, zz, p, j], self.xr.at[b, zz, p, j], to))
        return out

    def xall(self, b, zz, p, j):
        g = self.g
        ref = self.full.at[zz * 2 + g.c, b, self.half(p), pl.ds(0, self.C << j)]
        return remote(ref, ref, self.xs.at[b, zz, p, j], self.xr.at[b, zz, p, j], (g.s ^ g.order[p][j], g.f))

    def item(self, t):
        g = self.g
        h = 1 + t // (2 * self.NB)
        r = lax.rem(t, 2 * self.NB)
        b, below = r // 2, lax.rem(r, 2) == 0
        zz = jnp.where(below, g.z - h, g.z + h)
        ok = (t >= 0) & (t < self.nitems) & (zz >= 0) & (zz < g.Z)
        nxt = jnp.where(below, g.z + 1, g.z - 1)
        more = (nxt >= 0) & (nxt < g.Z)
        way = jnp.where(below, 0, 1)
        return b, zz, ok, nxt, more, way

    def step(self, t):
        g = self.g
        for j in reversed(range(g.nbits + 1)):
            b, zz, ok, nxt, more, way = self.item(t - self.LAG * j)
            @pl.when(ok)
            def _(j=j, b=b, zz=zz, nxt=nxt, more=more, way=way):
                if j == 0:
                    self.zcopy(self.zfull(b, zz), b, zz, 0, g.z).wait_recv()
                    @pl.when(more)
                    def _():
                        self.zcopy(self.zfull(b, zz), b, zz, way, nxt).start()
                else:
                    for p in range(2):
                        self.xall(b, zz, p, j - 1).wait_recv()
                if j < g.nbits:
                    for p in range(2):
                        for cp in self.xcopies(b, zz, p, j):
                            cp.start()
                else:
                    self.mate_copy(self.full.at[zz * 2 + g.c, b], b, zz, g.c).start()

    def run(self, lo, hi):
        @pl.loop(lo, hi)
        def _(t):
            self.step(t)

    def finish(self):
        g = self.g
        @pl.loop(0, self.NB)
        def _(b):
            blk = self.full.at[g.f, b]
            pltpu.make_async_copy(self.bounce.at[b], blk, self.ls.at[b]).wait()
            cp = self.mate_copy(blk, b, g.z, 1 - g.c)
            cp.wait_send()
            cp.wait_recv()
            @pl.when(g.z < g.Z - 1)
            def _():
                self.zcopy(self.zfull(b, g.z), b, g.z, 0, g.z + 1).wait_send()
            @pl.when(g.z > 0)
            def _():
                self.zcopy(self.zfull(b, g.z), b, g.z, 1, g.z - 1).wait_send()
        @pl.loop(0, self.nitems)
        def _(t):
            b, zz, ok, nxt, more, way = self.item(t)
            @pl.when(ok)
            def _():
                @pl.when(more)
                def _():
                    self.zcopy(self.zfull(b, zz), b, zz, way, nxt).wait_send()
                for p in range(2):
                    for j in range(g.nbits):
                        self.xall(b, zz, p, j).wait_send()
                cp = self.mate_copy(self.full.at[zz * 2 + g.c, b], b, zz, 1 - g.c)
                cp.wait_send()
                cp.wait_recv()


class Scatter:
    LAG = 4

    def __init__(self, g, NB, part, out, bufs, sems):
        self.g, self.NB, self.part, self.out = g, NB, part, out
        self.cs_buf, self.r0, self.xb, self.zb, self.fq = bufs
        self.own, self.c_s, self.c_r, self.x_s, self.x_r, self.z_s, self.z_r, self.a_s, self.a_r, self.o = sems
        self.R, self.D = part.shape[2:]
        self.C = self.D // g.S
        self.nitems = NB * g.Z
        self.tail = g.nbits * self.LAG
        self.steps = self.nitems + self.tail + 1 + (g.nbits + 2) * self.LAG * 2

    @staticmethod
    def scratch(S, F, NB, R, D, dtype=jnp.bfloat16):
        Z, nb = F // 2, S.bit_length() - 1
        C = D // S
        n = NB * Z
        return [
            pltpu.VMEM((n, R, D), dtype), pltpu.VMEM((n, R, D), dtype), pltpu.VMEM((n, 2, R // 2, D - C), dtype),
            pltpu.VMEM((NB, Z, R, C), dtype), pltpu.VMEM((NB, R, C), dtype),
            DMA((n,)), DMA((n,)), DMA((n,)), DMA((n, 2, nb)), DMA((n, 2, nb)),
            DMA((NB, Z)), DMA((NB, Z)), DMA((NB, 2, nb)), DMA((NB, 2, nb)), DMA((NB,)),
        ]

    def where(self, t):
        g = self.g
        b, r = t // g.Z, lax.rem(t, g.Z)
        zz = jnp.where(lax.rem(r, 2) == 0, r // 2, g.Z - 1 - r // 2)
        return b, zz

    def cols(self, q):
        return ds(q * self.C, self.C)

    def half(self, p):
        return pl.ds(p * (self.R // 2), self.R // 2)

    def load(self, t):
        b, zz = self.where(t)
        return pltpu.make_async_copy(self.part.at[zz * 2 + self.g.c, b], self.cs_buf.at[t], self.own.at[t])

    def swap(self, t):
        b, zz = self.where(t)
        return remote(self.part.at[zz * 2 + 1 - self.g.c, b], self.r0.at[t], self.c_s.at[t], self.c_r.at[t], self.g.mate)

    def offset(self, j):
        D, C, S = self.D, self.C, self.g.S
        return sum((S >> (i + 1)) * C for i in range(j))

    def halving(self, t, p, j):
        g = self.g
        order = g.order[p]
        mask = sum(order[: j + 1])
        base = (g.s ^ order[j]) & mask
        to = (g.s ^ order[j], g.f)
        out = []
        for i, m in enumerate(span(order[j + 1 :])):
            src = self.cs_buf.at[t, self.half(p), self.cols(base | m)]
            dst = self.xb.at[t, p, :, pl.ds(self.offset(j) + i * self.C, self.C)]
            out.append(remote(src, dst, self.x_s.at[t, p, j], self.x_r.at[t, p, j], to))
        return out

    def halved(self, t, p, j):
        g = self.g
        width = (g.S >> (j + 1)) * self.C
        ref = self.xb.at[t, p, :, pl.ds(self.offset(j), width)]
        return remote(ref, ref, self.x_s.at[t, p, j], self.x_r.at[t, p, j], (g.s ^ g.order[p][j], g.f))

    def add_halves(self, t, p, j):
        g = self.g
        order = g.order[p]
        mask = sum(order[: j + 1])
        base = g.s & mask
        for i, m in enumerate(span(order[j + 1 :])):
            q = self.cols(base | m)
            got = self.xb[t, p, :, pl.ds(self.offset(j) + i * self.C, self.C)]
            self.cs_buf[t, self.half(p), q] = self.cs_buf[t, self.half(p), q] + got

    def piece(self, t, b, zz):
        g = self.g
        return remote(self.cs_buf.at[t, :, self.cols(g.s)], self.zb.at[b, g.z], self.z_s.at[b, zz], self.z_r.at[b, g.z], g.at(zz))

    def arrived(self, b, zz):
        g = self.g
        return remote(self.zb.at[b, zz], self.zb.at[b, zz], self.z_s.at[b, zz], self.z_r.at[b, zz], g.at(zz))

    def doubling(self, b, p, j):
        g = self.g
        to = (g.s ^ g.order[p][j], g.f)
        out = []
        for m in span(g.order[p][:j]):
            dst = self.out.at[b, self.half(p), self.cols(g.s ^ m)]
            src = self.fq.at[b, self.half(p)] if m == 0 else dst
            out.append(remote(src, dst, self.a_s.at[b, p, j], self.a_r.at[b, p, j], to))
        return out

    def doubled(self, b, p, j):
        g = self.g
        ref = self.out.at[b, self.half(p), pl.ds(0, self.C << j)]
        return remote(ref, ref, self.a_s.at[b, p, j], self.a_r.at[b, p, j], (g.s ^ g.order[p][j], g.f))

    def start(self):
        @pl.loop(0, self.nitems)
        def _(t):
            self.swap(t).start()
            self.load(t).start()

    def step(self, t):
        g = self.g
        last = g.Z - 1
        for j in reversed(range(g.nbits + 1)):
            u = t - self.tail - self.LAG * 2 * (1 + j) - last
            @pl.when((u >= 0) & (u < self.nitems) & (lax.rem(u, g.Z) == 0))
            def _(j=j, u=u):
                b = u // g.Z
                if j == 0:
                    r = jnp.where(g.z < (g.Z + 1) // 2, 2 * g.z, 2 * (g.Z - 1 - g.z) + 1)
                    total = self.cs_buf[b * g.Z + r, :, self.cols(g.s)].astype(jnp.float32)
                    for k in range(1, g.Z):
                        zz = lax.rem(g.z + k, g.Z)
                        self.arrived(b, zz).wait_recv()
                        total = total + self.zb[b, zz].astype(jnp.float32)
                    self.fq[b] = total.astype(self.fq.dtype)
                    pltpu.make_async_copy(self.fq.at[b], self.out.at[b, :, self.cols(g.s)], self.o.at[b]).start()
                else:
                    for p in range(2):
                        self.doubled(b, p, j - 1).wait_recv()
                if j < g.nbits:
                    for p in range(2):
                        for cp in self.doubling(b, p, j):
                            cp.start()
        for j in reversed(range(g.nbits + 1)):
            u = t - self.LAG * j
            @pl.when((u >= 0) & (u < self.nitems))
            def _(j=j, u=u):
                b, zz = self.where(u)
                if j == 0:
                    self.load(u).wait()
                    self.swap(u).wait_recv()
                    self.cs_buf[u] = self.cs_buf[u] + self.r0[u]
                else:
                    for p in range(2):
                        self.halved(u, p, j - 1).wait_recv()
                        self.add_halves(u, p, j - 1)
                if j < g.nbits:
                    for p in range(2):
                        for cp in self.halving(u, p, j):
                            cp.start()
                else:
                    @pl.when(zz != g.z)
                    def _():
                        self.piece(u, b, zz).start()

    def run(self, lo, hi):
        @pl.loop(lo, hi)
        def _(t):
            self.step(t)

    def finish(self):
        g = self.g
        @pl.loop(0, self.nitems)
        def _(t):
            b, zz = self.where(t)
            self.swap(t).wait_send()
            for p in range(2):
                for j in range(g.nbits):
                    self.halved(t, p, j).wait_send()
            @pl.when(zz != g.z)
            def _():
                self.piece(t, b, zz).wait_send()
        @pl.loop(0, self.NB)
        def _(b):
            pltpu.make_async_copy(self.fq.at[b], self.out.at[b, :, self.cols(g.s)], self.o.at[b]).wait()
            for p in range(2):
                for j in range(g.nbits):
                    self.doubled(b, p, j).wait_send()


class VecGather:
    def __init__(self, g, vec, out, sems):
        self.g, self.vec, self.out = g, vec, out
        self.vs, self.vr, self.vl = sems

    @staticmethod
    def scratch(F):
        return [DMA((F - 1,)), DMA((F - 1,)), DMA((1,))]

    def copy(self, k):
        g = self.g
        return remote(self.vec, self.out.at[g.f], self.vs.at[k - 1], self.vr.at[k - 1], (g.s, lax.rem(g.f + k, g.F)))

    def start(self):
        for k in range(1, self.g.F):
            self.copy(k).start()
        pltpu.make_async_copy(self.vec, self.out.at[self.g.f], self.vl.at[0]).start()

    def finish(self):
        g = self.g
        pltpu.make_async_copy(self.vec, self.out.at[g.f], self.vl.at[0]).wait()
        for k in range(1, g.F):
            self.copy(k).wait_send()
            src = lax.rem(g.f + g.F - k, g.F)
            remote(self.vec, self.out.at[src], self.vs.at[k - 1], self.vr.at[k - 1], (g.s, src)).wait_recv()


class VecSum:
    def __init__(self, g, vec, out, bufs, sems):
        self.g, self.vec, self.out = g, vec, out
        self.fb, self.mid, self.sb = bufs
        self.vs, self.vr, self.ws, self.wr = sems

    @staticmethod
    def scratch(S, F, N, L):
        return [pltpu.VMEM((F, N, L), jnp.float32), pltpu.VMEM((N, L), jnp.float32), pltpu.VMEM((S, N, L), jnp.float32),
                DMA((F - 1,)), DMA((F - 1,)), DMA((S - 1,)), DMA((S - 1,))]

    def one(self, k):
        g = self.g
        to = lax.rem(g.f + k, g.F)
        return remote(self.vec.at[to], self.fb.at[g.f], self.vs.at[k - 1], self.vr.at[k - 1], (g.s, to))

    def two(self, k):
        g = self.g
        return remote(self.mid, self.sb.at[g.s], self.ws.at[k - 1], self.wr.at[k - 1], (g.s ^ k, g.f))

    def start(self):
        for k in range(1, self.g.F):
            self.one(k).start()

    def middle(self):
        g = self.g
        total = self.vec[g.f]
        for k in range(1, g.F):
            src = lax.rem(g.f + g.F - k, g.F)
            remote(self.fb.at[src], self.fb.at[src], self.vs.at[k - 1], self.vr.at[k - 1], (g.s, src)).wait_recv()
            total = total + self.fb[src]
        self.mid[...] = total
        for k in range(1, g.S):
            self.two(k).start()

    def finish(self):
        g = self.g
        total = self.mid[...]
        for k in range(1, g.S):
            src = g.s ^ k
            remote(self.mid, self.sb.at[src], self.ws.at[k - 1], self.wr.at[k - 1], (src, g.f)).wait_recv()
            total = total + self.sb[src]
        self.out[...] = total
        for k in range(1, g.F):
            self.one(k).wait_send()
        for k in range(1, g.S):
            self.two(k).wait_send()


PARAMS = dict(has_side_effects=True, vmem_limit_bytes=60 * 2**20)


def gather_call(S, F, cid, D, shards, vec, blocks):
    NB = len(blocks)
    R = shards[0].shape[0]

    def kernel(*refs):
        ins, vec_in = refs[: len(shards)], refs[len(shards)]
        full, vec_out = refs[len(shards) + 1 : len(shards) + 3]
        rest = refs[len(shards) + 3 :]
        g = Place(S, F)

        def own(b, cols):
            w, r0, c0 = blocks[b]
            if isinstance(cols, slice):
                return ins[w].at[pl.ds(r0, R), pl.ds(c0, D)]
            return ins[w].at[pl.ds(r0, R), pl.ds(pl.multiple_of(c0 + cols.start, cols.size), cols.size)]

        g.meet()
        vg = VecGather(g, vec_in, vec_out, rest[:3])
        ga = Gather(g, NB, own, full, rest[3], rest[4:])
        vg.start()
        ga.start()
        ga.run(0, ga.steps)
        ga.finish()
        vg.finish()

    return pl.pallas_call(
        kernel,
        out_shape=[jax.ShapeDtypeStruct((F, NB, R, D), jnp.bfloat16), jax.ShapeDtypeStruct((F,) + vec.shape, vec.dtype)],
        in_specs=[ANY] * (len(shards) + 1),
        out_specs=[ANY] * 2,
        scratch_shapes=VecGather.scratch(F) + Gather.scratch(S, F, NB, R, D),
        compiler_params=pltpu.CompilerParams(collective_id=cid, **PARAMS),
        name="weights_in",
    )(*shards, vec)


def scatter_call(S, F, cid, part, vec):
    _, NB, R, D = part.shape
    N, L = vec.shape[1:]

    def kernel(part, vec, out, vec_out, *rest):
        g = Place(S, F)
        g.meet()
        vsum = VecSum(g, vec, vec_out, rest[:3], rest[3:7])
        sc = Scatter(g, NB, part, out, rest[7:12], rest[12:])
        vsum.start()
        sc.start()
        vsum.middle()
        sc.run(0, sc.steps)
        sc.finish()
        vsum.finish()

    return pl.pallas_call(
        kernel,
        out_shape=[jax.ShapeDtypeStruct((NB, R, D), jnp.bfloat16), jax.ShapeDtypeStruct((N, L), jnp.float32)],
        in_specs=[ANY, VM],
        out_specs=[ANY, VM],
        scratch_shapes=VecSum.scratch(S, F, N, L) + Scatter.scratch(S, F, NB, R, D),
        compiler_params=pltpu.CompilerParams(collective_id=cid, **PARAMS),
        name="gradients_out",
    )(part, vec)


def fp32(x):
    return x.astype(jnp.float32)


def dot(a, b, dims=((1,), (0,))):
    return lax.dot_general(a, b, (dims, ((), ())), preferred_element_type=jnp.float32)


NT = ((1,), (1,))
TN = ((0,), (0,))


def mean_rows(x):
    return jnp.mean(x, axis=-1, keepdims=True)


def qkv_kernel(S, F, img, par, eb, wts, x1, heads, wv, stage, wsem, ssem, rsem):
    g = Place(S, F)
    g.meet(fsdp=False)
    slots, T, D = img.shape
    W = D // S
    loads = [pltpu.make_async_copy(wts.at[:, j], wv.at[j], wsem.at[j]) for j in range(3)]
    for cp in loads:
        cp.start()
    gain, shift = par[0:1], par[1:2]
    rows = min(128, T)

    @pl.loop(0, slots * T // rows)
    def _(r):
        i, t = r // (T // rows), lax.rem(r, T // rows)
        x = fp32(img[i, pl.ds(t * rows, rows)])
        x = x - mean_rows(x)
        inv = lax.rsqrt(mean_rows(x * x) + EPSILON)
        x1[ds(r * rows, rows)] = (x * inv * gain + shift).astype(x1.dtype)

    for cp in loads:
        cp.wait()

    def copy(k, j):
        src = stage.at[k, j]
        dst = heads.at[j, :, ds(g.s * T, T)]
        return remote(src, dst, ssem.at[k, j], rsem.at[k, j], (g.s ^ k, g.f))

    def local(j):
        return pltpu.make_async_copy(stage.at[0, j], heads.at[j, :, ds(g.s * T, T)], ssem.at[0, j])

    @pl.loop(0, S * 3)
    def _(n):
        k = lax.rem(1 + n // 3, S)
        j = lax.rem(n, 3)
        cols = ds((g.s ^ k) * W, W)
        w = wv[j, :, :, cols].reshape(D, W)
        out = dot(x1[...], w) + eb[j, :, cols]
        stage[k, j] = out.astype(stage.dtype).reshape(slots, T, W)

        @pl.when(k != 0)
        def _():
            copy(k, j).start()

        @pl.when(k == 0)
        def _():
            local(j).start()

    for j in range(3):
        local(j).wait()
        for k in range(1, S):
            cp = copy(k, j)
            cp.wait_send()
            remote(stage.at[k, j], heads.at[j, :, ds((g.s ^ k) * T, T)], ssem.at[k, j], rsem.at[k, j], (g.s ^ k, g.f)).wait_recv()


def qkv_call(S, F, cid, img, par, eb, wts):
    slots, T, D = img.shape
    _, _, R, _ = wts.shape
    W = D // S
    bf = jnp.bfloat16
    return pl.pallas_call(
        functools.partial(qkv_kernel, S, F),
        out_shape=[jax.ShapeDtypeStruct((slots * T, D), bf), jax.ShapeDtypeStruct((3, slots, S * T, W), bf)],
        in_specs=[VM, VM, VM, ANY],
        out_specs=[VM, ANY],
        scratch_shapes=[pltpu.VMEM((3, F, R, D), bf), pltpu.VMEM((S, 3, slots, T, W), bf), DMA((3,)), DMA((S, 3)), DMA((S, 3))],
        compiler_params=pltpu.CompilerParams(collective_id=cid, **PARAMS),
        name="project",
    )(img, par, eb, wts)


def head_lanes(rows, hh):
    lane = lax.broadcasted_iota(jnp.int32, (rows, 128), 1)
    mine = (lane >= hh * HEAD_DIM) & (lane < (hh + 1) * HEAD_DIM)
    spare = lane == (1 - hh) * HEAD_DIM
    return mine, spare


def masked_keys(k, length, hh):
    N = k.shape[0]
    mine, spare = head_lanes(N, hh)
    late = lax.broadcasted_iota(jnp.int32, (N, 128), 0) >= length
    return jnp.where(mine, fp32(k), jnp.where(spare & late, NEG_LARGE, 0.0)).astype(jnp.bfloat16)


def scaled_queries(q, hh):
    mine, spare = head_lanes(q.shape[0], hh)
    return jnp.where(mine, fp32(q) * HEAD_DIM ** (-0.5), jnp.where(spare, 1.0, 0.0)).astype(jnp.bfloat16)


def attend_kernel(S, F, QB, lengths, q, k, v, out_t, lse, att, kh, vt, o_t, o_buf, ssem, rsem):
    g = Place(S, F)
    i, hp = pl.program_id(0), pl.program_id(1)
    slots, pairs = pl.num_programs(0), pl.num_programs(1)
    N = q.shape[2]
    T = N // S
    W = att.shape[2] // S
    e = i * pairs + hp

    @pl.when(e == 0)
    def _():
        g.meet(fsdp=False)

    length = lengths[i]
    vt[...] = v[0, 0].T
    for hh in range(2):
        kh[hh] = masked_keys(k[0, 0], length, hh)

    @pl.loop(0, N // QB)
    def _(b):
        cols = ds(b * QB, QB)
        qb = q[0, 0, cols]
        for hh in range(2):
            sc = dot(kh[hh], scaled_queries(qb, hh), NT)
            top = jnp.max(sc, axis=0, keepdims=True)
            ex = jnp.exp(sc - top)
            total = jnp.sum(ex, axis=0, keepdims=True)
            w = (ex * (1.0 / total)).astype(jnp.bfloat16)
            o = dot(vt[hh * HEAD_DIM : (hh + 1) * HEAD_DIM], w).astype(jnp.bfloat16)
            o_t[hh * HEAD_DIM : (hh + 1) * HEAD_DIM, cols] = o
            lse[0, 0, hh : hh + 1, cols] = top + jnp.log(total)

    out_t[0] = o_t[...]
    o_buf[e] = o_t[...].T

    def copy(e, i, hp, kk):
        dst = att.at[i, :, pl.ds(pl.multiple_of(g.s * W + hp * 128, 128), 128)]
        return remote(o_buf.at[e, ds((g.s ^ kk) * T, T)], dst, ssem.at[e, kk], rsem.at[e, kk], (g.s ^ kk, g.f))

    def local(e, i, hp):
        dst = att.at[i, :, pl.ds(pl.multiple_of(g.s * W + hp * 128, 128), 128)]
        return pltpu.make_async_copy(o_buf.at[e, ds(g.s * T, T)], dst, ssem.at[e, 0])

    for kk in range(1, S):
        copy(e, i, hp, kk).start()
    local(e, i, hp).start()

    @pl.when(e == slots * pairs - 1)
    def _():
        @pl.loop(0, slots * pairs)
        def _(e):
            i, hp = e // pairs, lax.rem(e, pairs)
            local(e, i, hp).wait()
            for kk in range(1, S):
                cp = copy(e, i, hp, kk)
                cp.wait_send()
                cp.wait_recv()


def attend_call(S, F, cid, lengths, heads):
    _, slots, N, W = heads.shape
    pairs, T, D = W // 128, N // S, W * S
    bf = jnp.bfloat16
    QB = min(256, N)
    part = lambda j: pl.BlockSpec((1, 1, N, 128), lambda i, h: (j, i, 0, h))
    return pl.pallas_call(
        functools.partial(attend_kernel, S, F, QB),
        grid=(slots, pairs),
        out_shape=[
            jax.ShapeDtypeStruct((slots, W, N), bf),
            jax.ShapeDtypeStruct((slots, pairs, 8, N), jnp.float32),
            jax.ShapeDtypeStruct((slots, T, D), bf),
        ],
        in_specs=[pl.BlockSpec(memory_space=pltpu.SMEM), part(0), part(1), part(2)],
        out_specs=[
            pl.BlockSpec((1, 128, N), lambda i, h: (i, h, 0)),
            pl.BlockSpec((1, 1, 8, N), lambda i, h: (i, h, 0, 0)),
            ANY,
        ],
        scratch_shapes=[
            pltpu.VMEM((2, N, 128), bf), pltpu.VMEM((128, N), bf), pltpu.VMEM((128, N), bf),
            pltpu.VMEM((slots * pairs, N, 128), bf), DMA((slots * pairs, S)), DMA((slots * pairs, S)),
        ],
        compiler_params=pltpu.CompilerParams(collective_id=cid, dimension_semantics=("arbitrary",) * 2, **PARAMS),
        name="attend",
    )(lengths, heads, heads, heads)


def middle_kernel(S, F, lengths, held, img, cot, att, par, ub, wx, wu, wd,
                  layer, rescot, vecs, ubg, part, cots,
                  mixed, normed, inv2, x2, x2t, dcot, down, cot2, dwu, dwd, dwx, stage, ssem, rsem, psem):
    g = Place(S, F)
    j = pl.program_id(0)
    slots, T, D = img.shape
    M = slots * T
    W = D // S
    R = wx.shape[2]
    H = wu.shape[3]
    rows = min(128, T)
    nrows = M // rows
    exit_bias, scale1, gain2, shift2 = par[4:5], par[5:6], par[6:7], par[7:8]
    down_bias, scale2 = par[12:13], par[13:14]
    per_block = D // H

    def place(r):
        return r // (T // rows), lax.rem(r, T // rows) * rows

    def mask(r):
        i, t = place(r)
        limit = jnp.where(i < held[g.f], lengths[i], 0)
        pos = lax.broadcasted_iota(jnp.int32, (rows, 1), 0) + (g.s * T + t)
        return jnp.where(pos < limit, 1.0, 0.0)

    def residual(r, sl):
        i, t = place(r)
        return fp32(img[i, pl.ds(t, rows)]) + scale1 * mixed[sl]

    def upstream(r):
        i, t = place(r)
        return mask(r) * fp32(cot[i, pl.ds(t, rows)])

    @pl.when(j == 0)
    def _():
        g.meet(fsdp=False)
        w = wx[...].reshape(D, D)
        mixed[...] = dot(att[...], w) + exit_bias

        @pl.loop(0, nrows)
        def _(r):
            sl = ds(r * rows, rows)
            res = residual(r, sl)
            res = res - mean_rows(res)
            inv = lax.rsqrt(mean_rows(res * res) + EPSILON)
            n = res * inv
            normed[sl] = n
            inv2[sl] = jnp.broadcast_to(inv, (rows, 128))
            x2[sl] = (n * gain2 + shift2).astype(x2.dtype)
            dcot[sl] = (upstream(r) * scale2).astype(dcot.dtype)

        x2t[...] = x2[...].T

    wu_j = wu[...].reshape(D, H)
    wd_j = wd[...].reshape(H, D)
    pre = dot(x2[...], wu_j) + ub[...]
    cumul = 0.5 * (1.0 + lax.erf(pre * (1.0 / math.sqrt(2.0))))
    density = jnp.exp(-0.5 * pre * pre) * (1.0 / math.sqrt(2.0 * math.pi))
    act = (pre * cumul).astype(jnp.bfloat16)
    slope = cumul + pre * density
    pre_cot = dot(dcot[...], wd_j, NT) * slope
    ubg[...] = jnp.sum(pre_cot, axis=0, keepdims=True)
    low = pre_cot.astype(jnp.bfloat16)
    slot = lax.rem(j, 2)

    def put_up(jj, sl):
        cols = pl.ds(pl.multiple_of(lax.rem(jj, per_block) * H, H), H)
        return pltpu.make_async_copy(dwu.at[sl], part.at[:, 4 + jj // per_block, :, cols], psem.at[sl])

    def put_down(jj, sl):
        return pltpu.make_async_copy(dwd.at[sl], part.at[jj, pl.ds(0, 4)], psem.at[2 + sl])

    @pl.when(j >= 2)
    def _():
        put_up(j - 2, slot).wait()
        put_down(j - 2, slot).wait()

    dwu[slot] = dot(x2t[...], low).astype(jnp.bfloat16).reshape(F, R, H)
    dwd[slot] = dot(act, dcot[...], TN).astype(jnp.bfloat16).reshape(4, R, D)
    put_up(j, slot).start()
    put_down(j, slot).start()
    dd = dot(act, wd_j)
    dc = dot(low, wu_j, NT)

    @pl.when(j == 0)
    def _():
        down[...] = dd
        cot2[...] = dc

    @pl.when(j > 0)
    def _():
        down[...] += dd
        cot2[...] += dc

    @pl.when(j == F - 1)
    def _():
        vecs[...] = jnp.zeros_like(vecs)

        @pl.loop(0, nrows)
        def _(r):
            sl = ds(r * rows, rows)
            m = mask(r)
            up = upstream(r)
            out = down[sl] + down_bias
            layer[sl] = (m * (residual(r, sl) + scale2 * out)).astype(layer.dtype)
            n = normed[sl]
            inv = inv2[sl][:, 0:1]
            c2 = cot2[sl]
            c = c2 * gain2
            rc = up + inv * (c - mean_rows(c) - n * mean_rows(c * n))
            rescot[sl] = rc
            mc = rc * scale1
            x2[sl] = mc.astype(x2.dtype)
            total = lambda v: jnp.sum(v, axis=0, keepdims=True)
            vecs[0:1] += total(up * out)
            vecs[1:2] += total(up * scale2)
            vecs[2:3] += total(c2 * n)
            vecs[3:4] += total(c2)
            vecs[4:5] += total(rc * mixed[sl])
            vecs[5:6] += total(mc)

        for k in list(range(1, S)) + [0]:
            peer = g.s ^ k
            stage[k] = dot(x2[...], wx_rows(wx, peer, W), NT).astype(jnp.bfloat16).reshape(slots, T, W)
            dst = cots.at[:, ds(g.s * T, T)]
            if k:
                remote(stage.at[k], dst, ssem.at[k], rsem.at[k], (peer, g.f)).start()
            else:
                pltpu.make_async_copy(stage.at[0], dst, ssem.at[0]).start()
        dwx[...] = dot(att[...], x2[...], TN).astype(jnp.bfloat16).reshape(F, R, D)
        put_x = pltpu.make_async_copy(dwx, part.at[:, 8], psem.at[4])
        put_x.start()
        for jj in (F - 2, F - 1):
            put_up(jj, jj % 2).wait()
            put_down(jj, jj % 2).wait()
        put_x.wait()
        pltpu.make_async_copy(stage.at[0], cots.at[:, ds(g.s * T, T)], ssem.at[0]).wait()
        for k in range(1, S):
            cp = remote(stage.at[k], cots.at[:, ds((g.s ^ k) * T, T)], ssem.at[k], rsem.at[k], (g.s ^ k, g.f))
            cp.wait_send()
            cp.wait_recv()


def wx_rows(wx, peer, W):
    F, _, R, D = wx.shape
    n = W // R
    return wx[pl.ds(peer * n, n), 0].reshape(W, D)


def middle_call(S, F, cid, lengths, held, img, cot, att, par, ub, wts):
    slots, T, D = img.shape
    M = slots * T
    _, NB, R, _ = wts.shape
    FF = ub.shape[1]
    H = FF // F
    W = D // S
    per = D // H
    bf, fl = jnp.bfloat16, jnp.float32
    SM = pl.BlockSpec(memory_space=pltpu.SMEM)
    return pl.pallas_call(
        functools.partial(middle_kernel, S, F),
        grid=(F,),
        out_shape=[
            jax.ShapeDtypeStruct((M, D), bf), jax.ShapeDtypeStruct((M, D), fl), jax.ShapeDtypeStruct((8, D), fl),
            jax.ShapeDtypeStruct((1, FF), fl), jax.ShapeDtypeStruct((F, NB, R, D), bf),
            jax.ShapeDtypeStruct((slots, S * T, W), bf),
        ],
        in_specs=[SM, SM, VM, VM, VM, VM, pl.BlockSpec((1, H), lambda j: (0, j)),
                  pl.BlockSpec((F, 1, R, D), lambda j: (0, 8, 0, 0)),
                  pl.BlockSpec((F, 1, R, H), lambda j: (0, 4 + j // per, 0, lax.rem(j, per))),
                  pl.BlockSpec((1, 4, R, D), lambda j: (j, 0, 0, 0))],
        out_specs=[VM, VM, VM, pl.BlockSpec((1, H), lambda j: (0, j)), ANY, ANY],
        scratch_shapes=[
            pltpu.VMEM((M, D), fl), pltpu.VMEM((M, D), fl), pltpu.VMEM((M, 128), fl), pltpu.VMEM((M, D), bf),
            pltpu.VMEM((D, M), bf), pltpu.VMEM((M, D), bf), pltpu.VMEM((M, D), fl), pltpu.VMEM((M, D), fl),
            pltpu.VMEM((2, F, R, H), bf), pltpu.VMEM((2, 4, R, D), bf), pltpu.VMEM((F, R, D), bf),
            pltpu.VMEM((S, slots, T, W), bf), DMA((S,)), DMA((S,)), DMA((5,)),
        ],
        compiler_params=pltpu.CompilerParams(collective_id=cid, dimension_semantics=("arbitrary",), **PARAMS),
        name="feed_forward",
    )(lengths, held, img, cot, att, par, ub, wts, wts, wts)


def back_kernel(S, F, QB, lengths, q, k, v, out_t, lse, cot, back,
                kh, vh, kt, cot_t, delta, dq_t, dk, dv, stage, ssem, rsem):
    g = Place(S, F)
    i, hp = pl.program_id(0), pl.program_id(1)
    slots, pairs = pl.num_programs(0), pl.num_programs(1)
    N = q.shape[2]
    T = N // S
    D = back.shape[2] // 3
    W = D // S
    e = i * pairs + hp

    @pl.when(e == 0)
    def _():
        g.meet(fsdp=False)

    length = lengths[i]
    kt[...] = k[0, 0].T
    cot_t[...] = cot[0].T
    prod = fp32(cot_t[...]) * fp32(out_t[0])
    for hh in range(2):
        hs = slice(hh * HEAD_DIM, (hh + 1) * HEAD_DIM)
        delta[hh : hh + 1] = jnp.sum(prod[hs], axis=0, keepdims=True)
        kh[hh] = masked_keys(k[0, 0], length, hh)
        mine, _ = head_lanes(N, hh)
        vh[hh] = jnp.where(mine, fp32(v[0, 0]), 0.0).astype(jnp.bfloat16)
    dk[...] = jnp.zeros_like(dk)
    dv[...] = jnp.zeros_like(dv)

    @pl.loop(0, N // QB)
    def _(b):
        cols = ds(b * QB, QB)
        qb, cb = q[0, 0, cols], cot[0, cols]
        mines = [head_lanes(QB, hh)[0] for hh in range(2)]
        for hh in range(2):
            hs = slice(hh * HEAD_DIM, (hh + 1) * HEAD_DIM)
            qs = scaled_queries(qb, hh)
            prob = jnp.exp(dot(kh[hh], qs, NT) - lse[0, 0, hh : hh + 1, cols])
            sg = dot(vh[hh], cb, NT)
            sc = (prob * (sg - delta[hh : hh + 1, cols])).astype(jnp.bfloat16)
            w = prob.astype(jnp.bfloat16)
            dv[...] += dot(w, jnp.where(mines[hh], fp32(cb), 0.0).astype(jnp.bfloat16))
            dk[...] += dot(sc, jnp.where(mines[hh], fp32(qs), 0.0).astype(jnp.bfloat16))
            dq_t[hs, cols] = (dot(kt[hs], sc) * HEAD_DIM ** (-0.5)).astype(jnp.bfloat16)

    stage[e, 0] = dq_t[...].T
    stage[e, 1] = dk[...].astype(jnp.bfloat16)
    stage[e, 2] = dv[...].astype(jnp.bfloat16)

    def dst(i, hp, j):
        return back.at[i, :, pl.ds(pl.multiple_of(j * D + g.s * W + hp * 128, 128), 128)]

    def copy(e, i, hp, j, kk):
        return remote(stage.at[e, j, ds((g.s ^ kk) * T, T)], dst(i, hp, j), ssem.at[e, j, kk], rsem.at[e, j, kk], (g.s ^ kk, g.f))

    def local(e, i, hp, j):
        return pltpu.make_async_copy(stage.at[e, j, ds(g.s * T, T)], dst(i, hp, j), ssem.at[e, j, 0])

    for j in range(3):
        for kk in range(1, S):
            copy(e, i, hp, j, kk).start()
        local(e, i, hp, j).start()

    @pl.when(e == slots * pairs - 1)
    def _():
        @pl.loop(0, slots * pairs)
        def _(e):
            i, hp = e // pairs, lax.rem(e, pairs)
            for j in range(3):
                local(e, i, hp, j).wait()
                for kk in range(1, S):
                    cp = copy(e, i, hp, j, kk)
                    cp.wait_send()
                    cp.wait_recv()


def back_call(S, F, cid, lengths, heads, out_t, lse, cots):
    _, slots, N, W = heads.shape
    pairs, T, D = W // 128, N // S, W * S
    bf, fl = jnp.bfloat16, jnp.float32
    QB = min(256, N)
    part = lambda j: pl.BlockSpec((1, 1, N, 128), lambda i, h: (j, i, 0, h))
    return pl.pallas_call(
        functools.partial(back_kernel, S, F, QB),
        grid=(slots, pairs),
        out_shape=jax.ShapeDtypeStruct((slots, T, 3 * D), bf),
        in_specs=[pl.BlockSpec(memory_space=pltpu.SMEM), part(0), part(1), part(2),
                  pl.BlockSpec((1, 128, N), lambda i, h: (i, h, 0)),
                  pl.BlockSpec((1, 1, 8, N), lambda i, h: (i, h, 0, 0)),
                  pl.BlockSpec((1, N, 128), lambda i, h: (i, 0, h))],
        out_specs=ANY,
        scratch_shapes=[
            pltpu.VMEM((2, N, 128), bf), pltpu.VMEM((2, N, 128), bf), pltpu.VMEM((128, N), bf), pltpu.VMEM((128, N), bf),
            pltpu.VMEM((8, N), fl), pltpu.VMEM((128, N), bf), pltpu.VMEM((N, 128), fl), pltpu.VMEM((N, 128), fl),
            pltpu.VMEM((slots * pairs, 3, N, 128), bf), DMA((slots * pairs, 3, S)), DMA((slots * pairs, 3, S)),
        ],
        compiler_params=pltpu.CompilerParams(collective_id=cid, dimension_semantics=("arbitrary",) * 2, **PARAMS),
        name="attend_back",
    )(lengths, heads, heads, heads, out_t, lse, cots)


def entry_back_kernel(img, x1, e, rescot, par, w, dx, dw, vecs, acc):
    j = pl.program_id(0)
    slots, T, D = img.shape
    M = slots * T
    rows = min(128, T)
    gain = par[0:1]
    ej = e[...]
    d = dot(ej, w[...].reshape(D, D), NT)
    dw[...] = dot(x1[...], ej, TN).astype(dw.dtype).reshape(dw.shape)
    esum = jnp.sum(fp32(ej), axis=0, keepdims=True)

    @pl.when(j == 0)
    def _():
        acc[...] = d
        vecs[...] = jnp.zeros_like(vecs)
        vecs[2:3] = esum

    @pl.when(j > 0)
    def _():
        acc[...] += d

    @pl.when(j == 2)
    def _():
        vecs[3:4] = esum

        @pl.loop(0, M // rows)
        def _(r):
            sl = ds(r * rows, rows)
            i, t = r // (T // rows), lax.rem(r, T // rows) * rows
            x = fp32(img[i, pl.ds(t, rows)])
            x = x - mean_rows(x)
            inv = lax.rsqrt(mean_rows(x * x) + EPSILON)
            n = x * inv
            d1 = acc[sl]
            c = d1 * gain
            dx[sl] = rescot[sl] + inv * (c - mean_rows(c) - n * mean_rows(c * n))
            vecs[0:1] += jnp.sum(d1 * n, axis=0, keepdims=True)
            vecs[1:2] += jnp.sum(d1, axis=0, keepdims=True)


def entry_back_call(F, img, x1, e, rescot, par, wts):
    slots, T, D = img.shape
    M = slots * T
    R = wts.shape[2]
    fl = jnp.float32
    return pl.pallas_call(
        entry_back_kernel,
        grid=(3,),
        out_shape=[jax.ShapeDtypeStruct((M, D), fl), jax.ShapeDtypeStruct((F, 3, R, D), jnp.bfloat16), jax.ShapeDtypeStruct((8, D), fl)],
        in_specs=[VM, VM, pl.BlockSpec((M, D), lambda j: (0, j)), VM, VM, pl.BlockSpec((F, 1, R, D), lambda j: (0, j, 0, 0))],
        out_specs=[VM, pl.BlockSpec((F, 1, R, D), lambda j: (0, j, 0, 0)), VM],
        scratch_shapes=[pltpu.VMEM((M, D), fl)],
        compiler_params=pltpu.CompilerParams(dimension_semantics=("arbitrary",), vmem_limit_bytes=60 * 2**20),
        name="entry_back",
    )(img, x1, e, rescot, par, wts)


def body(S, F, images, out_grad, lengths, images_held, first_gain, first_shift, entry_weight, entry_bias, exit_weight,
         exit_bias, first_scale, second_gain, second_shift, up_weight, up_bias, down_weight, down_bias, second_scale):
    slots, T, D = images.shape
    M = slots * T
    R = entry_weight.shape[0]
    FF = up_weight.shape[1]
    fl = jnp.float32
    V = R
    rows = [first_gain, first_shift, entry_bias, exit_bias, first_scale, second_gain, second_shift, up_bias, down_bias, second_scale]
    own_vec = jnp.concatenate(rows).reshape(-1, V)
    own_vec = jnp.pad(own_vec, ((0, 16 - own_vec.shape[0]), (0, 128 - V)))
    first, vec = gather_call(S, F, 0, D, [entry_weight], own_vec, [(0, 0, j * D) for j in range(3)])
    other_blocks = [(2, j * R, 0) for j in range(4)] + [(1, 0, j * D) for j in range(4)] + [(0, 0, 0)]
    rest, _ = gather_call(S, F, 1, D, [exit_weight, up_weight, down_weight], own_vec, other_blocks)
    vec = vec[:, :, :V].astype(fl)
    par = vec.transpose(1, 0, 2).reshape(16, D)
    eb = vec[:, 2:4].reshape(2, D)
    eb = jnp.stack([eb[0], jnp.zeros_like(eb[0]), eb[1]]).reshape(3, 1, D)
    ub = vec[:, 8:12].reshape(1, FF)

    x1, heads = qkv_call(S, F, 2, images, par, eb, first)
    out_t, lse, att = attend_call(S, F, 3, lengths, heads)
    layer, rescot, vmid, ubg, part, cots = middle_call(
        S, F, 4, lengths, images_held, images, out_grad, att.reshape(M, D), par, ub, rest
    )
    back = back_call(S, F, 5, lengths, heads, out_t, lse, cots)
    dx, dw, vlast = entry_back_call(F, images, x1, back.reshape(M, 3 * D), rescot, par, first)

    eg = vlast[2:4].reshape(F, 2, V)
    ug = ubg.reshape(F, 4, V)
    one = lambda v: v.reshape(F, 1, V)
    slab = jnp.concatenate(
        [one(vlast[0]), one(vlast[1]), eg, one(vmid[5]), one(vmid[4]), one(vmid[2]), one(vmid[3]), ug, one(vmid[1]), one(vmid[0])], axis=1
    )
    slab = jnp.pad(slab, ((0, 0), (0, 2), (0, 128 - V)))
    none = jnp.zeros((F, 8, 128), fl)
    g_rest, _ = scatter_call(S, F, 6, part, none)
    g_first, small = scatter_call(S, F, 7, dw, slab)
    small = small[:, :V]
    row = lambda n, m=1: small[n : n + m].reshape(m * V)
    g_first, g_rest = g_first.astype(fl), g_rest.astype(fl)
    return (
        layer.reshape(slots, T, D),
        dx.reshape(slots, T, D),
        row(0),
        row(1),
        g_first.transpose(1, 0, 2).reshape(R, 3 * D),
        row(2, 2),
        g_rest[8],
        row(4),
        row(5),
        row(6),
        row(7),
        g_rest[4:8].transpose(1, 0, 2).reshape(R, 4 * D),
        row(8, 4),
        g_rest[0:4].reshape(4 * R, D),
        row(12),
        row(13),
    )


def solution(mesh):
    S, F = mesh.shape["seq"], mesh.shape["fsdp"]
    vector, matrix, tokens = P("fsdp"), P("fsdp", None), P("fsdp", "seq", None)
    return jax.shard_map(
        functools.partial(body, S, F),
        mesh=mesh,
        in_specs=(tokens, tokens, vector, P(), vector, vector, matrix, vector, matrix, vector, vector, vector, vector,
                  matrix, vector, matrix, vector, vector),
        out_specs=(tokens, tokens, vector, vector, matrix, vector, matrix, vector, vector, vector, vector, matrix, vector,
                   matrix, vector, vector),
        check_vma=False,
    )
```

```python
import functools
import math

import jax
import jax.numpy as jnp
from jax import lax
from jax.experimental import pallas as pl
from jax.experimental.pallas import tpu as pltpu
from jax.sharding import PartitionSpec as P

HEAD_DIM = 64
EPSILON = 1e-06
NEG_LARGE = -1e30

MESH = pl.DeviceIdType.MESH
DMA = pltpu.SemaphoreType.DMA
ANY = pl.BlockSpec(memory_space=pl.ANY)
VM = pl.BlockSpec(memory_space=pltpu.VMEM)


def remote(src, dst, ssem, rsem, dev):
    return pltpu.make_async_remote_copy(
        src_ref=src, dst_ref=dst, send_sem=ssem, recv_sem=rsem, device_id=dev, device_id_type=MESH
    )


class Place:
    def __init__(self, S, F):
        self.S, self.F, self.Z = S, F, F // 2
        self.bits = [1 << b for b in range(S.bit_length() - 1)]
        self.nbits = len(self.bits)
        self.order = [self.bits, self.bits[1:] + self.bits[:1]]
        self.s = lax.axis_index("seq")
        self.f = lax.axis_index("fsdp")
        self.z, self.c = self.f // 2, lax.rem(self.f, 2)
        self.mate = (self.s, self.f ^ 1)

    def at(self, zz):
        return (self.s, zz * 2 + self.c)

    def meet(self, fsdp=True, seq=True):
        bar = pltpu.get_barrier_semaphore()
        count = 0
        if fsdp:
            for k in range(1, self.F):
                pl.semaphore_signal(bar, inc=1, device_id=(self.s, lax.rem(self.f + k, self.F)), device_id_type=MESH)
            count += self.F - 1
        if seq:
            for k in range(1, self.S):
                pl.semaphore_signal(bar, inc=1, device_id=(self.s ^ k, self.f), device_id_type=MESH)
            count += self.S - 1
        pl.semaphore_wait(bar, count)


def span(bits):
    out = [0]
    for b in bits:
        out = out + [m | b for m in out]
    return out


def ds(start, size):
    return pl.ds(pl.multiple_of(start, size), size)


class Gather:
    def __init__(self, g, NB, b0, own, full, refs, wide=False, lag=8):
        self.g, self.NB, self.b0, self.own, self.full, self.lag = g, NB, b0, own, full, lag
        self.bounce, self.zs, self.zr, self.xs, self.xr, self.ms, self.ls = refs
        self.R, self.D = full.shape[2:]
        self.C = self.D if wide else self.D // g.S
        self.nbits = 0 if wide else g.nbits
        self.mine = 0 if wide else g.s
        self.nitems = (g.Z - 1) * NB * 2
        self.steps = self.nitems + lag * self.nbits

    @staticmethod
    def scratch(S, F, NB, R, D, bounce=True):
        Z, nb = F // 2, S.bit_length() - 1
        return [pltpu.VMEM((NB if bounce else 1, R, D), jnp.bfloat16), DMA((2,)), DMA((NB, Z)), DMA((nb,)),
                DMA((NB, Z, nb)), DMA((2,)), DMA((1,))]

    def cols(self, q):
        return ds(q * self.C, self.C)

    def half(self, p):
        return pl.ds(p * (self.R // 2), self.R // 2)

    def block(self, f, b):
        return self.full.at[f, self.b0 + b]

    def zfull(self, b, zz):
        return self.full.at[zz * 2 + self.g.c, self.b0 + b, :, self.cols(self.mine)]

    def zcopy(self, src, b, zz, way, to):
        return remote(src, self.zfull(b, zz), self.zs.at[way], self.zr.at[b, zz], self.g.at(to))

    def mate_copy(self, src, b, zz):
        return remote(src, self.block(zz * 2 + self.g.c, b), self.ms.at[0], self.ms.at[1], self.g.mate)

    def keeps(self):
        direct = self.bounce.shape[0] < self.NB
        for b in range(self.NB):
            dst = self.block(self.g.f, b) if direct else self.bounce.at[b]
            yield pltpu.make_async_copy(self.own(b, slice(None)), dst, self.ls.at[0])

    def stored(self):
        return pltpu.make_async_copy(self.bounce, self.full.at[self.g.f, pl.ds(self.b0, self.NB)], self.ls.at[0])

    def start(self):
        g = self.g
        for b in range(self.NB):
            piece = self.own(b, self.cols(self.mine))

            @pl.when(g.z < g.Z - 1)
            def _():
                self.zcopy(piece, b, g.z, 0, g.z + 1).start()

            @pl.when(g.z > 0)
            def _():
                self.zcopy(piece, b, g.z, 1, g.z - 1).start()

        for cp in self.keeps():
            cp.start()
        for b in range(self.NB):
            self.mate_copy(self.own(b, slice(None)), b, g.z).start()

    def kept(self):
        blocks = self.full.at[self.g.f, pl.ds(self.b0, self.NB)]
        pltpu.make_async_copy(blocks, blocks, self.ls.at[0]).wait()
        if self.bounce.shape[0] == self.NB:
            self.stored().start()

    def xcopies(self, b, zz, p, j):
        g = self.g
        to = (g.s ^ g.order[p][j], g.f)
        out = []
        for m in span(g.order[p][:j]):
            ref = self.full.at[zz * 2 + g.c, self.b0 + b, self.half(p), self.cols(g.s ^ m)]
            out.append(remote(ref, ref, self.xs.at[j], self.xr.at[b, zz, j], to))
        return out

    def doubled(self, b, zz, j):
        ref = self.full.at[zz * 2 + self.g.c, self.b0 + b, :, pl.ds(0, self.C << j)]
        return remote(ref, ref, self.xs.at[j], self.xr.at[b, zz, j], self.g.mate)

    def item(self, t):
        g = self.g
        h = 1 + t // (2 * self.NB)
        r = lax.rem(t, 2 * self.NB)
        b, below = r // 2, lax.rem(r, 2) == 0
        zz = jnp.where(below, g.z - h, g.z + h)
        ok = (t >= 0) & (t < self.nitems) & (zz >= 0) & (zz < g.Z)
        nxt = jnp.where(below, g.z + 1, g.z - 1)
        more = (nxt >= 0) & (nxt < g.Z)
        way = jnp.where(below, 0, 1)
        return b, zz, ok, nxt, more, way

    def step(self, t):
        g = self.g
        for j in reversed(range(self.nbits + 1)):
            b, zz, ok, nxt, more, way = self.item(t - self.lag * j)

            @pl.when(ok)
            def _(j=j, b=b, zz=zz, nxt=nxt, more=more, way=way):
                if j == 0:
                    piece = self.zfull(b, zz)
                    self.zcopy(piece, b, zz, 0, g.z).wait_recv()

                    @pl.when(more)
                    def _():
                        self.zcopy(piece, b, zz, way, nxt).start()
                else:
                    self.doubled(b, zz, j - 1).wait_recv()
                if j < self.nbits:
                    for p in range(2):
                        for cp in self.xcopies(b, zz, p, j):
                            cp.start()
                else:
                    self.mate_copy(self.block(zz * 2 + g.c, b), b, zz).start()

    def run(self, lo, hi):
        @pl.loop(lo, hi)
        def _(t):
            self.step(t)

    def part(self, chips, cols):
        ref = self.full.at[pl.ds(0, chips), pl.ds(self.b0, self.NB), :, pl.ds(0, cols)]
        return ref

    def finish_recv(self):
        if self.bounce.shape[0] == self.NB:
            self.stored().wait()
        ref = self.part(self.g.Z, self.D)
        remote(ref, ref, self.ms.at[0], self.ms.at[1], self.g.mate).wait_recv()

    def finish_send(self):
        g = self.g
        ref = self.part(g.Z, self.D)
        remote(ref, ref, self.ms.at[0], self.ms.at[1], g.mate).wait_send()
        for j in range(self.nbits):
            ref = self.part(g.Z - 1, self.C << j)
            remote(ref, ref, self.xs.at[j], self.xr.at[0, 0, j], g.mate).wait_send()
        for zz in range(g.Z):

            @pl.when(g.z == zz)
            def _(zz=zz):
                for way, n in ((0, zz + 1 if zz < g.Z - 1 else 0), (1, g.Z - zz if zz > 0 else 0)):
                    if n:
                        ref = self.part(n, self.C)
                        remote(ref, ref, self.zs.at[way], self.zr.at[0, 0], g.mate).wait_send()


class Scatter:
    LAG = 4

    def __init__(self, g, NB, part, out, bufs, sems):
        self.g, self.NB, self.part, self.out = g, NB, part, out
        self.cs_buf, self.r0, self.xb, self.zb, self.fq = bufs
        self.own, self.c_s, self.c_r, self.x_s, self.x_r, self.z_s, self.z_r, self.a_s, self.a_r, self.o = sems
        self.R, self.D = part.shape[2:]
        self.C = self.D // g.S
        self.nitems = NB * g.Z
        self.tail = g.nbits * self.LAG
        self.steps = self.nitems + self.tail + 1 + (g.nbits + 2) * self.LAG * 2

    @staticmethod
    def scratch(S, F, NB, R, D, dtype=jnp.bfloat16):
        Z, nb = F // 2, S.bit_length() - 1
        C = D // S
        n = NB * Z
        return [
            pltpu.VMEM((n, R, D), dtype), pltpu.VMEM((n, R, D), dtype), pltpu.VMEM((n, 2, R // 2, D - C), dtype),
            pltpu.VMEM((NB, Z, R, C), dtype), pltpu.VMEM((NB, R, C), dtype),
            DMA((n,)), DMA((1,)), DMA((n,)), DMA((nb,)), DMA((n, nb)),
            DMA((1,)), DMA((NB,)), DMA((nb,)), DMA((NB, nb)), DMA((1,)),
        ]

    def where(self, t):
        g = self.g
        b, r = t // g.Z, lax.rem(t, g.Z)
        zz = jnp.where(lax.rem(r, 2) == 0, r // 2, g.Z - 1 - r // 2)
        return b, zz

    def cols(self, q):
        return ds(q * self.C, self.C)

    def half(self, p):
        return pl.ds(p * (self.R // 2), self.R // 2)

    def load(self, t):
        b, zz = self.where(t)
        return pltpu.make_async_copy(self.part.at[zz * 2 + self.g.c, b], self.cs_buf.at[t], self.own.at[t])

    def swap(self, t):
        b, zz = self.where(t)
        return remote(self.part.at[zz * 2 + 1 - self.g.c, b], self.r0.at[t], self.c_s.at[0], self.c_r.at[t], self.g.mate)

    def offset(self, j):
        D, C, S = self.D, self.C, self.g.S
        return sum((S >> (i + 1)) * C for i in range(j))

    def halving(self, t, p, j):
        g = self.g
        order = g.order[p]
        mask = sum(order[: j + 1])
        base = (g.s ^ order[j]) & mask
        to = (g.s ^ order[j], g.f)
        out = []
        for i, m in enumerate(span(order[j + 1 :])):
            src = self.cs_buf.at[t, self.half(p), self.cols(base | m)]
            dst = self.xb.at[t, p, :, pl.ds(self.offset(j) + i * self.C, self.C)]
            out.append(remote(src, dst, self.x_s.at[j], self.x_r.at[t, j], to))
        return out

    def halved(self, t, j):
        ref = self.xb.at[t, :, :, pl.ds(self.offset(j), (self.g.S >> (j + 1)) * self.C)]
        return remote(ref, ref, self.x_s.at[j], self.x_r.at[t, j], self.g.mate)

    def add_halves(self, t, p, j):
        g = self.g
        order = g.order[p]
        mask = sum(order[: j + 1])
        base = g.s & mask
        for i, m in enumerate(span(order[j + 1 :])):
            q = self.cols(base | m)
            got = self.xb[t, p, :, pl.ds(self.offset(j) + i * self.C, self.C)]
            self.cs_buf[t, self.half(p), q] = self.cs_buf[t, self.half(p), q] + got

    def piece(self, t, b, zz):
        g = self.g
        return remote(self.cs_buf.at[t, :, self.cols(g.s)], self.zb.at[b, g.z], self.z_s.at[0], self.z_r.at[b], g.at(zz))

    def arrived(self, b):
        ref = self.zb.at[b, pl.ds(0, self.g.Z - 1)]
        return remote(ref, ref, self.z_s.at[0], self.z_r.at[b], self.g.mate)

    def doubling(self, b, p, j):
        g = self.g
        to = (g.s ^ g.order[p][j], g.f)
        out = []
        for m in span(g.order[p][:j]):
            dst = self.out.at[b, self.half(p), self.cols(g.s ^ m)]
            src = self.fq.at[b, self.half(p)] if m == 0 else dst
            out.append(remote(src, dst, self.a_s.at[j], self.a_r.at[b, j], to))
        return out

    def doubled(self, b, j):
        ref = self.out.at[b, :, pl.ds(0, self.C << j)]
        return remote(ref, ref, self.a_s.at[j], self.a_r.at[b, j], self.g.mate)

    def stored(self, b):
        return pltpu.make_async_copy(self.fq.at[b], self.out.at[b, :, self.cols(self.g.s)], self.o.at[0])

    def start(self):
        @pl.loop(0, self.nitems)
        def _(t):
            self.swap(t).start()
            self.load(t).start()

    def step(self, t):
        g = self.g
        last = g.Z - 1
        for j in reversed(range(g.nbits + 1)):
            u = t - self.tail - self.LAG * 2 * (1 + j) - last
            @pl.when((u >= 0) & (u < self.nitems) & (lax.rem(u, g.Z) == 0))
            def _(j=j, u=u):
                b = u // g.Z
                if j == 0:
                    r = jnp.where(g.z < (g.Z + 1) // 2, 2 * g.z, 2 * (g.Z - 1 - g.z) + 1)
                    total = self.cs_buf[b * g.Z + r, :, self.cols(g.s)].astype(jnp.float32)
                    self.arrived(b).wait_recv()
                    for k in range(1, g.Z):
                        total = total + self.zb[b, lax.rem(g.z + k, g.Z)].astype(jnp.float32)
                    self.fq[b] = total.astype(self.fq.dtype)
                    self.stored(b).start()
                else:
                    self.doubled(b, j - 1).wait_recv()
                if j < g.nbits:
                    for p in range(2):
                        for cp in self.doubling(b, p, j):
                            cp.start()
        for j in reversed(range(g.nbits + 1)):
            u = t - self.LAG * j
            @pl.when((u >= 0) & (u < self.nitems))
            def _(j=j, u=u):
                b, zz = self.where(u)
                if j == 0:
                    self.load(u).wait()
                    self.swap(u).wait_recv()
                    self.cs_buf[u] = self.cs_buf[u] + self.r0[u]
                else:
                    self.halved(u, j - 1).wait_recv()
                    for p in range(2):
                        self.add_halves(u, p, j - 1)
                if j < g.nbits:
                    for p in range(2):
                        for cp in self.halving(u, p, j):
                            cp.start()
                else:
                    @pl.when(zz != g.z)
                    def _():
                        self.piece(u, b, zz).start()

    def run(self, lo, hi):
        @pl.loop(lo, hi)
        def _(t):
            self.step(t)

    def finish(self):
        g = self.g
        NB, Z, n = self.NB, g.Z, self.nitems
        done = lambda ref, sem: remote(ref, ref, sem, self.z_r.at[0], g.mate).wait_send()
        done(self.r0, self.c_s.at[0])
        done(self.zb.at[:, pl.ds(0, Z - 1)], self.z_s.at[0])
        for j in range(g.nbits):
            done(self.xb.at[:, :, :, pl.ds(self.offset(j), (g.S >> (j + 1)) * self.C)], self.x_s.at[j])
            done(self.out.at[:, :, pl.ds(0, self.C << j)], self.a_s.at[j])
        ref = self.out.at[:, :, pl.ds(0, self.C)]
        pltpu.make_async_copy(ref, ref, self.o.at[0]).wait()


class VecGather:
    def __init__(self, g, vec, out, sems):
        self.g, self.vec, self.out, self.sems = g, vec, out, sems

    @staticmethod
    def scratch(F):
        return [DMA((3,))]

    def start(self):
        g, sems = self.g, self.sems
        pltpu.make_async_copy(self.vec, self.out.at[g.f], sems.at[2]).start()
        for k in range(1, g.F):
            remote(self.vec, self.out.at[g.f], sems.at[0], sems.at[1], (g.s, lax.rem(g.f + k, g.F))).start()

    def finish(self):
        g, sems = self.g, self.sems
        pltpu.make_async_copy(self.vec, self.out.at[g.f], sems.at[2]).wait()
        ref = self.out.at[pl.ds(0, g.F - 1)]
        cp = remote(ref, ref, sems.at[0], sems.at[1], g.mate)
        cp.wait_send()
        cp.wait_recv()


class VecSum:
    def __init__(self, g, vec, out, refs):
        self.g, self.vec, self.out = g, vec, out
        self.fb, self.mid, self.sb, self.sems = refs

    @staticmethod
    def scratch(S, F, N, L):
        fl = jnp.float32
        return [pltpu.VMEM((F, N, L), fl), pltpu.VMEM((N, L), fl), pltpu.VMEM((S, N, L), fl), DMA((4,))]

    def start(self):
        g = self.g
        for k in range(1, g.F):
            to = lax.rem(g.f + k, g.F)
            remote(self.vec.at[to], self.fb.at[g.f], self.sems.at[0], self.sems.at[1], (g.s, to)).start()

    def middle(self):
        g = self.g
        ref = self.fb.at[pl.ds(0, g.F - 1)]
        cp = remote(ref, ref, self.sems.at[0], self.sems.at[1], g.mate)
        cp.wait_recv()
        total = self.vec[g.f]
        for k in range(1, g.F):
            total = total + self.fb[lax.rem(g.f + k, g.F)]
        self.mid[...] = total
        for k in range(1, g.S):
            remote(self.mid, self.sb.at[g.s], self.sems.at[2], self.sems.at[3], (g.s ^ k, g.f)).start()
        cp.wait_send()

    def finish(self):
        g = self.g
        ref = self.sb.at[pl.ds(0, g.S - 1)]
        cp = remote(ref, ref, self.sems.at[2], self.sems.at[3], g.mate)
        cp.wait_recv()
        total = self.mid[...]
        for k in range(1, g.S):
            total = total + self.sb[g.s ^ k]
        self.out[...] = total
        cp.wait_send()


PARAMS = dict(has_side_effects=True, vmem_limit_bytes=60 * 2**20)


def scatter_call(S, F, cid, part, vec):
    _, NB, R, D = part.shape
    N, L = vec.shape[1:]

    def kernel(part, vec, out, vec_out, *rest):
        g = Place(S, F)
        g.meet()
        vsum = VecSum(g, vec, vec_out, rest[:4])
        sc = Scatter(g, NB, part, out, rest[4:9], rest[9:])
        vsum.start()
        sc.start()
        vsum.middle()
        sc.run(0, sc.steps)
        sc.finish()
        vsum.finish()

    return pl.pallas_call(
        kernel,
        out_shape=[jax.ShapeDtypeStruct((NB, R, D), jnp.bfloat16), jax.ShapeDtypeStruct((N, L), jnp.float32)],
        in_specs=[ANY, VM],
        out_specs=[ANY, VM],
        scratch_shapes=VecSum.scratch(S, F, N, L) + Scatter.scratch(S, F, NB, R, D),
        compiler_params=pltpu.CompilerParams(collective_id=cid, **PARAMS),
        name="gradients_out",
    )(part, vec)


def fp32(x):
    return x.astype(jnp.float32)


def dot(a, b, dims=((1,), (0,))):
    return lax.dot_general(a, b, (dims, ((), ())), preferred_element_type=jnp.float32)


NT = ((1,), (1,))
TN = ((0,), (0,))


def mean_rows(x):
    return jnp.mean(x, axis=-1, keepdims=True)


def head_lanes(rows, hh):
    lane = lax.broadcasted_iota(jnp.int32, (rows, 128), 1)
    mine = (lane >= hh * HEAD_DIM) & (lane < (hh + 1) * HEAD_DIM)
    spare = lane == (1 - hh) * HEAD_DIM
    return mine, spare


def masked_keys(k, length, hh):
    N = k.shape[0]
    mine, spare = head_lanes(N, hh)
    late = lax.broadcasted_iota(jnp.int32, (N, 128), 0) >= length
    return jnp.where(mine, fp32(k), jnp.where(spare & late, NEG_LARGE, 0.0)).astype(jnp.bfloat16)


def scaled_queries(q, hh):
    mine, spare = head_lanes(q.shape[0], hh)
    return jnp.where(mine, fp32(q) * HEAD_DIM ** (-0.5), jnp.where(spare, 1.0, 0.0)).astype(jnp.bfloat16)


def front_kernel(S, F, nwide, QB, lengths, img, vec, wq, wx, wu, wd,
                 first, rest, par, ub, x1, heads_out, out_t, lse, att,
                 vec_full, norm, eb, stage, heads, kh, vt, o_buf, asem, hsem, ssem, rsem, osem, *refs):
    g = Place(S, F)
    slots, T, D = img.shape
    R = first.shape[2]
    V = R
    W = D // S
    N = S * T
    pairs = W // 128
    vg = VecGather(g, vec, vec_full, refs[0])

    def own_first(b, cols):
        if isinstance(cols, slice):
            return wq.at[:, pl.ds(b * D, D)]
        return wq.at[:, pl.ds(pl.multiple_of(b * D + cols.start, 128), cols.size)]

    def own_rest(b0):
        def own(b, cols):
            b = b + b0
            ref, r0, c0 = (wd, b * R, 0) if b < 4 else (wu, 0, (b - 4) * D) if b < 8 else (wx, 0, 0)
            if isinstance(cols, slice):
                return ref.at[pl.ds(r0, R), pl.ds(c0, D)]
            return ref.at[pl.ds(r0, R), pl.ds(pl.multiple_of(c0 + cols.start, 128), cols.size)]

        return own

    entry = Gather(g, 3, 0, own_first, first, refs[1:8], lag=ENTRY_LAG)
    thin = Gather(g, 9 - nwide, nwide, own_rest(nwide), rest, refs[8:15])
    wide = Gather(g, nwide, 0, own_rest(0), rest, refs[15:22], wide=True)

    g.meet()
    vg.start()
    entry.start()
    rows = min(128, T)

    @pl.loop(0, slots * T // rows)
    def _(r):
        i, t = r // (T // rows), lax.rem(r, T // rows)
        x = fp32(img[i, pl.ds(t * rows, rows)])
        x = x - mean_rows(x)
        norm[ds(r * rows, rows)] = x * lax.rsqrt(mean_rows(x * x) + EPSILON)

    entry.kept()
    entry.run(0, entry.nitems)
    vg.finish()
    thin.start()
    wide.start()
    for f in range(F):
        v = fp32(vec_full[f])[:, :V]
        par[:, f * V : (f + 1) * V] = v
        for r in range(2):
            at = (f * 2 + r) * V
            eb[2 * (at // D), :, at % D : at % D + V] = v[2 + r : 3 + r]
        for r in range(4):
            at = (f * 4 + r) * V
            ub[:, at : at + V] = v[8 + r : 9 + r]
    eb[1] = jnp.zeros((1, D), jnp.float32)
    gain, shift = par[0:1], par[1:2]

    @pl.loop(0, slots * T // rows)
    def _(r):
        x1[ds(r * rows, rows)] = (norm[ds(r * rows, rows)] * gain + shift).astype(x1.dtype)

    entry.run(entry.nitems, entry.steps)
    thin.kept()
    wide.kept()
    entry.finish_recv()

    def copy(i, k, j):
        src = stage.at[i, k, j]
        dst = heads.at[j, i, ds(g.s * T, T)]
        return remote(src, dst, ssem.at[i, k, j], rsem.at[i, k, j], (g.s ^ k, g.f))

    def local(i, j):
        return pltpu.make_async_copy(stage.at[i, 0, j], heads.at[j, i, ds(g.s * T, T)], ssem.at[i, 0, j])

    def project(i):
        @pl.loop(0, S * 3)
        def _(n):
            k = lax.rem(1 + n // 3, S)
            j = lax.rem(n, 3)
            cols = ds((g.s ^ k) * W, W)
            w = first[:, j, :, cols].reshape(D, W)
            out = dot(x1[i * T : (i + 1) * T], w) + eb[j, :, cols]
            stage[i, k, j] = out.astype(stage.dtype)

            @pl.when(k != 0)
            def _():
                copy(i, k, j).start()

            @pl.when(k == 0)
            def _():
                local(i, j).start()

    def projected(i):
        for j in range(3):
            local(i, j).wait()
            for k in range(1, S):
                copy(i, k, j).wait_send()
                dst = heads.at[j, i, ds((g.s ^ k) * T, T)]
                remote(dst, dst, ssem.at[i, k, j], rsem.at[i, k, j], (g.s ^ k, g.f)).wait_recv()
        keep_heads(i).start()

    def keep_heads(i):
        return pltpu.make_async_copy(heads.at[:, i], heads_out.at[:, i], hsem.at[i])

    def out_copy(i, hp, kk):
        e = i * pairs + hp
        dst = att.at[i, :, pl.ds(pl.multiple_of(g.s * W + hp * 128, 128), 128)]
        if kk == 0:
            return pltpu.make_async_copy(o_buf.at[e, ds(g.s * T, T)], dst, osem.at[0, e, 0])
        return remote(o_buf.at[e, ds((g.s ^ kk) * T, T)], dst, osem.at[0, e, kk], osem.at[1, e, kk], (g.s ^ kk, g.f))

    def attend(i, hp):
        e = i * pairs + hp
        lanes = slice(hp * 128, (hp + 1) * 128)
        vt[...] = heads[2, i, :, lanes].T
        for hh in range(2):
            kh[hh] = masked_keys(heads[1, i, :, lanes], lengths[i], hh)

        @pl.loop(0, N // QB)
        def _(b):
            cols = ds(b * QB, QB)
            qb = heads[0, i, cols, lanes]
            for hh in range(2):
                sc = dot(kh[hh], scaled_queries(qb, hh), NT)
                top = jnp.max(sc, axis=0, keepdims=True)
                ex = jnp.exp(sc - top)
                total = jnp.sum(ex, axis=0, keepdims=True)
                w = (ex * (1.0 / total)).astype(jnp.bfloat16)
                o = dot(vt[hh * HEAD_DIM : (hh + 1) * HEAD_DIM], w).astype(jnp.bfloat16)
                at = hp * 128 + hh * HEAD_DIM
                out_t[i, at : at + HEAD_DIM, cols] = o
                lse[i, hp, hh : hh + 1, cols] = top + jnp.log(total)
            background(e * (N // QB) + b)

        o_buf[e] = out_t[i, lanes].T
        for kk in list(range(1, S)) + [0]:
            out_copy(i, hp, kk).start()

    units = [(i, hp) for i in range(slots) for hp in range(pairs)]
    early = thin.steps // EARLY
    per_unit = -(-(thin.steps - early) // (len(units) * (N // QB)))

    def background(n):
        @pl.when(n < wide.steps)
        def _():
            wide.step(n)

        for m in range(per_unit):
            thin.step(early + n * per_unit + m)

    for i in range(slots):
        project(i)
    thin.run(0, early)
    entry.finish_send()
    for n, (i, hp) in enumerate(units):
        if hp == 0:
            projected(i)
        attend(i, hp)
    wide.run(len(units) * (N // QB), wide.steps)
    for gather in (thin, wide):
        gather.finish_recv()
        gather.finish_send()
    for i, hp in units:
        for kk in range(S):
            cp = out_copy(i, hp, kk)
            if kk == 0:
                cp.wait()
            else:
                cp.wait_send()
                cp.wait_recv()
    for i in range(slots):
        keep_heads(i).wait()


ENTRY_LAG = 6
WIDE = 3
EARLY = 10


def front_call(S, F, cid, lengths, img, vec, wq, wx, wu, wd):
    slots, T, D = img.shape
    R, FF = wq.shape[0], wu.shape[1]
    W, N = D // S, S * T
    pairs = W // 128
    bf, fl = jnp.bfloat16, jnp.float32
    out = jax.ShapeDtypeStruct
    return pl.pallas_call(
        functools.partial(front_kernel, S, F, WIDE, min(256, N)),
        out_shape=[
            out((F, 3, R, D), bf), out((F, 9, R, D), bf), out((16, D), fl), out((1, FF), fl), out((slots * T, D), bf),
            out((3, slots, N, W), bf), out((slots, W, N), bf), out((slots, pairs, 8, N), fl), out((slots, T, D), bf),
        ],
        in_specs=[pl.BlockSpec(memory_space=pltpu.SMEM), VM, ANY, ANY, ANY, ANY, ANY],
        out_specs=[VM, ANY, VM, VM, VM, ANY, VM, VM, ANY],
        scratch_shapes=[
            pltpu.VMEM((F, 16, 128), bf), pltpu.VMEM((slots * T, D), fl), pltpu.VMEM((3, 1, D), fl), pltpu.VMEM((slots, S, 3, T, W), bf),
            pltpu.VMEM((3, slots, N, W), bf), pltpu.VMEM((2, N, 128), bf), pltpu.VMEM((128, N), bf),
            pltpu.VMEM((slots * pairs, N, 128), bf), DMA((1,)), DMA((slots,)), DMA((slots, S, 3)), DMA((slots, S, 3)),
            DMA((2, slots * pairs, S)),
        ]
        + VecGather.scratch(F)
        + Gather.scratch(S, F, 3, R, D, bounce=False)
        + Gather.scratch(S, F, 9 - WIDE, R, D)
        + Gather.scratch(S, F, WIDE, R, D),
        compiler_params=pltpu.CompilerParams(collective_id=cid, **PARAMS),
        name="front",
    )(lengths, img, vec, wq, wx, wu, wd)


def middle_kernel(S, F, lengths, held, img, cot, att, par, ub, wx, wu, wd,
                  layer, rescot, vecs, ubg, part, cots,
                  mixed, normed, inv2, x2, x2t, dcot, down, cot2, dwu, dwd, dwx, stage, ssem, rsem, psem):
    g = Place(S, F)
    j = pl.program_id(0)
    slots, T, D = img.shape
    M = slots * T
    W = D // S
    R = wx.shape[2]
    H = wu.shape[3]
    rows = min(128, T)
    nrows = M // rows
    exit_bias, scale1, gain2, shift2 = par[4:5], par[5:6], par[6:7], par[7:8]
    down_bias, scale2 = par[12:13], par[13:14]
    per_block = D // H

    def place(r):
        return r // (T // rows), lax.rem(r, T // rows) * rows

    def mask(r):
        i, t = place(r)
        limit = jnp.where(i < held[g.f], lengths[i], 0)
        pos = lax.broadcasted_iota(jnp.int32, (rows, 1), 0) + (g.s * T + t)
        return jnp.where(pos < limit, 1.0, 0.0)

    def residual(r, sl):
        i, t = place(r)
        return fp32(img[i, pl.ds(t, rows)]) + scale1 * mixed[sl]

    def upstream(r):
        i, t = place(r)
        return mask(r) * fp32(cot[i, pl.ds(t, rows)])

    @pl.when(j == 0)
    def _():
        g.meet(fsdp=False)
        w = wx[...].reshape(D, D)
        mixed[...] = dot(att[...], w) + exit_bias

        @pl.loop(0, nrows)
        def _(r):
            sl = ds(r * rows, rows)
            res = residual(r, sl)
            res = res - mean_rows(res)
            inv = lax.rsqrt(mean_rows(res * res) + EPSILON)
            n = res * inv
            normed[sl] = n
            inv2[sl] = jnp.broadcast_to(inv, (rows, 128))
            x2[sl] = (n * gain2 + shift2).astype(x2.dtype)
            dcot[sl] = (upstream(r) * scale2).astype(dcot.dtype)

        x2t[...] = x2[...].T

    wu_j = wu[...].reshape(D, H)
    wd_j = wd[...].reshape(H, D)
    pre = dot(x2[...], wu_j) + ub[...]
    cumul = 0.5 * (1.0 + lax.erf(pre * (1.0 / math.sqrt(2.0))))
    density = jnp.exp(-0.5 * pre * pre) * (1.0 / math.sqrt(2.0 * math.pi))
    act = (pre * cumul).astype(jnp.bfloat16)
    slope = cumul + pre * density
    pre_cot = dot(dcot[...], wd_j, NT) * slope
    ubg[...] = jnp.sum(pre_cot, axis=0, keepdims=True)
    low = pre_cot.astype(jnp.bfloat16)
    slot = lax.rem(j, 2)

    def put_up(jj, sl):
        cols = pl.ds(pl.multiple_of(lax.rem(jj, per_block) * H, H), H)
        return pltpu.make_async_copy(dwu.at[sl], part.at[:, 4 + jj // per_block, :, cols], psem.at[sl])

    def put_down(jj, sl):
        return pltpu.make_async_copy(dwd.at[sl], part.at[jj, pl.ds(0, 4)], psem.at[2 + sl])

    @pl.when(j >= 2)
    def _():
        put_up(j - 2, slot).wait()
        put_down(j - 2, slot).wait()

    dwu[slot] = dot(x2t[...], low).astype(jnp.bfloat16).reshape(F, R, H)
    dwd[slot] = dot(act, dcot[...], TN).astype(jnp.bfloat16).reshape(4, R, D)
    put_up(j, slot).start()
    put_down(j, slot).start()
    dd = dot(act, wd_j)
    dc = dot(low, wu_j, NT)

    @pl.when(j == 0)
    def _():
        down[...] = dd
        cot2[...] = dc

    @pl.when(j > 0)
    def _():
        down[...] += dd
        cot2[...] += dc

    @pl.when(j == F - 1)
    def _():
        vecs[...] = jnp.zeros_like(vecs)

        @pl.loop(0, nrows)
        def _(r):
            sl = ds(r * rows, rows)
            m = mask(r)
            up = upstream(r)
            out = down[sl] + down_bias
            layer[sl] = (m * (residual(r, sl) + scale2 * out)).astype(layer.dtype)
            n = normed[sl]
            inv = inv2[sl][:, 0:1]
            c2 = cot2[sl]
            c = c2 * gain2
            rc = up + inv * (c - mean_rows(c) - n * mean_rows(c * n))
            rescot[sl] = rc
            mc = rc * scale1
            x2[sl] = mc.astype(x2.dtype)
            total = lambda v: jnp.sum(v, axis=0, keepdims=True)
            vecs[0:1] += total(up * out)
            vecs[1:2] += total(up * scale2)
            vecs[2:3] += total(c2 * n)
            vecs[3:4] += total(c2)
            vecs[4:5] += total(rc * mixed[sl])
            vecs[5:6] += total(mc)

        for k in list(range(1, S)) + [0]:
            peer = g.s ^ k
            stage[k] = dot(x2[...], wx_rows(wx, peer, W), NT).astype(jnp.bfloat16).reshape(slots, T, W)
            dst = cots.at[:, ds(g.s * T, T)]
            if k:
                remote(stage.at[k], dst, ssem.at[k], rsem.at[k], (peer, g.f)).start()
            else:
                pltpu.make_async_copy(stage.at[0], dst, ssem.at[0]).start()
        dwx[...] = dot(att[...], x2[...], TN).astype(jnp.bfloat16).reshape(F, R, D)
        put_x = pltpu.make_async_copy(dwx, part.at[:, 8], psem.at[4])
        put_x.start()
        for jj in (F - 2, F - 1):
            put_up(jj, jj % 2).wait()
            put_down(jj, jj % 2).wait()
        put_x.wait()
        pltpu.make_async_copy(stage.at[0], cots.at[:, ds(g.s * T, T)], ssem.at[0]).wait()
        for k in range(1, S):
            cp = remote(stage.at[k], cots.at[:, ds((g.s ^ k) * T, T)], ssem.at[k], rsem.at[k], (g.s ^ k, g.f))
            cp.wait_send()
            cp.wait_recv()


def wx_rows(wx, peer, W):
    F, _, R, D = wx.shape
    n = W // R
    return wx[pl.ds(peer * n, n), 0].reshape(W, D)


def middle_call(S, F, cid, lengths, held, img, cot, att, par, ub, wts):
    slots, T, D = img.shape
    M = slots * T
    _, NB, R, _ = wts.shape
    FF = ub.shape[1]
    H = FF // F
    W = D // S
    per = D // H
    bf, fl = jnp.bfloat16, jnp.float32
    SM = pl.BlockSpec(memory_space=pltpu.SMEM)
    return pl.pallas_call(
        functools.partial(middle_kernel, S, F),
        grid=(F,),
        out_shape=[
            jax.ShapeDtypeStruct((M, D), bf), jax.ShapeDtypeStruct((M, D), fl), jax.ShapeDtypeStruct((8, D), fl),
            jax.ShapeDtypeStruct((1, FF), fl), jax.ShapeDtypeStruct((F, NB, R, D), bf),
            jax.ShapeDtypeStruct((slots, S * T, W), bf),
        ],
        in_specs=[SM, SM, VM, VM, VM, VM, pl.BlockSpec((1, H), lambda j: (0, j)),
                  pl.BlockSpec((F, 1, R, D), lambda j: (0, 8, 0, 0)),
                  pl.BlockSpec((F, 1, R, H), lambda j: (0, 4 + j // per, 0, lax.rem(j, per))),
                  pl.BlockSpec((1, 4, R, D), lambda j: (j, 0, 0, 0))],
        out_specs=[VM, VM, VM, pl.BlockSpec((1, H), lambda j: (0, j)), ANY, ANY],
        scratch_shapes=[
            pltpu.VMEM((M, D), fl), pltpu.VMEM((M, D), fl), pltpu.VMEM((M, 128), fl), pltpu.VMEM((M, D), bf),
            pltpu.VMEM((D, M), bf), pltpu.VMEM((M, D), bf), pltpu.VMEM((M, D), fl), pltpu.VMEM((M, D), fl),
            pltpu.VMEM((2, F, R, H), bf), pltpu.VMEM((2, 4, R, D), bf), pltpu.VMEM((F, R, D), bf),
            pltpu.VMEM((S, slots, T, W), bf), DMA((S,)), DMA((S,)), DMA((5,)),
        ],
        compiler_params=pltpu.CompilerParams(collective_id=cid, dimension_semantics=("arbitrary",), **PARAMS),
        name="feed_forward",
    )(lengths, held, img, cot, att, par, ub, wts, wts, wts)


def back_kernel(S, F, QB, lengths, q, k, v, out_t, lse, cot, back,
                kh, vh, kt, cot_t, delta, dq_t, dk, dv, stage, ssem, rsem):
    g = Place(S, F)
    i, hp = pl.program_id(0), pl.program_id(1)
    slots, pairs = pl.num_programs(0), pl.num_programs(1)
    N = q.shape[2]
    T = N // S
    D = back.shape[2] // 3
    W = D // S
    e = i * pairs + hp

    @pl.when(e == 0)
    def _():
        g.meet(fsdp=False)

    length = lengths[i]
    kt[...] = k[0, 0].T
    cot_t[...] = cot[0].T
    prod = fp32(cot_t[...]) * fp32(out_t[0])
    for hh in range(2):
        hs = slice(hh * HEAD_DIM, (hh + 1) * HEAD_DIM)
        delta[hh : hh + 1] = jnp.sum(prod[hs], axis=0, keepdims=True)
        kh[hh] = masked_keys(k[0, 0], length, hh)
        mine, _ = head_lanes(N, hh)
        vh[hh] = jnp.where(mine, fp32(v[0, 0]), 0.0).astype(jnp.bfloat16)
    dk[...] = jnp.zeros_like(dk)
    dv[...] = jnp.zeros_like(dv)

    @pl.loop(0, N // QB)
    def _(b):
        cols = ds(b * QB, QB)
        qb, cb = q[0, 0, cols], cot[0, cols]
        mines = [head_lanes(QB, hh)[0] for hh in range(2)]
        for hh in range(2):
            hs = slice(hh * HEAD_DIM, (hh + 1) * HEAD_DIM)
            qs = scaled_queries(qb, hh)
            prob = jnp.exp(dot(kh[hh], qs, NT) - lse[0, 0, hh : hh + 1, cols])
            sg = dot(vh[hh], cb, NT)
            sc = (prob * (sg - delta[hh : hh + 1, cols])).astype(jnp.bfloat16)
            w = prob.astype(jnp.bfloat16)
            dv[...] += dot(w, jnp.where(mines[hh], fp32(cb), 0.0).astype(jnp.bfloat16))
            dk[...] += dot(sc, jnp.where(mines[hh], fp32(qs), 0.0).astype(jnp.bfloat16))
            dq_t[hs, cols] = (dot(kt[hs], sc) * HEAD_DIM ** (-0.5)).astype(jnp.bfloat16)

    stage[e, 0] = dq_t[...].T
    stage[e, 1] = dk[...].astype(jnp.bfloat16)
    stage[e, 2] = dv[...].astype(jnp.bfloat16)

    def dst(i, hp, j):
        return back.at[i, :, pl.ds(pl.multiple_of(j * D + g.s * W + hp * 128, 128), 128)]

    def copy(e, i, hp, j, kk):
        return remote(stage.at[e, j, ds((g.s ^ kk) * T, T)], dst(i, hp, j), ssem.at[e, j, kk], rsem.at[e, j, kk], (g.s ^ kk, g.f))

    def local(e, i, hp, j):
        return pltpu.make_async_copy(stage.at[e, j, ds(g.s * T, T)], dst(i, hp, j), ssem.at[e, j, 0])

    for j in range(3):
        for kk in range(1, S):
            copy(e, i, hp, j, kk).start()
        local(e, i, hp, j).start()

    @pl.when(e == slots * pairs - 1)
    def _():
        @pl.loop(0, slots * pairs)
        def _(e):
            i, hp = e // pairs, lax.rem(e, pairs)
            for j in range(3):
                local(e, i, hp, j).wait()
                for kk in range(1, S):
                    cp = copy(e, i, hp, j, kk)
                    cp.wait_send()
                    cp.wait_recv()


def back_call(S, F, cid, lengths, heads, out_t, lse, cots):
    _, slots, N, W = heads.shape
    pairs, T, D = W // 128, N // S, W * S
    bf, fl = jnp.bfloat16, jnp.float32
    QB = min(256, N)
    part = lambda j: pl.BlockSpec((1, 1, N, 128), lambda i, h: (j, i, 0, h))
    return pl.pallas_call(
        functools.partial(back_kernel, S, F, QB),
        grid=(slots, pairs),
        out_shape=jax.ShapeDtypeStruct((slots, T, 3 * D), bf),
        in_specs=[pl.BlockSpec(memory_space=pltpu.SMEM), part(0), part(1), part(2),
                  pl.BlockSpec((1, 128, N), lambda i, h: (i, h, 0)),
                  pl.BlockSpec((1, 1, 8, N), lambda i, h: (i, h, 0, 0)),
                  pl.BlockSpec((1, N, 128), lambda i, h: (i, 0, h))],
        out_specs=ANY,
        scratch_shapes=[
            pltpu.VMEM((2, N, 128), bf), pltpu.VMEM((2, N, 128), bf), pltpu.VMEM((128, N), bf), pltpu.VMEM((128, N), bf),
            pltpu.VMEM((8, N), fl), pltpu.VMEM((128, N), bf), pltpu.VMEM((N, 128), fl), pltpu.VMEM((N, 128), fl),
            pltpu.VMEM((slots * pairs, 3, N, 128), bf), DMA((slots * pairs, 3, S)), DMA((slots * pairs, 3, S)),
        ],
        compiler_params=pltpu.CompilerParams(collective_id=cid, dimension_semantics=("arbitrary",) * 2, **PARAMS),
        name="attend_back",
    )(lengths, heads, heads, heads, out_t, lse, cots)


def entry_back_kernel(img, x1, e, rescot, par, w, dx, dw, vecs, acc):
    j = pl.program_id(0)
    slots, T, D = img.shape
    M = slots * T
    rows = min(128, T)
    gain = par[0:1]
    ej = e[...]
    d = dot(ej, w[...].reshape(D, D), NT)
    dw[...] = dot(x1[...], ej, TN).astype(dw.dtype).reshape(dw.shape)
    esum = jnp.sum(fp32(ej), axis=0, keepdims=True)

    @pl.when(j == 0)
    def _():
        acc[...] = d
        vecs[...] = jnp.zeros_like(vecs)
        vecs[2:3] = esum

    @pl.when(j > 0)
    def _():
        acc[...] += d

    @pl.when(j == 2)
    def _():
        vecs[3:4] = esum

        @pl.loop(0, M // rows)
        def _(r):
            sl = ds(r * rows, rows)
            i, t = r // (T // rows), lax.rem(r, T // rows) * rows
            x = fp32(img[i, pl.ds(t, rows)])
            x = x - mean_rows(x)
            inv = lax.rsqrt(mean_rows(x * x) + EPSILON)
            n = x * inv
            d1 = acc[sl]
            c = d1 * gain
            dx[sl] = rescot[sl] + inv * (c - mean_rows(c) - n * mean_rows(c * n))
            vecs[0:1] += jnp.sum(d1 * n, axis=0, keepdims=True)
            vecs[1:2] += jnp.sum(d1, axis=0, keepdims=True)


def entry_back_call(F, img, x1, e, rescot, par, wts):
    slots, T, D = img.shape
    M = slots * T
    R = wts.shape[2]
    fl = jnp.float32
    return pl.pallas_call(
        entry_back_kernel,
        grid=(3,),
        out_shape=[jax.ShapeDtypeStruct((M, D), fl), jax.ShapeDtypeStruct((F, 3, R, D), jnp.bfloat16), jax.ShapeDtypeStruct((8, D), fl)],
        in_specs=[VM, VM, pl.BlockSpec((M, D), lambda j: (0, j)), VM, VM, pl.BlockSpec((F, 1, R, D), lambda j: (0, j, 0, 0))],
        out_specs=[VM, pl.BlockSpec((F, 1, R, D), lambda j: (0, j, 0, 0)), VM],
        scratch_shapes=[pltpu.VMEM((M, D), fl)],
        compiler_params=pltpu.CompilerParams(dimension_semantics=("arbitrary",), vmem_limit_bytes=60 * 2**20),
        name="entry_back",
    )(img, x1, e, rescot, par, wts)


def body(S, F, images, out_grad, lengths, images_held, first_gain, first_shift, entry_weight, entry_bias, exit_weight,
         exit_bias, first_scale, second_gain, second_shift, up_weight, up_bias, down_weight, down_bias, second_scale):
    slots, T, D = images.shape
    M = slots * T
    R = entry_weight.shape[0]
    FF = up_weight.shape[1]
    fl = jnp.float32
    V = R
    rows = [first_gain, first_shift, entry_bias, exit_bias, first_scale, second_gain, second_shift, up_bias, down_bias, second_scale]
    own_vec, at = jnp.zeros((16, 128), jnp.bfloat16), 0
    for v in rows:
        n = v.shape[0] // V
        own_vec = own_vec + jnp.pad(v.reshape(n, V), ((at, 16 - at - n), (0, 128 - V)))
        at += n
    first, rest, par, ub, x1, heads, out_t, lse, att = front_call(
        S, F, 0, lengths, images, own_vec, entry_weight, exit_weight, up_weight, down_weight
    )
    layer, rescot, vmid, ubg, part, cots = middle_call(
        S, F, 4, lengths, images_held, images, out_grad, att.reshape(M, D), par, ub, rest
    )
    back = back_call(S, F, 5, lengths, heads, out_t, lse, cots)
    dx, dw, vlast = entry_back_call(F, images, x1, back.reshape(M, 3 * D), rescot, par, first)

    eg = vlast[2:4].reshape(F, 2, V)
    ug = ubg.reshape(F, 4, V)
    one = lambda v: v.reshape(F, 1, V)
    slab = jnp.concatenate(
        [one(vlast[0]), one(vlast[1]), eg, one(vmid[5]), one(vmid[4]), one(vmid[2]), one(vmid[3]), ug, one(vmid[1]), one(vmid[0])], axis=1
    )
    slab = jnp.pad(slab, ((0, 0), (0, 2), (0, 128 - V)))
    none = jnp.zeros((F, 8, 128), fl)
    g_rest, _ = scatter_call(S, F, 6, part, none)
    g_first, small = scatter_call(S, F, 7, dw, slab)
    small = small[:, :V]
    row = lambda n, m=1: small[n : n + m].reshape(m * V)
    g_first, g_rest = g_first.astype(fl), g_rest.astype(fl)
    return (
        layer.reshape(slots, T, D),
        dx.reshape(slots, T, D),
        row(0),
        row(1),
        g_first.transpose(1, 0, 2).reshape(R, 3 * D),
        row(2, 2),
        g_rest[8],
        row(4),
        row(5),
        row(6),
        row(7),
        g_rest[4:8].transpose(1, 0, 2).reshape(R, 4 * D),
        row(8, 4),
        g_rest[0:4].reshape(4 * R, D),
        row(12),
        row(13),
    )


def solution(mesh):
    S, F = mesh.shape["seq"], mesh.shape["fsdp"]
    vector, matrix, tokens = P("fsdp"), P("fsdp", None), P("fsdp", "seq", None)
    return jax.shard_map(
        functools.partial(body, S, F),
        mesh=mesh,
        in_specs=(tokens, tokens, vector, P(), vector, vector, matrix, vector, matrix, vector, vector, vector, vector,
                  matrix, vector, matrix, vector, vector),
        out_specs=(tokens, tokens, vector, vector, matrix, vector, matrix, vector, vector, vector, vector, matrix, vector,
                   matrix, vector, vector),
        check_vma=False,
    )
```

```python
import functools
import math

import jax
import jax.numpy as jnp
from jax import lax
from jax.experimental import pallas as pl
from jax.experimental.pallas import tpu as pltpu
from jax.sharding import PartitionSpec as P

HEAD_DIM = 64
EPSILON = 1e-06
NEG_LARGE = -1e30

MESH = pl.DeviceIdType.MESH
DMA = pltpu.SemaphoreType.DMA
ANY = pl.BlockSpec(memory_space=pl.ANY)
VM = pl.BlockSpec(memory_space=pltpu.VMEM)


def remote(src, dst, ssem, rsem, dev):
    return pltpu.make_async_remote_copy(
        src_ref=src, dst_ref=dst, send_sem=ssem, recv_sem=rsem, device_id=dev, device_id_type=MESH
    )


class Place:
    def __init__(self, S, F):
        self.S, self.F, self.Z = S, F, F // 2
        self.bits = [1 << b for b in range(S.bit_length() - 1)]
        self.nbits = len(self.bits)
        self.order = [self.bits, self.bits[1:] + self.bits[:1]]
        self.s = lax.axis_index("seq")
        self.f = lax.axis_index("fsdp")
        self.z, self.c = self.f // 2, lax.rem(self.f, 2)
        self.mate = (self.s, self.f ^ 1)

    def at(self, zz):
        return (self.s, zz * 2 + self.c)

    def greet(self):
        bar = pltpu.get_barrier_semaphore()
        for k in range(1, self.F):
            pl.semaphore_signal(bar, inc=1, device_id=(self.s, lax.rem(self.f + k, self.F)), device_id_type=MESH)
        for k in range(1, self.S):
            pl.semaphore_signal(bar, inc=1, device_id=(self.s ^ k, self.f), device_id_type=MESH)
        return lambda: pl.semaphore_wait(bar, self.F + self.S - 2)

    def meet(self):
        self.greet()()


def span(bits):
    out = [0]
    for b in bits:
        out = out + [m | b for m in out]
    return out


def ds(start, size):
    return pl.ds(pl.multiple_of(start, size), size)


class Gather:
    def __init__(self, g, NB, b0, own, full, refs, wide=False, lag=8):
        self.g, self.NB, self.b0, self.own, self.full, self.lag = g, NB, b0, own, full, lag
        self.bounce, self.zs, self.zr, self.xs, self.xr, self.ms, self.ls = refs
        self.R, self.D = full.shape[2:]
        self.C = self.D if wide else self.D // g.S
        self.nbits = 0 if wide else g.nbits
        self.mine = 0 if wide else g.s
        self.nitems = (g.Z - 1) * NB * 2
        self.steps = self.nitems + lag * self.nbits

    @staticmethod
    def scratch(S, F, NB, R, D, bounce=True):
        Z, nb = F // 2, S.bit_length() - 1
        return [pltpu.VMEM((NB if bounce else 1, R, D), jnp.bfloat16), DMA((2,)), DMA((NB, Z)), DMA((nb,)),
                DMA((NB, Z, nb)), DMA((2,)), DMA((1,))]

    def cols(self, q):
        return ds(q * self.C, self.C)

    def half(self, p):
        return pl.ds(p * (self.R // 2), self.R // 2)

    def block(self, f, b):
        return self.full.at[f, self.b0 + b]

    def zfull(self, b, zz):
        return self.full.at[zz * 2 + self.g.c, self.b0 + b, :, self.cols(self.mine)]

    def zcopy(self, src, b, zz, way, to):
        return remote(src, self.zfull(b, zz), self.zs.at[way], self.zr.at[b, zz], self.g.at(to))

    def mate_copy(self, src, b, zz):
        return remote(src, self.block(zz * 2 + self.g.c, b), self.ms.at[0], self.ms.at[1], self.g.mate)

    def keeps(self):
        direct = self.bounce.shape[0] < self.NB
        for b in range(self.NB):
            dst = self.block(self.g.f, b) if direct else self.bounce.at[b]
            yield pltpu.make_async_copy(self.own(b, slice(None)), dst, self.ls.at[0])

    def stored(self):
        return pltpu.make_async_copy(self.bounce, self.full.at[self.g.f, pl.ds(self.b0, self.NB)], self.ls.at[0])

    def start(self):
        g = self.g
        for b in range(self.NB):
            piece = self.own(b, self.cols(self.mine))

            @pl.when(g.z < g.Z - 1)
            def _():
                self.zcopy(piece, b, g.z, 0, g.z + 1).start()

            @pl.when(g.z > 0)
            def _():
                self.zcopy(piece, b, g.z, 1, g.z - 1).start()

        for cp in self.keeps():
            cp.start()
        for b in range(self.NB):
            self.mate_copy(self.own(b, slice(None)), b, g.z).start()

    def kept(self):
        blocks = self.full.at[self.g.f, pl.ds(self.b0, self.NB)]
        pltpu.make_async_copy(blocks, blocks, self.ls.at[0]).wait()
        if self.bounce.shape[0] == self.NB:
            self.stored().start()

    def xcopies(self, b, zz, p, j):
        g = self.g
        to = (g.s ^ g.order[p][j], g.f)
        out = []
        for m in span(g.order[p][:j]):
            ref = self.full.at[zz * 2 + g.c, self.b0 + b, self.half(p), self.cols(g.s ^ m)]
            out.append(remote(ref, ref, self.xs.at[j], self.xr.at[b, zz, j], to))
        return out

    def doubled(self, b, zz, j):
        ref = self.full.at[zz * 2 + self.g.c, self.b0 + b, :, pl.ds(0, self.C << j)]
        return remote(ref, ref, self.xs.at[j], self.xr.at[b, zz, j], self.g.mate)

    def item(self, t):
        g = self.g
        h = 1 + t // (2 * self.NB)
        r = lax.rem(t, 2 * self.NB)
        b, below = r // 2, lax.rem(r, 2) == 0
        zz = jnp.where(below, g.z - h, g.z + h)
        ok = (t >= 0) & (t < self.nitems) & (zz >= 0) & (zz < g.Z)
        nxt = jnp.where(below, g.z + 1, g.z - 1)
        more = (nxt >= 0) & (nxt < g.Z)
        way = jnp.where(below, 0, 1)
        return b, zz, ok, nxt, more, way

    def step(self, t):
        g = self.g
        for j in reversed(range(self.nbits + 1)):
            b, zz, ok, nxt, more, way = self.item(t - self.lag * j)

            @pl.when(ok)
            def _(j=j, b=b, zz=zz, nxt=nxt, more=more, way=way):
                if j == 0:
                    piece = self.zfull(b, zz)
                    self.zcopy(piece, b, zz, 0, g.z).wait_recv()

                    @pl.when(more)
                    def _():
                        self.zcopy(piece, b, zz, way, nxt).start()
                else:
                    self.doubled(b, zz, j - 1).wait_recv()
                if j < self.nbits:
                    for p in range(2):
                        for cp in self.xcopies(b, zz, p, j):
                            cp.start()
                else:
                    self.mate_copy(self.block(zz * 2 + g.c, b), b, zz).start()

    def run(self, lo, hi):
        @pl.loop(lo, hi)
        def _(t):
            self.step(t)

    def part(self, chips, cols):
        ref = self.full.at[pl.ds(0, chips), pl.ds(self.b0, self.NB), :, pl.ds(0, cols)]
        return ref

    def finish_recv(self):
        if self.bounce.shape[0] == self.NB:
            self.stored().wait()
        ref = self.part(self.g.Z, self.D)
        remote(ref, ref, self.ms.at[0], self.ms.at[1], self.g.mate).wait_recv()

    def finish_send(self):
        g = self.g
        ref = self.part(g.Z, self.D)
        remote(ref, ref, self.ms.at[0], self.ms.at[1], g.mate).wait_send()
        for j in range(self.nbits):
            ref = self.part(g.Z - 1, self.C << j)
            remote(ref, ref, self.xs.at[j], self.xr.at[0, 0, j], g.mate).wait_send()
        for zz in range(g.Z):

            @pl.when(g.z == zz)
            def _(zz=zz):
                for way, n in ((0, zz + 1 if zz < g.Z - 1 else 0), (1, g.Z - zz if zz > 0 else 0)):
                    if n:
                        ref = self.part(n, self.C)
                        remote(ref, ref, self.zs.at[way], self.zr.at[0, 0], g.mate).wait_send()


class Scatter:
    def __init__(self, g, part, out, refs, per=0, wide=False, lag=4, tail=0, above=False):
        self.g, self.part, self.out, self.per, self.wide, self.lag, self.above = g, part, out, per, wide, lag, above
        self.core, self.ring, self.xb, self.zb, self.fq = refs[:5]
        self.own, self.c_s, self.c_r, self.x_s, self.x_r, self.z_s, self.z_r, self.a_s, self.a_r, self.o, self.free = refs[5:]
        _, self.NB, self.R, self.D = part.shape
        self.C = self.D // g.S
        self.n = self.NB * g.Z
        self.K = self.ring.shape[0]
        self.tail = tail or (lag if wide else g.nbits * lag + 2 * lag)
        self.after = g.nbits if wide else 0
        self.steps = self.n + self.per + self.tail + lag * (self.after + g.nbits + 1) + 1

    @staticmethod
    def scratch(S, F, NB, R, D, wide=False, K=0):
        Z, nb = F // 2, S.bit_length() - 1
        K = K or NB * Z
        C, n, bf = D // S, NB * Z, jnp.bfloat16
        nx = NB if wide else n
        return [
            pltpu.VMEM((n, R, D), bf), pltpu.VMEM((K, R, D), bf), pltpu.VMEM((nx, 2, R // 2, D - C), bf),
            pltpu.VMEM((NB, Z - 1, R, D if wide else C), bf), pltpu.VMEM((NB, R, D if wide else C), bf),
            DMA((n,)), DMA((1,)), DMA((K,)), DMA((nb,)), DMA((nx, nb)), DMA((1,)), DMA((NB,)),
            DMA((nb,)), DMA((NB, nb)), DMA((1,)), pltpu.SemaphoreType.REGULAR,
        ]

    def fold(self, zz):
        Z = self.g.Z
        return jnp.where(zz < (Z + 1) // 2, 2 * zz, 2 * (Z - 1 - zz) + 1)

    def unfold(self, r):
        return jnp.where(lax.rem(r, 2) == 0, r // 2, self.g.Z - 1 - r // 2)

    def where(self, t):
        Z, per = self.g.Z, self.per
        b, zz = t // Z, self.unfold(lax.rem(t, Z))
        if per:
            rows = t < per * Z
            b, zz = jnp.where(rows, lax.rem(t, per), b), jnp.where(rows, t // per, zz)
        return b, zz

    def item_of(self, b, zz):
        Z, per = self.g.Z, self.per
        t = b * Z + self.fold(zz)
        return jnp.where(b < per, zz * per + b, t) if per else t

    def due(self, v):
        Z, per = self.g.Z, self.per
        ok = (v >= 0) & (v < self.n) & (lax.rem(v, Z) == Z - 1)
        b = v // Z
        if per:
            first = per * Z
            u = v - first + 1
            early = (u >= 0) & (u < per)
            w = v - per
            late = (w >= first) & (w < self.n) & (lax.rem(w, Z) == Z - 1)
            ok = early | late
            b = jnp.where(early, u, w // Z)
        return b, ok

    def cols(self, q):
        return ds(q * self.C, self.C)

    def half(self, p):
        return pl.ds(p * (self.R // 2), self.R // 2)

    def load(self, t):
        b, zz = self.where(t)
        return pltpu.make_async_copy(self.part.at[zz * 2 + self.g.c, b], self.core.at[t], self.own.at[t])

    def swap(self, t):
        b, zz = self.where(t)
        k = lax.rem(t, self.K)
        return remote(self.part.at[zz * 2 + 1 - self.g.c, b], self.ring.at[k], self.c_s.at[0], self.c_r.at[k], self.g.mate)

    def offset(self, j):
        return sum((self.g.S >> (i + 1)) * self.C for i in range(j))

    def halving(self, src, x, p, j):
        g = self.g
        order = g.order[p]
        base = (g.s ^ order[j]) & sum(order[: j + 1])
        to = (g.s ^ order[j], g.f)
        out = []
        for i, m in enumerate(span(order[j + 1 :])):
            dst = self.xb.at[x, p, :, pl.ds(self.offset(j) + i * self.C, self.C)]
            out.append(remote(src.at[self.half(p), self.cols(base | m)], dst, self.x_s.at[j], self.x_r.at[x, j], to))
        return out

    def halved(self, x, j):
        ref = self.xb.at[x, :, :, pl.ds(self.offset(j), (self.g.S >> (j + 1)) * self.C)]
        return remote(ref, ref, self.x_s.at[j], self.x_r.at[x, j], self.g.mate)

    def add_halves(self, buf, x, j):
        g = self.g
        for p in range(2):
            order = g.order[p]
            base = g.s & sum(order[: j + 1])
            for i, m in enumerate(span(order[j + 1 :])):
                q = self.cols(base | m)
                got = self.xb[x, p, :, pl.ds(self.offset(j) + i * self.C, self.C)]
                buf[self.half(p), q] = buf[self.half(p), q] + got

    def piece(self, t, b, zz):
        g = self.g
        src = self.core.at[t] if self.wide else self.core.at[t, :, self.cols(g.s)]
        slot = lax.rem(g.z - zz - 1 + g.Z, g.Z)
        return remote(src, self.zb.at[b, slot], self.z_s.at[0], self.z_r.at[b], g.at(zz))

    def arrived(self, b):
        ref = self.zb.at[b]
        return remote(ref, ref, self.z_s.at[0], self.z_r.at[b], self.g.mate)

    def final(self, b, rows=slice(None)):
        return self.fq.at[b, rows, self.cols(self.g.s)] if self.wide else self.fq.at[b, rows]

    def result(self, b, q, p=None):
        rows, start = (self.R, 0) if p is None else (self.R // 2, p * (self.R // 2))
        if self.above:
            return self.out.at[ds(b * self.R + start, rows), self.cols(q)]
        return self.out.at[pl.ds(start, rows), ds(b * self.D + q * self.C, self.C)]

    def doubling(self, b, p, j):
        g = self.g
        to = (g.s ^ g.order[p][j], g.f)
        out = []
        for m in span(g.order[p][:j]):
            dst = self.result(b, g.s ^ m, p)
            src = self.final(b, self.half(p)) if m == 0 else dst
            out.append(remote(src, dst, self.a_s.at[j], self.a_r.at[b, j], to))
        return out

    def doubled(self, b, j):
        ref = self.out.at[pl.ds(0, self.R), pl.ds(0, self.C << j)]
        return remote(ref, ref, self.a_s.at[j], self.a_r.at[b, j], self.g.mate)

    def stored(self, b):
        return pltpu.make_async_copy(self.final(b), self.result(b, self.g.s), self.o.at[0])

    def ready(self, lo, hi):
        @pl.loop(lo, hi)
        def _(t):
            self.load(t).start()

            @pl.when(t >= self.K)
            def _():
                pl.semaphore_wait(self.free, 1)

            self.swap(t).start()

    def step(self, t):
        g = self.g
        for j in reversed(range(self.after + g.nbits + 1)):
            b, ok = self.due(t - self.tail - self.lag * j)

            @pl.when(ok)
            def _(j=j, b=b):
                if j == 0:
                    self.arrived(b).wait_recv()
                    mine = self.core[self.item_of(b, g.z)] if self.wide else self.core[self.item_of(b, g.z), :, self.cols(g.s)]
                    total = mine.astype(jnp.float32)
                    for k in range(g.Z - 1):
                        total = total + self.zb[b, k].astype(jnp.float32)
                    self.fq[b] = total.astype(self.fq.dtype)
                elif j <= self.after:
                    self.halved(b, j - 1).wait_recv()
                    self.add_halves(self.fq.at[b], b, j - 1)
                else:
                    self.doubled(b, j - self.after - 1).wait_recv()
                if j < self.after:
                    for p in range(2):
                        for cp in self.halving(self.fq.at[b], b, p, j):
                            cp.start()
                elif j < self.after + g.nbits:
                    if j == self.after:
                        self.stored(b).start()
                    for p in range(2):
                        for cp in self.doubling(b, p, j - self.after):
                            cp.start()

        last = 0 if self.wide else g.nbits
        for j in reversed(range(last + 1)):
            u = t - self.lag * j

            @pl.when((u >= 0) & (u < self.n))
            def _(j=j, u=u):
                b, zz = self.where(u)
                buf = self.core.at[u]
                if j == 0:
                    self.load(u).wait()
                    self.swap(u).wait_recv()
                    buf[...] = buf[...] + self.ring[lax.rem(u, self.K)]

                    @pl.when(u + self.K < self.n)
                    def _():
                        pl.semaphore_signal(self.free, inc=1, device_id=g.mate, device_id_type=MESH)
                else:
                    self.halved(u, j - 1).wait_recv()
                    self.add_halves(buf, u, j - 1)
                if j < last:
                    for p in range(2):
                        for cp in self.halving(buf, u, p, j):
                            cp.start()
                else:

                    @pl.when(zz != g.z)
                    def _():
                        self.piece(u, b, zz).start()

    def run(self, lo, hi):
        @pl.loop(lo, hi)
        def _(t):
            self.step(t)

    def finish(self):
        g = self.g

        def done(ref, sem):
            remote(ref, ref, sem, self.z_r.at[0], g.mate).wait_send()

        done(self.core, self.c_s.at[0])
        done(self.zb, self.z_s.at[0])
        for j in range(g.nbits):
            done(self.xb.at[:, :, :, pl.ds(self.offset(j), (g.S >> (j + 1)) * self.C)], self.x_s.at[j])
            done(self.all_of(self.C << j), self.a_s.at[j])
        ref = self.all_of(self.C)
        pltpu.make_async_copy(ref, ref, self.o.at[0]).wait()

    def all_of(self, width):
        return self.out.at[:, pl.ds(0, width if self.above else width * self.NB)]


class VecGather:
    def __init__(self, g, vec, out, sems):
        self.g, self.vec, self.out, self.sems = g, vec, out, sems

    @staticmethod
    def scratch(F):
        return [DMA((3,))]

    def start(self):
        g, sems = self.g, self.sems
        pltpu.make_async_copy(self.vec, self.out.at[g.f], sems.at[2]).start()
        for k in range(1, g.F):
            remote(self.vec, self.out.at[g.f], sems.at[0], sems.at[1], (g.s, lax.rem(g.f + k, g.F))).start()

    def finish(self):
        g, sems = self.g, self.sems
        pltpu.make_async_copy(self.vec, self.out.at[g.f], sems.at[2]).wait()
        ref = self.out.at[pl.ds(0, g.F - 1)]
        cp = remote(ref, ref, sems.at[0], sems.at[1], g.mate)
        cp.wait_send()
        cp.wait_recv()


class VecSum:
    def __init__(self, g, vec, out, refs):
        self.g, self.vec, self.out = g, vec, out
        self.fb, self.mid, self.sb, self.sems = refs

    @staticmethod
    def scratch(S, F, N, L):
        fl = jnp.float32
        return [pltpu.VMEM((F, N, L), fl), pltpu.VMEM((N, L), fl), pltpu.VMEM((S, N, L), fl), DMA((4,))]

    def start(self):
        g = self.g
        for k in range(1, g.F):
            to = lax.rem(g.f + k, g.F)
            remote(self.vec.at[to], self.fb.at[g.f], self.sems.at[0], self.sems.at[1], (g.s, to)).start()

    def middle(self):
        g = self.g
        ref = self.fb.at[pl.ds(0, g.F - 1)]
        cp = remote(ref, ref, self.sems.at[0], self.sems.at[1], g.mate)
        cp.wait_recv()
        total = self.vec[g.f]
        for k in range(1, g.F):
            total = total + self.fb[lax.rem(g.f + k, g.F)]
        self.mid[...] = total
        for k in range(1, g.S):
            remote(self.mid, self.sb.at[g.s], self.sems.at[2], self.sems.at[3], (g.s ^ k, g.f)).start()
        cp.wait_send()

    def finish(self):
        g = self.g
        ref = self.sb.at[pl.ds(0, g.S - 1)]
        cp = remote(ref, ref, self.sems.at[2], self.sems.at[3], g.mate)
        cp.wait_recv()
        total = self.mid[...]
        for k in range(1, g.S):
            total = total + self.sb[g.s ^ k]
        self.out[...] = total
        cp.wait_send()


PARAMS = dict(has_side_effects=True, vmem_limit_bytes=62 * 2**20)


def fp32(x):
    return x.astype(jnp.float32)


def dot(a, b, dims=((1,), (0,))):
    return lax.dot_general(a, b, (dims, ((), ())), preferred_element_type=jnp.float32)


NT = ((1,), (1,))
TN = ((0,), (0,))


def mean_rows(x):
    return jnp.mean(x, axis=-1, keepdims=True)


def head_lanes(rows, hh):
    lane = lax.broadcasted_iota(jnp.int32, (rows, 128), 1)
    mine = (lane >= hh * HEAD_DIM) & (lane < (hh + 1) * HEAD_DIM)
    spare = lane == (1 - hh) * HEAD_DIM
    return mine, spare


def masked_keys(k, length, hh):
    N = k.shape[0]
    mine, spare = head_lanes(N, hh)
    late = lax.broadcasted_iota(jnp.int32, (N, 128), 0) >= length
    return jnp.where(mine, fp32(k), jnp.where(spare & late, NEG_LARGE, 0.0)).astype(jnp.bfloat16)


def scaled_queries(q, hh):
    mine, spare = head_lanes(q.shape[0], hh)
    return jnp.where(mine, fp32(q) * HEAD_DIM ** (-0.5), jnp.where(spare, 1.0, 0.0)).astype(jnp.bfloat16)


def front_kernel(S, F, nwide, QB, lengths, img, vec, wq, wx, wu, wd,
                 first, rest, par, ub, x1, heads_out, out_t, lse, att,
                 vec_full, norm, eb, stage, heads, kh, vt, o_buf, asem, hsem, ssem, rsem, osem, *refs):
    g = Place(S, F)
    slots, T, D = img.shape
    R = first.shape[2]
    V = R
    W = D // S
    N = S * T
    pairs = W // 128
    vg = VecGather(g, vec, vec_full, refs[0])

    def own_first(b, cols):
        if isinstance(cols, slice):
            return wq.at[:, pl.ds(b * D, D)]
        return wq.at[:, pl.ds(pl.multiple_of(b * D + cols.start, 128), cols.size)]

    def own_rest(b0):
        def own(b, cols):
            b = b + b0
            ref, r0, c0 = (wd, b * R, 0) if b < 4 else (wu, 0, (b - 4) * D) if b < 6 else (wx, 0, 0)
            if isinstance(cols, slice):
                return ref.at[pl.ds(r0, R), pl.ds(c0, D)]
            return ref.at[pl.ds(r0, R), pl.ds(pl.multiple_of(c0 + cols.start, 128), cols.size)]

        return own

    entry = Gather(g, 3, 0, own_first, first, refs[1:8], lag=ENTRY_LAG)
    thin = Gather(g, 7 - nwide, nwide, own_rest(nwide), rest, refs[8:15])
    wide = Gather(g, nwide, 0, own_rest(0), rest, refs[15:22], wide=True)

    g.meet()
    vg.start()
    entry.start()
    rows = min(128, T)

    @pl.loop(0, slots * T // rows)
    def _(r):
        i, t = r // (T // rows), lax.rem(r, T // rows)
        x = fp32(img[i, pl.ds(t * rows, rows)])
        x = x - mean_rows(x)
        norm[ds(r * rows, rows)] = x * lax.rsqrt(mean_rows(x * x) + EPSILON)

    entry.kept()
    entry.run(0, entry.nitems)
    vg.finish()
    thin.start()
    wide.start()
    for f in range(F):
        v = fp32(vec_full[f])[:, :V]
        par[:, f * V : (f + 1) * V] = v
        for r in range(2):
            at = (f * 2 + r) * V
            eb[2 * (at // D), :, at % D : at % D + V] = v[2 + r : 3 + r]
        for r in range(4):
            at = (f * 4 + r) * V
            ub[:, at : at + V] = v[8 + r : 9 + r]
    eb[1] = jnp.zeros((1, D), jnp.float32)
    gain, shift = par[0:1], par[1:2]

    @pl.loop(0, slots * T // rows)
    def _(r):
        x1[ds(r * rows, rows)] = (norm[ds(r * rows, rows)] * gain + shift).astype(x1.dtype)

    entry.run(entry.nitems, entry.steps)
    thin.kept()
    wide.kept()
    entry.finish_recv()

    def copy(i, k, j):
        src = stage.at[i, k, j]
        dst = heads.at[j, i, ds(g.s * T, T)]
        return remote(src, dst, ssem.at[i, k, j], rsem.at[i, k, j], (g.s ^ k, g.f))

    def local(i, j):
        return pltpu.make_async_copy(stage.at[i, 0, j], heads.at[j, i, ds(g.s * T, T)], ssem.at[i, 0, j])

    def project(i):
        @pl.loop(0, S * 3)
        def _(n):
            k = lax.rem(1 + n // 3, S)
            j = lax.rem(n, 3)
            cols = ds((g.s ^ k) * W, W)
            w = first[:, j, :, cols].reshape(D, W)
            out = dot(x1[i * T : (i + 1) * T], w) + eb[j, :, cols]
            stage[i, k, j] = out.astype(stage.dtype)

            @pl.when(k != 0)
            def _():
                copy(i, k, j).start()

            @pl.when(k == 0)
            def _():
                local(i, j).start()

    def projected(i):
        for j in range(3):
            local(i, j).wait()
            for k in range(1, S):
                copy(i, k, j).wait_send()
                dst = heads.at[j, i, ds((g.s ^ k) * T, T)]
                remote(dst, dst, ssem.at[i, k, j], rsem.at[i, k, j], (g.s ^ k, g.f)).wait_recv()
        keep_heads(i).start()

    def keep_heads(i):
        return pltpu.make_async_copy(heads.at[:, i], heads_out.at[:, i], hsem.at[i])

    def out_copy(i, hp, kk):
        e = i * pairs + hp
        dst = att.at[i, :, pl.ds(pl.multiple_of(g.s * W + hp * 128, 128), 128)]
        if kk == 0:
            return pltpu.make_async_copy(o_buf.at[e, ds(g.s * T, T)], dst, osem.at[0, e, 0])
        return remote(o_buf.at[e, ds((g.s ^ kk) * T, T)], dst, osem.at[0, e, kk], osem.at[1, e, kk], (g.s ^ kk, g.f))

    def attend(i, hp):
        e = i * pairs + hp
        lanes = slice(hp * 128, (hp + 1) * 128)
        vt[...] = heads[2, i, :, lanes].T
        for hh in range(2):
            kh[hh] = masked_keys(heads[1, i, :, lanes], lengths[i], hh)

        @pl.loop(0, N // QB)
        def _(b):
            cols = ds(b * QB, QB)
            qb = heads[0, i, cols, lanes]
            for hh in range(2):
                sc = dot(kh[hh], scaled_queries(qb, hh), NT)
                top = jnp.max(sc, axis=0, keepdims=True)
                ex = jnp.exp(sc - top)
                total = jnp.sum(ex, axis=0, keepdims=True)
                w = (ex * (1.0 / total)).astype(jnp.bfloat16)
                o = dot(vt[hh * HEAD_DIM : (hh + 1) * HEAD_DIM], w).astype(jnp.bfloat16)
                at = hp * 128 + hh * HEAD_DIM
                out_t[i, at : at + HEAD_DIM, cols] = o
                lse[i, hp, hh : hh + 1, cols] = top + jnp.log(total)
            background(e * (N // QB) + b)

        o_buf[e] = out_t[i, lanes].T
        for kk in list(range(1, S)) + [0]:
            out_copy(i, hp, kk).start()

    units = [(i, hp) for i in range(slots) for hp in range(pairs)]
    early = thin.steps // EARLY
    per_unit = -(-(thin.steps - early) // (len(units) * (N // QB)))

    def background(n):
        @pl.when(n < wide.steps)
        def _():
            wide.step(n)

        for m in range(per_unit):
            thin.step(early + n * per_unit + m)

    for i in range(slots):
        project(i)
    thin.run(0, early)
    entry.finish_send()
    for n, (i, hp) in enumerate(units):
        if hp == 0:
            projected(i)
        attend(i, hp)
    wide.run(len(units) * (N // QB), wide.steps)
    for gather in (thin, wide):
        gather.finish_recv()
        gather.finish_send()
    for i, hp in units:
        for kk in range(S):
            cp = out_copy(i, hp, kk)
            if kk == 0:
                cp.wait()
            else:
                cp.wait_send()
                cp.wait_recv()
    for i in range(slots):
        keep_heads(i).wait()


ENTRY_LAG = 6
WIDE = 3
EARLY = 10


def front_call(S, F, cid, lengths, img, vec, wq, wx, wu, wd):
    slots, T, D = img.shape
    R, FF = wq.shape[0], wu.shape[1]
    W, N = D // S, S * T
    pairs = W // 128
    bf, fl = jnp.bfloat16, jnp.float32
    out = jax.ShapeDtypeStruct
    return pl.pallas_call(
        functools.partial(front_kernel, S, F, WIDE, min(256, N)),
        out_shape=[
            out((F, 3, R, D), bf), out((F, 7, R, D), bf), out((16, D), fl), out((1, FF), fl), out((slots * T, D), bf),
            out((3, slots, N, W), bf), out((slots, W, N), bf), out((slots, pairs, 8, N), fl), out((slots, T, D), bf),
        ],
        in_specs=[pl.BlockSpec(memory_space=pltpu.SMEM), VM, ANY, ANY, ANY, ANY, ANY],
        out_specs=[VM, ANY, VM, VM, VM, ANY, VM, VM, ANY],
        scratch_shapes=[
            pltpu.VMEM((F, 16, 128), bf), pltpu.VMEM((slots * T, D), fl), pltpu.VMEM((3, 1, D), fl), pltpu.VMEM((slots, S, 3, T, W), bf),
            pltpu.VMEM((3, slots, N, W), bf), pltpu.VMEM((2, N, 128), bf), pltpu.VMEM((128, N), bf),
            pltpu.VMEM((slots * pairs, N, 128), bf), DMA((1,)), DMA((slots,)), DMA((slots, S, 3)), DMA((slots, S, 3)),
            DMA((2, slots * pairs, S)),
        ]
        + VecGather.scratch(F)
        + Gather.scratch(S, F, 3, R, D, bounce=False)
        + Gather.scratch(S, F, 7 - WIDE, R, D)
        + Gather.scratch(S, F, WIDE, R, D),
        compiler_params=pltpu.CompilerParams(collective_id=cid, **PARAMS),
        name="front",
    )(lengths, img, vec, wq, wx, wu, wd)


def rear_kernel(S, F, QB, lengths, held, img, cot, att, par, ub, wu_own, wts, heads, out_t, lse, x1, first,
                layer, dx, small, part_down, part_up, g_down, g_up, g_first, back, late,
                cots, vecs, ubg, slab, csem, esem, wsem, psem, hsem, *refs):
    g = Place(S, F)
    slots, T, D = img.shape
    M = slots * T
    W = D // S
    N = S * T
    pairs = W // 128
    R = wts.shape[2]
    H = ub.shape[2]
    rows = min(128, T)
    nrows = M // rows
    exit_bias, scale1, gain2, shift2 = par[4:5], par[5:6], par[6:7], par[7:8]
    down_bias, scale2 = par[12:13], par[13:14]
    per_block = D // H
    bf, fl = jnp.bfloat16, jnp.float32
    down_sum = Scatter(g, part_down, g_down, refs[:16], per=4, lag=LAG, above=True)
    up_sum = Scatter(g, part_up, g_up, refs[16:32], wide=True, lag=4, tail=UP_TAIL)
    vsum = VecSum(g, slab, small, refs[48:52])

    def own_late(b, cols):
        if isinstance(cols, slice):
            return wu_own.at[:, pl.ds((2 + b) * D, D)]
        return wu_own.at[:, pl.ds(pl.multiple_of((2 + b) * D + cols.start, 128), cols.size)]

    more = Gather(g, 2, 0, own_late, late, refs[52:59])
    units = slots * pairs
    chunks = F // 4
    done = (F - chunks - 2) * g.Z // chunks

    def place(r):
        return r // (T // rows), lax.rem(r, T // rows) * rows

    def mask(r):
        i, t = place(r)
        limit = jnp.where(i < held[g.f], lengths[i], 0)
        pos = lax.broadcasted_iota(jnp.int32, (rows, 1), 0) + (g.s * T + t)
        return jnp.where(pos < limit, 1.0, 0.0)

    def upstream(r):
        i, t = place(r)
        return mask(r) * fp32(cot[i, pl.ds(t, rows)])

    def cot_copies(stage, k):
        for i in range(slots):
            src, dst = stage.at[pl.ds(i * T, T), pl.ds(k * W, W)], cots.at[i, ds(g.s * T, T)]
            if k == 0:
                yield pltpu.make_async_copy(src, dst, csem.at[0, 0])
            else:
                yield remote(src, dst, csem.at[0, k], csem.at[1, k], (g.s ^ k, g.f))

    def feed_forward(mixed, x2, x2t, dcot, down, cot2, wu, wd, wx, dwu, dwd):
        def up_load(j):
            cols = pl.ds(pl.multiple_of(lax.rem(j, per_block) * H, H), H)
            slot = lax.rem(j, 2)
            block = j // per_block
            soon = pltpu.make_async_copy(wts.at[:, 4 + jnp.minimum(block, 1), :, cols], wu.at[slot], wsem.at[0, slot])
            return soon, pltpu.make_async_copy(late.at[:, jnp.maximum(block - 2, 0), :, cols], wu.at[slot], wsem.at[0, slot])

        def start_up(j):
            soon, later = up_load(j)

            @pl.when(j < F // 2)
            def _():
                soon.start()

            @pl.when(j >= F // 2)
            def _():
                later.start()

        def down_load(j):
            return pltpu.make_async_copy(wts.at[j, pl.ds(0, 4)], wd.at[lax.rem(j, 2)], wsem.at[1, lax.rem(j, 2)])

        def put_up(j):
            cols = pl.ds(pl.multiple_of(lax.rem(j, per_block) * H, H), H)
            return pltpu.make_async_copy(dwu, part_up.at[:, j // per_block, :, cols], psem.at[0])

        def put_down(j):
            return pltpu.make_async_copy(dwd, part_down.at[j, pl.ds(0, 4)], psem.at[1])

        x_load = pltpu.make_async_copy(wts.at[:, 6], wx, wsem.at[2, 0])
        x_load.start()
        start_up(0)
        down_load(0).start()
        more.kept()
        x_load.wait()
        mixed[...] = dot(att[...], wx[...].reshape(D, D)) + exit_bias

        def residual(r, sl):
            i, t = place(r)
            return fp32(img[i, pl.ds(t, rows)]) + scale1 * mixed[sl]

        def norm(res):
            res = res - mean_rows(res)
            inv = lax.rsqrt(mean_rows(res * res) + EPSILON)
            return res * inv, inv

        @pl.loop(0, nrows)
        def _(r):
            sl = ds(r * rows, rows)
            n, _ = norm(residual(r, sl))
            x2[sl] = (n * gain2 + shift2).astype(bf)
            dcot[sl] = (upstream(r) * scale2).astype(bf)

        x2t[...] = x2[...].T
        down[...] = jnp.zeros_like(down)
        cot2[...] = jnp.zeros_like(cot2)

        @pl.loop(0, F)
        def _(j):
            slot = lax.rem(j, 2)
            every = -(-more.steps // (F // 2 - 1))

            @pl.when(j < F // 2 - 1)
            def _():
                more.run(j * every, (j + 1) * every)

            @pl.when(j == F // 2 - 1)
            def _():
                more.finish_recv()

            @pl.when(j + 1 < F)
            def _():
                start_up(j + 1)
                down_load(j + 1).start()

            up_load(j)[0].wait()
            down_load(j).wait()
            wu_j = wu[slot].reshape(D, H)
            wd_j = wd[slot].reshape(H, D)
            pre = dot(x2[...], wu_j) + ub[j]
            cumul = 0.5 * (1.0 + lax.erf(pre * (1.0 / math.sqrt(2.0))))
            density = jnp.exp(-0.5 * pre * pre) * (1.0 / math.sqrt(2.0 * math.pi))
            act = (pre * cumul).astype(bf)
            slope = cumul + pre * density
            pre_cot = dot(dcot[...], wd_j, NT) * slope
            ubg[j] = jnp.sum(pre_cot, axis=0, keepdims=True)
            low = pre_cot.astype(bf)
            @pl.when(j > 0)
            def _():
                put_up(j - 1).wait()
                put_down(j - 1).wait()

            @pl.when((j > 0) & (lax.rem(j, chunks) == 0))
            def _():
                n = (j // chunks - 1) * g.Z
                up_sum.ready(n, n + g.Z)
                down_sum.ready(n, n + g.Z)

            dwu[...] = dot(x2t[...], low).astype(bf).reshape(F, R, H)
            dwd[...] = dot(act, dcot[...], TN).astype(bf).reshape(4, R, D)
            put_up(j).start()
            put_down(j).start()
            down[...] += dot(act, wd_j)
            cot2[...] += dot(low, wu_j, NT)

            @pl.when((j > chunks) & (j < F - 1))
            def _():
                first = (j - chunks - 1) * g.Z // chunks
                up_sum.run(first, first + g.Z // chunks)
                down_sum.run(first, first + g.Z // chunks)

        put_up(F - 1).wait()
        put_down(F - 1).wait()
        n = 3 * g.Z
        up_sum.ready(n, n + g.Z)
        down_sum.ready(n, n + g.Z)
        vecs[...] = jnp.zeros_like(vecs)

        @pl.loop(0, nrows)
        def _(r):
            sl = ds(r * rows, rows)
            m = mask(r)
            up = upstream(r)
            out = down[sl] + down_bias
            res = residual(r, sl)
            layer[sl] = (m * (res + scale2 * out)).astype(bf)
            n, inv = norm(res)
            c2 = cot2[sl]
            c = c2 * gain2
            rc = up + inv * (c - mean_rows(c) - n * mean_rows(c * n))
            dx[sl] = rc
            mc = rc * scale1
            x2[sl] = mc.astype(bf)
            total = lambda v: jnp.sum(v, axis=0, keepdims=True)
            vecs[0:1] += total(up * out)
            vecs[1:2] += total(up * scale2)
            vecs[2:3] += total(c2 * n)
            vecs[3:4] += total(c2)
            vecs[4:5] += total(rc * mixed[sl])
            vecs[5:6] += total(mc)

        for k in list(range(1, S)) + [0]:
            dcot[:, k * W : (k + 1) * W] = dot(x2[...], wx_rows(wx, g.s ^ k, W), NT).astype(bf)
            for cp in cot_copies(dcot, k):
                cp.start()
        for n in range(F // 4):
            at = n * 4 * R
            dwd[...] = dot(att[:, at : at + 4 * R], x2[...], TN).astype(bf).reshape(4, R, D)
            put_x = pltpu.make_async_copy(dwd, part_down.at[pl.ds(n * 4, 4), 4], psem.at[2])
            put_x.start()
            put_x.wait()
        up_sum.run(done, 3 * g.Z)
        down_sum.run(done, 3 * g.Z)
        down_sum.ready(4 * g.Z, 5 * g.Z)
        for k in range(S):
            for cp in cot_copies(dcot, k):
                if k == 0:
                    cp.wait()
        ref = dcot.at[:, pl.ds(0, W)]
        for k in range(1, S):
            remote(ref, ref, csem.at[0, k], csem.at[1, k], g.mate).wait_send()

    polls = units * (N // QB)

    def background(n):
        @pl.when(3 * g.Z + n < up_sum.steps)
        def _():
            up_sum.step(3 * g.Z + n)

        down_sum.step(3 * g.Z + n)

    def attend_back(hd, ot, ls, kh, vh, kt, cot_t, delta, dq_t, dk, dv, stage):
        loads = [pltpu.make_async_copy(a, b, hsem.at[n]) for n, (a, b) in enumerate(((heads, hd), (out_t, ot), (lse, ls)))]
        for cp in loads:
            cp.start()
        for k in range(1, S):
            ref = cots.at[:, ds((g.s ^ k) * T, T)]
            remote(ref, ref, csem.at[0, k], csem.at[1, k], (g.s ^ k, g.f)).wait_recv()
        for cp in loads:
            cp.wait()

        def copy(e, j, kk):
            i, hp = e // pairs, lax.rem(e, pairs)
            dst = back.at[i, :, ds(j * D + g.s * W + hp * 128, 128)]
            src = stage.at[e, j, ds((g.s ^ kk) * T, T)]
            if kk == 0:
                return pltpu.make_async_copy(src, dst, esem.at[2])
            return remote(src, dst, esem.at[0], esem.at[1], (g.s ^ kk, g.f))

        @pl.loop(0, units)
        def _(e):
            i, hp = e // pairs, lax.rem(e, pairs)
            lanes = ds(hp * 128, 128)
            length = lengths[i]
            kt[...] = hd[1, i, :, lanes].T
            cot_t[...] = cots[i, :, lanes].T
            prod = fp32(cot_t[...]) * fp32(ot[i, lanes])
            for hh in range(2):
                hs = slice(hh * HEAD_DIM, (hh + 1) * HEAD_DIM)
                delta[hh : hh + 1] = jnp.sum(prod[hs], axis=0, keepdims=True)
                kh[hh] = masked_keys(hd[1, i, :, lanes], length, hh)
                mine, _ = head_lanes(N, hh)
                vh[hh] = jnp.where(mine, fp32(hd[2, i, :, lanes]), 0.0).astype(bf)
            dk[...] = jnp.zeros_like(dk)
            dv[...] = jnp.zeros_like(dv)

            @pl.loop(0, N // QB)
            def _(b):
                cols = ds(b * QB, QB)
                qb, cb = hd[0, i, cols, lanes], cots[i, cols, lanes]
                for hh in range(2):
                    hs = slice(hh * HEAD_DIM, (hh + 1) * HEAD_DIM)
                    mine, _ = head_lanes(QB, hh)
                    qs = scaled_queries(qb, hh)
                    prob = jnp.exp(dot(kh[hh], qs, NT) - ls[i, hp, hh : hh + 1, cols])
                    sg = dot(vh[hh], cb, NT)
                    sc = (prob * (sg - delta[hh : hh + 1, cols])).astype(bf)
                    w = prob.astype(bf)
                    dv[...] += dot(w, jnp.where(mine, fp32(cb), 0.0).astype(bf))
                    dk[...] += dot(sc, jnp.where(mine, fp32(qs), 0.0).astype(bf))
                    dq_t[hs, cols] = (dot(kt[hs], sc) * HEAD_DIM ** (-0.5)).astype(bf)
                background(e * (N // QB) + b)

            stage[e, 0] = dq_t[...].T
            stage[e, 1] = dk[...].astype(bf)
            stage[e, 2] = dv[...].astype(bf)
            for j in range(3):
                for kk in list(range(1, S)) + [0]:
                    copy(e, j, kk).start()

        ref = stage.at[:, :, pl.ds(0, (S - 1) * T)]
        cp = remote(ref, ref, esem.at[0], esem.at[1], g.mate)
        cp.wait_send()
        cp.wait_recv()
        ref = stage.at[:, :, pl.ds(0, T)]
        pltpu.make_async_copy(ref, ref, esem.at[2]).wait()

    def entry(part, ein, win, x1v, x1t, acc, rows_v):
        entry_sum = Scatter(g, part, g_first, refs[32:48])
        loads = [pltpu.make_async_copy(back.at[:, :, pl.ds(j * D, D)], ein.at[j], hsem.at[j]) for j in range(3)]
        weights = [pltpu.make_async_copy(first.at[:, j], win.at[j % 2], wsem.at[2, j % 2]) for j in range(3)]
        x_load = pltpu.make_async_copy(x1, x1v, wsem.at[0, 0])
        for cp in [x_load] + loads + weights[:2]:
            cp.start()
        x_load.wait()
        x1t[...] = x1v[...].T
        at = 3 * g.Z + polls

        def others(n, k):
            for t in range(at + n, at + n + k):
                up_sum.step(t)
                down_sum.step(t)

        rows_v[...] = jnp.zeros_like(rows_v)
        cot_of = lambda j: ein[j].reshape(M, D)
        for j in range(3):
            loads[j].wait()
            part[:, j] = dot(x1t[...], cot_of(j)).astype(bf).reshape(F, R, D)
            if j:
                entry_sum.run((j - 1) * g.Z, j * g.Z)
            entry_sum.ready(j * g.Z, (j + 1) * g.Z)
            others(2 * j, 2)
        for j in range(3):
            weights[j].wait()
            d = dot(cot_of(j), win[j % 2].reshape(D, D), NT)
            if j == 0:
                weights[2].start()
                acc[...] = d
            else:
                acc[...] += d
            others(6 + 2 * j, 2)
            entry_sum.run(2 * g.Z + j, 2 * g.Z + j + 1)
        rows_v[2:3] = jnp.sum(fp32(cot_of(0)), axis=0, keepdims=True)
        rows_v[3:4] = jnp.sum(fp32(cot_of(2)), axis=0, keepdims=True)
        gain = par[0:1]

        @pl.loop(0, nrows)
        def _(r):
            sl = ds(r * rows, rows)
            i, t = place(r)
            x = fp32(img[i, pl.ds(t, rows)])
            x = x - mean_rows(x)
            inv = lax.rsqrt(mean_rows(x * x) + EPSILON)
            n = x * inv
            d1 = acc[sl]
            c = d1 * gain
            dx[sl] = dx[sl] + inv * (c - mean_rows(c) - n * mean_rows(c * n))
            rows_v[0:1] += jnp.sum(d1 * n, axis=0, keepdims=True)
            rows_v[1:2] += jnp.sum(d1, axis=0, keepdims=True)
            entry_sum.step(2 * g.Z + 3 + r)

        slab[...] = jnp.zeros_like(slab)
        own = [(0, rows_v, 0), (1, rows_v, 1), (4, vecs, 5), (5, vecs, 4), (6, vecs, 2), (7, vecs, 3), (12, vecs, 1), (13, vecs, 0)]
        V = R
        for f in range(F):
            for to, src, r in own:
                slab[f, to : to + 1, :V] = src[r : r + 1, f * V : (f + 1) * V]
            for r in range(2):
                p = (f * 2 + r) * V
                slab[f, 2 + r : 3 + r, :V] = rows_v[2 + p // D : 3 + p // D, p % D : p % D + V]
            for r in range(4):
                slab[f, 8 + r : 9 + r, :V] = ubg[f, :, r * V : (r + 1) * V]
        vsum.start()
        mark = 2 * g.Z + 3 + nrows
        entry_sum.run(mark, mark + 4)
        vsum.middle()
        left = max(down_sum.steps, up_sum.steps) - (at + 12)

        @pl.loop(0, max(left, entry_sum.steps - mark - 4))
        def _(t):
            up_sum.step(at + 12 + t)
            down_sum.step(at + 12 + t)
            entry_sum.step(mark + 4 + t)

        entry_sum.finish()

    g.meet()
    more.start()
    v = pltpu.VMEM
    pl.run_scoped(
        feed_forward, v((M, D), fl), v((M, D), bf), v((D, M), bf), v((M, D), bf), v((M, D), fl), v((M, D), fl),
        v((2, F, R, H), bf), v((2, 4, R, D), bf), v((F, R, D), bf), v((F, R, H), bf), v((4, R, D), bf),
    )
    pl.run_scoped(
        attend_back, v((3, slots, N, W), bf), v((slots, W, N), bf), v((slots, pairs, 8, N), fl), v((2, N, 128), bf),
        v((2, N, 128), bf), v((128, N), bf), v((128, N), bf), v((8, N), fl), v((128, N), bf), v((N, 128), fl),
        v((N, 128), fl), v((units, 3, N, 128), bf),
    )
    pl.run_scoped(
        entry, v((F, 3, R, D), bf), v((3, slots, T, D), bf), v((2, F, R, D), bf), v((M, D), bf), v((D, M), bf),
        v((M, D), fl), v((8, D), fl),
    )
    up_sum.finish()
    down_sum.finish()
    vsum.finish()
    more.finish_send()


def wx_rows(wx, peer, W):
    F, R, D = wx.shape
    n = W // R
    return wx[pl.ds(peer * n, n)].reshape(W, D)


LAG = 4
UP_TAIL = 17


def rear_call(S, F, cid, lengths, held, img, cot, att, par, ub, wu_own, wts, heads, out_t, lse, x1, first):
    slots, T, D = img.shape
    M = slots * T
    R = wts.shape[2]
    FF = ub.shape[1]
    H = FF // F
    W, N = D // S, S * T
    bf, fl = jnp.bfloat16, jnp.float32
    SM = pl.BlockSpec(memory_space=pltpu.SMEM)
    out, v = jax.ShapeDtypeStruct, pltpu.VMEM
    return pl.pallas_call(
        functools.partial(rear_kernel, S, F, min(256, N)),
        out_shape=[
            out((M, D), bf), out((M, D), fl), out((16, 128), fl), out((F, 5, R, D), bf), out((F, 4, R, D), bf),
            out((5 * R, D), bf), out((R, 4 * D), bf), out((R, 3 * D), bf), out((slots, T, 3 * D), bf), out((F, 2, R, D), bf),
        ],
        in_specs=[SM, SM, VM, VM, VM, VM, VM] + [ANY] * 7,
        out_specs=[VM, VM, VM] + [ANY] * 7,
        scratch_shapes=[v((slots, N, W), bf), v((8, D), fl), v((F, 1, H), fl), v((F, 16, 128), fl),
                        DMA((2, S)), DMA((3,)), DMA((3, 2)), DMA((3,)), DMA((3,))]
        + Scatter.scratch(S, F, 5, R, D, K=F)
        + Scatter.scratch(S, F, 4, R, D, wide=True, K=F)
        + Scatter.scratch(S, F, 3, R, D, K=F // 2)
        + VecSum.scratch(S, F, 16, 128)
        + Gather.scratch(S, F, 2, R, D),
        compiler_params=pltpu.CompilerParams(collective_id=cid, **PARAMS),
        name="rear",
    )(lengths, held, img, cot, att, par, ub.reshape(F, 1, H), wu_own, wts, heads, out_t, lse, x1, first)


def body(S, F, images, out_grad, lengths, images_held, first_gain, first_shift, entry_weight, entry_bias, exit_weight,
         exit_bias, first_scale, second_gain, second_shift, up_weight, up_bias, down_weight, down_bias, second_scale):
    slots, T, D = images.shape
    M = slots * T
    R = entry_weight.shape[0]
    FF = up_weight.shape[1]
    fl = jnp.float32
    V = R
    rows = [first_gain, first_shift, entry_bias, exit_bias, first_scale, second_gain, second_shift, up_bias, down_bias, second_scale]
    own_vec, at = jnp.zeros((16, 128), jnp.bfloat16), 0
    for v in rows:
        n = v.shape[0] // V
        own_vec = own_vec + jnp.pad(v.reshape(n, V), ((at, 16 - at - n), (0, 128 - V)))
        at += n
    first, rest, par, ub, x1, heads, out_t, lse, att = front_call(
        S, F, 0, lengths, images, own_vec, entry_weight, exit_weight, up_weight, down_weight
    )
    layer, dx, small, _, _, g_down, g_up, g_first, _, _ = rear_call(
        S, F, 1, lengths, images_held, images, out_grad, att.reshape(M, D), par, ub, up_weight, rest, heads, out_t, lse, x1, first
    )
    small = small[:, :V]
    row = lambda n, m=1: small[n : n + m].reshape(m * V)
    g_first, g_down, g_up = g_first.astype(fl), g_down.astype(fl), g_up.astype(fl)
    return (
        layer.reshape(slots, T, D),
        dx.reshape(slots, T, D),
        row(0),
        row(1),
        g_first,
        row(2, 2),
        g_down[4 * R :],
        row(4),
        row(5),
        row(6),
        row(7),
        g_up,
        row(8, 4),
        g_down[: 4 * R],
        row(12),
        row(13),
    )


def solution(mesh):
    S, F = mesh.shape["seq"], mesh.shape["fsdp"]
    vector, matrix, tokens = P("fsdp"), P("fsdp", None), P("fsdp", "seq", None)
    return jax.shard_map(
        functools.partial(body, S, F),
        mesh=mesh,
        in_specs=(tokens, tokens, vector, P(), vector, vector, matrix, vector, matrix, vector, vector, vector, vector,
                  matrix, vector, matrix, vector, vector),
        out_specs=(tokens, tokens, vector, vector, matrix, vector, matrix, vector, vector, vector, vector, matrix, vector,
                   matrix, vector, vector),
        check_vma=False,
    )
```

```python
import functools
import math

import jax
import jax.numpy as jnp
from jax import lax
from jax.experimental import pallas as pl
from jax.experimental.pallas import tpu as pltpu
from jax.sharding import PartitionSpec as P

HEAD_DIM = 64
EPSILON = 1e-06
NEG_LARGE = -1e30

MESH = pl.DeviceIdType.MESH
DMA = pltpu.SemaphoreType.DMA
ANY = pl.BlockSpec(memory_space=pl.ANY)
VM = pl.BlockSpec(memory_space=pltpu.VMEM)


def remote(src, dst, ssem, rsem, dev):
    return pltpu.make_async_remote_copy(
        src_ref=src, dst_ref=dst, send_sem=ssem, recv_sem=rsem, device_id=dev, device_id_type=MESH
    )


class Place:
    def __init__(self, S, F, slots):
        self.S, self.F, self.Z, self.slots = S, F, F // 2, slots
        self.bits = [1 << b for b in range(S.bit_length() - 1)]
        self.nbits = len(self.bits)
        self.order = [self.bits, self.bits[1:] + self.bits[:1]]
        self.s = lax.axis_index("seq")
        self.f = lax.axis_index("fsdp")
        self.z, self.c = self.f // 2, lax.rem(self.f, 2)
        self.mate = (self.s, self.f ^ 1)
        self.regroup = whole_images(S, slots)
        self.n = 2 if self.regroup else S
        self.me = self.c if self.regroup else self.s
        self.images = 1 if self.regroup else slots

    def at(self, zz):
        return (self.s, zz * 2 + self.c)

    def peer(self, k):
        return (self.s, self.f ^ k) if self.regroup else (self.s ^ k, self.f)

    def image(self, i):
        if self.regroup:
            return self.z * 2 + self.s // self.slots, lax.rem(self.s, self.slots)
        return self.f, i

    def goes(self, i):
        if not self.regroup:
            return self.mate, i, True
        to, core = self.c * self.slots + i, self.s // self.slots
        return (to, self.z * 2 + core), lax.rem(self.s, self.slots), (to == self.s) & (core == self.c)

    def came(self, r):
        if not self.regroup:
            return self.mate, r, True
        of, core = self.c * self.slots + r, self.s // self.slots
        return (of, self.z * 2 + core), lax.rem(self.s, self.slots), (of == self.s) & (core == self.c)

    def greet(self):
        bar = pltpu.get_barrier_semaphore()
        for k in range(1, self.F):
            pl.semaphore_signal(bar, inc=1, device_id=(self.s, lax.rem(self.f + k, self.F)), device_id_type=MESH)
        for k in range(1, self.S):
            for core in range(2 if self.regroup else 1):
                pl.semaphore_signal(bar, inc=1, device_id=(self.s ^ k, self.f ^ core), device_id_type=MESH)
        return lambda: pl.semaphore_wait(bar, self.F - 1 + (self.S - 1) * (2 if self.regroup else 1))

    def meet(self):
        self.greet()()


def whole_images(S, slots):
    return S == 2 * slots


class Regroup:
    def __init__(self, g, src, dst, sems, back=False):
        self.g, self.src, self.dst, self.sems = g, src, dst, sems
        self.out, self.into = (g.came, g.goes) if back else (g.goes, g.came)

    @staticmethod
    def scratch(slots):
        return [DMA((2, slots))]

    def each(self, way, local, remote_part):
        for p in range(self.g.slots):
            device, q, here = way(p)
            if here is True:
                local(p, q)
            else:
                pl.when(here)(lambda p=p, q=q: local(p, q))
                pl.when(jnp.logical_not(here))(lambda p=p, q=q, device=device: remote_part(p, q, device))

    def start(self):
        def local(p, q):
            pltpu.make_async_copy(self.src(p), self.dst(q), self.sems.at[0, p]).start()

        def away(p, q, device):
            remote(self.src(p), self.dst(q), self.sems.at[0, p], self.sems.at[1, q], device).start()

        self.each(self.out, local, away)

    def arrived(self):
        def away(p, q, device):
            remote(self.dst(p), self.dst(p), self.sems.at[0, p], self.sems.at[1, p], device).wait_recv()

        self.each(self.into, lambda p, q: None, away)

        def local(p, q):
            pltpu.make_async_copy(self.src(p), self.dst(q), self.sems.at[0, p]).wait()

        self.each(self.out, local, lambda p, q, device: None)

    def sent(self):
        def away(p, q, device):
            remote(self.src(p), self.dst(p), self.sems.at[0, p], self.sems.at[1, p], device).wait_send()

        self.each(self.out, lambda p, q: None, away)


def span(bits):
    out = [0]
    for b in bits:
        out = out + [m | b for m in out]
    return out


def ds(start, size):
    return pl.ds(pl.multiple_of(start, size), size)


class Gather:
    def __init__(self, g, NB, b0, own, full, refs, wide=False, lag=8):
        self.g, self.NB, self.b0, self.own, self.full, self.lag = g, NB, b0, own, full, lag
        self.bounce, self.zs, self.zr, self.xs, self.xr, self.ms, self.ls = refs
        self.R, self.D = full.shape[2:]
        self.C = self.D if wide else self.D // g.S
        self.nbits = 0 if wide else g.nbits
        self.mine = 0 if wide else g.s
        self.nitems = (g.Z - 1) * NB * 2
        self.steps = self.nitems + lag * self.nbits

    @staticmethod
    def scratch(S, F, NB, R, D, bounce=True):
        Z, nb = F // 2, S.bit_length() - 1
        return [pltpu.VMEM((NB if bounce else 1, R, D), jnp.bfloat16), DMA((2,)), DMA((NB, Z)), DMA((nb,)),
                DMA((NB, Z, nb)), DMA((2,)), DMA((1,))]

    def cols(self, q):
        return ds(q * self.C, self.C)

    def half(self, p):
        return pl.ds(p * (self.R // 2), self.R // 2)

    def block(self, f, b):
        return self.full.at[f, self.b0 + b]

    def zfull(self, b, zz):
        return self.full.at[zz * 2 + self.g.c, self.b0 + b, :, self.cols(self.mine)]

    def zcopy(self, src, b, zz, way, to):
        return remote(src, self.zfull(b, zz), self.zs.at[way], self.zr.at[b, zz], self.g.at(to))

    def mate_copy(self, src, b, zz):
        return remote(src, self.block(zz * 2 + self.g.c, b), self.ms.at[0], self.ms.at[1], self.g.mate)

    def keeps(self):
        direct = self.bounce.shape[0] < self.NB
        for b in range(self.NB):
            dst = self.block(self.g.f, b) if direct else self.bounce.at[b]
            yield pltpu.make_async_copy(self.own(b, slice(None)), dst, self.ls.at[0])

    def stored(self):
        return pltpu.make_async_copy(self.bounce, self.full.at[self.g.f, pl.ds(self.b0, self.NB)], self.ls.at[0])

    def start(self):
        g = self.g
        for b in range(self.NB):
            piece = self.own(b, self.cols(self.mine))

            @pl.when(g.z < g.Z - 1)
            def _():
                self.zcopy(piece, b, g.z, 0, g.z + 1).start()

            @pl.when(g.z > 0)
            def _():
                self.zcopy(piece, b, g.z, 1, g.z - 1).start()

        for cp in self.keeps():
            cp.start()
        for b in range(self.NB):
            self.mate_copy(self.own(b, slice(None)), b, g.z).start()

    def kept(self):
        blocks = self.full.at[self.g.f, pl.ds(self.b0, self.NB)]
        pltpu.make_async_copy(blocks, blocks, self.ls.at[0]).wait()
        if self.bounce.shape[0] == self.NB:
            self.stored().start()

    def xcopies(self, b, zz, p, j):
        g = self.g
        to = (g.s ^ g.order[p][j], g.f)
        out = []
        for m in span(g.order[p][:j]):
            ref = self.full.at[zz * 2 + g.c, self.b0 + b, self.half(p), self.cols(g.s ^ m)]
            out.append(remote(ref, ref, self.xs.at[j], self.xr.at[b, zz, j], to))
        return out

    def doubled(self, b, zz, j):
        ref = self.full.at[zz * 2 + self.g.c, self.b0 + b, :, pl.ds(0, self.C << j)]
        return remote(ref, ref, self.xs.at[j], self.xr.at[b, zz, j], self.g.mate)

    def item(self, t):
        g = self.g
        h = 1 + t // (2 * self.NB)
        r = lax.rem(t, 2 * self.NB)
        b, below = r // 2, lax.rem(r, 2) == 0
        zz = jnp.where(below, g.z - h, g.z + h)
        ok = (t >= 0) & (t < self.nitems) & (zz >= 0) & (zz < g.Z)
        nxt = jnp.where(below, g.z + 1, g.z - 1)
        more = (nxt >= 0) & (nxt < g.Z)
        way = jnp.where(below, 0, 1)
        return b, zz, ok, nxt, more, way

    def step(self, t):
        g = self.g
        for j in reversed(range(self.nbits + 1)):
            b, zz, ok, nxt, more, way = self.item(t - self.lag * j)

            @pl.when(ok)
            def _(j=j, b=b, zz=zz, nxt=nxt, more=more, way=way):
                if j == 0:
                    piece = self.zfull(b, zz)
                    self.zcopy(piece, b, zz, 0, g.z).wait_recv()

                    @pl.when(more)
                    def _():
                        self.zcopy(piece, b, zz, way, nxt).start()
                else:
                    self.doubled(b, zz, j - 1).wait_recv()
                if j < self.nbits:
                    for p in range(2):
                        for cp in self.xcopies(b, zz, p, j):
                            cp.start()
                else:
                    self.mate_copy(self.block(zz * 2 + g.c, b), b, zz).start()

    def run(self, lo, hi):
        @pl.loop(lo, hi)
        def _(t):
            self.step(t)

    def part(self, chips, cols):
        ref = self.full.at[pl.ds(0, chips), pl.ds(self.b0, self.NB), :, pl.ds(0, cols)]
        return ref

    def finish_recv(self):
        if self.bounce.shape[0] == self.NB:
            self.stored().wait()
        ref = self.part(self.g.Z, self.D)
        remote(ref, ref, self.ms.at[0], self.ms.at[1], self.g.mate).wait_recv()

    def finish_send(self):
        g = self.g
        ref = self.part(g.Z, self.D)
        remote(ref, ref, self.ms.at[0], self.ms.at[1], g.mate).wait_send()
        for j in range(self.nbits):
            ref = self.part(g.Z - 1, self.C << j)
            remote(ref, ref, self.xs.at[j], self.xr.at[0, 0, j], g.mate).wait_send()
        for zz in range(g.Z):

            @pl.when(g.z == zz)
            def _(zz=zz):
                for way, n in ((0, zz + 1 if zz < g.Z - 1 else 0), (1, g.Z - zz if zz > 0 else 0)):
                    if n:
                        ref = self.part(n, self.C)
                        remote(ref, ref, self.zs.at[way], self.zr.at[0, 0], g.mate).wait_send()


class Scatter:
    def __init__(self, g, part, out, refs, per=0, wide=False, lag=4, tail=0, above=False):
        self.g, self.part, self.out, self.per, self.wide, self.lag, self.above = g, part, out, per, wide, lag, above
        self.core, self.ring, self.xb, self.zb, self.fq = refs[:5]
        self.own, self.c_s, self.c_r, self.x_s, self.x_r, self.z_s, self.z_r, self.a_s, self.a_r, self.o, self.free = refs[5:]
        _, self.NB, self.R, self.D = part.shape
        self.C = self.D // g.S
        self.n = self.NB * g.Z
        self.K = self.ring.shape[0]
        self.tail = tail or (lag if wide else g.nbits * lag + 2 * lag)
        self.after = g.nbits if wide else 0
        self.steps = self.n + self.per + self.tail + lag * (self.after + g.nbits + 1) + 1

    @staticmethod
    def scratch(S, F, NB, R, D, wide=False, K=0):
        Z, nb = F // 2, S.bit_length() - 1
        K = K or NB * Z
        C, n, bf = D // S, NB * Z, jnp.bfloat16
        nx = NB if wide else n
        return [
            pltpu.VMEM((n, R, D), bf), pltpu.VMEM((K, R, D), bf), pltpu.VMEM((nx, 2, R // 2, D - C), bf),
            pltpu.VMEM((NB, Z - 1, R, D if wide else C), bf), pltpu.VMEM((NB, R, D if wide else C), bf),
            DMA((n,)), DMA((1,)), DMA((K,)), DMA((nb,)), DMA((nx, nb)), DMA((1,)), DMA((NB,)),
            DMA((nb,)), DMA((NB, nb)), DMA((1,)), pltpu.SemaphoreType.REGULAR,
        ]

    def fold(self, zz):
        Z = self.g.Z
        return jnp.where(zz < (Z + 1) // 2, 2 * zz, 2 * (Z - 1 - zz) + 1)

    def unfold(self, r):
        return jnp.where(lax.rem(r, 2) == 0, r // 2, self.g.Z - 1 - r // 2)

    def where(self, t):
        Z, per = self.g.Z, self.per
        b, zz = t // Z, self.unfold(lax.rem(t, Z))
        if per:
            rows = t < per * Z
            b, zz = jnp.where(rows, lax.rem(t, per), b), jnp.where(rows, t // per, zz)
        return b, zz

    def item_of(self, b, zz):
        Z, per = self.g.Z, self.per
        t = b * Z + self.fold(zz)
        return jnp.where(b < per, zz * per + b, t) if per else t

    def due(self, v):
        Z, per = self.g.Z, self.per
        ok = (v >= 0) & (v < self.n) & (lax.rem(v, Z) == Z - 1)
        b = v // Z
        if per:
            first = per * Z
            u = v - first + 1
            early = (u >= 0) & (u < per)
            w = v - per
            late = (w >= first) & (w < self.n) & (lax.rem(w, Z) == Z - 1)
            ok = early | late
            b = jnp.where(early, u, w // Z)
        return b, ok

    def cols(self, q):
        return ds(q * self.C, self.C)

    def half(self, p):
        return pl.ds(p * (self.R // 2), self.R // 2)

    def load(self, t):
        b, zz = self.where(t)
        return pltpu.make_async_copy(self.part.at[zz * 2 + self.g.c, b], self.core.at[t], self.own.at[t])

    def swap(self, t):
        b, zz = self.where(t)
        k = lax.rem(t, self.K)
        return remote(self.part.at[zz * 2 + 1 - self.g.c, b], self.ring.at[k], self.c_s.at[0], self.c_r.at[k], self.g.mate)

    def offset(self, j):
        return sum((self.g.S >> (i + 1)) * self.C for i in range(j))

    def halving(self, src, x, p, j):
        g = self.g
        order = g.order[p]
        base = (g.s ^ order[j]) & sum(order[: j + 1])
        to = (g.s ^ order[j], g.f)
        out = []
        for i, m in enumerate(span(order[j + 1 :])):
            dst = self.xb.at[x, p, :, pl.ds(self.offset(j) + i * self.C, self.C)]
            out.append(remote(src.at[self.half(p), self.cols(base | m)], dst, self.x_s.at[j], self.x_r.at[x, j], to))
        return out

    def halved(self, x, j):
        ref = self.xb.at[x, :, :, pl.ds(self.offset(j), (self.g.S >> (j + 1)) * self.C)]
        return remote(ref, ref, self.x_s.at[j], self.x_r.at[x, j], self.g.mate)

    def add_halves(self, buf, x, j):
        g = self.g
        for p in range(2):
            order = g.order[p]
            base = g.s & sum(order[: j + 1])
            for i, m in enumerate(span(order[j + 1 :])):
                q = self.cols(base | m)
                got = self.xb[x, p, :, pl.ds(self.offset(j) + i * self.C, self.C)]
                buf[self.half(p), q] = buf[self.half(p), q] + got

    def piece(self, t, b, zz):
        g = self.g
        src = self.core.at[t] if self.wide else self.core.at[t, :, self.cols(g.s)]
        slot = lax.rem(g.z - zz - 1 + g.Z, g.Z)
        return remote(src, self.zb.at[b, slot], self.z_s.at[0], self.z_r.at[b], g.at(zz))

    def arrived(self, b):
        ref = self.zb.at[b]
        return remote(ref, ref, self.z_s.at[0], self.z_r.at[b], self.g.mate)

    def final(self, b, rows=slice(None)):
        return self.fq.at[b, rows, self.cols(self.g.s)] if self.wide else self.fq.at[b, rows]

    def result(self, b, q, p=None):
        rows, start = (self.R, 0) if p is None else (self.R // 2, p * (self.R // 2))
        if self.above:
            return self.out.at[ds(b * self.R + start, rows), self.cols(q)]
        return self.out.at[pl.ds(start, rows), ds(b * self.D + q * self.C, self.C)]

    def doubling(self, b, p, j):
        g = self.g
        to = (g.s ^ g.order[p][j], g.f)
        out = []
        for m in span(g.order[p][:j]):
            dst = self.result(b, g.s ^ m, p)
            src = self.final(b, self.half(p)) if m == 0 else dst
            out.append(remote(src, dst, self.a_s.at[j], self.a_r.at[b, j], to))
        return out

    def doubled(self, b, j):
        ref = self.out.at[pl.ds(0, self.R), pl.ds(0, self.C << j)]
        return remote(ref, ref, self.a_s.at[j], self.a_r.at[b, j], self.g.mate)

    def stored(self, b):
        return pltpu.make_async_copy(self.final(b), self.result(b, self.g.s), self.o.at[0])

    def ready(self, lo, hi):
        @pl.loop(lo, hi)
        def _(t):
            self.load(t).start()

            @pl.when(t >= self.K)
            def _():
                pl.semaphore_wait(self.free, 1)

            self.swap(t).start()

    def step(self, t):
        g = self.g
        for j in reversed(range(self.after + g.nbits + 1)):
            b, ok = self.due(t - self.tail - self.lag * j)

            @pl.when(ok)
            def _(j=j, b=b):
                if j == 0:
                    self.arrived(b).wait_recv()
                    mine = self.core[self.item_of(b, g.z)] if self.wide else self.core[self.item_of(b, g.z), :, self.cols(g.s)]
                    total = mine.astype(jnp.float32)
                    for k in range(g.Z - 1):
                        total = total + self.zb[b, k].astype(jnp.float32)
                    self.fq[b] = total.astype(self.fq.dtype)
                elif j <= self.after:
                    self.halved(b, j - 1).wait_recv()
                    self.add_halves(self.fq.at[b], b, j - 1)
                else:
                    self.doubled(b, j - self.after - 1).wait_recv()
                if j < self.after:
                    for p in range(2):
                        for cp in self.halving(self.fq.at[b], b, p, j):
                            cp.start()
                elif j < self.after + g.nbits:
                    if j == self.after:
                        self.stored(b).start()
                    for p in range(2):
                        for cp in self.doubling(b, p, j - self.after):
                            cp.start()

        last = 0 if self.wide else g.nbits
        for j in reversed(range(last + 1)):
            u = t - self.lag * j

            @pl.when((u >= 0) & (u < self.n))
            def _(j=j, u=u):
                b, zz = self.where(u)
                buf = self.core.at[u]
                if j == 0:
                    self.load(u).wait()
                    self.swap(u).wait_recv()
                    buf[...] = buf[...] + self.ring[lax.rem(u, self.K)]

                    @pl.when(u + self.K < self.n)
                    def _():
                        pl.semaphore_signal(self.free, inc=1, device_id=g.mate, device_id_type=MESH)
                else:
                    self.halved(u, j - 1).wait_recv()
                    self.add_halves(buf, u, j - 1)
                if j < last:
                    for p in range(2):
                        for cp in self.halving(buf, u, p, j):
                            cp.start()
                else:

                    @pl.when(zz != g.z)
                    def _():
                        self.piece(u, b, zz).start()

    def run(self, lo, hi):
        @pl.loop(lo, hi)
        def _(t):
            self.step(t)

    def finish(self):
        g = self.g

        def done(ref, sem):
            remote(ref, ref, sem, self.z_r.at[0], g.mate).wait_send()

        done(self.core, self.c_s.at[0])
        done(self.zb, self.z_s.at[0])
        for j in range(g.nbits):
            done(self.xb.at[:, :, :, pl.ds(self.offset(j), (g.S >> (j + 1)) * self.C)], self.x_s.at[j])
            done(self.all_of(self.C << j), self.a_s.at[j])
        ref = self.all_of(self.C)
        pltpu.make_async_copy(ref, ref, self.o.at[0]).wait()

    def all_of(self, width):
        return self.out.at[:, pl.ds(0, width if self.above else width * self.NB)]


class VecGather:
    def __init__(self, g, vec, out, sems):
        self.g, self.vec, self.out, self.sems = g, vec, out, sems

    @staticmethod
    def scratch(F):
        return [DMA((3,))]

    def start(self):
        g, sems = self.g, self.sems
        pltpu.make_async_copy(self.vec, self.out.at[g.f], sems.at[2]).start()
        for k in range(1, g.F):
            remote(self.vec, self.out.at[g.f], sems.at[0], sems.at[1], (g.s, lax.rem(g.f + k, g.F))).start()

    def finish(self):
        g, sems = self.g, self.sems
        pltpu.make_async_copy(self.vec, self.out.at[g.f], sems.at[2]).wait()
        ref = self.out.at[pl.ds(0, g.F - 1)]
        cp = remote(ref, ref, sems.at[0], sems.at[1], g.mate)
        cp.wait_send()
        cp.wait_recv()


class VecSum:
    def __init__(self, g, vec, out, refs):
        self.g, self.vec, self.out = g, vec, out
        self.fb, self.mid, self.sb, self.sems = refs

    @staticmethod
    def scratch(S, F, N, L):
        fl = jnp.float32
        return [pltpu.VMEM((F, N, L), fl), pltpu.VMEM((N, L), fl), pltpu.VMEM((S, N, L), fl), DMA((4,))]

    def start(self):
        g = self.g
        for k in range(1, g.F):
            to = lax.rem(g.f + k, g.F)
            remote(self.vec.at[to], self.fb.at[g.f], self.sems.at[0], self.sems.at[1], (g.s, to)).start()

    def middle(self):
        g = self.g
        ref = self.fb.at[pl.ds(0, g.F - 1)]
        cp = remote(ref, ref, self.sems.at[0], self.sems.at[1], g.mate)
        cp.wait_recv()
        total = self.vec[g.f]
        for k in range(1, g.F):
            total = total + self.fb[lax.rem(g.f + k, g.F)]
        self.mid[...] = total
        for k in range(1, g.S):
            remote(self.mid, self.sb.at[g.s], self.sems.at[2], self.sems.at[3], (g.s ^ k, g.f)).start()
        cp.wait_send()

    def finish(self):
        g = self.g
        ref = self.sb.at[pl.ds(0, g.S - 1)]
        cp = remote(ref, ref, self.sems.at[2], self.sems.at[3], g.mate)
        cp.wait_recv()
        total = self.mid[...]
        for k in range(1, g.S):
            total = total + self.sb[g.s ^ k]
        self.out[...] = total
        cp.wait_send()


PARAMS = dict(has_side_effects=True, vmem_limit_bytes=62 * 2**20)


def fp32(x):
    return x.astype(jnp.float32)


def dot(a, b, dims=((1,), (0,))):
    return lax.dot_general(a, b, (dims, ((), ())), preferred_element_type=jnp.float32)


NT = ((1,), (1,))
TN = ((0,), (0,))


def mean_rows(x):
    return jnp.mean(x, axis=-1, keepdims=True)


def head_lanes(rows, hh):
    lane = lax.broadcasted_iota(jnp.int32, (rows, 128), 1)
    mine = (lane >= hh * HEAD_DIM) & (lane < (hh + 1) * HEAD_DIM)
    spare = lane == (1 - hh) * HEAD_DIM
    return mine, spare


def length_of(par, group, slot, V):
    lane = lax.broadcasted_iota(jnp.int32, (1, par.shape[1]), 1)
    value = par[14:15] * 32.0 + par[15:16]
    return jnp.sum(jnp.where(lane == group * V + slot, value, 0.0), axis=1, keepdims=True)


def masked_keys(k, length, hh):
    N = k.shape[0]
    mine, spare = head_lanes(N, hh)
    late = fp32(lax.broadcasted_iota(jnp.int32, (N, 128), 0)) >= length
    return jnp.where(mine, fp32(k), jnp.where(spare & late, NEG_LARGE, 0.0)).astype(jnp.bfloat16)


def scaled_queries(q, hh):
    mine, spare = head_lanes(q.shape[0], hh)
    return jnp.where(mine, fp32(q) * HEAD_DIM ** (-0.5), jnp.where(spare, 1.0, 0.0)).astype(jnp.bfloat16)


def front_kernel(S, F, nwide, QB, img, vec, wq, wx, wu, wd,
                 first_out, rest, par, ub, x1, heads_out, out_t, lse, att, tok_out,
                 first, tok, fsem, tsem, vec_full, norm, eb, stage, heads, kh, vt, o_buf, asem, hsem, ssem, rsem, osem, *refs):
    slots, piece, D = img.shape
    g = Place(S, F, slots)
    images = g.images
    T = slots * piece // images
    R = first.shape[2]
    V = R
    W = D // g.n
    N = g.n * T
    pairs = W // 128
    tokens = Regroup(g, lambda p: img.at[p], lambda q: tok.at[ds(q * piece, piece)], tsem)
    vg = VecGather(g, vec, vec_full, refs[0])

    def own_first(b, cols):
        if isinstance(cols, slice):
            return wq.at[:, pl.ds(b * D, D)]
        return wq.at[:, pl.ds(pl.multiple_of(b * D + cols.start, 128), cols.size)]

    def own_rest(b0):
        def own(b, cols):
            b = b + b0
            ref, r0, c0 = (wd, b * R, 0) if b < 4 else (wu, 0, (b - 4) * D) if b < 6 else (wx, 0, 0)
            if isinstance(cols, slice):
                return ref.at[pl.ds(r0, R), pl.ds(c0, D)]
            return ref.at[pl.ds(r0, R), pl.ds(pl.multiple_of(c0 + cols.start, 128), cols.size)]

        return own

    entry = Gather(g, 3, 0, own_first, first, refs[1:8], lag=ENTRY_LAG)
    thin = Gather(g, 7 - nwide, nwide, own_rest(nwide), rest, refs[8:15])
    wide = Gather(g, nwide, 0, own_rest(0), rest, refs[15:22], wide=True)

    g.meet()
    entry.start()
    tokens.start()
    vg.start()
    rows = min(128, piece)
    entry.kept()
    entry.run(0, entry.nitems)
    tokens.arrived()
    keep_tok = pltpu.make_async_copy(tok, tok_out, fsem.at[1])
    keep_tok.start()

    @pl.loop(0, slots * piece // rows)
    def _(r):
        x = fp32(tok[ds(r * rows, rows)])
        x = x - mean_rows(x)
        norm[ds(r * rows, rows)] = x * lax.rsqrt(mean_rows(x * x) + EPSILON)

    vg.finish()
    thin.start()
    wide.start()
    for f in range(F):
        v = fp32(vec_full[f])[:, :V]
        par[:, f * V : (f + 1) * V] = v
        for r in range(2):
            at = (f * 2 + r) * V
            eb[2 * (at // D), :, at % D : at % D + V] = v[2 + r : 3 + r]
        for r in range(4):
            at = (f * 4 + r) * V
            ub[:, at : at + V] = v[8 + r : 9 + r]
    eb[1] = jnp.zeros((1, D), jnp.float32)
    gain, shift = par[0:1], par[1:2]

    @pl.loop(0, slots * piece // rows)
    def _(r):
        x1[ds(r * rows, rows)] = (norm[ds(r * rows, rows)] * gain + shift).astype(x1.dtype)

    entry.run(entry.nitems, entry.steps)
    thin.kept()
    wide.kept()
    entry.finish_recv()
    keep_first = pltpu.make_async_copy(first, first_out, fsem.at[0])
    keep_first.start()

    def copy(i, k, j):
        src = stage.at[i, k, j]
        dst = heads.at[j, i, ds(g.me * T, T)]
        return remote(src, dst, ssem.at[i, k, j], rsem.at[i, k, j], g.peer(k))

    def local(i, j):
        return pltpu.make_async_copy(stage.at[i, 0, j], heads.at[j, i, ds(g.me * T, T)], ssem.at[i, 0, j])

    def project(i):
        @pl.loop(0, g.n * 3)
        def _(n):
            k = lax.rem(1 + n // 3, g.n)
            j = lax.rem(n, 3)
            cols = ds((g.me ^ k) * W, W)
            w = first[:, j, :, cols].reshape(D, W)
            out = dot(x1[i * T : (i + 1) * T], w) + eb[j, :, cols]
            stage[i, k, j] = out.astype(stage.dtype)

            @pl.when(k != 0)
            def _():
                copy(i, k, j).start()

            @pl.when(k == 0)
            def _():
                local(i, j).start()

    def projected(i):
        for j in range(3):
            local(i, j).wait()
            for k in range(1, g.n):
                copy(i, k, j).wait_send()
                dst = heads.at[j, i, ds((g.me ^ k) * T, T)]
                remote(dst, dst, ssem.at[i, k, j], rsem.at[i, k, j], g.peer(k)).wait_recv()
        keep_heads(i).start()

    def keep_heads(i):
        return pltpu.make_async_copy(heads.at[:, i], heads_out.at[:, i], hsem.at[i])

    def out_copy(i, hp, kk):
        e = i * pairs + hp
        dst = att.at[i, :, pl.ds(pl.multiple_of(g.me * W + hp * 128, 128), 128)]
        if kk == 0:
            return pltpu.make_async_copy(o_buf.at[e, ds(g.me * T, T)], dst, osem.at[0, e, 0])
        return remote(o_buf.at[e, ds((g.me ^ kk) * T, T)], dst, osem.at[0, e, kk], osem.at[1, e, kk], g.peer(kk))

    def attend(i, hp):
        e = i * pairs + hp
        lanes = slice(hp * 128, (hp + 1) * 128)
        vt[...] = heads[2, i, :, lanes].T
        length = length_of(par, *g.image(i), V)
        for hh in range(2):
            kh[hh] = masked_keys(heads[1, i, :, lanes], length, hh)

        @pl.loop(0, N // QB)
        def _(b):
            cols = ds(b * QB, QB)
            qb = heads[0, i, cols, lanes]
            for hh in range(2):
                sc = dot(kh[hh], scaled_queries(qb, hh), NT)
                top = jnp.max(sc, axis=0, keepdims=True)
                ex = jnp.exp(sc - top)
                total = jnp.sum(ex, axis=0, keepdims=True)
                w = (ex * (1.0 / total)).astype(jnp.bfloat16)
                o = dot(vt[hh * HEAD_DIM : (hh + 1) * HEAD_DIM], w).astype(jnp.bfloat16)
                at = hp * 128 + hh * HEAD_DIM
                out_t[i, at : at + HEAD_DIM, cols] = o
                lse[i, hp, hh : hh + 1, cols] = top + jnp.log(total)
            background(e * (N // QB) + b)

        o_buf[e] = out_t[i, lanes].T
        for kk in list(range(1, g.n)) + [0]:
            out_copy(i, hp, kk).start()

    units = [(i, hp) for i in range(images) for hp in range(pairs)]
    early = thin.steps // EARLY
    per_unit = -(-(thin.steps - early) // (len(units) * (N // QB)))

    def background(n):
        @pl.when(n < wide.steps)
        def _():
            wide.step(n)

        for m in range(per_unit):
            thin.step(early + n * per_unit + m)

    for i in range(images):
        project(i)
    thin.run(0, early)
    entry.finish_send()
    for n, (i, hp) in enumerate(units):
        if hp == 0:
            projected(i)
        attend(i, hp)
    wide.run(len(units) * (N // QB), wide.steps)
    for gather in (thin, wide):
        gather.finish_recv()
        gather.finish_send()
    for i, hp in units:
        for kk in range(g.n):
            cp = out_copy(i, hp, kk)
            if kk == 0:
                cp.wait()
            else:
                cp.wait_send()
                cp.wait_recv()
    for i in range(images):
        keep_heads(i).wait()
    keep_tok.wait()
    keep_first.wait()
    tokens.sent()


ENTRY_LAG = 8
WIDE = 2
EARLY = 4


def front_call(S, F, cid, img, vec, wq, wx, wu, wd):
    slots, piece, D = img.shape
    M = slots * piece
    n, images = (2, 1) if whole_images(S, slots) else (S, slots)
    T = M // images
    R, FF = wq.shape[0], wu.shape[1]
    W, N = D // n, n * T
    pairs = W // 128
    bf, fl = jnp.bfloat16, jnp.float32
    out = jax.ShapeDtypeStruct
    return pl.pallas_call(
        functools.partial(front_kernel, S, F, WIDE, min(256, N)),
        out_shape=[
            out((F, 3, R, D), bf), out((F, 7, R, D), bf), out((16, D), fl), out((1, FF), fl), out((M, D), bf),
            out((3, images, N, W), bf), out((images, W, N), bf), out((images, pairs, 8, N), fl), out((images, T, D), bf), out((M, D), bf),
        ],
        in_specs=[ANY] * 6,
        out_specs=[ANY, ANY, VM, VM, VM, ANY, VM, VM, ANY, ANY],
        scratch_shapes=[
            pltpu.VMEM((F, 3, R, D), bf), pltpu.VMEM((M, D), bf), DMA((2,)), DMA((2, slots)),
            pltpu.VMEM((F, 16, 128), bf), pltpu.VMEM((M, D), fl), pltpu.VMEM((3, 1, D), fl), pltpu.VMEM((images, n, 3, T, W), bf),
            pltpu.VMEM((3, images, N, W), bf), pltpu.VMEM((2, N, 128), bf), pltpu.VMEM((128, N), bf),
            pltpu.VMEM((images * pairs, N, 128), bf), DMA((1,)), DMA((images,)), DMA((images, n, 3)), DMA((images, n, 3)),
            DMA((2, images * pairs, n)),
        ]
        + VecGather.scratch(F)
        + Gather.scratch(S, F, 3, R, D, bounce=False)
        + Gather.scratch(S, F, 7 - WIDE, R, D)
        + Gather.scratch(S, F, WIDE, R, D),
        compiler_params=pltpu.CompilerParams(collective_id=cid, **PARAMS),
        name="front",
    )(img, vec, wq, wx, wu, wd)


def rear_kernel(S, F, QB, held, tok, att, par, ub, cot_in, wu_own, wts, heads, out_t, lse, x1, first,
                layer_out, dx_out, small, part_down, part_a, part_b, g_down, g_up, g_first, back, late,
                cot, layer, dx, msem, cots, vecs, ubg, slab, csem, esem, wsem, psem, hsem, *refs):
    slots, piece, D = cot_in.shape
    g = Place(S, F, slots)
    images = g.images
    M = slots * piece
    T = M // images
    W = D // g.n
    N = g.n * T
    pairs = W // 128
    R = wts.shape[2]
    H = ub.shape[2]
    rows = min(128, piece)
    nrows = M // rows
    exit_bias, scale1, gain2, shift2 = par[4:5], par[5:6], par[6:7], par[7:8]
    down_bias, scale2 = par[12:13], par[13:14]
    per_block = D // H
    bf, fl = jnp.bfloat16, jnp.float32
    down_sum = Scatter(g, part_down, g_down, refs[:16], per=4, lag=LAG, above=True)
    up_a = Scatter(g, part_a, g_up.at[:, pl.ds(0, 2 * D)], refs[16:32], wide=True, lag=4, tail=UP_TAIL)
    up_b = Scatter(g, part_b, g_up.at[:, pl.ds(2 * D, 2 * D)], refs[32:48], lag=LAG)
    vsum = VecSum(g, slab, small, refs[64:68])

    def own_late(b, cols):
        if isinstance(cols, slice):
            return wu_own.at[:, pl.ds((2 + b) * D, D)]
        return wu_own.at[:, pl.ds(pl.multiple_of((2 + b) * D + cols.start, 128), cols.size)]

    more = Gather(g, 2, 0, own_late, late, refs[68:75])
    units = images * pairs
    part_of = lambda ref: lambda p: ref.at[ds(p * piece, piece)]
    cots_in = Regroup(g, lambda p: cot_in.at[p], part_of(cot), msem.at[0])
    layers = Regroup(g, part_of(layer), lambda q: layer_out.at[q], msem.at[1], back=True)
    chunks = F // 4

    def place(r):
        return r // (T // rows), lax.rem(r, T // rows) * rows

    def mask(r):
        i, t = place(r)
        group, slot = g.image(i)
        limit = jnp.where(slot < held[group], length_of(par, group, slot, R), 0.0)
        pos = lax.broadcasted_iota(jnp.int32, (rows, 1), 0) + (g.me * T + t)
        return jnp.where(fp32(pos) < limit, 1.0, 0.0)

    def upstream(r):
        return mask(r) * fp32(cot[ds(r * rows, rows)])

    def cot_copies(stage, k):
        for i in range(images):
            src, dst = stage.at[pl.ds(i * T, T), pl.ds(k * W, W)], cots.at[i, ds(g.me * T, T)]
            if k == 0:
                yield pltpu.make_async_copy(src, dst, csem.at[0, 0])
            else:
                yield remote(src, dst, csem.at[0, k], csem.at[1, k], g.peer(k))

    def feed_forward(mixed, x2, x2t, dcot, down, cot2, wu, wd, wx, dwu, dwd):
        def up_load(j):
            cols = pl.ds(pl.multiple_of(lax.rem(j, per_block) * H, H), H)
            slot = lax.rem(j, 2)
            block = j // per_block
            soon = pltpu.make_async_copy(wts.at[:, 4 + jnp.minimum(block, 1), :, cols], wu.at[slot], wsem.at[0, slot])
            return soon, pltpu.make_async_copy(late.at[:, jnp.maximum(block - 2, 0), :, cols], wu.at[slot], wsem.at[0, slot])

        def start_either(j, copies):
            soon, later = copies

            @pl.when(j < F // 2)
            def _():
                soon.start()

            @pl.when(j >= F // 2)
            def _():
                later.start()

        def down_load(j):
            return pltpu.make_async_copy(wts.at[j, pl.ds(0, 4)], wd.at[lax.rem(j, 2)], wsem.at[1, lax.rem(j, 2)])

        def put_up(j):
            cols = pl.ds(pl.multiple_of(lax.rem(j, per_block) * H, H), H)
            block = j // per_block
            soon = pltpu.make_async_copy(dwu, part_a.at[:, jnp.minimum(block, 1), :, cols], psem.at[0])
            return soon, pltpu.make_async_copy(dwu, part_b.at[:, jnp.maximum(block - 2, 0), :, cols], psem.at[0])

        def put_down(j):
            return pltpu.make_async_copy(dwd, part_down.at[j, pl.ds(0, 4)], psem.at[1])

        x_load = pltpu.make_async_copy(wts.at[:, 6], wx, wsem.at[2, 0])
        x_load.start()
        start_either(0, up_load(0))
        down_load(0).start()
        more.kept()
        x_load.wait()
        mixed[...] = dot(att[...], wx[...].reshape(D, D)) + exit_bias

        def residual(r, sl):
            return fp32(tok[sl]) + scale1 * mixed[sl]

        cots_in.arrived()

        def norm(res):
            res = res - mean_rows(res)
            inv = lax.rsqrt(mean_rows(res * res) + EPSILON)
            return res * inv, inv

        @pl.loop(0, nrows)
        def _(r):
            sl = ds(r * rows, rows)
            n, _ = norm(residual(r, sl))
            x2[sl] = (n * gain2 + shift2).astype(bf)
            dcot[sl] = (upstream(r) * scale2).astype(bf)

        x2t[...] = x2[...].T
        down[...] = jnp.zeros_like(down)
        cot2[...] = jnp.zeros_like(cot2)

        @pl.loop(0, F)
        def _(j):
            slot = lax.rem(j, 2)
            every = -(-more.steps // (F // 2 - 1))

            @pl.when(j < F // 2 - 1)
            def _():
                more.run(j * every, (j + 1) * every)

            @pl.when(j == F // 2 - 1)
            def _():
                more.finish_recv()

            @pl.when(j + 1 < F)
            def _():
                start_either(j + 1, up_load(j + 1))
                down_load(j + 1).start()

            up_load(j)[0].wait()
            down_load(j).wait()
            wu_j = wu[slot].reshape(D, H)
            wd_j = wd[slot].reshape(H, D)
            pre = dot(x2[...], wu_j) + ub[j]
            cumul = 0.5 * (1.0 + lax.erf(pre * (1.0 / math.sqrt(2.0))))
            density = jnp.exp(-0.5 * pre * pre) * (1.0 / math.sqrt(2.0 * math.pi))
            act = (pre * cumul).astype(bf)
            slope = cumul + pre * density
            pre_cot = dot(dcot[...], wd_j, NT) * slope
            ubg[j] = jnp.sum(pre_cot, axis=0, keepdims=True)
            low = pre_cot.astype(bf)
            @pl.when(j > 0)
            def _():
                put_up(j - 1)[0].wait()
                put_down(j - 1).wait()

            @pl.when((j > 0) & (lax.rem(j, chunks) == 0))
            def _():
                n = (j // chunks - 1) * g.Z
                @pl.when(j <= 2 * chunks)
                def _():
                    up_a.ready(n, n + g.Z)

                @pl.when(j > 2 * chunks)
                def _():
                    up_b.ready(n - 2 * g.Z, n - g.Z)

                down_sum.ready(n, n + g.Z)

            dwu[...] = dot(x2t[...], low).astype(bf).reshape(F, R, H)
            dwd[...] = dot(act, dcot[...], TN).astype(bf).reshape(4, R, D)
            start_either(j, put_up(j))
            put_down(j).start()
            down[...] += dot(act, wd_j)
            cot2[...] += dot(low, wu_j, NT)

            @pl.when((j > 0) & (lax.rem(j, chunks) == 1))
            def _():
                first = (j // chunks - 1) * g.Z

                @pl.when(first >= 0)
                def _():
                    @pl.when(first < 2 * g.Z)
                    def _():
                        up_a.run(first, first + g.Z)

                    @pl.when(first >= 2 * g.Z)
                    def _():
                        up_a.run(first, first + g.Z)
                        up_b.run(first - 2 * g.Z, first - g.Z)

                    down_sum.run(first, first + g.Z)

        put_up(F - 1)[0].wait()
        put_down(F - 1).wait()
        n = 3 * g.Z
        up_b.ready(n - 2 * g.Z, n - g.Z)
        down_sum.ready(n, n + g.Z)
        vecs[...] = jnp.zeros_like(vecs)

        @pl.loop(0, nrows)
        def _(r):
            sl = ds(r * rows, rows)
            m = mask(r)
            up = upstream(r)
            out = down[sl] + down_bias
            res = residual(r, sl)
            layer[sl] = (m * (res + scale2 * out)).astype(bf)
            n, inv = norm(res)
            c2 = cot2[sl]
            c = c2 * gain2
            rc = up + inv * (c - mean_rows(c) - n * mean_rows(c * n))
            dx[sl] = rc
            mc = rc * scale1
            x2[sl] = mc.astype(bf)
            total = lambda v: jnp.sum(v, axis=0, keepdims=True)
            vecs[0:1] += total(up * out)
            vecs[1:2] += total(up * scale2)
            vecs[2:3] += total(c2 * n)
            vecs[3:4] += total(c2)
            vecs[4:5] += total(rc * mixed[sl])
            vecs[5:6] += total(mc)

        for k in list(range(1, g.n)) + [0]:
            dcot[:, k * W : (k + 1) * W] = dot(x2[...], wx_rows(wx, g.me ^ k, W), NT).astype(bf)
            for cp in cot_copies(dcot, k):
                cp.start()
        for n in range(F // 4):
            at = n * 4 * R
            dwd[...] = dot(att[:, at : at + 4 * R], x2[...], TN).astype(bf).reshape(4, R, D)
            put_x = pltpu.make_async_copy(dwd, part_down.at[pl.ds(n * 4, 4), 4], psem.at[2])
            put_x.start()
            put_x.wait()
        down_sum.ready(4 * g.Z, 5 * g.Z)
        layers.start()
        for cp in cot_copies(dcot, 0):
            cp.wait()
        ref = dcot.at[:, pl.ds(0, W)]
        for k in range(1, g.n):
            remote(ref, ref, csem.at[0, k], csem.at[1, k], g.mate).wait_send()

    polls = units * (N // QB)

    def background(n):
        t = 3 * g.Z + n // EVERY

        @pl.when(lax.rem(n, EVERY) == 0)
        def _():
            step_all(t)

    def step_all(t):
        up_a.step(t)
        up_b.step(t - 2 * g.Z)
        down_sum.step(t)

    def attend_back(hd, ot, ls, kh, vh, kt, cot_t, delta, dq_t, dk, dv, stage):
        loads = [pltpu.make_async_copy(a, b, hsem.at[n]) for n, (a, b) in enumerate(((heads, hd), (out_t, ot), (lse, ls)))]
        for cp in loads:
            cp.start()
        for k in range(1, g.n):
            ref = cots.at[:, ds((g.me ^ k) * T, T)]
            remote(ref, ref, csem.at[0, k], csem.at[1, k], g.peer(k)).wait_recv()
        for cp in loads:
            cp.wait()

        def copy(e, j, kk):
            i, hp = e // pairs, lax.rem(e, pairs)
            dst = back.at[i, :, ds(j * D + g.me * W + hp * 128, 128)]
            src = stage.at[e, j, ds((g.me ^ kk) * T, T)]
            if kk == 0:
                return pltpu.make_async_copy(src, dst, esem.at[2])
            return remote(src, dst, esem.at[0], esem.at[1], g.peer(kk))

        @pl.loop(0, units)
        def _(e):
            i, hp = e // pairs, lax.rem(e, pairs)
            lanes = ds(hp * 128, 128)
            length = length_of(par, *g.image(i), R)
            kt[...] = hd[1, i, :, lanes].T
            cot_t[...] = cots[i, :, lanes].T
            prod = fp32(cot_t[...]) * fp32(ot[i, lanes])
            for hh in range(2):
                hs = slice(hh * HEAD_DIM, (hh + 1) * HEAD_DIM)
                delta[hh : hh + 1] = jnp.sum(prod[hs], axis=0, keepdims=True)
                kh[hh] = masked_keys(hd[1, i, :, lanes], length, hh)
                mine, _ = head_lanes(N, hh)
                vh[hh] = jnp.where(mine, fp32(hd[2, i, :, lanes]), 0.0).astype(bf)
            dk[...] = jnp.zeros_like(dk)
            dv[...] = jnp.zeros_like(dv)

            @pl.loop(0, N // QB)
            def _(b):
                cols = ds(b * QB, QB)
                qb, cb = hd[0, i, cols, lanes], cots[i, cols, lanes]
                for hh in range(2):
                    hs = slice(hh * HEAD_DIM, (hh + 1) * HEAD_DIM)
                    mine, _ = head_lanes(QB, hh)
                    qs = scaled_queries(qb, hh)
                    prob = jnp.exp(dot(kh[hh], qs, NT) - ls[i, hp, hh : hh + 1, cols])
                    sg = dot(vh[hh], cb, NT)
                    sc = (prob * (sg - delta[hh : hh + 1, cols])).astype(bf)
                    w = prob.astype(bf)
                    dv[...] += dot(w, jnp.where(mine, fp32(cb), 0.0).astype(bf))
                    dk[...] += dot(sc, jnp.where(mine, fp32(qs), 0.0).astype(bf))
                    dq_t[hs, cols] = (dot(kt[hs], sc) * HEAD_DIM ** (-0.5)).astype(bf)
                background(e * (N // QB) + b)

            stage[e, 0] = dq_t[...].T
            stage[e, 1] = dk[...].astype(bf)
            stage[e, 2] = dv[...].astype(bf)
            for j in range(3):
                for kk in list(range(1, g.n)) + [0]:
                    copy(e, j, kk).start()

        ref = stage.at[:, :, pl.ds(0, (g.n - 1) * T)]
        cp = remote(ref, ref, esem.at[0], esem.at[1], g.mate)
        cp.wait_send()
        cp.wait_recv()
        ref = stage.at[:, :, pl.ds(0, T)]
        pltpu.make_async_copy(ref, ref, esem.at[2]).wait()

    def entry(part, ein, win, x1v, x1t, acc, rows_v, dxl):
        grads = Regroup(g, part_of(dxl), lambda q: dx_out.at[q], msem.at[2], back=True)
        entry_sum = Scatter(g, part, g_first, refs[48:64])
        loads = [pltpu.make_async_copy(back.at[:, :, pl.ds(j * D, D)], ein.at[j], hsem.at[j]) for j in range(3)]
        weights = [pltpu.make_async_copy(first.at[:, j], win.at[j % 2], wsem.at[2, j % 2]) for j in range(3)]
        x_load = pltpu.make_async_copy(x1, x1v, wsem.at[0, 0])
        for cp in [x_load] + loads + weights[:2]:
            cp.start()
        x_load.wait()
        x1t[...] = x1v[...].T
        at = 3 * g.Z + polls // EVERY

        def others(n, k):
            for t in range(at + n, at + n + k):
                step_all(t)

        rows_v[...] = jnp.zeros_like(rows_v)
        cot_of = lambda j: ein[j].reshape(M, D)
        for j in range(3):
            loads[j].wait()
            part[:, j] = dot(x1t[...], cot_of(j)).astype(bf).reshape(F, R, D)
            if j:
                entry_sum.run((j - 1) * g.Z, j * g.Z)
            entry_sum.ready(j * g.Z, (j + 1) * g.Z)
            others(2 * j, 2)
        for j in range(3):
            weights[j].wait()
            d = dot(cot_of(j), win[j % 2].reshape(D, D), NT)
            if j == 0:
                weights[2].start()
                acc[...] = d
            else:
                acc[...] += d
            others(6 + 2 * j, 2)
            entry_sum.run(2 * g.Z + j, 2 * g.Z + j + 1)
        rows_v[2:3] = jnp.sum(fp32(cot_of(0)), axis=0, keepdims=True)
        rows_v[3:4] = jnp.sum(fp32(cot_of(2)), axis=0, keepdims=True)
        gain = par[0:1]

        @pl.loop(0, nrows)
        def _(r):
            sl = ds(r * rows, rows)
            x = fp32(tok[sl])
            x = x - mean_rows(x)
            inv = lax.rsqrt(mean_rows(x * x) + EPSILON)
            n = x * inv
            d1 = acc[sl]
            c = d1 * gain
            dxl[sl] = (dx[sl] + inv * (c - mean_rows(c) - n * mean_rows(c * n))).astype(bf)
            rows_v[0:1] += jnp.sum(d1 * n, axis=0, keepdims=True)
            rows_v[1:2] += jnp.sum(d1, axis=0, keepdims=True)
            entry_sum.step(2 * g.Z + 3 + r)

        grads.start()
        slab[...] = jnp.zeros_like(slab)
        own = [(0, rows_v, 0), (1, rows_v, 1), (4, vecs, 5), (5, vecs, 4), (6, vecs, 2), (7, vecs, 3), (12, vecs, 1), (13, vecs, 0)]
        V = R
        for f in range(F):
            for to, src, r in own:
                slab[f, to : to + 1, :V] = src[r : r + 1, f * V : (f + 1) * V]
            for r in range(2):
                p = (f * 2 + r) * V
                slab[f, 2 + r : 3 + r, :V] = rows_v[2 + p // D : 3 + p // D, p % D : p % D + V]
            for r in range(4):
                slab[f, 8 + r : 9 + r, :V] = ubg[f, :, r * V : (r + 1) * V]
        vsum.start()
        mark = 2 * g.Z + 3 + nrows
        entry_sum.run(mark, mark + 4)
        vsum.middle()
        left = max(down_sum.steps, up_a.steps, up_b.steps + 2 * g.Z) - (at + 12)

        @pl.loop(0, max(left, entry_sum.steps - mark - 4))
        def _(t):
            step_all(at + 12 + t)
            entry_sum.step(mark + 4 + t)

        entry_sum.finish()
        grads.arrived()
        grads.sent()

    g.meet()
    more.start()
    cots_in.start()
    v = pltpu.VMEM
    pl.run_scoped(
        feed_forward, v((M, D), fl), v((M, D), bf), v((D, M), bf), v((M, D), bf), v((M, D), fl), v((M, D), fl),
        v((2, F, R, H), bf), v((2, 4, R, D), bf), v((F, R, D), bf), v((F, R, H), bf), v((4, R, D), bf),
    )
    pl.run_scoped(
        attend_back, v((3, images, N, W), bf), v((images, W, N), bf), v((images, pairs, 8, N), fl), v((2, N, 128), bf),
        v((2, N, 128), bf), v((128, N), bf), v((128, N), bf), v((8, N), fl), v((128, N), bf), v((N, 128), fl),
        v((N, 128), fl), v((units, 3, N, 128), bf),
    )
    pl.run_scoped(
        entry, v((F, 3, R, D), bf), v((3, images, T, D), bf), v((2, F, R, D), bf), v((M, D), bf), v((D, M), bf),
        v((M, D), fl), v((8, D), fl), v((M, D), bf),
    )
    up_a.finish()
    up_b.finish()
    down_sum.finish()
    vsum.finish()
    more.finish_send()
    cots_in.sent()
    layers.arrived()
    layers.sent()


def wx_rows(wx, peer, W):
    F, R, D = wx.shape
    n = W // R
    return wx[pl.ds(peer * n, n)].reshape(W, D)


LAG = 4
UP_TAIL = 10
EVERY = 2


def rear_call(S, F, cid, held, tok, att, par, ub, cot, wu_own, wts, heads, out_t, lse, x1, first):
    slots, piece, D = cot.shape
    M = slots * piece
    n, images = (2, 1) if whole_images(S, slots) else (S, slots)
    T = M // images
    R = wts.shape[2]
    FF = ub.shape[1]
    H = FF // F
    W, N = D // n, n * T
    bf, fl = jnp.bfloat16, jnp.float32
    SM = pl.BlockSpec(memory_space=pltpu.SMEM)
    out, v = jax.ShapeDtypeStruct, pltpu.VMEM
    return pl.pallas_call(
        functools.partial(rear_kernel, S, F, min(256, N)),
        out_shape=[
            out(cot.shape, bf), out(cot.shape, bf), out((16, 128), fl), out((F, 5, R, D), bf), out((F, 2, R, D), bf), out((F, 2, R, D), bf),
            out((5 * R, D), bf), out((R, 4 * D), bf), out((R, 3 * D), bf), out((images, T, 3 * D), bf), out((F, 2, R, D), bf),
        ],
        in_specs=[SM, VM, VM, VM, VM] + [ANY] * 8,
        out_specs=[ANY, ANY, VM] + [ANY] * 8,
        scratch_shapes=[v((M, D), bf), v((M, D), bf), v((M, D), fl), DMA((3, 2, slots)), v((images, N, W), bf), v((8, D), fl), v((F, 1, H), fl), v((F, 16, 128), fl),
                        DMA((2, n)), DMA((3,)), DMA((3, 2)), DMA((3,)), DMA((3,))]
        + Scatter.scratch(S, F, 5, R, D, K=F)
        + Scatter.scratch(S, F, 2, R, D, wide=True, K=F // 2)
        + Scatter.scratch(S, F, 2, R, D, K=F // 2)
        + Scatter.scratch(S, F, 3, R, D, K=F // 2)
        + VecSum.scratch(S, F, 16, 128)
        + Gather.scratch(S, F, 2, R, D),
        compiler_params=pltpu.CompilerParams(collective_id=cid, **PARAMS),
        name="rear",
    )(held, tok, att, par, ub.reshape(F, 1, H), cot, wu_own, wts, heads, out_t, lse, x1, first)


def body(S, F, images, out_grad, lengths, images_held, first_gain, first_shift, entry_weight, entry_bias, exit_weight,
         exit_bias, first_scale, second_gain, second_shift, up_weight, up_bias, down_weight, down_bias, second_scale):
    slots, T, D = images.shape
    M = slots * T
    R = entry_weight.shape[0]
    FF = up_weight.shape[1]
    fl = jnp.float32
    V = R
    rows = [first_gain, first_shift, entry_bias, exit_bias, first_scale, second_gain, second_shift, up_bias, down_bias, second_scale]
    own_vec, at = jnp.zeros((16, 128), jnp.bfloat16), 0
    for v in rows:
        n = v.shape[0] // V
        own_vec = own_vec + jnp.pad(v.reshape(n, V), ((at, 16 - at - n), (0, 128 - V)))
        at += n
    for v in (lengths // 32, lengths % 32):
        own_vec = own_vec + jnp.pad(v.astype(jnp.bfloat16).reshape(1, slots), ((at, 15 - at), (0, 128 - slots)))
        at += 1
    first, rest, par, ub, x1, heads, out_t, lse, att, tok = front_call(
        S, F, 0, images, own_vec, entry_weight, exit_weight, up_weight, down_weight
    )
    layer, dx, small, _, _, _, g_down, g_up, g_first, _, _ = rear_call(
        S, F, 1, images_held, tok, att.reshape(M, D), par, ub, out_grad, up_weight, rest, heads, out_t, lse, x1, first
    )
    small = small[:, :V]
    row = lambda n, m=1: small[n : n + m].reshape(m * V)
    g_first, g_down, g_up = g_first.astype(fl), g_down.astype(fl), g_up.astype(fl)
    return (
        layer,
        dx.astype(fl),
        row(0),
        row(1),
        g_first,
        row(2, 2),
        g_down[4 * R :],
        row(4),
        row(5),
        row(6),
        row(7),
        g_up,
        row(8, 4),
        g_down[: 4 * R],
        row(12),
        row(13),
    )


def solution(mesh):
    S, F = mesh.shape["seq"], mesh.shape["fsdp"]
    vector, matrix, tokens = P("fsdp"), P("fsdp", None), P("fsdp", "seq", None)
    return jax.shard_map(
        functools.partial(body, S, F),
        mesh=mesh,
        in_specs=(tokens, tokens, vector, P(), vector, vector, matrix, vector, matrix, vector, vector, vector, vector,
                  matrix, vector, matrix, vector, vector),
        out_specs=(tokens, tokens, vector, vector, matrix, vector, matrix, vector, vector, vector, vector, matrix, vector,
                   matrix, vector, vector),
        check_vma=False,
    )
```

```python
import functools
import math

import jax
import jax.numpy as jnp
from jax import lax
from jax.experimental import pallas as pl
from jax.experimental.pallas import tpu as pltpu
from jax.sharding import PartitionSpec as P

HEAD_DIM = 64
EPSILON = 1e-06
NEG_LARGE = -1e30

MESH = pl.DeviceIdType.MESH
DMA = pltpu.SemaphoreType.DMA
ANY = pl.BlockSpec(memory_space=pl.ANY)
VM = pl.BlockSpec(memory_space=pltpu.VMEM)


def remote(src, dst, ssem, rsem, dev):
    return pltpu.make_async_remote_copy(
        src_ref=src, dst_ref=dst, send_sem=ssem, recv_sem=rsem, device_id=dev, device_id_type=MESH
    )


class Place:
    def __init__(self, S, F, slots):
        self.S, self.F, self.Z, self.slots = S, F, F // 2, slots
        self.bits = [1 << b for b in range(S.bit_length() - 1)]
        self.nbits = len(self.bits)
        self.order = [self.bits, self.bits[1:] + self.bits[:1]]
        self.s = lax.axis_index("seq")
        self.f = lax.axis_index("fsdp")
        self.z, self.c = self.f // 2, lax.rem(self.f, 2)
        self.mate = (self.s, self.f ^ 1)
        self.regroup = whole_images(S, slots)
        self.n = 2 if self.regroup else S
        self.me = self.c if self.regroup else self.s
        self.images = 1 if self.regroup else slots

    def at(self, zz):
        return (self.s, zz * 2 + self.c)

    def peer(self, k):
        return (self.s, self.f ^ k) if self.regroup else (self.s ^ k, self.f)

    def image(self, i):
        if self.regroup:
            return self.z * 2 + self.s // self.slots, lax.rem(self.s, self.slots)
        return self.f, i

    def goes(self, i):
        if not self.regroup:
            return self.mate, i, True
        to, core = self.c * self.slots + i, self.s // self.slots
        return (to, self.z * 2 + core), lax.rem(self.s, self.slots), (to == self.s) & (core == self.c)

    def came(self, r):
        if not self.regroup:
            return self.mate, r, True
        of, core = self.c * self.slots + r, self.s // self.slots
        return (of, self.z * 2 + core), lax.rem(self.s, self.slots), (of == self.s) & (core == self.c)

    def greet(self):
        bar = pltpu.get_barrier_semaphore()
        for k in range(1, self.F):
            pl.semaphore_signal(bar, inc=1, device_id=(self.s, lax.rem(self.f + k, self.F)), device_id_type=MESH)
        for k in range(1, self.S):
            for core in range(2 if self.regroup else 1):
                pl.semaphore_signal(bar, inc=1, device_id=(self.s ^ k, self.f ^ core), device_id_type=MESH)
        return lambda: pl.semaphore_wait(bar, self.F - 1 + (self.S - 1) * (2 if self.regroup else 1))

    def meet(self):
        self.greet()()


def whole_images(S, slots):
    return S == 2 * slots


class Regroup:
    def __init__(self, g, src, dst, sems, back=False):
        self.g, self.src, self.dst, self.sems = g, src, dst, sems
        self.out, self.into = (g.came, g.goes) if back else (g.goes, g.came)

    @staticmethod
    def scratch(slots):
        return [DMA((2, slots))]

    def each(self, way, local, remote_part):
        for p in range(self.g.slots):
            device, q, here = way(p)
            if here is True:
                local(p, q)
            else:
                pl.when(here)(lambda p=p, q=q: local(p, q))
                pl.when(jnp.logical_not(here))(lambda p=p, q=q, device=device: remote_part(p, q, device))

    def start(self):
        def local(p, q):
            pltpu.make_async_copy(self.src(p), self.dst(q), self.sems.at[0, p]).start()

        def away(p, q, device):
            remote(self.src(p), self.dst(q), self.sems.at[0, p], self.sems.at[1, q], device).start()

        self.each(self.out, local, away)

    def arrived(self):
        def away(p, q, device):
            remote(self.dst(p), self.dst(p), self.sems.at[0, p], self.sems.at[1, p], device).wait_recv()

        self.each(self.into, lambda p, q: None, away)

        def local(p, q):
            pltpu.make_async_copy(self.src(p), self.dst(q), self.sems.at[0, p]).wait()

        self.each(self.out, local, lambda p, q, device: None)

    def sent(self):
        def away(p, q, device):
            remote(self.src(p), self.dst(p), self.sems.at[0, p], self.sems.at[1, p], device).wait_send()

        self.each(self.out, lambda p, q: None, away)


def span(bits):
    out = [0]
    for b in bits:
        out = out + [m | b for m in out]
    return out


def ds(start, size):
    return pl.ds(pl.multiple_of(start, size), size)


class Gather:
    def __init__(self, g, NB, b0, own, full, refs, wide=False, lag=8):
        self.g, self.NB, self.b0, self.own, self.full, self.lag = g, NB, b0, own, full, lag
        self.bounce, self.zs, self.zr, self.xs, self.xr, self.ms, self.ls = refs
        self.R, self.D = full.shape[2:]
        self.C = self.D if wide else self.D // g.S
        self.nbits = 0 if wide else g.nbits
        self.mine = 0 if wide else g.s
        self.nitems = (g.Z - 1) * NB * 2
        self.steps = self.nitems + lag * self.nbits

    @staticmethod
    def scratch(S, F, NB, R, D, bounce=True):
        Z, nb = F // 2, S.bit_length() - 1
        return [pltpu.VMEM((NB if bounce else 1, R, D), jnp.bfloat16), DMA((2,)), DMA((NB, Z)), DMA((nb,)),
                DMA((NB, Z, nb)), DMA((2,)), DMA((1,))]

    def cols(self, q):
        return ds(q * self.C, self.C)

    def half(self, p):
        return pl.ds(p * (self.R // 2), self.R // 2)

    def block(self, f, b):
        return self.full.at[f, self.b0 + b]

    def zfull(self, b, zz):
        return self.full.at[zz * 2 + self.g.c, self.b0 + b, :, self.cols(self.mine)]

    def zcopy(self, src, b, zz, way, to):
        return remote(src, self.zfull(b, zz), self.zs.at[way], self.zr.at[b, zz], self.g.at(to))

    def mate_copy(self, src, b, zz):
        return remote(src, self.block(zz * 2 + self.g.c, b), self.ms.at[0], self.ms.at[1], self.g.mate)

    def keeps(self):
        direct = self.bounce.shape[0] < self.NB
        for b in range(self.NB):
            dst = self.block(self.g.f, b) if direct else self.bounce.at[b]
            yield pltpu.make_async_copy(self.own(b, slice(None)), dst, self.ls.at[0])

    def stored(self):
        return pltpu.make_async_copy(self.bounce, self.full.at[self.g.f, pl.ds(self.b0, self.NB)], self.ls.at[0])

    def start(self):
        g = self.g
        for b in range(self.NB):
            piece = self.own(b, self.cols(self.mine))

            @pl.when(g.z < g.Z - 1)
            def _():
                self.zcopy(piece, b, g.z, 0, g.z + 1).start()

            @pl.when(g.z > 0)
            def _():
                self.zcopy(piece, b, g.z, 1, g.z - 1).start()

        for cp in self.keeps():
            cp.start()
        for b in range(self.NB):
            self.mate_copy(self.own(b, slice(None)), b, g.z).start()

    def kept(self):
        blocks = self.full.at[self.g.f, pl.ds(self.b0, self.NB)]
        pltpu.make_async_copy(blocks, blocks, self.ls.at[0]).wait()
        if self.bounce.shape[0] == self.NB:
            self.stored().start()

    def xcopies(self, b, zz, p, j):
        g = self.g
        to = (g.s ^ g.order[p][j], g.f)
        out = []
        for m in span(g.order[p][:j]):
            ref = self.full.at[zz * 2 + g.c, self.b0 + b, self.half(p), self.cols(g.s ^ m)]
            out.append(remote(ref, ref, self.xs.at[j], self.xr.at[b, zz, j], to))
        return out

    def doubled(self, b, zz, j):
        ref = self.full.at[zz * 2 + self.g.c, self.b0 + b, :, pl.ds(0, self.C << j)]
        return remote(ref, ref, self.xs.at[j], self.xr.at[b, zz, j], self.g.mate)

    def item(self, t):
        g = self.g
        h = 1 + t // (2 * self.NB)
        r = lax.rem(t, 2 * self.NB)
        b, below = r // 2, lax.rem(r, 2) == 0
        zz = jnp.where(below, g.z - h, g.z + h)
        ok = (t >= 0) & (t < self.nitems) & (zz >= 0) & (zz < g.Z)
        nxt = jnp.where(below, g.z + 1, g.z - 1)
        more = (nxt >= 0) & (nxt < g.Z)
        way = jnp.where(below, 0, 1)
        return b, zz, ok, nxt, more, way

    def step(self, t):
        g = self.g
        for j in reversed(range(self.nbits + 1)):
            b, zz, ok, nxt, more, way = self.item(t - self.lag * j)

            @pl.when(ok)
            def _(j=j, b=b, zz=zz, nxt=nxt, more=more, way=way):
                if j == 0:
                    piece = self.zfull(b, zz)
                    self.zcopy(piece, b, zz, 0, g.z).wait_recv()

                    @pl.when(more)
                    def _():
                        self.zcopy(piece, b, zz, way, nxt).start()
                else:
                    self.doubled(b, zz, j - 1).wait_recv()
                if j < self.nbits:
                    for p in range(2):
                        for cp in self.xcopies(b, zz, p, j):
                            cp.start()
                else:
                    self.mate_copy(self.block(zz * 2 + g.c, b), b, zz).start()

    def run(self, lo, hi):
        @pl.loop(lo, hi)
        def _(t):
            self.step(t)

    def part(self, chips, cols):
        ref = self.full.at[pl.ds(0, chips), pl.ds(self.b0, self.NB), :, pl.ds(0, cols)]
        return ref

    def finish_recv(self):
        if self.bounce.shape[0] == self.NB:
            self.stored().wait()
        ref = self.part(self.g.Z, self.D)
        remote(ref, ref, self.ms.at[0], self.ms.at[1], self.g.mate).wait_recv()

    def finish_send(self):
        g = self.g
        ref = self.part(g.Z, self.D)
        remote(ref, ref, self.ms.at[0], self.ms.at[1], g.mate).wait_send()
        for j in range(self.nbits):
            ref = self.part(g.Z - 1, self.C << j)
            remote(ref, ref, self.xs.at[j], self.xr.at[0, 0, j], g.mate).wait_send()
        for zz in range(g.Z):

            @pl.when(g.z == zz)
            def _(zz=zz):
                for way, n in ((0, zz + 1 if zz < g.Z - 1 else 0), (1, g.Z - zz if zz > 0 else 0)):
                    if n:
                        ref = self.part(n, self.C)
                        remote(ref, ref, self.zs.at[way], self.zr.at[0, 0], g.mate).wait_send()


class Scatter:
    def __init__(self, g, part, out, refs, per=0, wide=False, lag=4, tail=0, above=False):
        self.g, self.part, self.out, self.per, self.wide, self.lag, self.above = g, part, out, per, wide, lag, above
        self.core, self.ring, self.xb, self.zb, self.fq = refs[:5]
        self.own, self.c_s, self.c_r, self.x_s, self.x_r, self.z_s, self.z_r, self.a_s, self.a_r, self.o, self.free = refs[5:]
        _, self.NB, self.R, self.D = part.shape
        self.C = self.D // g.S
        self.n = self.NB * g.Z
        self.K = self.ring.shape[0]
        self.tail = tail or (lag if wide else g.nbits * lag + 2 * lag)
        self.after = g.nbits if wide else 0
        self.steps = self.n + self.per + self.tail + lag * (self.after + g.nbits + 1) + 1

    @staticmethod
    def scratch(S, F, NB, R, D, wide=False, K=0):
        Z, nb = F // 2, S.bit_length() - 1
        K = K or NB * Z
        C, n, bf = D // S, NB * Z, jnp.bfloat16
        nx = NB if wide else n
        return [
            pltpu.VMEM((n, R, D), bf), pltpu.VMEM((K, R, D), bf), pltpu.VMEM((nx, 2, R // 2, D - C), bf),
            pltpu.VMEM((NB, Z - 1, R, D if wide else C), bf), pltpu.VMEM((NB, R, D if wide else C), bf),
            DMA((n,)), DMA((1,)), DMA((K,)), DMA((nb,)), DMA((nx, nb)), DMA((1,)), DMA((NB,)),
            DMA((nb,)), DMA((NB, nb)), DMA((1,)), pltpu.SemaphoreType.REGULAR,
        ]

    def fold(self, zz):
        Z = self.g.Z
        return jnp.where(zz < (Z + 1) // 2, 2 * zz, 2 * (Z - 1 - zz) + 1)

    def unfold(self, r):
        return jnp.where(lax.rem(r, 2) == 0, r // 2, self.g.Z - 1 - r // 2)

    def where(self, t):
        Z, per = self.g.Z, self.per
        b, zz = t // Z, self.unfold(lax.rem(t, Z))
        if per:
            rows = t < per * Z
            b, zz = jnp.where(rows, lax.rem(t, per), b), jnp.where(rows, t // per, zz)
        return b, zz

    def item_of(self, b, zz):
        Z, per = self.g.Z, self.per
        t = b * Z + self.fold(zz)
        return jnp.where(b < per, zz * per + b, t) if per else t

    def due(self, v):
        Z, per = self.g.Z, self.per
        ok = (v >= 0) & (v < self.n) & (lax.rem(v, Z) == Z - 1)
        b = v // Z
        if per:
            first = per * Z
            u = v - first + 1
            early = (u >= 0) & (u < per)
            w = v - per
            late = (w >= first) & (w < self.n) & (lax.rem(w, Z) == Z - 1)
            ok = early | late
            b = jnp.where(early, u, w // Z)
        return b, ok

    def cols(self, q):
        return ds(q * self.C, self.C)

    def half(self, p):
        return pl.ds(p * (self.R // 2), self.R // 2)

    def load(self, t):
        b, zz = self.where(t)
        return pltpu.make_async_copy(self.part.at[zz * 2 + self.g.c, b], self.core.at[t], self.own.at[t])

    def swap(self, t):
        b, zz = self.where(t)
        k = lax.rem(t, self.K)
        return remote(self.part.at[zz * 2 + 1 - self.g.c, b], self.ring.at[k], self.c_s.at[0], self.c_r.at[k], self.g.mate)

    def offset(self, j):
        return sum((self.g.S >> (i + 1)) * self.C for i in range(j))

    def halving(self, src, x, p, j):
        g = self.g
        order = g.order[p]
        base = (g.s ^ order[j]) & sum(order[: j + 1])
        to = (g.s ^ order[j], g.f)
        out = []
        for i, m in enumerate(span(order[j + 1 :])):
            dst = self.xb.at[x, p, :, pl.ds(self.offset(j) + i * self.C, self.C)]
            out.append(remote(src.at[self.half(p), self.cols(base | m)], dst, self.x_s.at[j], self.x_r.at[x, j], to))
        return out

    def halved(self, x, j):
        ref = self.xb.at[x, :, :, pl.ds(self.offset(j), (self.g.S >> (j + 1)) * self.C)]
        return remote(ref, ref, self.x_s.at[j], self.x_r.at[x, j], self.g.mate)

    def add_halves(self, buf, x, j):
        g = self.g
        for p in range(2):
            order = g.order[p]
            base = g.s & sum(order[: j + 1])
            for i, m in enumerate(span(order[j + 1 :])):
                q = self.cols(base | m)
                got = self.xb[x, p, :, pl.ds(self.offset(j) + i * self.C, self.C)]
                buf[self.half(p), q] = buf[self.half(p), q] + got

    def piece(self, t, b, zz):
        g = self.g
        src = self.core.at[t] if self.wide else self.core.at[t, :, self.cols(g.s)]
        slot = lax.rem(g.z - zz - 1 + g.Z, g.Z)
        return remote(src, self.zb.at[b, slot], self.z_s.at[0], self.z_r.at[b], g.at(zz))

    def arrived(self, b):
        ref = self.zb.at[b]
        return remote(ref, ref, self.z_s.at[0], self.z_r.at[b], self.g.mate)

    def final(self, b, rows=slice(None)):
        return self.fq.at[b, rows, self.cols(self.g.s)] if self.wide else self.fq.at[b, rows]

    def result(self, b, q, p=None):
        rows, start = (self.R, 0) if p is None else (self.R // 2, p * (self.R // 2))
        if self.above:
            return self.out.at[ds(b * self.R + start, rows), self.cols(q)]
        return self.out.at[pl.ds(start, rows), ds(b * self.D + q * self.C, self.C)]

    def doubling(self, b, p, j):
        g = self.g
        to = (g.s ^ g.order[p][j], g.f)
        out = []
        for m in span(g.order[p][:j]):
            dst = self.result(b, g.s ^ m, p)
            src = self.final(b, self.half(p)) if m == 0 else dst
            out.append(remote(src, dst, self.a_s.at[j], self.a_r.at[b, j], to))
        return out

    def doubled(self, b, j):
        ref = self.out.at[pl.ds(0, self.R), pl.ds(0, self.C << j)]
        return remote(ref, ref, self.a_s.at[j], self.a_r.at[b, j], self.g.mate)

    def stored(self, b):
        return pltpu.make_async_copy(self.final(b), self.result(b, self.g.s), self.o.at[0])

    def ready(self, lo, hi):
        @pl.loop(lo, hi)
        def _(t):
            self.load(t).start()

            @pl.when(t >= self.K)
            def _():
                pl.semaphore_wait(self.free, 1)

            self.swap(t).start()

    def step(self, t):
        g = self.g
        for j in reversed(range(self.after + g.nbits + 1)):
            b, ok = self.due(t - self.tail - self.lag * j)

            @pl.when(ok)
            def _(j=j, b=b):
                if j == 0:
                    self.arrived(b).wait_recv()
                    mine = self.core[self.item_of(b, g.z)] if self.wide else self.core[self.item_of(b, g.z), :, self.cols(g.s)]
                    total = mine.astype(jnp.float32)
                    for k in range(g.Z - 1):
                        total = total + self.zb[b, k].astype(jnp.float32)
                    self.fq[b] = total.astype(self.fq.dtype)
                elif j <= self.after:
                    self.halved(b, j - 1).wait_recv()
                    self.add_halves(self.fq.at[b], b, j - 1)
                else:
                    self.doubled(b, j - self.after - 1).wait_recv()
                if j < self.after:
                    for p in range(2):
                        for cp in self.halving(self.fq.at[b], b, p, j):
                            cp.start()
                elif j < self.after + g.nbits:
                    if j == self.after:
                        self.stored(b).start()
                    for p in range(2):
                        for cp in self.doubling(b, p, j - self.after):
                            cp.start()

        last = 0 if self.wide else g.nbits
        for j in reversed(range(last + 1)):
            u = t - self.lag * j

            @pl.when((u >= 0) & (u < self.n))
            def _(j=j, u=u):
                b, zz = self.where(u)
                buf = self.core.at[u]
                if j == 0:
                    self.load(u).wait()
                    self.swap(u).wait_recv()
                    buf[...] = buf[...] + self.ring[lax.rem(u, self.K)]

                    @pl.when(u + self.K < self.n)
                    def _():
                        pl.semaphore_signal(self.free, inc=1, device_id=g.mate, device_id_type=MESH)
                else:
                    self.halved(u, j - 1).wait_recv()
                    self.add_halves(buf, u, j - 1)
                if j < last:
                    for p in range(2):
                        for cp in self.halving(buf, u, p, j):
                            cp.start()
                else:

                    @pl.when(zz != g.z)
                    def _():
                        self.piece(u, b, zz).start()

    def run(self, lo, hi):
        @pl.loop(lo, hi)
        def _(t):
            self.step(t)

    def finish(self):
        g = self.g

        def done(ref, sem):
            remote(ref, ref, sem, self.z_r.at[0], g.mate).wait_send()

        done(self.core, self.c_s.at[0])
        done(self.zb, self.z_s.at[0])
        for j in range(g.nbits):
            done(self.xb.at[:, :, :, pl.ds(self.offset(j), (g.S >> (j + 1)) * self.C)], self.x_s.at[j])
            done(self.all_of(self.C << j), self.a_s.at[j])
        ref = self.all_of(self.C)
        pltpu.make_async_copy(ref, ref, self.o.at[0]).wait()

    def all_of(self, width):
        return self.out.at[:, pl.ds(0, width if self.above else width * self.NB)]


class VecGather:
    def __init__(self, g, vec, out, sems):
        self.g, self.vec, self.out, self.sems = g, vec, out, sems

    @staticmethod
    def scratch(F):
        return [DMA((3,))]

    def start(self):
        g, sems = self.g, self.sems
        pltpu.make_async_copy(self.vec, self.out.at[g.f], sems.at[2]).start()
        for k in range(1, g.F):
            remote(self.vec, self.out.at[g.f], sems.at[0], sems.at[1], (g.s, lax.rem(g.f + k, g.F))).start()

    def finish(self):
        g, sems = self.g, self.sems
        pltpu.make_async_copy(self.vec, self.out.at[g.f], sems.at[2]).wait()
        ref = self.out.at[pl.ds(0, g.F - 1)]
        cp = remote(ref, ref, sems.at[0], sems.at[1], g.mate)
        cp.wait_send()
        cp.wait_recv()


class VecSum:
    def __init__(self, g, vec, out, refs):
        self.g, self.vec, self.out = g, vec, out
        self.fb, self.mid, self.sb, self.sems = refs

    @staticmethod
    def scratch(S, F, N, L):
        fl = jnp.float32
        return [pltpu.VMEM((F, N, L), fl), pltpu.VMEM((N, L), fl), pltpu.VMEM((S, N, L), fl), DMA((4,))]

    def start(self):
        g = self.g
        for k in range(1, g.F):
            to = lax.rem(g.f + k, g.F)
            remote(self.vec.at[to], self.fb.at[g.f], self.sems.at[0], self.sems.at[1], (g.s, to)).start()

    def middle(self):
        g = self.g
        ref = self.fb.at[pl.ds(0, g.F - 1)]
        cp = remote(ref, ref, self.sems.at[0], self.sems.at[1], g.mate)
        cp.wait_recv()
        total = self.vec[g.f]
        for k in range(1, g.F):
            total = total + self.fb[lax.rem(g.f + k, g.F)]
        self.mid[...] = total
        for k in range(1, g.S):
            remote(self.mid, self.sb.at[g.s], self.sems.at[2], self.sems.at[3], (g.s ^ k, g.f)).start()
        cp.wait_send()

    def finish(self):
        g = self.g
        ref = self.sb.at[pl.ds(0, g.S - 1)]
        cp = remote(ref, ref, self.sems.at[2], self.sems.at[3], g.mate)
        cp.wait_recv()
        total = self.mid[...]
        for k in range(1, g.S):
            total = total + self.sb[g.s ^ k]
        self.out[...] = total
        cp.wait_send()


PARAMS = dict(has_side_effects=True, vmem_limit_bytes=62 * 2**20)


def fp32(x):
    return x.astype(jnp.float32)


def dot(a, b, dims=((1,), (0,))):
    return lax.dot_general(a, b, (dims, ((), ())), preferred_element_type=jnp.float32)


NT = ((1,), (1,))
TN = ((0,), (0,))


def mean_rows(x):
    return jnp.mean(x, axis=-1, keepdims=True)


def head_lanes(rows, hh):
    lane = lax.broadcasted_iota(jnp.int32, (rows, 128), 1)
    mine = (lane >= hh * HEAD_DIM) & (lane < (hh + 1) * HEAD_DIM)
    spare = lane == (1 - hh) * HEAD_DIM
    return mine, spare


def length_of(par, group, slot, V):
    lane = lax.broadcasted_iota(jnp.int32, (1, par.shape[1]), 1)
    value = par[14:15] * 32.0 + par[15:16]
    return jnp.sum(jnp.where(lane == group * V + slot, value, 0.0), axis=1, keepdims=True)


def masked_keys(k, length, hh):
    N = k.shape[0]
    mine, spare = head_lanes(N, hh)
    late = fp32(lax.broadcasted_iota(jnp.int32, (N, 128), 0)) >= length
    return jnp.where(mine, fp32(k), jnp.where(spare & late, NEG_LARGE, 0.0)).astype(jnp.bfloat16)


def scaled_queries(q, hh):
    mine, spare = head_lanes(q.shape[0], hh)
    return jnp.where(mine, fp32(q) * HEAD_DIM ** (-0.5), jnp.where(spare, 1.0, 0.0)).astype(jnp.bfloat16)


def front_kernel(S, F, nwide, QB, img, cot, vec, wq, wx, wu, wd,
                 first_out, rest, par, ub, x1, heads_out, out_t, lse, att, tok_out, cot_out,
                 first, tok, cot_v, fsem, tsem, csem, vec_full, norm, eb, stage, heads, kh, vt, o_buf, asem, hsem, ssem, rsem, osem, *refs):
    slots, piece, D = img.shape
    g = Place(S, F, slots)
    images = g.images
    T = slots * piece // images
    R = first.shape[2]
    V = R
    W = D // g.n
    N = g.n * T
    pairs = W // 128
    tokens = Regroup(g, lambda p: img.at[p], lambda q: tok.at[ds(q * piece, piece)], tsem)
    cots = Regroup(g, lambda p: cot.at[p], lambda q: cot_v.at[ds(q * piece, piece)], csem)
    vg = VecGather(g, vec, vec_full, refs[0])

    def own_first(b, cols):
        if isinstance(cols, slice):
            return wq.at[:, pl.ds(b * D, D)]
        return wq.at[:, pl.ds(pl.multiple_of(b * D + cols.start, 128), cols.size)]

    def own_rest(b0):
        def own(b, cols):
            b = b + b0
            ref, r0, c0 = (wd, b * R, 0) if b < 4 else (wu, 0, (b - 4) * D) if b < 6 else (wx, 0, 0)
            if isinstance(cols, slice):
                return ref.at[pl.ds(r0, R), pl.ds(c0, D)]
            return ref.at[pl.ds(r0, R), pl.ds(pl.multiple_of(c0 + cols.start, 128), cols.size)]

        return own

    entry = Gather(g, 3, 0, own_first, first, refs[1:8], lag=ENTRY_LAG)
    thin = Gather(g, 7 - nwide, nwide, own_rest(nwide), rest, refs[8:15])
    wide = Gather(g, nwide, 0, own_rest(0), rest, refs[15:22], wide=True)

    g.meet()
    entry.start()
    tokens.start()
    vg.start()
    rows = min(128, piece)
    entry.kept()
    entry.run(0, entry.nitems)
    tokens.arrived()
    keep_tok = pltpu.make_async_copy(tok, tok_out, fsem.at[1])
    keep_tok.start()

    @pl.loop(0, slots * piece // rows)
    def _(r):
        x = fp32(tok[ds(r * rows, rows)])
        x = x - mean_rows(x)
        norm[ds(r * rows, rows)] = x * lax.rsqrt(mean_rows(x * x) + EPSILON)

    vg.finish()
    thin.start()
    wide.start()
    for f in range(F):
        v = fp32(vec_full[f])[:, :V]
        par[:, f * V : (f + 1) * V] = v
        for r in range(2):
            at = (f * 2 + r) * V
            eb[2 * (at // D), :, at % D : at % D + V] = v[2 + r : 3 + r]
        for r in range(4):
            at = (f * 4 + r) * V
            ub[:, at : at + V] = v[8 + r : 9 + r]
    eb[1] = jnp.zeros((1, D), jnp.float32)
    gain, shift = par[0:1], par[1:2]

    @pl.loop(0, slots * piece // rows)
    def _(r):
        x1[ds(r * rows, rows)] = (norm[ds(r * rows, rows)] * gain + shift).astype(x1.dtype)

    entry.run(entry.nitems, entry.steps)
    thin.kept()
    wide.kept()
    cots.start()
    entry.finish_recv()
    keep_first = pltpu.make_async_copy(first, first_out, fsem.at[0])
    keep_first.start()

    def copy(i, k, j):
        src = stage.at[i, k, j]
        dst = heads.at[j, i, ds(g.me * T, T)]
        return remote(src, dst, ssem.at[i, k, j], rsem.at[i, k, j], g.peer(k))

    def local(i, j):
        return pltpu.make_async_copy(stage.at[i, 0, j], heads.at[j, i, ds(g.me * T, T)], ssem.at[i, 0, j])

    def project(i):
        @pl.loop(0, g.n * 3)
        def _(n):
            k = lax.rem(1 + n // 3, g.n)
            j = lax.rem(n, 3)
            cols = ds((g.me ^ k) * W, W)
            w = first[:, j, :, cols].reshape(D, W)
            out = dot(x1[i * T : (i + 1) * T], w) + eb[j, :, cols]
            stage[i, k, j] = out.astype(stage.dtype)

            @pl.when(k != 0)
            def _():
                copy(i, k, j).start()

            @pl.when(k == 0)
            def _():
                local(i, j).start()

    def projected(i):
        for j in range(3):
            local(i, j).wait()
            for k in range(1, g.n):
                copy(i, k, j).wait_send()
                dst = heads.at[j, i, ds((g.me ^ k) * T, T)]
                remote(dst, dst, ssem.at[i, k, j], rsem.at[i, k, j], g.peer(k)).wait_recv()
        keep_heads(i).start()

    def keep_heads(i):
        return pltpu.make_async_copy(heads.at[:, i], heads_out.at[:, i], hsem.at[i])

    def out_copy(i, hp, kk):
        e = i * pairs + hp
        dst = att.at[i, :, pl.ds(pl.multiple_of(g.me * W + hp * 128, 128), 128)]
        if kk == 0:
            return pltpu.make_async_copy(o_buf.at[e, ds(g.me * T, T)], dst, osem.at[0, e, 0])
        return remote(o_buf.at[e, ds((g.me ^ kk) * T, T)], dst, osem.at[0, e, kk], osem.at[1, e, kk], g.peer(kk))

    def attend(i, hp):
        e = i * pairs + hp
        lanes = slice(hp * 128, (hp + 1) * 128)
        vt[...] = heads[2, i, :, lanes].T
        length = length_of(par, *g.image(i), V)
        for hh in range(2):
            kh[hh] = masked_keys(heads[1, i, :, lanes], length, hh)

        @pl.loop(0, N // QB)
        def _(b):
            cols = ds(b * QB, QB)
            qb = heads[0, i, cols, lanes]
            for hh in range(2):
                sc = dot(kh[hh], scaled_queries(qb, hh), NT)
                top = jnp.max(sc, axis=0, keepdims=True)
                ex = jnp.exp(sc - top)
                total = jnp.sum(ex, axis=0, keepdims=True)
                w = (ex * (1.0 / total)).astype(jnp.bfloat16)
                o = dot(vt[hh * HEAD_DIM : (hh + 1) * HEAD_DIM], w).astype(jnp.bfloat16)
                at = hp * 128 + hh * HEAD_DIM
                out_t[i, at : at + HEAD_DIM, cols] = o
                lse[i, hp, hh : hh + 1, cols] = top + jnp.log(total)
            background(e * (N // QB) + b)

        o_buf[e] = out_t[i, lanes].T
        for kk in list(range(1, g.n)) + [0]:
            out_copy(i, hp, kk).start()

    units = [(i, hp) for i in range(images) for hp in range(pairs)]
    early = thin.steps // EARLY
    per_unit = -(-(thin.steps - early) // (len(units) * (N // QB)))

    def background(n):
        @pl.when(n < wide.steps)
        def _():
            wide.step(n)

        for m in range(per_unit):
            thin.step(early + n * per_unit + m)

    for i in range(images):
        project(i)
    thin.run(0, early)
    entry.finish_send()
    for n, (i, hp) in enumerate(units):
        if hp == 0:
            projected(i)
        attend(i, hp)
    wide.run(len(units) * (N // QB), wide.steps)
    cots.arrived()
    keep_cot = pltpu.make_async_copy(cot_v, cot_out, fsem.at[2])
    keep_cot.start()
    for gather in (thin, wide):
        gather.finish_recv()
        gather.finish_send()
    for i, hp in units:
        for kk in range(g.n):
            cp = out_copy(i, hp, kk)
            if kk == 0:
                cp.wait()
            else:
                cp.wait_send()
                cp.wait_recv()
    for i in range(images):
        keep_heads(i).wait()
    keep_tok.wait()
    keep_first.wait()
    tokens.sent()
    cots.sent()
    keep_cot.wait()


ENTRY_LAG = 10
WIDE = 3
EARLY = 4


def front_call(S, F, cid, img, cot, vec, wq, wx, wu, wd):
    slots, piece, D = img.shape
    M = slots * piece
    n, images = (2, 1) if whole_images(S, slots) else (S, slots)
    T = M // images
    R, FF = wq.shape[0], wu.shape[1]
    W, N = D // n, n * T
    pairs = W // 128
    bf, fl = jnp.bfloat16, jnp.float32
    out = jax.ShapeDtypeStruct
    return pl.pallas_call(
        functools.partial(front_kernel, S, F, WIDE, min(256, N)),
        out_shape=[
            out((F, 3, R, D), bf), out((F, 7, R, D), bf), out((16, D), fl), out((1, FF), fl), out((M, D), bf),
            out((3, images, N, W), bf), out((images, W, N), bf), out((images, pairs, 8, N), fl), out((images, T, D), bf), out((M, D), bf), out((M, D), bf),
        ],
        in_specs=[ANY] * 7,
        out_specs=[ANY, ANY, VM, VM, VM, ANY, VM, VM, ANY, ANY, ANY],
        scratch_shapes=[
            pltpu.VMEM((F, 3, R, D), bf), pltpu.VMEM((M, D), bf), pltpu.VMEM((M, D), bf), DMA((3,)), DMA((2, slots)), DMA((2, slots)),
            pltpu.VMEM((F, 16, 128), bf), pltpu.VMEM((M, D), fl), pltpu.VMEM((3, 1, D), fl), pltpu.VMEM((images, n, 3, T, W), bf),
            pltpu.VMEM((3, images, N, W), bf), pltpu.VMEM((2, N, 128), bf), pltpu.VMEM((128, N), bf),
            pltpu.VMEM((images * pairs, N, 128), bf), DMA((1,)), DMA((images,)), DMA((images, n, 3)), DMA((images, n, 3)),
            DMA((2, images * pairs, n)),
        ]
        + VecGather.scratch(F)
        + Gather.scratch(S, F, 3, R, D, bounce=False)
        + Gather.scratch(S, F, 7 - WIDE, R, D)
        + Gather.scratch(S, F, WIDE, R, D),
        compiler_params=pltpu.CompilerParams(collective_id=cid, **PARAMS),
        name="front",
    )(img, cot, vec, wq, wx, wu, wd)


def rear_kernel(S, F, QB, held, tok, cot, att, par, ub, wu_own, wts, heads, out_t, lse, x1, first,
                layer_out, dx_out, small, part_down, part_a, part_b, g_down, g_up, g_first, back, late,
                layer, dx, msem, cots, vecs, ubg, slab, csem, esem, wsem, psem, hsem, *refs):
    slots, piece, D = layer_out.shape
    g = Place(S, F, slots)
    images = g.images
    M = slots * piece
    T = M // images
    W = D // g.n
    N = g.n * T
    pairs = W // 128
    R = wts.shape[2]
    H = ub.shape[2]
    rows = min(128, piece)
    nrows = M // rows
    exit_bias, scale1, gain2, shift2 = par[4:5], par[5:6], par[6:7], par[7:8]
    down_bias, scale2 = par[12:13], par[13:14]
    per_block = D // H
    bf, fl = jnp.bfloat16, jnp.float32
    down_sum = Scatter(g, part_down, g_down, refs[:16], per=4, lag=LAG, above=True)
    up_a = Scatter(g, part_a, g_up.at[:, pl.ds(0, 2 * D)], refs[16:32], wide=True, lag=4, tail=UP_TAIL)
    up_b = Scatter(g, part_b, g_up.at[:, pl.ds(2 * D, 2 * D)], refs[32:48], lag=LAG)
    vsum = VecSum(g, slab, small, refs[64:68])

    def own_late(b, cols):
        if isinstance(cols, slice):
            return wu_own.at[:, pl.ds((2 + b) * D, D)]
        return wu_own.at[:, pl.ds(pl.multiple_of((2 + b) * D + cols.start, 128), cols.size)]

    more = Gather(g, 2, 0, own_late, late, refs[68:75])
    units = images * pairs
    part_of = lambda ref: lambda p: ref.at[ds(p * piece, piece)]
    layers = Regroup(g, part_of(layer), lambda q: layer_out.at[q], msem.at[1], back=True)
    chunks = F // 4

    def place(r):
        return r // (T // rows), lax.rem(r, T // rows) * rows

    def mask(r):
        i, t = place(r)
        group, slot = g.image(i)
        limit = jnp.where(slot < held[group], length_of(par, group, slot, R), 0.0)
        pos = lax.broadcasted_iota(jnp.int32, (rows, 1), 0) + (g.me * T + t)
        return jnp.where(fp32(pos) < limit, 1.0, 0.0)

    def upstream(r):
        return mask(r) * fp32(cot[ds(r * rows, rows)])

    def cot_copies(stage, k):
        for i in range(images):
            src, dst = stage.at[pl.ds(i * T, T), pl.ds(k * W, W)], cots.at[i, ds(g.me * T, T)]
            if k == 0:
                yield pltpu.make_async_copy(src, dst, csem.at[0, 0])
            else:
                yield remote(src, dst, csem.at[0, k], csem.at[1, k], g.peer(k))

    def feed_forward(mixed, x2, x2t, dcot, down, cot2, wu, wd, wx, dwu, dwd):
        def up_load(j):
            cols = pl.ds(pl.multiple_of(lax.rem(j, per_block) * H, H), H)
            slot = lax.rem(j, 2)
            block = j // per_block
            soon = pltpu.make_async_copy(wts.at[:, 4 + jnp.minimum(block, 1), :, cols], wu.at[slot], wsem.at[0, slot])
            return soon, pltpu.make_async_copy(late.at[:, jnp.maximum(block - 2, 0), :, cols], wu.at[slot], wsem.at[0, slot])

        def start_either(j, copies):
            soon, later = copies

            @pl.when(j < F // 2)
            def _():
                soon.start()

            @pl.when(j >= F // 2)
            def _():
                later.start()

        def down_load(j):
            return pltpu.make_async_copy(wts.at[j, pl.ds(0, 4)], wd.at[lax.rem(j, 2)], wsem.at[1, lax.rem(j, 2)])

        def put_up(j):
            cols = pl.ds(pl.multiple_of(lax.rem(j, per_block) * H, H), H)
            block = j // per_block
            soon = pltpu.make_async_copy(dwu, part_a.at[:, jnp.minimum(block, 1), :, cols], psem.at[0])
            return soon, pltpu.make_async_copy(dwu, part_b.at[:, jnp.maximum(block - 2, 0), :, cols], psem.at[0])

        def put_down(j):
            return pltpu.make_async_copy(dwd, part_down.at[j, pl.ds(0, 4)], psem.at[1])

        x_load = pltpu.make_async_copy(wts.at[:, 6], wx, wsem.at[2, 0])
        x_load.start()
        start_either(0, up_load(0))
        down_load(0).start()
        x_load.wait()
        mixed[...] = dot(att[...], wx[...].reshape(D, D)) + exit_bias

        def residual(r, sl):
            return fp32(tok[sl]) + scale1 * mixed[sl]

        hello()
        more.start()

        def norm(res):
            res = res - mean_rows(res)
            inv = lax.rsqrt(mean_rows(res * res) + EPSILON)
            return res * inv, inv

        @pl.loop(0, nrows)
        def _(r):
            sl = ds(r * rows, rows)
            n, _ = norm(residual(r, sl))
            x2[sl] = (n * gain2 + shift2).astype(bf)
            dcot[sl] = (upstream(r) * scale2).astype(bf)

        x2t[...] = x2[...].T
        more.kept()
        down[...] = jnp.zeros_like(down)
        cot2[...] = jnp.zeros_like(cot2)

        @pl.loop(0, F)
        def _(j):
            slot = lax.rem(j, 2)
            every = -(-more.steps // (F // 2 - 1))

            @pl.when(j < F // 2 - 1)
            def _():
                more.run(j * every, (j + 1) * every)

            @pl.when(j == F // 2 - 1)
            def _():
                more.finish_recv()

            @pl.when(j + 1 < F)
            def _():
                start_either(j + 1, up_load(j + 1))
                down_load(j + 1).start()

            up_load(j)[0].wait()
            down_load(j).wait()
            wu_j = wu[slot].reshape(D, H)
            wd_j = wd[slot].reshape(H, D)
            pre = dot(x2[...], wu_j) + ub[j]
            cumul = 0.5 * (1.0 + lax.erf(pre * (1.0 / math.sqrt(2.0))))
            density = jnp.exp(-0.5 * pre * pre) * (1.0 / math.sqrt(2.0 * math.pi))
            act = (pre * cumul).astype(bf)
            slope = cumul + pre * density
            pre_cot = dot(dcot[...], wd_j, NT) * slope
            ubg[j] = jnp.sum(pre_cot, axis=0, keepdims=True)
            low = pre_cot.astype(bf)
            @pl.when(j > 0)
            def _():
                put_up(j - 1)[0].wait()
                put_down(j - 1).wait()

            @pl.when((j > 0) & (lax.rem(j, chunks) == 0))
            def _():
                n = (j // chunks - 1) * g.Z
                @pl.when(j <= 2 * chunks)
                def _():
                    up_a.ready(n, n + g.Z)

                @pl.when(j > 2 * chunks)
                def _():
                    up_b.ready(n - 2 * g.Z, n - g.Z)

                down_sum.ready(n, n + g.Z)

            dwu[...] = dot(x2t[...], low).astype(bf).reshape(F, R, H)
            dwd[...] = dot(act, dcot[...], TN).astype(bf).reshape(4, R, D)
            start_either(j, put_up(j))
            put_down(j).start()
            down[...] += dot(act, wd_j)
            cot2[...] += dot(low, wu_j, NT)

            @pl.when((j > 0) & (lax.rem(j, chunks) == 1))
            def _():
                first = (j // chunks - 1) * g.Z

                @pl.when(first >= 0)
                def _():
                    @pl.when(first < 2 * g.Z)
                    def _():
                        up_a.run(first, first + g.Z)

                    @pl.when(first >= 2 * g.Z)
                    def _():
                        up_a.run(first, first + g.Z)
                        up_b.run(first - 2 * g.Z, first - g.Z)

                    down_sum.run(first, first + g.Z)

        put_up(F - 1)[0].wait()
        put_down(F - 1).wait()
        n = 3 * g.Z
        up_b.ready(n - 2 * g.Z, n - g.Z)
        down_sum.ready(n, n + g.Z)
        vecs[...] = jnp.zeros_like(vecs)

        @pl.loop(0, nrows)
        def _(r):
            sl = ds(r * rows, rows)
            m = mask(r)
            up = upstream(r)
            out = down[sl] + down_bias
            res = residual(r, sl)
            layer[sl] = (m * (res + scale2 * out)).astype(bf)
            n, inv = norm(res)
            c2 = cot2[sl]
            c = c2 * gain2
            rc = up + inv * (c - mean_rows(c) - n * mean_rows(c * n))
            dx[sl] = rc
            mc = rc * scale1
            x2[sl] = mc.astype(bf)
            total = lambda v: jnp.sum(v, axis=0, keepdims=True)
            vecs[0:1] += total(up * out)
            vecs[1:2] += total(up * scale2)
            vecs[2:3] += total(c2 * n)
            vecs[3:4] += total(c2)
            vecs[4:5] += total(rc * mixed[sl])
            vecs[5:6] += total(mc)

        for k in list(range(1, g.n)) + [0]:
            dcot[:, k * W : (k + 1) * W] = dot(x2[...], wx_rows(wx, g.me ^ k, W), NT).astype(bf)
            for cp in cot_copies(dcot, k):
                cp.start()
        for n in range(F // 4):
            at = n * 4 * R
            dwd[...] = dot(att[:, at : at + 4 * R], x2[...], TN).astype(bf).reshape(4, R, D)
            put_x = pltpu.make_async_copy(dwd, part_down.at[pl.ds(n * 4, 4), 4], psem.at[2])
            put_x.start()
            put_x.wait()
        down_sum.ready(4 * g.Z, 5 * g.Z)
        layers.start()
        for cp in cot_copies(dcot, 0):
            cp.wait()
        ref = dcot.at[:, pl.ds(0, W)]
        for k in range(1, g.n):
            remote(ref, ref, csem.at[0, k], csem.at[1, k], g.mate).wait_send()

    polls = units * (N // QB)

    def background(n):
        t = 3 * g.Z + n // EVERY

        @pl.when(lax.rem(n, EVERY) == 0)
        def _():
            step_all(t)

    def step_all(t):
        up_a.step(t)
        up_b.step(t - 2 * g.Z)
        down_sum.step(t)

    def attend_back(hd, ot, ls, kh, vh, kt, cot_t, delta, dq_t, dk, dv, stage):
        loads = [pltpu.make_async_copy(a, b, hsem.at[n]) for n, (a, b) in enumerate(((heads, hd), (out_t, ot), (lse, ls)))]
        for cp in loads:
            cp.start()
        for k in range(1, g.n):
            ref = cots.at[:, ds((g.me ^ k) * T, T)]
            remote(ref, ref, csem.at[0, k], csem.at[1, k], g.peer(k)).wait_recv()
        for cp in loads:
            cp.wait()

        def copy(e, j, kk):
            i, hp = e // pairs, lax.rem(e, pairs)
            dst = back.at[i, :, ds(j * D + g.me * W + hp * 128, 128)]
            src = stage.at[e, j, ds((g.me ^ kk) * T, T)]
            if kk == 0:
                return pltpu.make_async_copy(src, dst, esem.at[2])
            return remote(src, dst, esem.at[0], esem.at[1], g.peer(kk))

        @pl.loop(0, units)
        def _(e):
            i, hp = e // pairs, lax.rem(e, pairs)
            lanes = ds(hp * 128, 128)
            length = length_of(par, *g.image(i), R)
            kt[...] = hd[1, i, :, lanes].T
            cot_t[...] = cots[i, :, lanes].T
            prod = fp32(cot_t[...]) * fp32(ot[i, lanes])
            for hh in range(2):
                hs = slice(hh * HEAD_DIM, (hh + 1) * HEAD_DIM)
                delta[hh : hh + 1] = jnp.sum(prod[hs], axis=0, keepdims=True)
                kh[hh] = masked_keys(hd[1, i, :, lanes], length, hh)
                mine, _ = head_lanes(N, hh)
                vh[hh] = jnp.where(mine, fp32(hd[2, i, :, lanes]), 0.0).astype(bf)
            dk[...] = jnp.zeros_like(dk)
            dv[...] = jnp.zeros_like(dv)

            @pl.loop(0, N // QB)
            def _(b):
                cols = ds(b * QB, QB)
                qb, cb = hd[0, i, cols, lanes], cots[i, cols, lanes]
                for hh in range(2):
                    hs = slice(hh * HEAD_DIM, (hh + 1) * HEAD_DIM)
                    mine, _ = head_lanes(QB, hh)
                    qs = scaled_queries(qb, hh)
                    prob = jnp.exp(dot(kh[hh], qs, NT) - ls[i, hp, hh : hh + 1, cols])
                    sg = dot(vh[hh], cb, NT)
                    sc = (prob * (sg - delta[hh : hh + 1, cols])).astype(bf)
                    w = prob.astype(bf)
                    dv[...] += dot(w, jnp.where(mine, fp32(cb), 0.0).astype(bf))
                    dk[...] += dot(sc, jnp.where(mine, fp32(qs), 0.0).astype(bf))
                    dq_t[hs, cols] = (dot(kt[hs], sc) * HEAD_DIM ** (-0.5)).astype(bf)
                background(e * (N // QB) + b)

            stage[e, 0] = dq_t[...].T
            stage[e, 1] = dk[...].astype(bf)
            stage[e, 2] = dv[...].astype(bf)
            for j in range(3):
                for kk in list(range(1, g.n)) + [0]:
                    copy(e, j, kk).start()

        ref = stage.at[:, :, pl.ds(0, (g.n - 1) * T)]
        cp = remote(ref, ref, esem.at[0], esem.at[1], g.mate)
        cp.wait_send()
        cp.wait_recv()
        ref = stage.at[:, :, pl.ds(0, T)]
        pltpu.make_async_copy(ref, ref, esem.at[2]).wait()

    def entry(part, ein, win, x1v, x1t, acc, rows_v, dxl):
        grads = Regroup(g, part_of(dxl), lambda q: dx_out.at[q], msem.at[2], back=True)
        entry_sum = Scatter(g, part, g_first, refs[48:64])
        loads = [pltpu.make_async_copy(back.at[:, :, pl.ds(j * D, D)], ein.at[j], hsem.at[j]) for j in range(3)]
        weights = [pltpu.make_async_copy(first.at[:, j], win.at[j % 2], wsem.at[2, j % 2]) for j in range(3)]
        x_load = pltpu.make_async_copy(x1, x1v, wsem.at[0, 0])
        for cp in [x_load] + loads + weights[:2]:
            cp.start()
        x_load.wait()
        x1t[...] = x1v[...].T
        at = 3 * g.Z + polls // EVERY

        def others(n, k):
            for t in range(at + n, at + n + k):
                step_all(t)

        rows_v[...] = jnp.zeros_like(rows_v)
        cot_of = lambda j: ein[j].reshape(M, D)
        for j in range(3):
            loads[j].wait()
            part[:, j] = dot(x1t[...], cot_of(j)).astype(bf).reshape(F, R, D)
            if j:
                entry_sum.run((j - 1) * g.Z, j * g.Z)
            entry_sum.ready(j * g.Z, (j + 1) * g.Z)
            others(2 * j, 2)
        for j in range(3):
            weights[j].wait()
            d = dot(cot_of(j), win[j % 2].reshape(D, D), NT)
            if j == 0:
                weights[2].start()
                acc[...] = d
            else:
                acc[...] += d
            others(6 + 2 * j, 2)
            entry_sum.run(2 * g.Z + j, 2 * g.Z + j + 1)
        rows_v[2:3] = jnp.sum(fp32(cot_of(0)), axis=0, keepdims=True)
        rows_v[3:4] = jnp.sum(fp32(cot_of(2)), axis=0, keepdims=True)
        gain = par[0:1]

        @pl.loop(0, nrows)
        def _(r):
            sl = ds(r * rows, rows)
            x = fp32(tok[sl])
            x = x - mean_rows(x)
            inv = lax.rsqrt(mean_rows(x * x) + EPSILON)
            n = x * inv
            d1 = acc[sl]
            c = d1 * gain
            dxl[sl] = (dx[sl] + inv * (c - mean_rows(c) - n * mean_rows(c * n))).astype(bf)
            rows_v[0:1] += jnp.sum(d1 * n, axis=0, keepdims=True)
            rows_v[1:2] += jnp.sum(d1, axis=0, keepdims=True)
            entry_sum.step(2 * g.Z + 3 + r)

        grads.start()
        slab[...] = jnp.zeros_like(slab)
        own = [(0, rows_v, 0), (1, rows_v, 1), (4, vecs, 5), (5, vecs, 4), (6, vecs, 2), (7, vecs, 3), (12, vecs, 1), (13, vecs, 0)]
        V = R
        for f in range(F):
            for to, src, r in own:
                slab[f, to : to + 1, :V] = src[r : r + 1, f * V : (f + 1) * V]
            for r in range(2):
                p = (f * 2 + r) * V
                slab[f, 2 + r : 3 + r, :V] = rows_v[2 + p // D : 3 + p // D, p % D : p % D + V]
            for r in range(4):
                slab[f, 8 + r : 9 + r, :V] = ubg[f, :, r * V : (r + 1) * V]
        vsum.start()
        mark = 2 * g.Z + 3 + nrows
        entry_sum.run(mark, mark + 4)
        vsum.middle()
        left = max(down_sum.steps, up_a.steps, up_b.steps + 2 * g.Z) - (at + 12)

        @pl.loop(0, max(left, entry_sum.steps - mark - 4))
        def _(t):
            step_all(at + 12 + t)
            entry_sum.step(mark + 4 + t)

        entry_sum.finish()
        grads.arrived()
        grads.sent()

    hello = g.greet()
    v = pltpu.VMEM
    pl.run_scoped(
        feed_forward, v((M, D), fl), v((M, D), bf), v((D, M), bf), v((M, D), bf), v((M, D), fl), v((M, D), fl),
        v((2, F, R, H), bf), v((2, 4, R, D), bf), v((F, R, D), bf), v((F, R, H), bf), v((4, R, D), bf),
    )
    pl.run_scoped(
        attend_back, v((3, images, N, W), bf), v((images, W, N), bf), v((images, pairs, 8, N), fl), v((2, N, 128), bf),
        v((2, N, 128), bf), v((128, N), bf), v((128, N), bf), v((8, N), fl), v((128, N), bf), v((N, 128), fl),
        v((N, 128), fl), v((units, 3, N, 128), bf),
    )
    pl.run_scoped(
        entry, v((F, 3, R, D), bf), v((3, images, T, D), bf), v((2, F, R, D), bf), v((M, D), bf), v((D, M), bf),
        v((M, D), fl), v((8, D), fl), v((M, D), bf),
    )
    up_a.finish()
    up_b.finish()
    down_sum.finish()
    vsum.finish()
    more.finish_send()
    layers.arrived()
    layers.sent()


def wx_rows(wx, peer, W):
    F, R, D = wx.shape
    n = W // R
    return wx[pl.ds(peer * n, n)].reshape(W, D)


LAG = 4
UP_TAIL = 10
EVERY = 2


def rear_call(S, F, cid, slots, held, tok, cot, att, par, ub, wu_own, wts, heads, out_t, lse, x1, first):
    M, D = cot.shape
    piece = M // slots
    n, images = (2, 1) if whole_images(S, slots) else (S, slots)
    T = M // images
    R = wts.shape[2]
    FF = ub.shape[1]
    H = FF // F
    W, N = D // n, n * T
    bf, fl = jnp.bfloat16, jnp.float32
    SM = pl.BlockSpec(memory_space=pltpu.SMEM)
    out, v = jax.ShapeDtypeStruct, pltpu.VMEM
    return pl.pallas_call(
        functools.partial(rear_kernel, S, F, min(256, N)),
        out_shape=[
            out((slots, piece, D), bf), out((slots, piece, D), bf), out((16, 128), fl), out((F, 5, R, D), bf), out((F, 2, R, D), bf), out((F, 2, R, D), bf),
            out((5 * R, D), bf), out((R, 4 * D), bf), out((R, 3 * D), bf), out((images, T, 3 * D), bf), out((F, 2, R, D), bf),
        ],
        in_specs=[SM, VM, VM, VM, VM, VM] + [ANY] * 7,
        out_specs=[ANY, ANY, VM] + [ANY] * 8,
        scratch_shapes=[v((M, D), bf), v((M, D), fl), DMA((3, 2, slots)), v((images, N, W), bf), v((8, D), fl), v((F, 1, H), fl), v((F, 16, 128), fl),
                        DMA((2, n)), DMA((3,)), DMA((3, 2)), DMA((3,)), DMA((3,))]
        + Scatter.scratch(S, F, 5, R, D, K=F)
        + Scatter.scratch(S, F, 2, R, D, wide=True, K=F // 2)
        + Scatter.scratch(S, F, 2, R, D, K=F // 2)
        + Scatter.scratch(S, F, 3, R, D, K=F // 2)
        + VecSum.scratch(S, F, 16, 128)
        + Gather.scratch(S, F, 2, R, D),
        compiler_params=pltpu.CompilerParams(collective_id=cid, **PARAMS),
        name="rear",
    )(held, tok, cot, att, par, ub.reshape(F, 1, H), wu_own, wts, heads, out_t, lse, x1, first)


def body(S, F, images, out_grad, lengths, images_held, first_gain, first_shift, entry_weight, entry_bias, exit_weight,
         exit_bias, first_scale, second_gain, second_shift, up_weight, up_bias, down_weight, down_bias, second_scale):
    slots, T, D = images.shape
    M = slots * T
    R = entry_weight.shape[0]
    FF = up_weight.shape[1]
    fl = jnp.float32
    V = R
    rows = [first_gain, first_shift, entry_bias, exit_bias, first_scale, second_gain, second_shift, up_bias, down_bias, second_scale]
    own_vec, at = jnp.zeros((16, 128), jnp.bfloat16), 0
    for v in rows:
        n = v.shape[0] // V
        own_vec = own_vec + jnp.pad(v.reshape(n, V), ((at, 16 - at - n), (0, 128 - V)))
        at += n
    for v in (lengths // 32, lengths % 32):
        own_vec = own_vec + jnp.pad(v.astype(jnp.bfloat16).reshape(1, slots), ((at, 15 - at), (0, 128 - slots)))
        at += 1
    first, rest, par, ub, x1, heads, out_t, lse, att, tok, cot = front_call(
        S, F, 0, images, out_grad, own_vec, entry_weight, exit_weight, up_weight, down_weight
    )
    layer, dx, small, _, _, _, g_down, g_up, g_first, _, _ = rear_call(
        S, F, 1, slots, images_held, tok, cot, att.reshape(M, D), par, ub, up_weight, rest, heads, out_t, lse, x1, first
    )
    vectors = [v.shape[0] for v in rows]
    down, exit_, up, first, dx, layer, *small = results_call(V, g_down, g_up, g_first, dx, layer, small, vectors)
    return (
        layer.reshape(slots, T, D), dx.reshape(slots, T, D), small[0], small[1], first, small[2], exit_, small[3], small[4],
        small[5], small[6], up, small[7], down, small[8], small[9],
    )


def results_kernel(V, down, out, up, first, dx, layer, small, *outs):
    for src, dst in zip((down, out, up, first, dx, layer), outs):
        dst[...] = src[...].astype(dst.dtype)

    @pl.when(pl.program_id(0) == 0)
    def _():
        at = 0
        for dst in outs[6:]:
            n = dst.shape[0] // V
            for r in range(n):
                dst[r * V : (r + 1) * V] = small[at + r, :V]
            at += n


def results_call(V, g_down, g_up, g_first, dx, layer, small, vectors):
    slots, T, D = dx.shape
    R = g_up.shape[0]
    steps = 4
    fl = jnp.float32
    out = jax.ShapeDtypeStruct
    q = R // steps
    t = slots * T // steps
    row = lambda n, width, first=0: pl.BlockSpec((n, width), lambda i: (first + i, 0))
    whole = lambda *shape: pl.BlockSpec(shape, lambda i: (0,) * len(shape))
    tokens = (slots * T, D)
    res = pl.pallas_call(
        functools.partial(results_kernel, V),
        grid=(steps,),
        out_shape=[out((4 * R, D), fl), out((R, D), fl), out(g_up.shape, fl), out(g_first.shape, fl), out(tokens, fl),
                   out(tokens, layer.dtype)] + [out((n,), fl) for n in vectors],
        in_specs=[row(R, D), row(q, D, 4 * steps), row(q, 4 * D), row(q, 3 * D), row(t, D), row(t, D), whole(16, 128)],
        out_specs=[row(R, D), row(q, D), row(q, 4 * D), row(q, 3 * D), row(t, D), row(t, D)] + [whole(n) for n in vectors],
        compiler_params=pltpu.CompilerParams(vmem_limit_bytes=62 * 2**20),
        name="results",
    )(g_down, g_down, g_up, g_first, dx.reshape(tokens), layer.reshape(tokens), small)
    return res


def solution(mesh):
    S, F = mesh.shape["seq"], mesh.shape["fsdp"]
    vector, matrix, tokens = P("fsdp"), P("fsdp", None), P("fsdp", "seq", None)
    return jax.shard_map(
        functools.partial(body, S, F),
        mesh=mesh,
        in_specs=(tokens, tokens, vector, P(), vector, vector, matrix, vector, matrix, vector, vector, vector, vector,
                  matrix, vector, matrix, vector, vector),
        out_specs=(tokens, tokens, vector, vector, matrix, vector, matrix, vector, vector, vector, vector, matrix, vector,
                   matrix, vector, vector),
        check_vma=False,
    )
```

```python
import functools
import math

import jax
import jax.numpy as jnp
from jax import lax
from jax.experimental import pallas as pl
from jax.experimental.pallas import tpu as pltpu
from jax.sharding import PartitionSpec as P

HEAD_DIM = 64
EPSILON = 1e-06
NEG_LARGE = -1e30

MESH = pl.DeviceIdType.MESH
DMA = pltpu.SemaphoreType.DMA
ANY = pl.BlockSpec(memory_space=pl.ANY)
VM = pl.BlockSpec(memory_space=pltpu.VMEM)


def remote(src, dst, ssem, rsem, dev):
    return pltpu.make_async_remote_copy(
        src_ref=src, dst_ref=dst, send_sem=ssem, recv_sem=rsem, device_id=dev, device_id_type=MESH
    )


class Place:
    def __init__(self, S, F, slots):
        self.S, self.F, self.Z, self.slots = S, F, F // 2, slots
        self.bits = [1 << b for b in range(S.bit_length() - 1)]
        self.nbits = len(self.bits)
        self.order = [self.bits, self.bits[1:] + self.bits[:1]]
        self.s = lax.axis_index("seq")
        self.f = lax.axis_index("fsdp")
        self.z, self.c = self.f // 2, lax.rem(self.f, 2)
        self.mate = (self.s, self.f ^ 1)
        self.regroup = whole_images(S, slots)
        self.n = 2 if self.regroup else S
        self.me = self.c if self.regroup else self.s
        self.images = 1 if self.regroup else slots

    def at(self, zz):
        return (self.s, zz * 2 + self.c)

    def peer(self, k):
        return (self.s, self.f ^ k) if self.regroup else (self.s ^ k, self.f)

    def image(self, i):
        if self.regroup:
            return self.z * 2 + self.s // self.slots, lax.rem(self.s, self.slots)
        return self.f, i

    def goes(self, i):
        if not self.regroup:
            return self.mate, i, True
        to, core = self.c * self.slots + i, self.s // self.slots
        return (to, self.z * 2 + core), lax.rem(self.s, self.slots), (to == self.s) & (core == self.c)

    def came(self, r):
        if not self.regroup:
            return self.mate, r, True
        of, core = self.c * self.slots + r, self.s // self.slots
        return (of, self.z * 2 + core), lax.rem(self.s, self.slots), (of == self.s) & (core == self.c)

    def greet(self):
        bar = pltpu.get_barrier_semaphore()
        for k in range(1, self.F):
            pl.semaphore_signal(bar, inc=1, device_id=(self.s, lax.rem(self.f + k, self.F)), device_id_type=MESH)
        for k in range(1, self.S):
            for core in range(2 if self.regroup else 1):
                pl.semaphore_signal(bar, inc=1, device_id=(self.s ^ k, self.f ^ core), device_id_type=MESH)
        return lambda: pl.semaphore_wait(bar, self.F - 1 + (self.S - 1) * (2 if self.regroup else 1))

    def meet(self):
        self.greet()()


def whole_images(S, slots):
    return S == 2 * slots


class Regroup:
    def __init__(self, g, src, dst, sems, back=False):
        self.g, self.src, self.dst, self.sems = g, src, dst, sems
        self.out, self.into = (g.came, g.goes) if back else (g.goes, g.came)

    @staticmethod
    def scratch(slots):
        return [DMA((2, slots))]

    def each(self, way, local, remote_part):
        for p in range(self.g.slots):
            device, q, here = way(p)
            if here is True:
                local(p, q)
            else:
                pl.when(here)(lambda p=p, q=q: local(p, q))
                pl.when(jnp.logical_not(here))(lambda p=p, q=q, device=device: remote_part(p, q, device))

    def start(self):
        def local(p, q):
            pltpu.make_async_copy(self.src(p), self.dst(q), self.sems.at[0, p]).start()

        def away(p, q, device):
            remote(self.src(p), self.dst(q), self.sems.at[0, p], self.sems.at[1, q], device).start()

        self.each(self.out, local, away)

    def arrived(self):
        def away(p, q, device):
            remote(self.dst(p), self.dst(p), self.sems.at[0, p], self.sems.at[1, p], device).wait_recv()

        self.each(self.into, lambda p, q: None, away)

        def local(p, q):
            pltpu.make_async_copy(self.src(p), self.dst(q), self.sems.at[0, p]).wait()

        self.each(self.out, local, lambda p, q, device: None)

    def sent(self):
        def away(p, q, device):
            remote(self.src(p), self.dst(p), self.sems.at[0, p], self.sems.at[1, p], device).wait_send()

        self.each(self.out, lambda p, q: None, away)


def span(bits):
    out = [0]
    for b in bits:
        out = out + [m | b for m in out]
    return out


def ds(start, size):
    return pl.ds(pl.multiple_of(start, size), size)


class Gather:
    def __init__(self, g, NB, b0, own, full, refs, wide=False, lag=8):
        self.g, self.NB, self.b0, self.own, self.full, self.lag = g, NB, b0, own, full, lag
        self.bounce, self.zs, self.zr, self.xs, self.xr, self.ms, self.ls = refs
        self.R, self.D = full.shape[2:]
        self.C = self.D if wide else self.D // g.S
        self.nbits = 0 if wide else g.nbits
        self.mine = 0 if wide else g.s
        self.nitems = (g.Z - 1) * NB * 2
        self.steps = self.nitems + lag * self.nbits

    @staticmethod
    def scratch(S, F, NB, R, D, bounce=True):
        Z, nb = F // 2, S.bit_length() - 1
        return [pltpu.VMEM((NB if bounce else 1, R, D), jnp.bfloat16), DMA((2,)), DMA((NB, Z)), DMA((nb,)),
                DMA((NB, Z, nb)), DMA((2,)), DMA((1,))]

    def cols(self, q):
        return ds(q * self.C, self.C)

    def half(self, p):
        return pl.ds(p * (self.R // 2), self.R // 2)

    def block(self, f, b):
        return self.full.at[f, self.b0 + b]

    def zfull(self, b, zz):
        return self.full.at[zz * 2 + self.g.c, self.b0 + b, :, self.cols(self.mine)]

    def zcopy(self, src, b, zz, way, to):
        return remote(src, self.zfull(b, zz), self.zs.at[way], self.zr.at[b, zz], self.g.at(to))

    def mate_copy(self, src, b, zz):
        return remote(src, self.block(zz * 2 + self.g.c, b), self.ms.at[0], self.ms.at[1], self.g.mate)

    def keeps(self):
        direct = self.bounce.shape[0] < self.NB
        for b in range(self.NB):
            dst = self.block(self.g.f, b) if direct else self.bounce.at[b]
            yield pltpu.make_async_copy(self.own(b, slice(None)), dst, self.ls.at[0])

    def stored(self):
        return pltpu.make_async_copy(self.bounce, self.full.at[self.g.f, pl.ds(self.b0, self.NB)], self.ls.at[0])

    def start(self):
        g = self.g
        for b in range(self.NB):
            piece = self.own(b, self.cols(self.mine))

            @pl.when(g.z < g.Z - 1)
            def _():
                self.zcopy(piece, b, g.z, 0, g.z + 1).start()

            @pl.when(g.z > 0)
            def _():
                self.zcopy(piece, b, g.z, 1, g.z - 1).start()

        for cp in self.keeps():
            cp.start()
        for b in range(self.NB):
            self.mate_copy(self.own(b, slice(None)), b, g.z).start()

    def kept(self):
        blocks = self.full.at[self.g.f, pl.ds(self.b0, self.NB)]
        pltpu.make_async_copy(blocks, blocks, self.ls.at[0]).wait()
        if self.bounce.shape[0] == self.NB:
            self.stored().start()

    def xcopies(self, b, zz, p, j):
        g = self.g
        to = (g.s ^ g.order[p][j], g.f)
        out = []
        for m in span(g.order[p][:j]):
            ref = self.full.at[zz * 2 + g.c, self.b0 + b, self.half(p), self.cols(g.s ^ m)]
            out.append(remote(ref, ref, self.xs.at[j], self.xr.at[b, zz, j], to))
        return out

    def doubled(self, b, zz, j):
        ref = self.full.at[zz * 2 + self.g.c, self.b0 + b, :, pl.ds(0, self.C << j)]
        return remote(ref, ref, self.xs.at[j], self.xr.at[b, zz, j], self.g.mate)

    def item(self, t):
        g = self.g
        h = 1 + t // (2 * self.NB)
        r = lax.rem(t, 2 * self.NB)
        b, below = r // 2, lax.rem(r, 2) == 0
        zz = jnp.where(below, g.z - h, g.z + h)
        ok = (t >= 0) & (t < self.nitems) & (zz >= 0) & (zz < g.Z)
        nxt = jnp.where(below, g.z + 1, g.z - 1)
        more = (nxt >= 0) & (nxt < g.Z)
        way = jnp.where(below, 0, 1)
        return b, zz, ok, nxt, more, way

    def step(self, t):
        g = self.g
        for j in reversed(range(self.nbits + 1)):
            b, zz, ok, nxt, more, way = self.item(t - self.lag * j)

            @pl.when(ok)
            def _(j=j, b=b, zz=zz, nxt=nxt, more=more, way=way):
                if j == 0:
                    piece = self.zfull(b, zz)
                    self.zcopy(piece, b, zz, 0, g.z).wait_recv()

                    @pl.when(more)
                    def _():
                        self.zcopy(piece, b, zz, way, nxt).start()
                else:
                    self.doubled(b, zz, j - 1).wait_recv()
                if j < self.nbits:
                    for p in range(2):
                        for cp in self.xcopies(b, zz, p, j):
                            cp.start()
                else:
                    self.mate_copy(self.block(zz * 2 + g.c, b), b, zz).start()

    def run(self, lo, hi):
        @pl.loop(lo, hi)
        def _(t):
            self.step(t)

    def part(self, chips, cols):
        ref = self.full.at[pl.ds(0, chips), pl.ds(self.b0, self.NB), :, pl.ds(0, cols)]
        return ref

    def finish_recv(self):
        if self.bounce.shape[0] == self.NB:
            self.stored().wait()
        ref = self.part(self.g.Z, self.D)
        remote(ref, ref, self.ms.at[0], self.ms.at[1], self.g.mate).wait_recv()

    def finish_send(self):
        g = self.g
        ref = self.part(g.Z, self.D)
        remote(ref, ref, self.ms.at[0], self.ms.at[1], g.mate).wait_send()
        for j in range(self.nbits):
            ref = self.part(g.Z - 1, self.C << j)
            remote(ref, ref, self.xs.at[j], self.xr.at[0, 0, j], g.mate).wait_send()
        for zz in range(g.Z):

            @pl.when(g.z == zz)
            def _(zz=zz):
                for way, n in ((0, zz + 1 if zz < g.Z - 1 else 0), (1, g.Z - zz if zz > 0 else 0)):
                    if n:
                        ref = self.part(n, self.C)
                        remote(ref, ref, self.zs.at[way], self.zr.at[0, 0], g.mate).wait_send()


class Scatter:
    def __init__(self, g, part, out, refs, per=0, wide=False, lag=4, tail=0, above=False):
        self.g, self.part, self.out, self.per, self.wide, self.lag, self.above = g, part, out, per, wide, lag, above
        self.core, self.ring, self.xb, self.zb, self.fq = refs[:5]
        self.own, self.c_s, self.c_r, self.x_s, self.x_r, self.z_s, self.z_r, self.a_s, self.a_r, self.o, self.free = refs[5:]
        _, self.NB, self.R, self.D = part.shape
        self.C = self.D // g.S
        self.n = self.NB * g.Z
        self.K = self.ring.shape[0]
        self.tail = tail or (lag if wide else g.nbits * lag + 2 * lag)
        self.after = g.nbits if wide else 0
        self.steps = self.n + self.per + self.tail + lag * (self.after + g.nbits + 1) + 1

    @staticmethod
    def scratch(S, F, NB, R, D, wide=False, K=0):
        Z, nb = F // 2, S.bit_length() - 1
        K = K or NB * Z
        C, n, bf = D // S, NB * Z, jnp.bfloat16
        nx = NB if wide else n
        return [
            pltpu.VMEM((n, R, D), bf), pltpu.VMEM((K, R, D), bf), pltpu.VMEM((nx, 2, R // 2, D - C), bf),
            pltpu.VMEM((NB, Z - 1, R, D if wide else C), bf), pltpu.VMEM((NB, R, D if wide else C), bf),
            DMA((n,)), DMA((1,)), DMA((K,)), DMA((nb,)), DMA((nx, nb)), DMA((1,)), DMA((NB,)),
            DMA((nb,)), DMA((NB, nb)), DMA((1,)), pltpu.SemaphoreType.REGULAR,
        ]

    def fold(self, zz):
        Z = self.g.Z
        return jnp.where(zz < (Z + 1) // 2, 2 * zz, 2 * (Z - 1 - zz) + 1)

    def unfold(self, r):
        return jnp.where(lax.rem(r, 2) == 0, r // 2, self.g.Z - 1 - r // 2)

    def where(self, t):
        Z, per = self.g.Z, self.per
        b, zz = t // Z, self.unfold(lax.rem(t, Z))
        if per:
            rows = t < per * Z
            b, zz = jnp.where(rows, lax.rem(t, per), b), jnp.where(rows, t // per, zz)
        return b, zz

    def item_of(self, b, zz):
        Z, per = self.g.Z, self.per
        t = b * Z + self.fold(zz)
        return jnp.where(b < per, zz * per + b, t) if per else t

    def due(self, v):
        Z, per = self.g.Z, self.per
        ok = (v >= 0) & (v < self.n) & (lax.rem(v, Z) == Z - 1)
        b = v // Z
        if per:
            first = per * Z
            u = v - first + 1
            early = (u >= 0) & (u < per)
            w = v - per
            late = (w >= first) & (w < self.n) & (lax.rem(w, Z) == Z - 1)
            ok = early | late
            b = jnp.where(early, u, w // Z)
        return b, ok

    def cols(self, q):
        return ds(q * self.C, self.C)

    def half(self, p):
        return pl.ds(p * (self.R // 2), self.R // 2)

    def load(self, t):
        b, zz = self.where(t)
        return pltpu.make_async_copy(self.part.at[zz * 2 + self.g.c, b], self.core.at[t], self.own.at[t])

    def swap(self, t):
        b, zz = self.where(t)
        k = lax.rem(t, self.K)
        return remote(self.part.at[zz * 2 + 1 - self.g.c, b], self.ring.at[k], self.c_s.at[0], self.c_r.at[k], self.g.mate)

    def offset(self, j):
        return sum((self.g.S >> (i + 1)) * self.C for i in range(j))

    def halving(self, src, x, p, j):
        g = self.g
        order = g.order[p]
        base = (g.s ^ order[j]) & sum(order[: j + 1])
        to = (g.s ^ order[j], g.f)
        out = []
        for i, m in enumerate(span(order[j + 1 :])):
            dst = self.xb.at[x, p, :, pl.ds(self.offset(j) + i * self.C, self.C)]
            out.append(remote(src.at[self.half(p), self.cols(base | m)], dst, self.x_s.at[j], self.x_r.at[x, j], to))
        return out

    def halved(self, x, j):
        ref = self.xb.at[x, :, :, pl.ds(self.offset(j), (self.g.S >> (j + 1)) * self.C)]
        return remote(ref, ref, self.x_s.at[j], self.x_r.at[x, j], self.g.mate)

    def add_halves(self, buf, x, j):
        g = self.g
        for p in range(2):
            order = g.order[p]
            base = g.s & sum(order[: j + 1])
            for i, m in enumerate(span(order[j + 1 :])):
                q = self.cols(base | m)
                got = self.xb[x, p, :, pl.ds(self.offset(j) + i * self.C, self.C)]
                buf[self.half(p), q] = buf[self.half(p), q] + got

    def piece(self, t, b, zz):
        g = self.g
        src = self.core.at[t] if self.wide else self.core.at[t, :, self.cols(g.s)]
        slot = lax.rem(g.z - zz - 1 + g.Z, g.Z)
        return remote(src, self.zb.at[b, slot], self.z_s.at[0], self.z_r.at[b], g.at(zz))

    def arrived(self, b):
        ref = self.zb.at[b]
        return remote(ref, ref, self.z_s.at[0], self.z_r.at[b], self.g.mate)

    def final(self, b, rows=slice(None)):
        return self.fq.at[b, rows, self.cols(self.g.s)] if self.wide else self.fq.at[b, rows]

    def result(self, b, q, p=None):
        rows, start = (self.R, 0) if p is None else (self.R // 2, p * (self.R // 2))
        if self.above:
            return self.out.at[ds(b * self.R + start, rows), self.cols(q)]
        return self.out.at[pl.ds(start, rows), ds(b * self.D + q * self.C, self.C)]

    def doubling(self, b, p, j):
        g = self.g
        to = (g.s ^ g.order[p][j], g.f)
        out = []
        for m in span(g.order[p][:j]):
            dst = self.result(b, g.s ^ m, p)
            src = self.final(b, self.half(p)) if m == 0 else dst
            out.append(remote(src, dst, self.a_s.at[j], self.a_r.at[b, j], to))
        return out

    def doubled(self, b, j):
        ref = self.out.at[pl.ds(0, self.R), pl.ds(0, self.C << j)]
        return remote(ref, ref, self.a_s.at[j], self.a_r.at[b, j], self.g.mate)

    def stored(self, b):
        return pltpu.make_async_copy(self.final(b), self.result(b, self.g.s), self.o.at[0])

    def ready(self, lo, hi):
        @pl.loop(lo, hi)
        def _(t):
            self.load(t).start()

            @pl.when(t >= self.K)
            def _():
                pl.semaphore_wait(self.free, 1)

            self.swap(t).start()

    def step(self, t):
        g = self.g
        for j in reversed(range(self.after + g.nbits + 1)):
            b, ok = self.due(t - self.tail - self.lag * j)

            @pl.when(ok)
            def _(j=j, b=b):
                if j == 0:
                    self.arrived(b).wait_recv()
                    mine = self.core[self.item_of(b, g.z)] if self.wide else self.core[self.item_of(b, g.z), :, self.cols(g.s)]
                    total = mine.astype(jnp.float32)
                    for k in range(g.Z - 1):
                        total = total + self.zb[b, k].astype(jnp.float32)
                    self.fq[b] = total.astype(self.fq.dtype)
                elif j <= self.after:
                    self.halved(b, j - 1).wait_recv()
                    self.add_halves(self.fq.at[b], b, j - 1)
                else:
                    self.doubled(b, j - self.after - 1).wait_recv()
                if j < self.after:
                    for p in range(2):
                        for cp in self.halving(self.fq.at[b], b, p, j):
                            cp.start()
                elif j < self.after + g.nbits:
                    if j == self.after:
                        self.stored(b).start()
                    for p in range(2):
                        for cp in self.doubling(b, p, j - self.after):
                            cp.start()

        last = 0 if self.wide else g.nbits
        for j in reversed(range(last + 1)):
            u = t - self.lag * j

            @pl.when((u >= 0) & (u < self.n))
            def _(j=j, u=u):
                b, zz = self.where(u)
                buf = self.core.at[u]
                if j == 0:
                    self.load(u).wait()
                    self.swap(u).wait_recv()
                    buf[...] = buf[...] + self.ring[lax.rem(u, self.K)]

                    @pl.when(u + self.K < self.n)
                    def _():
                        pl.semaphore_signal(self.free, inc=1, device_id=g.mate, device_id_type=MESH)
                else:
                    self.halved(u, j - 1).wait_recv()
                    self.add_halves(buf, u, j - 1)
                if j < last:
                    for p in range(2):
                        for cp in self.halving(buf, u, p, j):
                            cp.start()
                else:

                    @pl.when(zz != g.z)
                    def _():
                        self.piece(u, b, zz).start()

    def run(self, lo, hi):
        @pl.loop(lo, hi)
        def _(t):
            self.step(t)

    def finish(self):
        g = self.g

        def done(ref, sem):
            remote(ref, ref, sem, self.z_r.at[0], g.mate).wait_send()

        done(self.core, self.c_s.at[0])
        done(self.zb, self.z_s.at[0])
        for j in range(g.nbits):
            done(self.xb.at[:, :, :, pl.ds(self.offset(j), (g.S >> (j + 1)) * self.C)], self.x_s.at[j])
            done(self.all_of(self.C << j), self.a_s.at[j])
        ref = self.all_of(self.C)
        pltpu.make_async_copy(ref, ref, self.o.at[0]).wait()

    def all_of(self, width):
        return self.out.at[:, pl.ds(0, width if self.above else width * self.NB)]


class VecGather:
    def __init__(self, g, vec, out, sems):
        self.g, self.vec, self.out, self.sems = g, vec, out, sems

    @staticmethod
    def scratch(F):
        return [DMA((3,))]

    def start(self):
        g, sems = self.g, self.sems
        pltpu.make_async_copy(self.vec, self.out.at[g.f], sems.at[2]).start()
        for k in range(1, g.F):
            remote(self.vec, self.out.at[g.f], sems.at[0], sems.at[1], (g.s, lax.rem(g.f + k, g.F))).start()

    def finish(self):
        g, sems = self.g, self.sems
        pltpu.make_async_copy(self.vec, self.out.at[g.f], sems.at[2]).wait()
        ref = self.out.at[pl.ds(0, g.F - 1)]
        cp = remote(ref, ref, sems.at[0], sems.at[1], g.mate)
        cp.wait_send()
        cp.wait_recv()


class VecSum:
    def __init__(self, g, vec, out, refs):
        self.g, self.vec, self.out = g, vec, out
        self.fb, self.mid, self.sb, self.sems = refs

    @staticmethod
    def scratch(S, F, N, L):
        fl = jnp.float32
        return [pltpu.VMEM((F, N, L), fl), pltpu.VMEM((N, L), fl), pltpu.VMEM((S, N, L), fl), DMA((4,))]

    def start(self):
        g = self.g
        for k in range(1, g.F):
            to = lax.rem(g.f + k, g.F)
            remote(self.vec.at[to], self.fb.at[g.f], self.sems.at[0], self.sems.at[1], (g.s, to)).start()

    def middle(self):
        g = self.g
        ref = self.fb.at[pl.ds(0, g.F - 1)]
        cp = remote(ref, ref, self.sems.at[0], self.sems.at[1], g.mate)
        cp.wait_recv()
        total = self.vec[g.f]
        for k in range(1, g.F):
            total = total + self.fb[lax.rem(g.f + k, g.F)]
        self.mid[...] = total
        for k in range(1, g.S):
            remote(self.mid, self.sb.at[g.s], self.sems.at[2], self.sems.at[3], (g.s ^ k, g.f)).start()
        cp.wait_send()

    def finish(self):
        g = self.g
        ref = self.sb.at[pl.ds(0, g.S - 1)]
        cp = remote(ref, ref, self.sems.at[2], self.sems.at[3], g.mate)
        cp.wait_recv()
        total = self.mid[...]
        for k in range(1, g.S):
            total = total + self.sb[g.s ^ k]
        self.out[...] = total
        cp.wait_send()


PARAMS = dict(has_side_effects=True, vmem_limit_bytes=62 * 2**20)


def fp32(x):
    return x.astype(jnp.float32)


def dot(a, b, dims=((1,), (0,))):
    return lax.dot_general(a, b, (dims, ((), ())), preferred_element_type=jnp.float32)


NT = ((1,), (1,))
TN = ((0,), (0,))


def mean_rows(x):
    return jnp.mean(x, axis=-1, keepdims=True)


def head_lanes(rows, hh):
    lane = lax.broadcasted_iota(jnp.int32, (rows, 128), 1)
    mine = (lane >= hh * HEAD_DIM) & (lane < (hh + 1) * HEAD_DIM)
    spare = lane == (1 - hh) * HEAD_DIM
    return mine, spare


def length_of(par, group, slot, V):
    lane = lax.broadcasted_iota(jnp.int32, (1, par.shape[1]), 1)
    value = par[14:15] * 32.0 + par[15:16]
    return jnp.sum(jnp.where(lane == group * V + slot, value, 0.0), axis=1, keepdims=True)


def masked_keys(k, length, hh):
    N = k.shape[0]
    mine, spare = head_lanes(N, hh)
    late = fp32(lax.broadcasted_iota(jnp.int32, (N, 128), 0)) >= length
    return jnp.where(mine, fp32(k), jnp.where(spare & late, NEG_LARGE, 0.0)).astype(jnp.bfloat16)


def scaled_queries(q, hh):
    mine, spare = head_lanes(q.shape[0], hh)
    return jnp.where(mine, fp32(q) * HEAD_DIM ** (-0.5), jnp.where(spare, 1.0, 0.0)).astype(jnp.bfloat16)


def front_kernel(S, F, nwide, QB, img, cot, vec, wq, wx, wu, wd,
                 first_out, rest, par, ub, x1, heads_out, out_t, lse, att, tok_out, cot_out,
                 first, tok, cot_v, fsem, tsem, csem, vec_full, norm, eb, stage, heads, kh, vt, o_buf, asem, hsem, ssem, rsem, osem, *refs):
    slots, piece, D = img.shape
    g = Place(S, F, slots)
    images = g.images
    T = slots * piece // images
    R = first.shape[2]
    V = R
    W = D // g.n
    N = g.n * T
    pairs = W // 128
    tokens = Regroup(g, lambda p: img.at[p], lambda q: tok.at[ds(q * piece, piece)], tsem)
    cots = Regroup(g, lambda p: cot.at[p], lambda q: cot_v.at[ds(q * piece, piece)], csem)
    vg = VecGather(g, vec, vec_full, refs[0])

    def own_first(b, cols):
        if isinstance(cols, slice):
            return wq.at[:, pl.ds(b * D, D)]
        return wq.at[:, pl.ds(pl.multiple_of(b * D + cols.start, 128), cols.size)]

    def own_rest(b0):
        def own(b, cols):
            b = b + b0
            ref, r0, c0 = (wd, b * R, 0) if b < 4 else (wu, 0, (b - 4) * D) if b < 6 else (wx, 0, 0)
            if isinstance(cols, slice):
                return ref.at[pl.ds(r0, R), pl.ds(c0, D)]
            return ref.at[pl.ds(r0, R), pl.ds(pl.multiple_of(c0 + cols.start, 128), cols.size)]

        return own

    entry = Gather(g, 3, 0, own_first, first, refs[1:8], lag=ENTRY_LAG)
    thin = Gather(g, 7 - nwide, nwide, own_rest(nwide), rest, refs[8:15], lag=10)
    wide = Gather(g, nwide, 0, own_rest(0), rest, refs[15:22], wide=True)

    g.meet()
    entry.start()
    tokens.start()
    vg.start()
    rows = min(128, piece)
    entry.kept()
    entry.run(0, entry.nitems)
    tokens.arrived()
    keep_tok = pltpu.make_async_copy(tok, tok_out, fsem.at[1])
    keep_tok.start()

    @pl.loop(0, slots * piece // rows)
    def _(r):
        x = fp32(tok[ds(r * rows, rows)])
        x = x - mean_rows(x)
        norm[ds(r * rows, rows)] = x * lax.rsqrt(mean_rows(x * x) + EPSILON)

    vg.finish()
    thin.start()
    wide.start()
    for f in range(F):
        v = fp32(vec_full[f])[:, :V]
        par[:, f * V : (f + 1) * V] = v
        for r in range(2):
            at = (f * 2 + r) * V
            eb[2 * (at // D), :, at % D : at % D + V] = v[2 + r : 3 + r]
        for r in range(4):
            at = (f * 4 + r) * V
            ub[:, at : at + V] = v[8 + r : 9 + r]
    eb[1] = jnp.zeros((1, D), jnp.float32)
    gain, shift = par[0:1], par[1:2]

    @pl.loop(0, slots * piece // rows)
    def _(r):
        x1[ds(r * rows, rows)] = (norm[ds(r * rows, rows)] * gain + shift).astype(x1.dtype)

    entry.run(entry.nitems, entry.steps)
    thin.kept()
    wide.kept()
    cots.start()
    entry.finish_recv()
    keep_first = pltpu.make_async_copy(first, first_out, fsem.at[0])
    keep_first.start()

    def copy(i, k, j):
        src = stage.at[i, k, j]
        dst = heads.at[j, i, ds(g.me * T, T)]
        return remote(src, dst, ssem.at[i, k, j], rsem.at[i, k, j], g.peer(k))

    def local(i, j):
        return pltpu.make_async_copy(stage.at[i, 0, j], heads.at[j, i, ds(g.me * T, T)], ssem.at[i, 0, j])

    def project(i):
        @pl.loop(0, g.n * 3)
        def _(n):
            k = lax.rem(1 + n // 3, g.n)
            j = lax.rem(n, 3)
            cols = ds((g.me ^ k) * W, W)
            w = first[:, j, :, cols].reshape(D, W)
            out = dot(x1[i * T : (i + 1) * T], w) + eb[j, :, cols]
            stage[i, k, j] = out.astype(stage.dtype)

            @pl.when(k != 0)
            def _():
                copy(i, k, j).start()

            @pl.when(k == 0)
            def _():
                local(i, j).start()

    def projected(i):
        for j in range(3):
            local(i, j).wait()
            for k in range(1, g.n):
                copy(i, k, j).wait_send()
                dst = heads.at[j, i, ds((g.me ^ k) * T, T)]
                remote(dst, dst, ssem.at[i, k, j], rsem.at[i, k, j], g.peer(k)).wait_recv()
        keep_heads(i).start()

    def keep_heads(i):
        return pltpu.make_async_copy(heads.at[:, i], heads_out.at[:, i], hsem.at[i])

    def out_copy(i, hp, kk):
        e = i * pairs + hp
        dst = att.at[i, :, pl.ds(pl.multiple_of(g.me * W + hp * 128, 128), 128)]
        if kk == 0:
            return pltpu.make_async_copy(o_buf.at[e, ds(g.me * T, T)], dst, osem.at[0, e, 0])
        return remote(o_buf.at[e, ds((g.me ^ kk) * T, T)], dst, osem.at[0, e, kk], osem.at[1, e, kk], g.peer(kk))

    def attend(i, hp):
        e = i * pairs + hp
        lanes = slice(hp * 128, (hp + 1) * 128)
        vt[...] = heads[2, i, :, lanes].T
        length = length_of(par, *g.image(i), V)
        for hh in range(2):
            kh[hh] = masked_keys(heads[1, i, :, lanes], length, hh)

        @pl.loop(0, N // QB)
        def _(b):
            cols = ds(b * QB, QB)
            qb = heads[0, i, cols, lanes]
            for hh in range(2):
                sc = dot(kh[hh], scaled_queries(qb, hh), NT)
                top = jnp.max(sc, axis=0, keepdims=True)
                ex = jnp.exp(sc - top)
                total = jnp.sum(ex, axis=0, keepdims=True)
                w = (ex * (1.0 / total)).astype(jnp.bfloat16)
                o = dot(vt[hh * HEAD_DIM : (hh + 1) * HEAD_DIM], w).astype(jnp.bfloat16)
                at = hp * 128 + hh * HEAD_DIM
                out_t[i, at : at + HEAD_DIM, cols] = o
                lse[i, hp, hh : hh + 1, cols] = top + jnp.log(total)
            background(e * (N // QB) + b)

        o_buf[e] = out_t[i, lanes].T
        for kk in list(range(1, g.n)) + [0]:
            out_copy(i, hp, kk).start()

    units = [(i, hp) for i in range(images) for hp in range(pairs)]
    early = thin.steps // EARLY
    per_unit = -(-(thin.steps - early) // (len(units) * (N // QB)))

    def background(n):
        @pl.when(n < wide.steps)
        def _():
            wide.step(n)

        for m in range(per_unit):
            thin.step(early + n * per_unit + m)

    for i in range(images):
        project(i)
    thin.run(0, early)
    entry.finish_send()
    for n, (i, hp) in enumerate(units):
        if hp == 0:
            projected(i)
        attend(i, hp)
    wide.run(len(units) * (N // QB), wide.steps)
    cots.arrived()
    keep_cot = pltpu.make_async_copy(cot_v, cot_out, fsem.at[2])
    keep_cot.start()
    for gather in (thin, wide):
        gather.finish_recv()
        gather.finish_send()
    for i, hp in units:
        for kk in range(g.n):
            cp = out_copy(i, hp, kk)
            if kk == 0:
                cp.wait()
            else:
                cp.wait_send()
                cp.wait_recv()
    for i in range(images):
        keep_heads(i).wait()
    keep_tok.wait()
    keep_first.wait()
    tokens.sent()
    cots.sent()
    keep_cot.wait()


ENTRY_LAG = 10
WIDE = 2
EARLY = 10


def front_call(S, F, cid, img, cot, vec, wq, wx, wu, wd):
    slots, piece, D = img.shape
    M = slots * piece
    n, images = (2, 1) if whole_images(S, slots) else (S, slots)
    T = M // images
    R, FF = wq.shape[0], wu.shape[1]
    W, N = D // n, n * T
    pairs = W // 128
    bf, fl = jnp.bfloat16, jnp.float32
    out = jax.ShapeDtypeStruct
    return pl.pallas_call(
        functools.partial(front_kernel, S, F, WIDE, min(256, N)),
        out_shape=[
            out((F, 3, R, D), bf), out((F, 7, R, D), bf), out((16, D), fl), out((1, FF), fl), out((M, D), bf),
            out((3, images, N, W), bf), out((images, W, N), bf), out((images, pairs, 8, N), fl), out((images, T, D), bf), out((M, D), bf), out((M, D), bf),
        ],
        in_specs=[ANY] * 7,
        out_specs=[ANY, ANY, VM, VM, VM, ANY, VM, VM, ANY, ANY, ANY],
        scratch_shapes=[
            pltpu.VMEM((F, 3, R, D), bf), pltpu.VMEM((M, D), bf), pltpu.VMEM((M, D), bf), DMA((3,)), DMA((2, slots)), DMA((2, slots)),
            pltpu.VMEM((F, 16, 128), bf), pltpu.VMEM((M, D), fl), pltpu.VMEM((3, 1, D), fl), pltpu.VMEM((images, n, 3, T, W), bf),
            pltpu.VMEM((3, images, N, W), bf), pltpu.VMEM((2, N, 128), bf), pltpu.VMEM((128, N), bf),
            pltpu.VMEM((images * pairs, N, 128), bf), DMA((1,)), DMA((images,)), DMA((images, n, 3)), DMA((images, n, 3)),
            DMA((2, images * pairs, n)),
        ]
        + VecGather.scratch(F)
        + Gather.scratch(S, F, 3, R, D, bounce=False)
        + Gather.scratch(S, F, 7 - WIDE, R, D)
        + Gather.scratch(S, F, WIDE, R, D),
        compiler_params=pltpu.CompilerParams(collective_id=cid, **PARAMS),
        name="front",
    )(img, cot, vec, wq, wx, wu, wd)


def rear_kernel(S, F, QB, held, tok, cot, att, par, ub, wu_own, wts, heads, out_t, lse, x1, first,
                layer_out, dx_out, small, part_down, part_a, part_b, g_down, g_up, g_first, back, late,
                layer, dx, msem, cots, vecs, ubg, slab, csem, esem, wsem, psem, hsem, *refs):
    slots, piece, D = layer_out.shape
    g = Place(S, F, slots)
    images = g.images
    M = slots * piece
    T = M // images
    W = D // g.n
    N = g.n * T
    pairs = W // 128
    R = wts.shape[2]
    H = ub.shape[2]
    rows = min(128, piece)
    nrows = M // rows
    exit_bias, scale1, gain2, shift2 = par[4:5], par[5:6], par[6:7], par[7:8]
    down_bias, scale2 = par[12:13], par[13:14]
    per_block = D // H
    bf, fl = jnp.bfloat16, jnp.float32
    down_sum = Scatter(g, part_down, g_down, refs[:16], per=4, lag=LAG, above=True)
    up_a = Scatter(g, part_a, g_up.at[:, pl.ds(0, 2 * D)], refs[16:32], wide=True, lag=4, tail=UP_TAIL)
    up_b = Scatter(g, part_b, g_up.at[:, pl.ds(2 * D, 2 * D)], refs[32:48], lag=LAG)
    vsum = VecSum(g, slab, small, refs[64:68])

    def own_late(b, cols):
        if isinstance(cols, slice):
            return wu_own.at[:, pl.ds((2 + b) * D, D)]
        return wu_own.at[:, pl.ds(pl.multiple_of((2 + b) * D + cols.start, 128), cols.size)]

    more = Gather(g, 2, 0, own_late, late, refs[68:75])
    units = images * pairs
    part_of = lambda ref: lambda p: ref.at[ds(p * piece, piece)]
    layers = Regroup(g, part_of(layer), lambda q: layer_out.at[q], msem.at[1], back=True)
    chunks = F // 4

    def place(r):
        return r // (T // rows), lax.rem(r, T // rows) * rows

    def mask(r):
        i, t = place(r)
        group, slot = g.image(i)
        limit = jnp.where(slot < held[group], length_of(par, group, slot, R), 0.0)
        pos = lax.broadcasted_iota(jnp.int32, (rows, 1), 0) + (g.me * T + t)
        return jnp.where(fp32(pos) < limit, 1.0, 0.0)

    def upstream(r):
        return mask(r) * fp32(cot[ds(r * rows, rows)])

    def cot_copies(stage, k):
        for i in range(images):
            src, dst = stage.at[pl.ds(i * T, T), pl.ds(k * W, W)], cots.at[i, ds(g.me * T, T)]
            if k == 0:
                yield pltpu.make_async_copy(src, dst, csem.at[0, 0])
            else:
                yield remote(src, dst, csem.at[0, k], csem.at[1, k], g.peer(k))

    def feed_forward(mixed, x2, x2t, dcot, down, cot2, wu, wd, wx, dwu, dwd):
        def up_load(j):
            cols = pl.ds(pl.multiple_of(lax.rem(j, per_block) * H, H), H)
            slot = lax.rem(j, 2)
            block = j // per_block
            soon = pltpu.make_async_copy(wts.at[:, 4 + jnp.minimum(block, 1), :, cols], wu.at[slot], wsem.at[0, slot])
            return soon, pltpu.make_async_copy(late.at[:, jnp.maximum(block - 2, 0), :, cols], wu.at[slot], wsem.at[0, slot])

        def start_either(j, copies):
            soon, later = copies

            @pl.when(j < F // 2)
            def _():
                soon.start()

            @pl.when(j >= F // 2)
            def _():
                later.start()

        def down_load(j):
            return pltpu.make_async_copy(wts.at[j, pl.ds(0, 4)], wd.at[lax.rem(j, 2)], wsem.at[1, lax.rem(j, 2)])

        def put_up(j):
            cols = pl.ds(pl.multiple_of(lax.rem(j, per_block) * H, H), H)
            block = j // per_block
            soon = pltpu.make_async_copy(dwu, part_a.at[:, jnp.minimum(block, 1), :, cols], psem.at[0])
            return soon, pltpu.make_async_copy(dwu, part_b.at[:, jnp.maximum(block - 2, 0), :, cols], psem.at[0])

        def put_down(j):
            return pltpu.make_async_copy(dwd, part_down.at[j, pl.ds(0, 4)], psem.at[1])

        x_load = pltpu.make_async_copy(wts.at[:, 6], wx, wsem.at[2, 0])
        x_load.start()
        start_either(0, up_load(0))
        down_load(0).start()
        x_load.wait()
        mixed[...] = dot(att[...], wx[...].reshape(D, D)) + exit_bias

        def residual(r, sl):
            return fp32(tok[sl]) + scale1 * mixed[sl]

        hello()
        more.start()

        def norm(res):
            res = res - mean_rows(res)
            inv = lax.rsqrt(mean_rows(res * res) + EPSILON)
            return res * inv, inv

        @pl.loop(0, nrows)
        def _(r):
            sl = ds(r * rows, rows)
            n, _ = norm(residual(r, sl))
            x2[sl] = (n * gain2 + shift2).astype(bf)
            dcot[sl] = (upstream(r) * scale2).astype(bf)

        x2t[...] = x2[...].T
        more.kept()
        down[...] = jnp.zeros_like(down)
        cot2[...] = jnp.zeros_like(cot2)

        @pl.loop(0, F)
        def _(j):
            slot = lax.rem(j, 2)
            every = -(-more.steps // (F // 2 - 1))

            @pl.when(j < F // 2 - 1)
            def _():
                more.run(j * every, (j + 1) * every)

            @pl.when(j == F // 2 - 1)
            def _():
                more.finish_recv()

            @pl.when(j + 1 < F)
            def _():
                start_either(j + 1, up_load(j + 1))
                down_load(j + 1).start()

            up_load(j)[0].wait()
            down_load(j).wait()
            wu_j = wu[slot].reshape(D, H)
            wd_j = wd[slot].reshape(H, D)
            pre = dot(x2[...], wu_j) + ub[j]
            cumul = 0.5 * (1.0 + lax.erf(pre * (1.0 / math.sqrt(2.0))))
            density = jnp.exp(-0.5 * pre * pre) * (1.0 / math.sqrt(2.0 * math.pi))
            act = (pre * cumul).astype(bf)
            slope = cumul + pre * density
            pre_cot = dot(dcot[...], wd_j, NT) * slope
            ubg[j] = jnp.sum(pre_cot, axis=0, keepdims=True)
            low = pre_cot.astype(bf)
            @pl.when(j > 0)
            def _():
                put_up(j - 1)[0].wait()
                put_down(j - 1).wait()

            @pl.when((j > 0) & (lax.rem(j, chunks) == 0))
            def _():
                n = (j // chunks - 1) * g.Z
                @pl.when(j <= 2 * chunks)
                def _():
                    up_a.ready(n, n + g.Z)

                @pl.when(j > 2 * chunks)
                def _():
                    up_b.ready(n - 2 * g.Z, n - g.Z)

                down_sum.ready(n, n + g.Z)

            dwu[...] = dot(x2t[...], low).astype(bf).reshape(F, R, H)
            dwd[...] = dot(act, dcot[...], TN).astype(bf).reshape(4, R, D)
            start_either(j, put_up(j))
            put_down(j).start()
            down[...] += dot(act, wd_j)
            cot2[...] += dot(low, wu_j, NT)

            @pl.when((j > 0) & (lax.rem(j, chunks) == 1))
            def _():
                first = (j // chunks - 1) * g.Z

                @pl.when(first >= 0)
                def _():
                    @pl.when(first < 2 * g.Z)
                    def _():
                        up_a.run(first, first + g.Z)

                    @pl.when(first >= 2 * g.Z)
                    def _():
                        up_a.run(first, first + g.Z)
                        up_b.run(first - 2 * g.Z, first - g.Z)

                    down_sum.run(first, first + g.Z)

        put_up(F - 1)[0].wait()
        put_down(F - 1).wait()
        n = 3 * g.Z
        up_b.ready(n - 2 * g.Z, n - g.Z)
        down_sum.ready(n, n + g.Z)
        vecs[...] = jnp.zeros_like(vecs)

        @pl.loop(0, nrows)
        def _(r):
            sl = ds(r * rows, rows)
            m = mask(r)
            up = upstream(r)
            out = down[sl] + down_bias
            res = residual(r, sl)
            layer[sl] = (m * (res + scale2 * out)).astype(bf)
            n, inv = norm(res)
            c2 = cot2[sl]
            c = c2 * gain2
            rc = up + inv * (c - mean_rows(c) - n * mean_rows(c * n))
            dx[sl] = rc
            mc = rc * scale1
            x2[sl] = mc.astype(bf)
            total = lambda v: jnp.sum(v, axis=0, keepdims=True)
            vecs[0:1] += total(up * out)
            vecs[1:2] += total(up * scale2)
            vecs[2:3] += total(c2 * n)
            vecs[3:4] += total(c2)
            vecs[4:5] += total(rc * mixed[sl])
            vecs[5:6] += total(mc)

        for k in list(range(1, g.n)) + [0]:
            dcot[:, k * W : (k + 1) * W] = dot(x2[...], wx_rows(wx, g.me ^ k, W), NT).astype(bf)
            for cp in cot_copies(dcot, k):
                cp.start()
        for n in range(F // 4):
            at = n * 4 * R
            dwd[...] = dot(att[:, at : at + 4 * R], x2[...], TN).astype(bf).reshape(4, R, D)
            put_x = pltpu.make_async_copy(dwd, part_down.at[pl.ds(n * 4, 4), 4], psem.at[2])
            put_x.start()
            put_x.wait()
        down_sum.ready(4 * g.Z, 5 * g.Z)
        layers.start()
        for cp in cot_copies(dcot, 0):
            cp.wait()
        ref = dcot.at[:, pl.ds(0, W)]
        for k in range(1, g.n):
            remote(ref, ref, csem.at[0, k], csem.at[1, k], g.mate).wait_send()

    polls = units * (N // QB)

    def background(n):
        t = 3 * g.Z + n // EVERY

        @pl.when(lax.rem(n, EVERY) == 0)
        def _():
            step_all(t)

    def step_all(t):
        up_a.step(t)
        up_b.step(t - 2 * g.Z)
        down_sum.step(t)

    def attend_back(hd, ot, ls, kh, vh, kt, cot_t, delta, dq_t, dk, dv, stage):
        loads = [pltpu.make_async_copy(a, b, hsem.at[n]) for n, (a, b) in enumerate(((heads, hd), (out_t, ot), (lse, ls)))]
        for cp in loads:
            cp.start()
        for k in range(1, g.n):
            ref = cots.at[:, ds((g.me ^ k) * T, T)]
            remote(ref, ref, csem.at[0, k], csem.at[1, k], g.peer(k)).wait_recv()
        for cp in loads:
            cp.wait()

        def copy(e, j, kk):
            i, hp = e // pairs, lax.rem(e, pairs)
            dst = back.at[i, :, ds(j * D + g.me * W + hp * 128, 128)]
            src = stage.at[e, j, ds((g.me ^ kk) * T, T)]
            if kk == 0:
                return pltpu.make_async_copy(src, dst, esem.at[2])
            return remote(src, dst, esem.at[0], esem.at[1], g.peer(kk))

        @pl.loop(0, units)
        def _(e):
            i, hp = e // pairs, lax.rem(e, pairs)
            lanes = ds(hp * 128, 128)
            length = length_of(par, *g.image(i), R)
            kt[...] = hd[1, i, :, lanes].T
            cot_t[...] = cots[i, :, lanes].T
            prod = fp32(cot_t[...]) * fp32(ot[i, lanes])
            for hh in range(2):
                hs = slice(hh * HEAD_DIM, (hh + 1) * HEAD_DIM)
                delta[hh : hh + 1] = jnp.sum(prod[hs], axis=0, keepdims=True)
                kh[hh] = masked_keys(hd[1, i, :, lanes], length, hh)
                mine, _ = head_lanes(N, hh)
                vh[hh] = jnp.where(mine, fp32(hd[2, i, :, lanes]), 0.0).astype(bf)
            dk[...] = jnp.zeros_like(dk)
            dv[...] = jnp.zeros_like(dv)

            @pl.loop(0, N // QB)
            def _(b):
                cols = ds(b * QB, QB)
                qb, cb = hd[0, i, cols, lanes], cots[i, cols, lanes]
                for hh in range(2):
                    hs = slice(hh * HEAD_DIM, (hh + 1) * HEAD_DIM)
                    mine, _ = head_lanes(QB, hh)
                    qs = scaled_queries(qb, hh)
                    prob = jnp.exp(dot(kh[hh], qs, NT) - ls[i, hp, hh : hh + 1, cols])
                    sg = dot(vh[hh], cb, NT)
                    sc = (prob * (sg - delta[hh : hh + 1, cols])).astype(bf)
                    w = prob.astype(bf)
                    dv[...] += dot(w, jnp.where(mine, fp32(cb), 0.0).astype(bf))
                    dk[...] += dot(sc, jnp.where(mine, fp32(qs), 0.0).astype(bf))
                    dq_t[hs, cols] = (dot(kt[hs], sc) * HEAD_DIM ** (-0.5)).astype(bf)
                background(e * (N // QB) + b)

            stage[e, 0] = dq_t[...].T
            stage[e, 1] = dk[...].astype(bf)
            stage[e, 2] = dv[...].astype(bf)
            for j in range(3):
                for kk in list(range(1, g.n)) + [0]:
                    copy(e, j, kk).start()

        ref = stage.at[:, :, pl.ds(0, (g.n - 1) * T)]
        cp = remote(ref, ref, esem.at[0], esem.at[1], g.mate)
        cp.wait_send()
        cp.wait_recv()
        ref = stage.at[:, :, pl.ds(0, T)]
        pltpu.make_async_copy(ref, ref, esem.at[2]).wait()

    def entry(part, ein, win, x1v, x1t, acc, rows_v, dxl):
        grads = Regroup(g, part_of(dxl), lambda q: dx_out.at[q], msem.at[2], back=True)
        entry_sum = Scatter(g, part, g_first, refs[48:64])
        loads = [pltpu.make_async_copy(back.at[:, :, pl.ds(j * D, D)], ein.at[j], hsem.at[j]) for j in range(3)]
        weights = [pltpu.make_async_copy(first.at[:, j], win.at[j % 2], wsem.at[2, j % 2]) for j in range(3)]
        x_load = pltpu.make_async_copy(x1, x1v, wsem.at[0, 0])
        for cp in [x_load] + loads + weights[:2]:
            cp.start()
        x_load.wait()
        x1t[...] = x1v[...].T
        at = 3 * g.Z + polls // EVERY

        def others(n, k):
            for t in range(at + n, at + n + k):
                step_all(t)

        rows_v[...] = jnp.zeros_like(rows_v)
        cot_of = lambda j: ein[j].reshape(M, D)
        for j in range(3):
            loads[j].wait()
            part[:, j] = dot(x1t[...], cot_of(j)).astype(bf).reshape(F, R, D)
            if j:
                entry_sum.run((j - 1) * g.Z, j * g.Z)
            entry_sum.ready(j * g.Z, (j + 1) * g.Z)
            others(2 * j, 2)
        for j in range(3):
            weights[j].wait()
            d = dot(cot_of(j), win[j % 2].reshape(D, D), NT)
            if j == 0:
                weights[2].start()
                acc[...] = d
            else:
                acc[...] += d
            others(6 + 2 * j, 2)
            entry_sum.run(2 * g.Z + j, 2 * g.Z + j + 1)
        rows_v[2:3] = jnp.sum(fp32(cot_of(0)), axis=0, keepdims=True)
        rows_v[3:4] = jnp.sum(fp32(cot_of(2)), axis=0, keepdims=True)
        gain = par[0:1]

        @pl.loop(0, nrows)
        def _(r):
            sl = ds(r * rows, rows)
            x = fp32(tok[sl])
            x = x - mean_rows(x)
            inv = lax.rsqrt(mean_rows(x * x) + EPSILON)
            n = x * inv
            d1 = acc[sl]
            c = d1 * gain
            dxl[sl] = (dx[sl] + inv * (c - mean_rows(c) - n * mean_rows(c * n))).astype(bf)
            rows_v[0:1] += jnp.sum(d1 * n, axis=0, keepdims=True)
            rows_v[1:2] += jnp.sum(d1, axis=0, keepdims=True)
            entry_sum.step(2 * g.Z + 3 + r)

        grads.start()
        slab[...] = jnp.zeros_like(slab)
        own = [(0, rows_v, 0), (1, rows_v, 1), (4, vecs, 5), (5, vecs, 4), (6, vecs, 2), (7, vecs, 3), (12, vecs, 1), (13, vecs, 0)]
        V = R
        for f in range(F):
            for to, src, r in own:
                slab[f, to : to + 1, :V] = src[r : r + 1, f * V : (f + 1) * V]
            for r in range(2):
                p = (f * 2 + r) * V
                slab[f, 2 + r : 3 + r, :V] = rows_v[2 + p // D : 3 + p // D, p % D : p % D + V]
            for r in range(4):
                slab[f, 8 + r : 9 + r, :V] = ubg[f, :, r * V : (r + 1) * V]
        vsum.start()
        mark = 2 * g.Z + 3 + nrows
        entry_sum.run(mark, mark + 4)
        vsum.middle()
        left = max(down_sum.steps, up_a.steps, up_b.steps + 2 * g.Z) - (at + 12)

        @pl.loop(0, max(left, entry_sum.steps - mark - 4))
        def _(t):
            step_all(at + 12 + t)
            entry_sum.step(mark + 4 + t)

        entry_sum.finish()
        grads.arrived()
        grads.sent()

    hello = g.greet()
    v = pltpu.VMEM
    pl.run_scoped(
        feed_forward, v((M, D), fl), v((M, D), bf), v((D, M), bf), v((M, D), bf), v((M, D), fl), v((M, D), fl),
        v((2, F, R, H), bf), v((2, 4, R, D), bf), v((F, R, D), bf), v((F, R, H), bf), v((4, R, D), bf),
    )
    pl.run_scoped(
        attend_back, v((3, images, N, W), bf), v((images, W, N), bf), v((images, pairs, 8, N), fl), v((2, N, 128), bf),
        v((2, N, 128), bf), v((128, N), bf), v((128, N), bf), v((8, N), fl), v((128, N), bf), v((N, 128), fl),
        v((N, 128), fl), v((units, 3, N, 128), bf),
    )
    pl.run_scoped(
        entry, v((F, 3, R, D), bf), v((3, images, T, D), bf), v((2, F, R, D), bf), v((M, D), bf), v((D, M), bf),
        v((M, D), fl), v((8, D), fl), v((M, D), bf),
    )
    up_a.finish()
    up_b.finish()
    down_sum.finish()
    vsum.finish()
    more.finish_send()
    layers.arrived()
    layers.sent()


def wx_rows(wx, peer, W):
    F, R, D = wx.shape
    n = W // R
    return wx[pl.ds(peer * n, n)].reshape(W, D)


LAG = 4
UP_TAIL = 13
EVERY = 2


def rear_call(S, F, cid, slots, held, tok, cot, att, par, ub, wu_own, wts, heads, out_t, lse, x1, first):
    M, D = cot.shape
    piece = M // slots
    n, images = (2, 1) if whole_images(S, slots) else (S, slots)
    T = M // images
    R = wts.shape[2]
    FF = ub.shape[1]
    H = FF // F
    W, N = D // n, n * T
    bf, fl = jnp.bfloat16, jnp.float32
    SM = pl.BlockSpec(memory_space=pltpu.SMEM)
    out, v = jax.ShapeDtypeStruct, pltpu.VMEM
    return pl.pallas_call(
        functools.partial(rear_kernel, S, F, min(256, N)),
        out_shape=[
            out((slots, piece, D), bf), out((slots, piece, D), bf), out((16, 128), fl), out((F, 5, R, D), bf), out((F, 2, R, D), bf), out((F, 2, R, D), bf),
            out((5 * R, D), bf), out((R, 4 * D), bf), out((R, 3 * D), bf), out((images, T, 3 * D), bf), out((F, 2, R, D), bf),
        ],
        in_specs=[SM, VM, VM, VM, VM, VM] + [ANY] * 7,
        out_specs=[ANY, ANY, VM] + [ANY] * 8,
        scratch_shapes=[v((M, D), bf), v((M, D), fl), DMA((3, 2, slots)), v((images, N, W), bf), v((8, D), fl), v((F, 1, H), fl), v((F, 16, 128), fl),
                        DMA((2, n)), DMA((3,)), DMA((3, 2)), DMA((3,)), DMA((3,))]
        + Scatter.scratch(S, F, 5, R, D, K=F)
        + Scatter.scratch(S, F, 2, R, D, wide=True, K=F // 2)
        + Scatter.scratch(S, F, 2, R, D, K=F // 2)
        + Scatter.scratch(S, F, 3, R, D, K=F // 2)
        + VecSum.scratch(S, F, 16, 128)
        + Gather.scratch(S, F, 2, R, D),
        compiler_params=pltpu.CompilerParams(collective_id=cid, **PARAMS),
        name="rear",
    )(held, tok, cot, att, par, ub.reshape(F, 1, H), wu_own, wts, heads, out_t, lse, x1, first)


def body(S, F, images, out_grad, lengths, images_held, first_gain, first_shift, entry_weight, entry_bias, exit_weight,
         exit_bias, first_scale, second_gain, second_shift, up_weight, up_bias, down_weight, down_bias, second_scale):
    slots, T, D = images.shape
    M = slots * T
    R = entry_weight.shape[0]
    FF = up_weight.shape[1]
    fl = jnp.float32
    V = R
    rows = [first_gain, first_shift, entry_bias, exit_bias, first_scale, second_gain, second_shift, up_bias, down_bias, second_scale]
    own_vec, at = jnp.zeros((16, 128), jnp.bfloat16), 0
    for v in rows:
        n = v.shape[0] // V
        own_vec = own_vec + jnp.pad(v.reshape(n, V), ((at, 16 - at - n), (0, 128 - V)))
        at += n
    for v in (lengths // 32, lengths % 32):
        own_vec = own_vec + jnp.pad(v.astype(jnp.bfloat16).reshape(1, slots), ((at, 15 - at), (0, 128 - slots)))
        at += 1
    first, rest, par, ub, x1, heads, out_t, lse, att, tok, cot = front_call(
        S, F, 0, images, out_grad, own_vec, entry_weight, exit_weight, up_weight, down_weight
    )
    layer, dx, small, _, _, _, g_down, g_up, g_first, _, _ = rear_call(
        S, F, 1, slots, images_held, tok, cot, att.reshape(M, D), par, ub, up_weight, rest, heads, out_t, lse, x1, first
    )
    vectors = [v.shape[0] for v in rows]
    down, exit_, up, first, dx, layer, *small = results_call(V, g_down, g_up, g_first, dx, layer, small, vectors)
    return (
        layer.reshape(slots, T, D), dx.reshape(slots, T, D), small[0], small[1], first, small[2], exit_, small[3], small[4],
        small[5], small[6], up, small[7], down, small[8], small[9],
    )


def results_kernel(V, down, out, up, first, dx, layer, small, *outs):
    for src, dst in zip((down, out, up, first, dx, layer), outs):
        dst[...] = src[...].astype(dst.dtype)

    @pl.when(pl.program_id(0) == 0)
    def _():
        at = 0
        for dst in outs[6:]:
            n = dst.shape[0] // V
            for r in range(n):
                dst[r * V : (r + 1) * V] = small[at + r, :V]
            at += n


def results_call(V, g_down, g_up, g_first, dx, layer, small, vectors):
    slots, T, D = dx.shape
    R = g_up.shape[0]
    steps = 4
    fl = jnp.float32
    out = jax.ShapeDtypeStruct
    q = R // steps
    t = slots * T // steps
    row = lambda n, width, first=0: pl.BlockSpec((n, width), lambda i: (first + i, 0))
    whole = lambda *shape: pl.BlockSpec(shape, lambda i: (0,) * len(shape))
    tokens = (slots * T, D)
    res = pl.pallas_call(
        functools.partial(results_kernel, V),
        grid=(steps,),
        out_shape=[out((4 * R, D), fl), out((R, D), fl), out(g_up.shape, fl), out(g_first.shape, fl), out(tokens, fl),
                   out(tokens, layer.dtype)] + [out((n,), fl) for n in vectors],
        in_specs=[row(R, D), row(q, D, 4 * steps), row(q, 4 * D), row(q, 3 * D), row(t, D), row(t, D), whole(16, 128)],
        out_specs=[row(R, D), row(q, D), row(q, 4 * D), row(q, 3 * D), row(t, D), row(t, D)] + [whole(n) for n in vectors],
        compiler_params=pltpu.CompilerParams(vmem_limit_bytes=62 * 2**20),
        name="results",
    )(g_down, g_down, g_up, g_first, dx.reshape(tokens), layer.reshape(tokens), small)
    return res


def solution(mesh):
    S, F = mesh.shape["seq"], mesh.shape["fsdp"]
    vector, matrix, tokens = P("fsdp"), P("fsdp", None), P("fsdp", "seq", None)
    return jax.shard_map(
        functools.partial(body, S, F),
        mesh=mesh,
        in_specs=(tokens, tokens, vector, P(), vector, vector, matrix, vector, matrix, vector, vector, vector, vector,
                  matrix, vector, matrix, vector, vector),
        out_specs=(tokens, tokens, vector, vector, matrix, vector, matrix, vector, vector, vector, vector, matrix, vector,
                   matrix, vector, vector),
        check_vma=False,
    )
```

```python
import functools
import math

import jax
import jax.numpy as jnp
from jax import lax
from jax.experimental import pallas as pl
from jax.experimental.pallas import tpu as pltpu
from jax.sharding import PartitionSpec as P

HEAD_DIM = 64
EPSILON = 1e-06
NEG_LARGE = -1e30

MESH = pl.DeviceIdType.MESH
DMA = pltpu.SemaphoreType.DMA
ANY = pl.BlockSpec(memory_space=pl.ANY)
VM = pl.BlockSpec(memory_space=pltpu.VMEM)


def remote(src, dst, ssem, rsem, dev):
    return pltpu.make_async_remote_copy(
        src_ref=src, dst_ref=dst, send_sem=ssem, recv_sem=rsem, device_id=dev, device_id_type=MESH
    )


class Place:
    def __init__(self, S, F, slots):
        self.S, self.F, self.Z, self.slots = S, F, F // 2, slots
        self.bits = [1 << b for b in range(S.bit_length() - 1)]
        self.nbits = len(self.bits)
        self.order = [self.bits, self.bits[1:] + self.bits[:1]]
        self.s = lax.axis_index("seq")
        self.f = lax.axis_index("fsdp")
        self.z, self.c = self.f // 2, lax.rem(self.f, 2)
        self.mate = (self.s, self.f ^ 1)
        self.regroup = whole_images(S, slots)
        self.n = 2 if self.regroup else S
        self.me = self.c if self.regroup else self.s
        self.images = 1 if self.regroup else slots

    def at(self, zz):
        return (self.s, zz * 2 + self.c)

    def peer(self, k):
        return (self.s, self.f ^ k) if self.regroup else (self.s ^ k, self.f)

    def image(self, i):
        if self.regroup:
            return self.z * 2 + self.s // self.slots, lax.rem(self.s, self.slots)
        return self.f, i

    def goes(self, i):
        if not self.regroup:
            return self.mate, i, True
        to, core = self.c * self.slots + i, self.s // self.slots
        return (to, self.z * 2 + core), lax.rem(self.s, self.slots), (to == self.s) & (core == self.c)

    def came(self, r):
        if not self.regroup:
            return self.mate, r, True
        of, core = self.c * self.slots + r, self.s // self.slots
        return (of, self.z * 2 + core), lax.rem(self.s, self.slots), (of == self.s) & (core == self.c)

    def greet(self):
        bar = pltpu.get_barrier_semaphore()
        for k in range(1, self.F):
            pl.semaphore_signal(bar, inc=1, device_id=(self.s, lax.rem(self.f + k, self.F)), device_id_type=MESH)
        for k in range(1, self.S):
            for core in range(2 if self.regroup else 1):
                pl.semaphore_signal(bar, inc=1, device_id=(self.s ^ k, self.f ^ core), device_id_type=MESH)
        return lambda: pl.semaphore_wait(bar, self.F - 1 + (self.S - 1) * (2 if self.regroup else 1))

    def meet(self):
        self.greet()()


def whole_images(S, slots):
    return S == 2 * slots


class Regroup:
    def __init__(self, g, src, dst, sems, back=False):
        self.g, self.src, self.dst, self.sems = g, src, dst, sems
        self.out, self.into = (g.came, g.goes) if back else (g.goes, g.came)

    @staticmethod
    def scratch(slots):
        return [DMA((2, slots))]

    def each(self, way, local, remote_part):
        for p in range(self.g.slots):
            device, q, here = way(p)
            if here is True:
                local(p, q)
            else:
                pl.when(here)(lambda p=p, q=q: local(p, q))
                pl.when(jnp.logical_not(here))(lambda p=p, q=q, device=device: remote_part(p, q, device))

    def start(self):
        def local(p, q):
            pltpu.make_async_copy(self.src(p), self.dst(q), self.sems.at[0, p]).start()

        def away(p, q, device):
            remote(self.src(p), self.dst(q), self.sems.at[0, p], self.sems.at[1, q], device).start()

        self.each(self.out, local, away)

    def arrived(self):
        def away(p, q, device):
            remote(self.dst(p), self.dst(p), self.sems.at[0, p], self.sems.at[1, p], device).wait_recv()

        self.each(self.into, lambda p, q: None, away)

        def local(p, q):
            pltpu.make_async_copy(self.src(p), self.dst(q), self.sems.at[0, p]).wait()

        self.each(self.out, local, lambda p, q, device: None)

    def sent(self):
        def away(p, q, device):
            remote(self.src(p), self.dst(p), self.sems.at[0, p], self.sems.at[1, p], device).wait_send()

        self.each(self.out, lambda p, q: None, away)


def span(bits):
    out = [0]
    for b in bits:
        out = out + [m | b for m in out]
    return out


def ds(start, size):
    return pl.ds(pl.multiple_of(start, size), size)


class Gather:
    def __init__(self, g, NB, b0, own, full, refs, wide=False, lag=8):
        self.g, self.NB, self.b0, self.own, self.full, self.lag = g, NB, b0, own, full, lag
        self.bounce, self.zs, self.zr, self.xs, self.xr, self.ms, self.ls = refs
        self.R, self.D = full.shape[2:]
        self.C = self.D if wide else self.D // g.S
        self.nbits = 0 if wide else g.nbits
        self.mine = 0 if wide else g.s
        self.nitems = (g.Z - 1) * NB * 2
        self.steps = self.nitems + lag * self.nbits

    @staticmethod
    def scratch(S, F, NB, R, D, bounce=True):
        Z, nb = F // 2, S.bit_length() - 1
        return [pltpu.VMEM((NB if bounce else 1, R, D), jnp.bfloat16), DMA((2,)), DMA((NB, Z)), DMA((nb,)),
                DMA((NB, Z, nb)), DMA((2,)), DMA((1,))]

    def cols(self, q):
        return ds(q * self.C, self.C)

    def half(self, p):
        return pl.ds(p * (self.R // 2), self.R // 2)

    def block(self, f, b):
        return self.full.at[f, self.b0 + b]

    def zfull(self, b, zz):
        return self.full.at[zz * 2 + self.g.c, self.b0 + b, :, self.cols(self.mine)]

    def zcopy(self, src, b, zz, way, to):
        return remote(src, self.zfull(b, zz), self.zs.at[way], self.zr.at[b, zz], self.g.at(to))

    def mate_copy(self, src, b, zz):
        return remote(src, self.block(zz * 2 + self.g.c, b), self.ms.at[0], self.ms.at[1], self.g.mate)

    def keeps(self):
        direct = self.bounce.shape[0] < self.NB
        for b in range(self.NB):
            dst = self.block(self.g.f, b) if direct else self.bounce.at[b]
            yield pltpu.make_async_copy(self.own(b, slice(None)), dst, self.ls.at[0])

    def stored(self):
        return pltpu.make_async_copy(self.bounce, self.full.at[self.g.f, pl.ds(self.b0, self.NB)], self.ls.at[0])

    def start(self):
        g = self.g
        for b in range(self.NB):
            piece = self.own(b, self.cols(self.mine))

            @pl.when(g.z < g.Z - 1)
            def _():
                self.zcopy(piece, b, g.z, 0, g.z + 1).start()

            @pl.when(g.z > 0)
            def _():
                self.zcopy(piece, b, g.z, 1, g.z - 1).start()

        for cp in self.keeps():
            cp.start()
        for b in range(self.NB):
            self.mate_copy(self.own(b, slice(None)), b, g.z).start()

    def kept(self):
        blocks = self.full.at[self.g.f, pl.ds(self.b0, self.NB)]
        pltpu.make_async_copy(blocks, blocks, self.ls.at[0]).wait()
        if self.bounce.shape[0] == self.NB:
            self.stored().start()

    def xcopies(self, b, zz, p, j):
        g = self.g
        to = (g.s ^ g.order[p][j], g.f)
        out = []
        for m in span(g.order[p][:j]):
            ref = self.full.at[zz * 2 + g.c, self.b0 + b, self.half(p), self.cols(g.s ^ m)]
            out.append(remote(ref, ref, self.xs.at[j], self.xr.at[b, zz, j], to))
        return out

    def doubled(self, b, zz, j):
        ref = self.full.at[zz * 2 + self.g.c, self.b0 + b, :, pl.ds(0, self.C << j)]
        return remote(ref, ref, self.xs.at[j], self.xr.at[b, zz, j], self.g.mate)

    def item(self, t):
        g = self.g
        h = 1 + t // (2 * self.NB)
        r = lax.rem(t, 2 * self.NB)
        b, below = r // 2, lax.rem(r, 2) == 0
        zz = jnp.where(below, g.z - h, g.z + h)
        ok = (t >= 0) & (t < self.nitems) & (zz >= 0) & (zz < g.Z)
        nxt = jnp.where(below, g.z + 1, g.z - 1)
        more = (nxt >= 0) & (nxt < g.Z)
        way = jnp.where(below, 0, 1)
        return b, zz, ok, nxt, more, way

    def step(self, t):
        g = self.g
        for j in reversed(range(self.nbits + 1)):
            b, zz, ok, nxt, more, way = self.item(t - self.lag * j)

            @pl.when(ok)
            def _(j=j, b=b, zz=zz, nxt=nxt, more=more, way=way):
                if j == 0:
                    piece = self.zfull(b, zz)
                    self.zcopy(piece, b, zz, 0, g.z).wait_recv()

                    @pl.when(more)
                    def _():
                        self.zcopy(piece, b, zz, way, nxt).start()
                else:
                    self.doubled(b, zz, j - 1).wait_recv()
                if j < self.nbits:
                    for p in range(2):
                        for cp in self.xcopies(b, zz, p, j):
                            cp.start()
                else:
                    self.mate_copy(self.block(zz * 2 + g.c, b), b, zz).start()

    def run(self, lo, hi):
        @pl.loop(lo, hi)
        def _(t):
            self.step(t)

    def part(self, chips, cols):
        ref = self.full.at[pl.ds(0, chips), pl.ds(self.b0, self.NB), :, pl.ds(0, cols)]
        return ref

    def finish_recv(self):
        if self.bounce.shape[0] == self.NB:
            self.stored().wait()
        ref = self.part(self.g.Z, self.D)
        remote(ref, ref, self.ms.at[0], self.ms.at[1], self.g.mate).wait_recv()

    def finish_send(self):
        g = self.g
        ref = self.part(g.Z, self.D)
        remote(ref, ref, self.ms.at[0], self.ms.at[1], g.mate).wait_send()
        for j in range(self.nbits):
            ref = self.part(g.Z - 1, self.C << j)
            remote(ref, ref, self.xs.at[j], self.xr.at[0, 0, j], g.mate).wait_send()
        for zz in range(g.Z):

            @pl.when(g.z == zz)
            def _(zz=zz):
                for way, n in ((0, zz + 1 if zz < g.Z - 1 else 0), (1, g.Z - zz if zz > 0 else 0)):
                    if n:
                        ref = self.part(n, self.C)
                        remote(ref, ref, self.zs.at[way], self.zr.at[0, 0], g.mate).wait_send()


class Scatter:
    def __init__(self, g, part, out, refs, per=0, wide=False, lag=4, tail=0, above=False):
        self.g, self.part, self.out, self.per, self.wide, self.lag, self.above = g, part, out, per, wide, lag, above
        self.core, self.ring, self.xb, self.zb, self.fq = refs[:5]
        self.own, self.c_s, self.c_r, self.x_s, self.x_r, self.z_s, self.z_r, self.a_s, self.a_r, self.o, self.free = refs[5:]
        _, self.NB, self.R, self.D = part.shape
        self.C = self.D // g.S
        self.n = self.NB * g.Z
        self.K = self.ring.shape[0]
        self.tail = tail or (lag if wide else g.nbits * lag + 2 * lag)
        self.after = g.nbits if wide else 0
        self.steps = self.n + self.per + self.tail + lag * (self.after + g.nbits + 1) + 1

    @staticmethod
    def scratch(S, F, NB, R, D, wide=False, K=0):
        Z, nb = F // 2, S.bit_length() - 1
        K = K or NB * Z
        C, n, bf = D // S, NB * Z, jnp.bfloat16
        nx = NB if wide else n
        return [
            pltpu.VMEM((n, R, D), bf), pltpu.VMEM((K, R, D), bf), pltpu.VMEM((nx, 2, R // 2, D - C), bf),
            pltpu.VMEM((NB, Z - 1, R, D if wide else C), bf), pltpu.VMEM((NB, R, D if wide else C), bf),
            DMA((n,)), DMA((1,)), DMA((K,)), DMA((nb,)), DMA((nx, nb)), DMA((1,)), DMA((NB,)),
            DMA((nb,)), DMA((NB, nb)), DMA((1,)), pltpu.SemaphoreType.REGULAR,
        ]

    def fold(self, zz):
        Z = self.g.Z
        return jnp.where(zz < (Z + 1) // 2, 2 * zz, 2 * (Z - 1 - zz) + 1)

    def unfold(self, r):
        return jnp.where(lax.rem(r, 2) == 0, r // 2, self.g.Z - 1 - r // 2)

    def where(self, t):
        Z, per = self.g.Z, self.per
        b, zz = t // Z, self.unfold(lax.rem(t, Z))
        if per:
            rows = t < per * Z
            b, zz = jnp.where(rows, lax.rem(t, per), b), jnp.where(rows, t // per, zz)
        return b, zz

    def item_of(self, b, zz):
        Z, per = self.g.Z, self.per
        t = b * Z + self.fold(zz)
        return jnp.where(b < per, zz * per + b, t) if per else t

    def due(self, v):
        Z, per = self.g.Z, self.per
        ok = (v >= 0) & (v < self.n) & (lax.rem(v, Z) == Z - 1)
        b = v // Z
        if per:
            first = per * Z
            u = v - first + 1
            early = (u >= 0) & (u < per)
            w = v - per
            late = (w >= first) & (w < self.n) & (lax.rem(w, Z) == Z - 1)
            ok = early | late
            b = jnp.where(early, u, w // Z)
        return b, ok

    def cols(self, q):
        return ds(q * self.C, self.C)

    def half(self, p):
        return pl.ds(p * (self.R // 2), self.R // 2)

    def load(self, t):
        b, zz = self.where(t)
        return pltpu.make_async_copy(self.part.at[zz * 2 + self.g.c, b], self.core.at[t], self.own.at[t])

    def swap(self, t):
        b, zz = self.where(t)
        k = lax.rem(t, self.K)
        return remote(self.part.at[zz * 2 + 1 - self.g.c, b], self.ring.at[k], self.c_s.at[0], self.c_r.at[k], self.g.mate)

    def offset(self, j):
        return sum((self.g.S >> (i + 1)) * self.C for i in range(j))

    def halving(self, src, x, p, j):
        g = self.g
        order = g.order[p]
        base = (g.s ^ order[j]) & sum(order[: j + 1])
        to = (g.s ^ order[j], g.f)
        out = []
        for i, m in enumerate(span(order[j + 1 :])):
            dst = self.xb.at[x, p, :, pl.ds(self.offset(j) + i * self.C, self.C)]
            out.append(remote(src.at[self.half(p), self.cols(base | m)], dst, self.x_s.at[j], self.x_r.at[x, j], to))
        return out

    def halved(self, x, j):
        ref = self.xb.at[x, :, :, pl.ds(self.offset(j), (self.g.S >> (j + 1)) * self.C)]
        return remote(ref, ref, self.x_s.at[j], self.x_r.at[x, j], self.g.mate)

    def add_halves(self, buf, x, j):
        g = self.g
        for p in range(2):
            order = g.order[p]
            base = g.s & sum(order[: j + 1])
            for i, m in enumerate(span(order[j + 1 :])):
                q = self.cols(base | m)
                got = self.xb[x, p, :, pl.ds(self.offset(j) + i * self.C, self.C)]
                buf[self.half(p), q] = buf[self.half(p), q] + got

    def piece(self, t, b, zz):
        g = self.g
        src = self.core.at[t] if self.wide else self.core.at[t, :, self.cols(g.s)]
        slot = lax.rem(g.z - zz - 1 + g.Z, g.Z)
        return remote(src, self.zb.at[b, slot], self.z_s.at[0], self.z_r.at[b], g.at(zz))

    def arrived(self, b):
        ref = self.zb.at[b]
        return remote(ref, ref, self.z_s.at[0], self.z_r.at[b], self.g.mate)

    def final(self, b, rows=slice(None)):
        return self.fq.at[b, rows, self.cols(self.g.s)] if self.wide else self.fq.at[b, rows]

    def result(self, b, q, p=None):
        rows, start = (self.R, 0) if p is None else (self.R // 2, p * (self.R // 2))
        if self.above:
            return self.out.at[ds(b * self.R + start, rows), self.cols(q)]
        return self.out.at[pl.ds(start, rows), ds(b * self.D + q * self.C, self.C)]

    def doubling(self, b, p, j):
        g = self.g
        to = (g.s ^ g.order[p][j], g.f)
        out = []
        for m in span(g.order[p][:j]):
            dst = self.result(b, g.s ^ m, p)
            src = self.final(b, self.half(p)) if m == 0 else dst
            out.append(remote(src, dst, self.a_s.at[j], self.a_r.at[b, j], to))
        return out

    def doubled(self, b, j):
        ref = self.out.at[pl.ds(0, self.R), pl.ds(0, self.C << j)]
        return remote(ref, ref, self.a_s.at[j], self.a_r.at[b, j], self.g.mate)

    def stored(self, b):
        return pltpu.make_async_copy(self.final(b), self.result(b, self.g.s), self.o.at[0])

    def ready(self, lo, hi):
        @pl.loop(lo, hi)
        def _(t):
            self.load(t).start()

            @pl.when(t >= self.K)
            def _():
                pl.semaphore_wait(self.free, 1)

            self.swap(t).start()

    def step(self, t):
        g = self.g
        for j in reversed(range(self.after + g.nbits + 1)):
            b, ok = self.due(t - self.tail - self.lag * j)

            @pl.when(ok)
            def _(j=j, b=b):
                if j == 0:
                    self.arrived(b).wait_recv()
                    mine = self.core[self.item_of(b, g.z)] if self.wide else self.core[self.item_of(b, g.z), :, self.cols(g.s)]
                    total = mine.astype(jnp.float32)
                    for k in range(g.Z - 1):
                        total = total + self.zb[b, k].astype(jnp.float32)
                    self.fq[b] = total.astype(self.fq.dtype)
                elif j <= self.after:
                    self.halved(b, j - 1).wait_recv()
                    self.add_halves(self.fq.at[b], b, j - 1)
                else:
                    self.doubled(b, j - self.after - 1).wait_recv()
                if j < self.after:
                    for p in range(2):
                        for cp in self.halving(self.fq.at[b], b, p, j):
                            cp.start()
                elif j < self.after + g.nbits:
                    if j == self.after:
                        self.stored(b).start()
                    for p in range(2):
                        for cp in self.doubling(b, p, j - self.after):
                            cp.start()

        last = 0 if self.wide else g.nbits
        for j in reversed(range(last + 1)):
            u = t - self.lag * j

            @pl.when((u >= 0) & (u < self.n))
            def _(j=j, u=u):
                b, zz = self.where(u)
                buf = self.core.at[u]
                if j == 0:
                    self.load(u).wait()
                    self.swap(u).wait_recv()
                    buf[...] = buf[...] + self.ring[lax.rem(u, self.K)]

                    @pl.when(u + self.K < self.n)
                    def _():
                        pl.semaphore_signal(self.free, inc=1, device_id=g.mate, device_id_type=MESH)
                else:
                    self.halved(u, j - 1).wait_recv()
                    self.add_halves(buf, u, j - 1)
                if j < last:
                    for p in range(2):
                        for cp in self.halving(buf, u, p, j):
                            cp.start()
                else:

                    @pl.when(zz != g.z)
                    def _():
                        self.piece(u, b, zz).start()

    def run(self, lo, hi):
        @pl.loop(lo, hi)
        def _(t):
            self.step(t)

    def finish(self):
        g = self.g

        def done(ref, sem):
            remote(ref, ref, sem, self.z_r.at[0], g.mate).wait_send()

        done(self.core, self.c_s.at[0])
        done(self.zb, self.z_s.at[0])
        for j in range(g.nbits):
            done(self.xb.at[:, :, :, pl.ds(self.offset(j), (g.S >> (j + 1)) * self.C)], self.x_s.at[j])
            done(self.all_of(self.C << j), self.a_s.at[j])
        ref = self.all_of(self.C)
        pltpu.make_async_copy(ref, ref, self.o.at[0]).wait()

    def all_of(self, width):
        return self.out.at[:, pl.ds(0, width if self.above else width * self.NB)]


class VecGather:
    def __init__(self, g, vec, out, sems):
        self.g, self.vec, self.out, self.sems = g, vec, out, sems

    @staticmethod
    def scratch(F):
        return [DMA((3,))]

    def start(self):
        g, sems = self.g, self.sems
        pltpu.make_async_copy(self.vec, self.out.at[g.f], sems.at[2]).start()
        for k in range(1, g.F):
            remote(self.vec, self.out.at[g.f], sems.at[0], sems.at[1], (g.s, lax.rem(g.f + k, g.F))).start()

    def finish(self):
        g, sems = self.g, self.sems
        pltpu.make_async_copy(self.vec, self.out.at[g.f], sems.at[2]).wait()
        ref = self.out.at[pl.ds(0, g.F - 1)]
        cp = remote(ref, ref, sems.at[0], sems.at[1], g.mate)
        cp.wait_send()
        cp.wait_recv()


class VecSum:
    def __init__(self, g, vec, out, refs):
        self.g, self.vec, self.out = g, vec, out
        self.fb, self.mid, self.sb, self.sems = refs

    @staticmethod
    def scratch(S, F, N, L):
        fl = jnp.float32
        return [pltpu.VMEM((F, N, L), fl), pltpu.VMEM((N, L), fl), pltpu.VMEM((S, N, L), fl), DMA((4,))]

    def start(self):
        g = self.g
        for k in range(1, g.F):
            to = lax.rem(g.f + k, g.F)
            remote(self.vec.at[to], self.fb.at[g.f], self.sems.at[0], self.sems.at[1], (g.s, to)).start()

    def middle(self):
        g = self.g
        ref = self.fb.at[pl.ds(0, g.F - 1)]
        cp = remote(ref, ref, self.sems.at[0], self.sems.at[1], g.mate)
        cp.wait_recv()
        total = self.vec[g.f]
        for k in range(1, g.F):
            total = total + self.fb[lax.rem(g.f + k, g.F)]
        self.mid[...] = total
        for k in range(1, g.S):
            remote(self.mid, self.sb.at[g.s], self.sems.at[2], self.sems.at[3], (g.s ^ k, g.f)).start()
        cp.wait_send()

    def finish(self):
        g = self.g
        ref = self.sb.at[pl.ds(0, g.S - 1)]
        cp = remote(ref, ref, self.sems.at[2], self.sems.at[3], g.mate)
        cp.wait_recv()
        total = self.mid[...]
        for k in range(1, g.S):
            total = total + self.sb[g.s ^ k]
        self.out[...] = total
        cp.wait_send()


PARAMS = dict(has_side_effects=True, vmem_limit_bytes=62 * 2**20)


def fp32(x):
    return x.astype(jnp.float32)


def dot(a, b, dims=((1,), (0,))):
    return lax.dot_general(a, b, (dims, ((), ())), preferred_element_type=jnp.float32)


NT = ((1,), (1,))
TN = ((0,), (0,))


def mean_rows(x):
    return jnp.mean(x, axis=-1, keepdims=True)


def head_lanes(rows, hh):
    lane = lax.broadcasted_iota(jnp.int32, (rows, 128), 1)
    mine = (lane >= hh * HEAD_DIM) & (lane < (hh + 1) * HEAD_DIM)
    spare = lane == (1 - hh) * HEAD_DIM
    return mine, spare


def length_of(par, group, slot, V):
    lane = lax.broadcasted_iota(jnp.int32, (1, par.shape[1]), 1)
    value = par[14:15] * 32.0 + par[15:16]
    return jnp.sum(jnp.where(lane == group * V + slot, value, 0.0), axis=1, keepdims=True)


def masked_keys(k, length, hh):
    N = k.shape[0]
    mine, spare = head_lanes(N, hh)
    late = fp32(lax.broadcasted_iota(jnp.int32, (N, 128), 0)) >= length
    return jnp.where(mine, fp32(k), jnp.where(spare & late, NEG_LARGE, 0.0)).astype(jnp.bfloat16)


def scaled_queries(q, hh):
    mine, spare = head_lanes(q.shape[0], hh)
    return jnp.where(mine, fp32(q) * HEAD_DIM ** (-0.5), jnp.where(spare, 1.0, 0.0)).astype(jnp.bfloat16)


def front_kernel(S, F, nwide, QB, img, cot, vec, wq, wx, wu, wd,
                 first_out, rest, par, ub, x1, heads_out, out_t, lse, att, tok_out, cot_out,
                 first, tok, cot_v, fsem, tsem, csem, vec_full, norm, eb, stage, heads, kh, vt, o_buf, asem, hsem, ssem, rsem, osem, *refs):
    slots, piece, D = img.shape
    g = Place(S, F, slots)
    images = g.images
    T = slots * piece // images
    R = first.shape[2]
    V = R
    W = D // g.n
    N = g.n * T
    pairs = W // 128
    tokens = Regroup(g, lambda p: img.at[p], lambda q: tok.at[ds(q * piece, piece)], tsem)
    cots = Regroup(g, lambda p: cot.at[p], lambda q: cot_v.at[ds(q * piece, piece)], csem)
    vg = VecGather(g, vec, vec_full, refs[0])

    def own_first(b, cols):
        if isinstance(cols, slice):
            return wq.at[:, pl.ds(b * D, D)]
        return wq.at[:, pl.ds(pl.multiple_of(b * D + cols.start, 128), cols.size)]

    def own_rest(b0):
        def own(b, cols):
            b = b + b0
            ref, r0, c0 = (wd, b * R, 0) if b < 4 else (wu, 0, (b - 4) * D) if b < 6 else (wx, 0, 0)
            if isinstance(cols, slice):
                return ref.at[pl.ds(r0, R), pl.ds(c0, D)]
            return ref.at[pl.ds(r0, R), pl.ds(pl.multiple_of(c0 + cols.start, 128), cols.size)]

        return own

    entry = Gather(g, 3, 0, own_first, first, refs[1:8], lag=ENTRY_LAG)
    thin = Gather(g, 7 - nwide, nwide, own_rest(nwide), rest, refs[8:15], lag=10)
    wide = Gather(g, nwide, 0, own_rest(0), rest, refs[15:22], wide=True)

    g.meet()
    entry.start()
    tokens.start()
    vg.start()
    rows = min(128, piece)
    entry.kept()
    entry.run(0, entry.nitems)
    tokens.arrived()
    keep_tok = pltpu.make_async_copy(tok, tok_out, fsem.at[1])
    keep_tok.start()

    @pl.loop(0, slots * piece // rows)
    def _(r):
        x = fp32(tok[ds(r * rows, rows)])
        x = x - mean_rows(x)
        norm[ds(r * rows, rows)] = x * lax.rsqrt(mean_rows(x * x) + EPSILON)

    vg.finish()
    thin.start()
    wide.start()
    for f in range(F):
        v = fp32(vec_full[f])[:, :V]
        par[:, f * V : (f + 1) * V] = v
        for r in range(2):
            at = (f * 2 + r) * V
            eb[2 * (at // D), :, at % D : at % D + V] = v[2 + r : 3 + r]
        for r in range(4):
            at = (f * 4 + r) * V
            ub[:, at : at + V] = v[8 + r : 9 + r]
    eb[1] = jnp.zeros((1, D), jnp.float32)
    gain, shift = par[0:1], par[1:2]

    @pl.loop(0, slots * piece // rows)
    def _(r):
        x1[ds(r * rows, rows)] = (norm[ds(r * rows, rows)] * gain + shift).astype(x1.dtype)

    entry.run(entry.nitems, entry.steps)
    thin.kept()
    wide.kept()
    cots.start()
    entry.finish_recv()
    keep_first = pltpu.make_async_copy(first, first_out, fsem.at[0])
    keep_first.start()

    def copy(i, k, j):
        src = stage.at[i, k, j]
        dst = heads.at[j, i, ds(g.me * T, T)]
        return remote(src, dst, ssem.at[i, k, j], rsem.at[i, k, j], g.peer(k))

    def local(i, j):
        return pltpu.make_async_copy(stage.at[i, 0, j], heads.at[j, i, ds(g.me * T, T)], ssem.at[i, 0, j])

    def project(i):
        @pl.loop(0, g.n * 3)
        def _(n):
            k = lax.rem(1 + n // 3, g.n)
            j = lax.rem(n, 3)
            cols = ds((g.me ^ k) * W, W)
            w = first[:, j, :, cols].reshape(D, W)
            out = dot(x1[i * T : (i + 1) * T], w) + eb[j, :, cols]
            stage[i, k, j] = out.astype(stage.dtype)

            @pl.when(k != 0)
            def _():
                copy(i, k, j).start()

            @pl.when(k == 0)
            def _():
                local(i, j).start()

    def projected(i):
        for j in range(3):
            local(i, j).wait()
            for k in range(1, g.n):
                copy(i, k, j).wait_send()
                dst = heads.at[j, i, ds((g.me ^ k) * T, T)]
                remote(dst, dst, ssem.at[i, k, j], rsem.at[i, k, j], g.peer(k)).wait_recv()
        keep_heads(i).start()

    def keep_heads(i):
        return pltpu.make_async_copy(heads.at[:, i], heads_out.at[:, i], hsem.at[i])

    def out_copy(i, hp, kk):
        e = i * pairs + hp
        dst = att.at[i, :, pl.ds(pl.multiple_of(g.me * W + hp * 128, 128), 128)]
        if kk == 0:
            return pltpu.make_async_copy(o_buf.at[e, ds(g.me * T, T)], dst, osem.at[0, e, 0])
        return remote(o_buf.at[e, ds((g.me ^ kk) * T, T)], dst, osem.at[0, e, kk], osem.at[1, e, kk], g.peer(kk))

    def attend(i, hp):
        e = i * pairs + hp
        lanes = slice(hp * 128, (hp + 1) * 128)
        vt[...] = heads[2, i, :, lanes].T
        length = length_of(par, *g.image(i), V)
        for hh in range(2):
            kh[hh] = masked_keys(heads[1, i, :, lanes], length, hh)

        @pl.loop(0, N // QB)
        def _(b):
            cols = ds(b * QB, QB)
            qb = heads[0, i, cols, lanes]
            for hh in range(2):
                sc = dot(kh[hh], scaled_queries(qb, hh), NT)
                top = jnp.max(sc, axis=0, keepdims=True)
                ex = jnp.exp(sc - top)
                total = jnp.sum(ex, axis=0, keepdims=True)
                w = (ex * (1.0 / total)).astype(jnp.bfloat16)
                o = dot(vt[hh * HEAD_DIM : (hh + 1) * HEAD_DIM], w).astype(jnp.bfloat16)
                at = hp * 128 + hh * HEAD_DIM
                out_t[i, at : at + HEAD_DIM, cols] = o
                lse[i, hp, hh : hh + 1, cols] = top + jnp.log(total)
            background(e * (N // QB) + b)

        o_buf[e] = out_t[i, lanes].T
        for kk in list(range(1, g.n)) + [0]:
            out_copy(i, hp, kk).start()

    units = [(i, hp) for i in range(images) for hp in range(pairs)]
    early = thin.steps // EARLY
    per_unit = -(-(thin.steps - early) // (len(units) * (N // QB)))

    def background(n):
        @pl.when(n < wide.steps)
        def _():
            wide.step(n)

        for m in range(per_unit):
            thin.step(early + n * per_unit + m)

    for i in range(images):
        project(i)
    thin.run(0, early)
    entry.finish_send()
    for n, (i, hp) in enumerate(units):
        if hp == 0:
            projected(i)
        attend(i, hp)
    wide.run(len(units) * (N // QB), wide.steps)
    cots.arrived()
    keep_cot = pltpu.make_async_copy(cot_v, cot_out, fsem.at[2])
    keep_cot.start()
    for gather in (thin, wide):
        gather.finish_recv()
        gather.finish_send()
    for i, hp in units:
        for kk in range(g.n):
            cp = out_copy(i, hp, kk)
            if kk == 0:
                cp.wait()
            else:
                cp.wait_send()
                cp.wait_recv()
    for i in range(images):
        keep_heads(i).wait()
    keep_tok.wait()
    keep_first.wait()
    tokens.sent()
    cots.sent()
    keep_cot.wait()


ENTRY_LAG = 12
WIDE = 2
EARLY = 10


def front_call(S, F, cid, img, cot, vec, wq, wx, wu, wd):
    slots, piece, D = img.shape
    M = slots * piece
    n, images = (2, 1) if whole_images(S, slots) else (S, slots)
    T = M // images
    R, FF = wq.shape[0], wu.shape[1]
    W, N = D // n, n * T
    pairs = W // 128
    bf, fl = jnp.bfloat16, jnp.float32
    out = jax.ShapeDtypeStruct
    return pl.pallas_call(
        functools.partial(front_kernel, S, F, WIDE, min(256, N)),
        out_shape=[
            out((F, 3, R, D), bf), out((F, 7, R, D), bf), out((16, D), fl), out((1, FF), fl), out((M, D), bf),
            out((3, images, N, W), bf), out((images, W, N), bf), out((images, pairs, 8, N), fl), out((images, T, D), bf), out((M, D), bf), out((M, D), bf),
        ],
        in_specs=[ANY] * 7,
        out_specs=[ANY, ANY, VM, VM, VM, ANY, VM, VM, ANY, ANY, ANY],
        scratch_shapes=[
            pltpu.VMEM((F, 3, R, D), bf), pltpu.VMEM((M, D), bf), pltpu.VMEM((M, D), bf), DMA((3,)), DMA((2, slots)), DMA((2, slots)),
            pltpu.VMEM((F, 16, 128), bf), pltpu.VMEM((M, D), fl), pltpu.VMEM((3, 1, D), fl), pltpu.VMEM((images, n, 3, T, W), bf),
            pltpu.VMEM((3, images, N, W), bf), pltpu.VMEM((2, N, 128), bf), pltpu.VMEM((128, N), bf),
            pltpu.VMEM((images * pairs, N, 128), bf), DMA((1,)), DMA((images,)), DMA((images, n, 3)), DMA((images, n, 3)),
            DMA((2, images * pairs, n)),
        ]
        + VecGather.scratch(F)
        + Gather.scratch(S, F, 3, R, D, bounce=False)
        + Gather.scratch(S, F, 7 - WIDE, R, D)
        + Gather.scratch(S, F, WIDE, R, D),
        compiler_params=pltpu.CompilerParams(collective_id=cid, **PARAMS),
        name="front",
    )(img, cot, vec, wq, wx, wu, wd)


def rear_kernel(S, F, QB, held, tok, cot, att, par, ub, wu_own, wts, heads, out_t, lse, x1, first,
                layer_out, dx_out, small, part_down, part_a, part_b, g_down, g_up, g_first, back, late,
                layer, dx, msem, cots, vecs, ubg, slab, csem, esem, wsem, psem, hsem, *refs):
    slots, piece, D = layer_out.shape
    g = Place(S, F, slots)
    images = g.images
    M = slots * piece
    T = M // images
    W = D // g.n
    N = g.n * T
    pairs = W // 128
    R = wts.shape[2]
    H = ub.shape[2]
    rows = min(128, piece)
    nrows = M // rows
    exit_bias, scale1, gain2, shift2 = par[4:5], par[5:6], par[6:7], par[7:8]
    down_bias, scale2 = par[12:13], par[13:14]
    per_block = D // H
    bf, fl = jnp.bfloat16, jnp.float32
    down_sum = Scatter(g, part_down, g_down, refs[:16], per=4, lag=LAG, above=True)
    up_a = Scatter(g, part_a, g_up.at[:, pl.ds(0, 2 * D)], refs[16:32], wide=True, lag=4, tail=UP_TAIL)
    up_b = Scatter(g, part_b, g_up.at[:, pl.ds(2 * D, 2 * D)], refs[32:48], lag=LAG)
    vsum = VecSum(g, slab, small, refs[64:68])

    def own_late(b, cols):
        if isinstance(cols, slice):
            return wu_own.at[:, pl.ds((2 + b) * D, D)]
        return wu_own.at[:, pl.ds(pl.multiple_of((2 + b) * D + cols.start, 128), cols.size)]

    more = Gather(g, 2, 0, own_late, late, refs[68:75])
    units = images * pairs
    part_of = lambda ref: lambda p: ref.at[ds(p * piece, piece)]
    layers = Regroup(g, part_of(layer), lambda q: layer_out.at[q], msem.at[1], back=True)
    chunks = F // 4

    def place(r):
        return r // (T // rows), lax.rem(r, T // rows) * rows

    def mask(r):
        i, t = place(r)
        group, slot = g.image(i)
        limit = jnp.where(slot < held[group], length_of(par, group, slot, R), 0.0)
        pos = lax.broadcasted_iota(jnp.int32, (rows, 1), 0) + (g.me * T + t)
        return jnp.where(fp32(pos) < limit, 1.0, 0.0)

    def upstream(r):
        return mask(r) * fp32(cot[ds(r * rows, rows)])

    def cot_copies(stage, k):
        for i in range(images):
            src, dst = stage.at[pl.ds(i * T, T), pl.ds(k * W, W)], cots.at[i, ds(g.me * T, T)]
            if k == 0:
                yield pltpu.make_async_copy(src, dst, csem.at[0, 0])
            else:
                yield remote(src, dst, csem.at[0, k], csem.at[1, k], g.peer(k))

    def feed_forward(mixed, x2, x2t, dcot, down, cot2, wu, wd, wx, dwu, dwd):
        def up_load(j):
            cols = pl.ds(pl.multiple_of(lax.rem(j, per_block) * H, H), H)
            slot = lax.rem(j, 2)
            block = j // per_block
            soon = pltpu.make_async_copy(wts.at[:, 4 + jnp.minimum(block, 1), :, cols], wu.at[slot], wsem.at[0, slot])
            return soon, pltpu.make_async_copy(late.at[:, jnp.maximum(block - 2, 0), :, cols], wu.at[slot], wsem.at[0, slot])

        def start_either(j, copies):
            soon, later = copies

            @pl.when(j < F // 2)
            def _():
                soon.start()

            @pl.when(j >= F // 2)
            def _():
                later.start()

        def down_load(j):
            return pltpu.make_async_copy(wts.at[j, pl.ds(0, 4)], wd.at[lax.rem(j, 2)], wsem.at[1, lax.rem(j, 2)])

        def put_up(j):
            cols = pl.ds(pl.multiple_of(lax.rem(j, per_block) * H, H), H)
            block = j // per_block
            soon = pltpu.make_async_copy(dwu, part_a.at[:, jnp.minimum(block, 1), :, cols], psem.at[0])
            return soon, pltpu.make_async_copy(dwu, part_b.at[:, jnp.maximum(block - 2, 0), :, cols], psem.at[0])

        def put_down(j):
            return pltpu.make_async_copy(dwd, part_down.at[j, pl.ds(0, 4)], psem.at[1])

        x_load = pltpu.make_async_copy(wts.at[:, 6], wx, wsem.at[2, 0])
        x_load.start()
        start_either(0, up_load(0))
        down_load(0).start()
        x_load.wait()
        mixed[...] = dot(att[...], wx[...].reshape(D, D)) + exit_bias

        def residual(r, sl):
            return fp32(tok[sl]) + scale1 * mixed[sl]

        hello()
        more.start()

        def norm(res):
            res = res - mean_rows(res)
            inv = lax.rsqrt(mean_rows(res * res) + EPSILON)
            return res * inv, inv

        @pl.loop(0, nrows)
        def _(r):
            sl = ds(r * rows, rows)
            n, _ = norm(residual(r, sl))
            x2[sl] = (n * gain2 + shift2).astype(bf)
            dcot[sl] = (upstream(r) * scale2).astype(bf)

        x2t[...] = x2[...].T
        more.kept()
        down[...] = jnp.zeros_like(down)
        cot2[...] = jnp.zeros_like(cot2)

        @pl.loop(0, F)
        def _(j):
            slot = lax.rem(j, 2)
            every = -(-more.steps // (F // 2 - 1))

            @pl.when(j < F // 2 - 1)
            def _():
                more.run(j * every, (j + 1) * every)

            @pl.when(j == F // 2 - 1)
            def _():
                more.finish_recv()

            @pl.when(j + 1 < F)
            def _():
                start_either(j + 1, up_load(j + 1))
                down_load(j + 1).start()

            up_load(j)[0].wait()
            down_load(j).wait()
            wu_j = wu[slot].reshape(D, H)
            wd_j = wd[slot].reshape(H, D)
            pre = dot(x2[...], wu_j) + ub[j]
            cumul = 0.5 * (1.0 + lax.erf(pre * (1.0 / math.sqrt(2.0))))
            density = jnp.exp(-0.5 * pre * pre) * (1.0 / math.sqrt(2.0 * math.pi))
            act = (pre * cumul).astype(bf)
            slope = cumul + pre * density
            pre_cot = dot(dcot[...], wd_j, NT) * slope
            ubg[j] = jnp.sum(pre_cot, axis=0, keepdims=True)
            low = pre_cot.astype(bf)
            @pl.when(j > 0)
            def _():
                put_up(j - 1)[0].wait()
                put_down(j - 1).wait()

            @pl.when((j > 0) & (lax.rem(j, chunks) == 0))
            def _():
                n = (j // chunks - 1) * g.Z
                @pl.when(j <= 2 * chunks)
                def _():
                    up_a.ready(n, n + g.Z)

                @pl.when(j > 2 * chunks)
                def _():
                    up_b.ready(n - 2 * g.Z, n - g.Z)

                down_sum.ready(n, n + g.Z)

            dwu[...] = dot(x2t[...], low).astype(bf).reshape(F, R, H)
            dwd[...] = dot(act, dcot[...], TN).astype(bf).reshape(4, R, D)
            start_either(j, put_up(j))
            put_down(j).start()
            down[...] += dot(act, wd_j)
            cot2[...] += dot(low, wu_j, NT)

            @pl.when((j > 0) & (lax.rem(j, chunks) == 1))
            def _():
                first = (j // chunks - 1) * g.Z

                @pl.when(first >= 0)
                def _():
                    @pl.when(first < 2 * g.Z)
                    def _():
                        up_a.run(first, first + g.Z)

                    @pl.when(first >= 2 * g.Z)
                    def _():
                        up_a.run(first, first + g.Z)
                        up_b.run(first - 2 * g.Z, first - g.Z)

                    down_sum.run(first, first + g.Z)

        put_up(F - 1)[0].wait()
        put_down(F - 1).wait()
        n = 3 * g.Z
        up_b.ready(n - 2 * g.Z, n - g.Z)
        down_sum.ready(n, n + g.Z)
        vecs[...] = jnp.zeros_like(vecs)

        @pl.loop(0, nrows)
        def _(r):
            sl = ds(r * rows, rows)
            m = mask(r)
            up = upstream(r)
            out = down[sl] + down_bias
            res = residual(r, sl)
            layer[sl] = (m * (res + scale2 * out)).astype(bf)
            n, inv = norm(res)
            c2 = cot2[sl]
            c = c2 * gain2
            rc = up + inv * (c - mean_rows(c) - n * mean_rows(c * n))
            dx[sl] = rc
            mc = rc * scale1
            x2[sl] = mc.astype(bf)
            total = lambda v: jnp.sum(v, axis=0, keepdims=True)
            vecs[0:1] += total(up * out)
            vecs[1:2] += total(up * scale2)
            vecs[2:3] += total(c2 * n)
            vecs[3:4] += total(c2)
            vecs[4:5] += total(rc * mixed[sl])
            vecs[5:6] += total(mc)

        for k in list(range(1, g.n)) + [0]:
            dcot[:, k * W : (k + 1) * W] = dot(x2[...], wx_rows(wx, g.me ^ k, W), NT).astype(bf)
            for cp in cot_copies(dcot, k):
                cp.start()
        for n in range(F // 4):
            at = n * 4 * R
            dwd[...] = dot(att[:, at : at + 4 * R], x2[...], TN).astype(bf).reshape(4, R, D)
            put_x = pltpu.make_async_copy(dwd, part_down.at[pl.ds(n * 4, 4), 4], psem.at[2])
            put_x.start()
            put_x.wait()
        down_sum.ready(4 * g.Z, 5 * g.Z)
        layers.start()
        for cp in cot_copies(dcot, 0):
            cp.wait()
        ref = dcot.at[:, pl.ds(0, W)]
        for k in range(1, g.n):
            remote(ref, ref, csem.at[0, k], csem.at[1, k], g.mate).wait_send()

    polls = units * (N // QB)

    def background(n):
        t = 3 * g.Z + n // EVERY

        @pl.when(lax.rem(n, EVERY) == 0)
        def _():
            step_all(t)

    def step_all(t):
        up_a.step(t)
        up_b.step(t - 2 * g.Z)
        down_sum.step(t)

    def attend_back(hd, ot, ls, kh, vh, kt, cot_t, delta, dq_t, dk, dv, stage):
        loads = [pltpu.make_async_copy(a, b, hsem.at[n]) for n, (a, b) in enumerate(((heads, hd), (out_t, ot), (lse, ls)))]
        for cp in loads:
            cp.start()
        for k in range(1, g.n):
            ref = cots.at[:, ds((g.me ^ k) * T, T)]
            remote(ref, ref, csem.at[0, k], csem.at[1, k], g.peer(k)).wait_recv()
        for cp in loads:
            cp.wait()

        def copy(e, j, kk):
            i, hp = e // pairs, lax.rem(e, pairs)
            dst = back.at[i, :, ds(j * D + g.me * W + hp * 128, 128)]
            src = stage.at[e, j, ds((g.me ^ kk) * T, T)]
            if kk == 0:
                return pltpu.make_async_copy(src, dst, esem.at[2])
            return remote(src, dst, esem.at[0], esem.at[1], g.peer(kk))

        @pl.loop(0, units)
        def _(e):
            i, hp = e // pairs, lax.rem(e, pairs)
            lanes = ds(hp * 128, 128)
            length = length_of(par, *g.image(i), R)
            kt[...] = hd[1, i, :, lanes].T
            cot_t[...] = cots[i, :, lanes].T
            prod = fp32(cot_t[...]) * fp32(ot[i, lanes])
            for hh in range(2):
                hs = slice(hh * HEAD_DIM, (hh + 1) * HEAD_DIM)
                delta[hh : hh + 1] = jnp.sum(prod[hs], axis=0, keepdims=True)
                kh[hh] = masked_keys(hd[1, i, :, lanes], length, hh)
                mine, _ = head_lanes(N, hh)
                vh[hh] = jnp.where(mine, fp32(hd[2, i, :, lanes]), 0.0).astype(bf)
            dk[...] = jnp.zeros_like(dk)
            dv[...] = jnp.zeros_like(dv)

            @pl.loop(0, N // QB)
            def _(b):
                cols = ds(b * QB, QB)
                qb, cb = hd[0, i, cols, lanes], cots[i, cols, lanes]
                for hh in range(2):
                    hs = slice(hh * HEAD_DIM, (hh + 1) * HEAD_DIM)
                    mine, _ = head_lanes(QB, hh)
                    qs = scaled_queries(qb, hh)
                    prob = jnp.exp(dot(kh[hh], qs, NT) - ls[i, hp, hh : hh + 1, cols])
                    sg = dot(vh[hh], cb, NT)
                    sc = (prob * (sg - delta[hh : hh + 1, cols])).astype(bf)
                    w = prob.astype(bf)
                    dv[...] += dot(w, jnp.where(mine, fp32(cb), 0.0).astype(bf))
                    dk[...] += dot(sc, jnp.where(mine, fp32(qs), 0.0).astype(bf))
                    dq_t[hs, cols] = (dot(kt[hs], sc) * HEAD_DIM ** (-0.5)).astype(bf)
                background(e * (N // QB) + b)

            stage[e, 0] = dq_t[...].T
            stage[e, 1] = dk[...].astype(bf)
            stage[e, 2] = dv[...].astype(bf)
            for j in range(3):
                for kk in list(range(1, g.n)) + [0]:
                    copy(e, j, kk).start()

        ref = stage.at[:, :, pl.ds(0, (g.n - 1) * T)]
        cp = remote(ref, ref, esem.at[0], esem.at[1], g.mate)
        cp.wait_send()
        cp.wait_recv()
        ref = stage.at[:, :, pl.ds(0, T)]
        pltpu.make_async_copy(ref, ref, esem.at[2]).wait()

    def entry(part, ein, win, x1v, x1t, acc, rows_v, dxl):
        grads = Regroup(g, part_of(dxl), lambda q: dx_out.at[q], msem.at[2], back=True)
        entry_sum = Scatter(g, part, g_first, refs[48:64])
        loads = [pltpu.make_async_copy(back.at[:, :, pl.ds(j * D, D)], ein.at[j], hsem.at[j]) for j in range(3)]
        weights = [pltpu.make_async_copy(first.at[:, j], win.at[j % 2], wsem.at[2, j % 2]) for j in range(3)]
        x_load = pltpu.make_async_copy(x1, x1v, wsem.at[0, 0])
        for cp in [x_load] + loads + weights[:2]:
            cp.start()
        x_load.wait()
        x1t[...] = x1v[...].T
        at = 3 * g.Z + polls // EVERY

        def others(n, k):
            for t in range(at + n, at + n + k):
                step_all(t)

        rows_v[...] = jnp.zeros_like(rows_v)
        cot_of = lambda j: ein[j].reshape(M, D)
        for j in range(3):
            loads[j].wait()
            part[:, j] = dot(x1t[...], cot_of(j)).astype(bf).reshape(F, R, D)
            if j:
                entry_sum.run((j - 1) * g.Z, j * g.Z)
            entry_sum.ready(j * g.Z, (j + 1) * g.Z)
            others(2 * j, 2)
        for j in range(3):
            weights[j].wait()
            d = dot(cot_of(j), win[j % 2].reshape(D, D), NT)
            if j == 0:
                weights[2].start()
                acc[...] = d
            else:
                acc[...] += d
            others(6 + 2 * j, 2)
            entry_sum.run(2 * g.Z + j, 2 * g.Z + j + 1)
        rows_v[2:3] = jnp.sum(fp32(cot_of(0)), axis=0, keepdims=True)
        rows_v[3:4] = jnp.sum(fp32(cot_of(2)), axis=0, keepdims=True)
        gain = par[0:1]

        @pl.loop(0, nrows)
        def _(r):
            sl = ds(r * rows, rows)
            x = fp32(tok[sl])
            x = x - mean_rows(x)
            inv = lax.rsqrt(mean_rows(x * x) + EPSILON)
            n = x * inv
            d1 = acc[sl]
            c = d1 * gain
            dxl[sl] = (dx[sl] + inv * (c - mean_rows(c) - n * mean_rows(c * n))).astype(bf)
            rows_v[0:1] += jnp.sum(d1 * n, axis=0, keepdims=True)
            rows_v[1:2] += jnp.sum(d1, axis=0, keepdims=True)
            entry_sum.step(2 * g.Z + 3 + r)

        grads.start()
        slab[...] = jnp.zeros_like(slab)
        own = [(0, rows_v, 0), (1, rows_v, 1), (4, vecs, 5), (5, vecs, 4), (6, vecs, 2), (7, vecs, 3), (12, vecs, 1), (13, vecs, 0)]
        V = R
        for f in range(F):
            for to, src, r in own:
                slab[f, to : to + 1, :V] = src[r : r + 1, f * V : (f + 1) * V]
            for r in range(2):
                p = (f * 2 + r) * V
                slab[f, 2 + r : 3 + r, :V] = rows_v[2 + p // D : 3 + p // D, p % D : p % D + V]
            for r in range(4):
                slab[f, 8 + r : 9 + r, :V] = ubg[f, :, r * V : (r + 1) * V]
        vsum.start()
        mark = 2 * g.Z + 3 + nrows
        entry_sum.run(mark, mark + 4)
        vsum.middle()
        left = max(down_sum.steps, up_a.steps, up_b.steps + 2 * g.Z) - (at + 12)

        @pl.loop(0, max(left, entry_sum.steps - mark - 4))
        def _(t):
            step_all(at + 12 + t)
            entry_sum.step(mark + 4 + t)

        entry_sum.finish()
        grads.arrived()
        grads.sent()

    hello = g.greet()
    v = pltpu.VMEM
    pl.run_scoped(
        feed_forward, v((M, D), fl), v((M, D), bf), v((D, M), bf), v((M, D), bf), v((M, D), fl), v((M, D), fl),
        v((2, F, R, H), bf), v((2, 4, R, D), bf), v((F, R, D), bf), v((F, R, H), bf), v((4, R, D), bf),
    )
    pl.run_scoped(
        attend_back, v((3, images, N, W), bf), v((images, W, N), bf), v((images, pairs, 8, N), fl), v((2, N, 128), bf),
        v((2, N, 128), bf), v((128, N), bf), v((128, N), bf), v((8, N), fl), v((128, N), bf), v((N, 128), fl),
        v((N, 128), fl), v((units, 3, N, 128), bf),
    )
    pl.run_scoped(
        entry, v((F, 3, R, D), bf), v((3, images, T, D), bf), v((2, F, R, D), bf), v((M, D), bf), v((D, M), bf),
        v((M, D), fl), v((8, D), fl), v((M, D), bf),
    )
    up_a.finish()
    up_b.finish()
    down_sum.finish()
    vsum.finish()
    more.finish_send()
    layers.arrived()
    layers.sent()


def wx_rows(wx, peer, W):
    F, R, D = wx.shape
    n = W // R
    return wx[pl.ds(peer * n, n)].reshape(W, D)


LAG = 4
UP_TAIL = 13
EVERY = 2


def rear_call(S, F, cid, slots, held, tok, cot, att, par, ub, wu_own, wts, heads, out_t, lse, x1, first):
    M, D = cot.shape
    piece = M // slots
    n, images = (2, 1) if whole_images(S, slots) else (S, slots)
    T = M // images
    R = wts.shape[2]
    FF = ub.shape[1]
    H = FF // F
    W, N = D // n, n * T
    bf, fl = jnp.bfloat16, jnp.float32
    SM = pl.BlockSpec(memory_space=pltpu.SMEM)
    out, v = jax.ShapeDtypeStruct, pltpu.VMEM
    return pl.pallas_call(
        functools.partial(rear_kernel, S, F, min(256, N)),
        out_shape=[
            out((slots, piece, D), bf), out((slots, piece, D), bf), out((16, 128), fl), out((F, 5, R, D), bf), out((F, 2, R, D), bf), out((F, 2, R, D), bf),
            out((5 * R, D), bf), out((R, 4 * D), bf), out((R, 3 * D), bf), out((images, T, 3 * D), bf), out((F, 2, R, D), bf),
        ],
        in_specs=[SM, VM, VM, VM, VM, VM] + [ANY] * 7,
        out_specs=[ANY, ANY, VM] + [ANY] * 8,
        scratch_shapes=[v((M, D), bf), v((M, D), fl), DMA((3, 2, slots)), v((images, N, W), bf), v((8, D), fl), v((F, 1, H), fl), v((F, 16, 128), fl),
                        DMA((2, n)), DMA((3,)), DMA((3, 2)), DMA((3,)), DMA((3,))]
        + Scatter.scratch(S, F, 5, R, D, K=F)
        + Scatter.scratch(S, F, 2, R, D, wide=True, K=F // 2)
        + Scatter.scratch(S, F, 2, R, D, K=F // 2)
        + Scatter.scratch(S, F, 3, R, D, K=F // 2)
        + VecSum.scratch(S, F, 16, 128)
        + Gather.scratch(S, F, 2, R, D),
        compiler_params=pltpu.CompilerParams(collective_id=cid, **PARAMS),
        name="rear",
    )(held, tok, cot, att, par, ub.reshape(F, 1, H), wu_own, wts, heads, out_t, lse, x1, first)


def body(S, F, images, out_grad, lengths, images_held, first_gain, first_shift, entry_weight, entry_bias, exit_weight,
         exit_bias, first_scale, second_gain, second_shift, up_weight, up_bias, down_weight, down_bias, second_scale):
    slots, T, D = images.shape
    M = slots * T
    R = entry_weight.shape[0]
    FF = up_weight.shape[1]
    fl = jnp.float32
    V = R
    rows = [first_gain, first_shift, entry_bias, exit_bias, first_scale, second_gain, second_shift, up_bias, down_bias, second_scale]
    own_vec, at = jnp.zeros((16, 128), jnp.bfloat16), 0
    for v in rows:
        n = v.shape[0] // V
        own_vec = own_vec + jnp.pad(v.reshape(n, V), ((at, 16 - at - n), (0, 128 - V)))
        at += n
    for v in (lengths // 32, lengths % 32):
        own_vec = own_vec + jnp.pad(v.astype(jnp.bfloat16).reshape(1, slots), ((at, 15 - at), (0, 128 - slots)))
        at += 1
    first, rest, par, ub, x1, heads, out_t, lse, att, tok, cot = front_call(
        S, F, 0, images, out_grad, own_vec, entry_weight, exit_weight, up_weight, down_weight
    )
    layer, dx, small, _, _, _, g_down, g_up, g_first, _, _ = rear_call(
        S, F, 1, slots, images_held, tok, cot, att.reshape(M, D), par, ub, up_weight, rest, heads, out_t, lse, x1, first
    )
    vectors = [v.shape[0] for v in rows]
    down, exit_, up, first, dx, layer, *small = results_call(V, g_down, g_up, g_first, dx, layer, small, vectors)
    return (
        layer.reshape(slots, T, D), dx.reshape(slots, T, D), small[0], small[1], first, small[2], exit_, small[3], small[4],
        small[5], small[6], up, small[7], down, small[8], small[9],
    )


def results_kernel(V, down, out, up, first, dx, layer, small, *outs):
    for src, dst in zip((down, out, up, first, dx, layer), outs):
        dst[...] = src[...].astype(dst.dtype)

    @pl.when(pl.program_id(0) == 0)
    def _():
        at = 0
        for dst in outs[6:]:
            n = dst.shape[0] // V
            for r in range(n):
                dst[r * V : (r + 1) * V] = small[at + r, :V]
            at += n


def results_call(V, g_down, g_up, g_first, dx, layer, small, vectors):
    slots, T, D = dx.shape
    R = g_up.shape[0]
    steps = min(8, R // 16)
    fl = jnp.float32
    out = jax.ShapeDtypeStruct
    q = R // steps
    t = slots * T // steps
    row = lambda n, width, first=0: pl.BlockSpec((n, width), lambda i: (first + i, 0))
    whole = lambda *shape: pl.BlockSpec(shape, lambda i: (0,) * len(shape))
    tokens = (slots * T, D)
    res = pl.pallas_call(
        functools.partial(results_kernel, V),
        grid=(steps,),
        out_shape=[out((4 * R, D), fl), out((R, D), fl), out(g_up.shape, fl), out(g_first.shape, fl), out(tokens, fl),
                   out(tokens, layer.dtype)] + [out((n,), fl) for n in vectors],
        in_specs=[row(4 * q, D), row(q, D, 4 * steps), row(q, 4 * D), row(q, 3 * D), row(t, D), row(t, D), whole(16, 128)],
        out_specs=[row(4 * q, D), row(q, D), row(q, 4 * D), row(q, 3 * D), row(t, D), row(t, D)] + [whole(n) for n in vectors],
        compiler_params=pltpu.CompilerParams(vmem_limit_bytes=62 * 2**20),
        name="results",
    )(g_down, g_down, g_up, g_first, dx.reshape(tokens), layer.reshape(tokens), small)
    return res


def solution(mesh):
    S, F = mesh.shape["seq"], mesh.shape["fsdp"]
    vector, matrix, tokens = P("fsdp"), P("fsdp", None), P("fsdp", "seq", None)
    return jax.shard_map(
        functools.partial(body, S, F),
        mesh=mesh,
        in_specs=(tokens, tokens, vector, P(), vector, vector, matrix, vector, matrix, vector, vector, vector, vector,
                  matrix, vector, matrix, vector, vector),
        out_specs=(tokens, tokens, vector, vector, matrix, vector, matrix, vector, vector, vector, vector, matrix, vector,
                   matrix, vector, vector),
        check_vma=False,
    )
```
